32 devices in a mesh: batch: 2 (over x), seq: 4 (over y, core), head: 4 (over z).
Axes of the slice: x: 2, y: 2, z: 4, core: 2. Of those that a mesh axis runs over, the one named last changes fastest.
Arguments:
- tokens: bfloat16 [2, 4, 512, 768], P(None, 'batch', 'seq'), may hold values from -6 to 6
- spatial: bfloat16 [4, 512, 768], P('batch', 'seq'), may hold values from -6 to 6
- positions: int32 [4, 512], P('batch', 'seq'), may hold values from 0 to 511, each once within a row
- boxes: int32 [2, 4, 512], P(None, 'batch', 'seq'), may hold values from 0 to 127
- query_key_value_weight: bfloat16 [2, 3, 768, 768], P(None, None, None, 'head'), may hold values from -0.21875 to 0.21875
- w_spatial: bfloat16 [2, 768, 768], P(None, None, 'head'), may hold values from -0.21875 to 0.21875
- rel_tables: float32 [2, 3, 12, 128], P(None, None, 'head'), may hold values from -3 to 3
- exit_matrix: bfloat16 [2, 768, 768], P(None, 'head'), may hold values from -1.75 to 1.75
- ln_gains: float32 [2, 2, 768], replicated, may hold values from 0.1 to 1.9
- ln_shifts: float32 [2, 2, 768], replicated, may hold values from -2 to 2
- up_weight: bfloat16 [2, 768, 3072], P(None, None, 'head'), may hold values from -0.21875 to 0.21875
- hidden_bias: float32 [2, 3072], P(None, 'head'), may hold values from -3 to 3
- shrink_projection_array: bfloat16 [2, 3072, 768], P(None, 'head'), may hold values from -0.109375 to 0.109375
- b_down: float32 [2, 768], replicated, may hold values from -2 to 2
- cotangent: bfloat16 [2, 4, 512, 768], P(None, 'batch', 'seq'), may hold values from -6 to 6
Outputs:
- output: bfloat16 [2, 4, 512, 768], P(None, 'batch', 'seq')
- grad_tokens: float32 [2, 4, 512, 768], P(None, 'batch', 'seq')
- grad_spatial: float32 [4, 512, 768], P('batch', 'seq')
- grad_qkv: float32 [2, 3, 768, 768], P(None, None, None, 'head')
- grad_spatial_w: float32 [2, 768, 768], P(None, None, 'head')
- grad_tables: float32 [2, 3, 12, 128], P(None, None, 'head')
- output_weight_gradient: float32 [2, 768, 768], P(None, 'head')
- grad_gains: float32 [2, 2, 768], P(None, None, 'head')
- grad_shifts: float32 [2, 2, 768], P(None, None, 'head')
- grad_up: float32 [2, 768, 3072], P(None, None, 'head')
- grad_b_up: float32 [2, 3072], P(None, 'head')
- grad_down: float32 [2, 3072, 768], P(None, 'head')
- grad_b_down: float32 [2, 768], P(None, 'head')
The draws below stay inside these ranges and needn't reach their ends.
Inputs may be any that keep to these rules, and one draw needn't show every extreme that they name: `positions`: each page's row holds every reading position from 0 to 511 once.
All inputs are finite; a program needn't handle non-finite values.
Results may differ from the reference program's by a relative error of at most 0.02.
Values may be sent and summed in bfloat16 or wider, within the bound.
No kernel may reach another device: no remote copies, remote signals or barrier semaphores. Data moves between devices by JAX's collectives and lax.ppermute only.
A program may use at most 128 MiB of HBM per device.

```python
import jax
import jax.numpy as jnp
from jax import lax

D = 768
HEADS = 12
DH = 64
FF = 3072
L = 512
NBUCK = 128
PAGES = 4
HALF = 64


def touch_ends(values, rng, least, high):
    index_at = [jax.random.randint(jax.random.fold_in(rng, axis), (), 0, length) for axis, length in enumerate(values.shape)]
    main_axis = values.shape.index(max(values.shape))
    neighbour = index_at[:main_axis] + [(index_at[main_axis] + 1) % values.shape[main_axis]] + index_at[main_axis + 1:]
    return values.at[tuple(index_at)].set(least).at[tuple(neighbour)].set(high)


def steps_of(key, extent, pieces, least, top_value):
    def one(axis_at, parts):
        steps = jax.random.uniform(jax.random.fold_in(jax.random.fold_in(key, 6), axis_at), (parts,), jnp.float32, least / len(pieces), top_value / len(pieces))
        return jnp.repeat(jnp.exp(steps), extent[axis_at] // parts).reshape((-1,) + (1,) * (len(extent) - axis_at - 1))

    level = one(*pieces[0])
    for cut in pieces[1:]:
        level = level * one(*cut)
    return level


def scatter_about(key, dims, width, most, pieces=(), held_as=jnp.bfloat16):
    level = steps_of(key, dims, pieces, -0.22, 0.18) if pieces else 1.0
    result = jax.random.normal(key, dims, jnp.float32) * width * level
    return jnp.minimum(jnp.maximum(result, -most), most).astype(held_as)


def setup_inputs(seed: int = 0) -> dict:
    splits = jax.random.split(jax.random.key(seed), 16)
    return {
        "tokens": scatter_about(splits[0], (2, PAGES, L, D), 1.0, 6.0, ((1, 2), (2, 4))),
        "spatial": scatter_about(splits[1], (PAGES, L, D), 1.0, 6.0, ((0, 2), (1, 4))),
        "positions": jax.vmap(lambda own: jax.random.permutation(own, L))(jax.random.split(splits[2], PAGES)).reshape((PAGES, L)).astype(jnp.int32),
        "boxes": touch_ends(jax.random.randint(splits[3], (2, PAGES, L), 0, NBUCK), jax.random.fold_in(splits[3], 1), 0, NBUCK - 1).astype(jnp.int32),
        "query_key_value_weight": scatter_about(splits[4], (2, 3, D, D), D ** -0.5, 0.21875, ((3, 4),)),
        "w_spatial": scatter_about(splits[5], (2, D, D), D ** -0.5, 0.21875, ((2, 4),)),
        "rel_tables": scatter_about(splits[6], (2, 3, HEADS, NBUCK), 0.5, 3.0, ((2, 4),), jnp.float32),
        "exit_matrix": scatter_about(splits[7], (2, D, D), (D // 64) ** -0.5, 1.75, ((1, 4),)),
        "ln_gains": jnp.clip(1.0 + 0.18 * jax.random.normal(splits[8], (2, 2, D), jnp.float32), 0.1, 1.9),
        "ln_shifts": scatter_about(splits[9], (2, 2, D), 0.3, 2.0, (), jnp.float32),
        "up_weight": scatter_about(splits[10], (2, D, FF), D ** -0.5, 0.21875, ((2, 4),)),
        "hidden_bias": scatter_about(splits[11], (2, FF), 0.5, 3.0, ((1, 4),), jnp.float32),
        "shrink_projection_array": scatter_about(splits[12], (2, FF, D), FF ** -0.5, 0.109375, ((1, 4),)),
        "b_down": scatter_about(splits[13], (2, D), 0.3, 2.0, (), jnp.float32),
        "cotangent": scatter_about(splits[14], (2, PAGES, L, D), 1.0, 6.0, ((1, 2), (2, 4))),
    }


EPSILON = 1e-05
precise_product = lax.Precision.HIGHEST

@jax.custom_vjp
def reduced_precision(v):
    return lax.optimization_barrier(v.astype(jnp.bfloat16)).astype(jnp.float32)

@jax.custom_vjp
def reduced_backward(v):
    return v

def low_keep(v):
    return (reduced_precision(v), None)

def low_pass(kept, grad):
    return (grad,)

def retained_for_reverse(v):
    return (v, None)

def back_low(kept, grad):
    return (reduced_precision(grad),)
reduced_precision.defvjp(low_keep, low_pass)
reduced_backward.defvjp(retained_for_reverse, back_low)

def norm_rows(row_data, gain_row, shift_row):
    centre = row_data - lax.optimization_barrier(jnp.mean(row_data, axis=-1, keepdims=True))
    spread = lax.optimization_barrier(jnp.mean(centre * centre, axis=-1, keepdims=True))
    return centre * lax.rsqrt(spread + EPSILON) * gain_row + shift_row

def bucket(query_place, key_place):
    return jnp.clip(key_place[None, :] - query_place[:, None], -HALF, HALF - 1) + HALF

def page_layer(token_page_rows, page_spatial, page_places, page_boxes, params):
    query_key_value_weight, w_spatial, rel_tables, exit_matrix, ln_gains, ln_shifts, up_weight, hidden_bias, shrink_projection_array, b_down = params
    score_scale = DH ** (-0.5)
    projected_rows = reduced_precision(reduced_backward(jnp.einsum('qwb,qybf->qywf', token_page_rows, query_key_value_weight, precision=precise_product)))
    spatial_qk = reduced_precision(reduced_backward(jnp.einsum('ld,kde->kle', page_spatial, w_spatial, precision=precise_product)))
    head_split = projected_rows.reshape(2, 3, L, HEADS, DH)
    spatial_heads = spatial_qk.reshape(2, L, HEADS, DH)
    plain_part = jnp.einsum('sihd,sjhd->shij', head_split[:, 0], head_split[:, 1], precision=precise_product)
    shared_part = jnp.einsum('ihd,jhd->hij', spatial_heads[0], spatial_heads[1], precision=precise_product)
    first_index = bucket(page_places, page_places)
    second_index = bucket(page_boxes[0], page_boxes[0])
    third_index = bucket(page_boxes[1], page_boxes[1])
    bias_sum = rel_tables[:, 0][:, :, first_index] + rel_tables[:, 1][:, :, second_index] + rel_tables[:, 2][:, :, third_index]
    scores = reduced_backward((plain_part + shared_part[None]) * score_scale + bias_sum)
    soft = jax.nn.softmax(scores, axis=-1)
    attended_values = jnp.einsum('shij,sjhd->sihd', reduced_precision(soft), head_split[:, 2], precision=precise_product).reshape(2, L, D)
    attended_values = reduced_precision(reduced_backward(attended_values))
    mixed = reduced_backward(jnp.einsum('sle,sed->ld', attended_values, exit_matrix, precision=precise_product))
    normalized_rows = norm_rows(token_page_rows + mixed[None], ln_gains[:, 0][:, None, :], ln_shifts[:, 0][:, None, :])
    upper_half = reduced_backward(jnp.einsum('uxt,utw->uxw', reduced_precision(normalized_rows), up_weight, precision=precise_product) + hidden_bias[:, None, :])
    nonzero_neurons = reduced_precision(jax.nn.gelu(upper_half, approximate=False))
    reduced_input = reduced_backward(jnp.einsum('jke,jeh->jkh', nonzero_neurons, shrink_projection_array, precision=precise_product))
    return norm_rows(normalized_rows + reduced_input + b_down[:, None, :], ln_gains[:, 1][:, None, :], ln_shifts[:, 1][:, None, :])

def reference(tokens, spatial, positions, boxes, query_key_value_weight, w_spatial, rel_tables, exit_matrix, ln_gains, ln_shifts, up_weight, hidden_bias, shrink_projection_array, b_down, cotangent):

    def forward(tokens_f, spatial_f, w_qkv_f, w_spatial_f, tables_f, w_out_f, layernorm_multipliers_wide, shifts_f, w_up_f, b_up_f, w_down_f, b_down_f):
        params = (w_qkv_f, w_spatial_f, tables_f, w_out_f, layernorm_multipliers_wide, shifts_f, w_up_f, b_up_f, w_down_f, b_down_f)

        def one_page(page_item):
            return page_layer(page_item[0], page_item[1], page_item[2], page_item[3], params)
        paged = lax.map(jax.checkpoint(one_page), (jnp.moveaxis(tokens_f, 1, 0), spatial_f, positions, jnp.moveaxis(boxes, 1, 0)))
        return jnp.moveaxis(paged, 0, 1)
    single_width_numbers = (tokens.astype(jnp.float32), spatial.astype(jnp.float32), query_key_value_weight.astype(jnp.float32), w_spatial.astype(jnp.float32), rel_tables.astype(jnp.float32), exit_matrix.astype(jnp.float32), ln_gains.astype(jnp.float32), ln_shifts.astype(jnp.float32), up_weight.astype(jnp.float32), hidden_bias.astype(jnp.float32), shrink_projection_array.astype(jnp.float32), b_down.astype(jnp.float32))
    final, pullback = jax.vjp(forward, *single_width_numbers)
    grads = pullback(cotangent.astype(jnp.float32))
    return (final.astype(jnp.bfloat16), grads[0], grads[1], grads[2], grads[3], grads[4], grads[5], grads[6], grads[7], grads[8], grads[9], grads[10], grads[11])
```

```python
import functools

import jax
import jax.numpy as jnp
from jax import lax
from jax.experimental import pallas as pl
from jax.experimental.pallas import tpu as pltpu
from jax.sharding import Mesh, PartitionSpec as P

DH = 64
NBUCK = 128
HALF = 64
EPSILON = 1e-05
F32 = jnp.float32
BF16 = jnp.bfloat16
VMEM_BYTES = 56 * 1024 * 1024
NN = (((1,), (0,)), ((), ()))
NT = (((1,), (1,)), ((), ()))
TN = (((0,), (0,)), ((), ()))


def mm(left, right, dims=NN):
    return lax.dot_general(left, right, dims, preferred_element_type=F32)


def kernel_call(body, stream, operands, outs, flops, scratch=()):
    specs, arrays, moved = [], [], 0
    for array, per_stream in operands:
        if per_stream:
            rest = array.shape[1:]
            specs.append(
                pl.BlockSpec(
                    (None,) + rest, lambda g, s, n=len(rest): (s[0],) + (0,) * n
                )
            )
        else:
            rest = array.shape
            specs.append(pl.BlockSpec(rest, lambda g, s, n=len(rest): (0,) * n))
        arrays.append(array)
        size = array.dtype.itemsize
        for extent in rest:
            size *= extent
        moved += size
    out_specs = [
        pl.BlockSpec(shape, lambda g, s, n=len(shape): (0,) * n) for shape, _ in outs
    ]
    for shape, dtype in outs:
        size = jnp.dtype(dtype).itemsize
        for extent in shape:
            size *= extent
        moved += size
    return pl.pallas_call(
        body,
        out_shape=[jax.ShapeDtypeStruct(shape, dtype) for shape, dtype in outs],
        grid_spec=pltpu.PrefetchScalarGridSpec(
            num_scalar_prefetch=1,
            grid=(1,),
            in_specs=specs,
            out_specs=out_specs,
            scratch_shapes=list(scratch),
        ),
        compiler_params=pltpu.CompilerParams(
            dimension_semantics=("arbitrary",), vmem_limit_bytes=VMEM_BYTES
        ),
        cost_estimate=pl.CostEstimate(
            flops=flops, bytes_accessed=moved, transcendentals=0
        ),
    )(stream, *arrays)


def centred(rows):
    centre = rows - jnp.mean(rows, axis=-1, keepdims=True)
    spread = lax.rsqrt(jnp.mean(centre * centre, axis=-1, keepdims=True) + EPSILON)
    return centre * spread, spread


def norm_back(unit, spread, tilted):
    return spread * (
        tilted
        - jnp.mean(tilted, axis=-1, keepdims=True)
        - unit * jnp.mean(tilted * unit, axis=-1, keepdims=True)
    )


def pick(table_row, index):
    width = index.shape[1]
    table = jnp.broadcast_to(table_row, (index.shape[0], NBUCK))
    parts = [
        jnp.take_along_axis(
            table,
            index[:, at : at + NBUCK],
            axis=1,
            mode="promise_in_bounds",
        )
        for at in range(0, width, NBUCK)
    ]
    return jnp.concatenate(parts, axis=1)


def attention_kernel(
    s_ref,
    x_ref,
    sp_ref,
    w_ref,
    ws_ref,
    table_ref,
    rowidx_ref,
    colidx_ref,
    exit_ref,
    proj_ref,
    spat_ref,
    soft_ref,
    att_ref,
    mixed_ref,
    *,
    heads,
    block,
):
    x = x_ref[...]
    sp = sp_ref[...]
    for k in range(3):
        proj_ref[k] = mm(x, w_ref[k]).astype(BF16)
    for k in range(2):
        spat_ref[k] = mm(sp, ws_ref[k]).astype(BF16)
    length = x.shape[0]

    def step(at, carry):
        rows = pl.ds(pl.multiple_of(at * block, block), block)
        index = []
        for kind in range(3):
            own = colidx_ref[rows, kind : kind + 1]
            every = rowidx_ref[kind : kind + 1, :]
            index.append(jnp.clip(every - own, -HALF, HALF - 1) + HALF)
        for h in range(heads):
            cols = slice(h * DH, (h + 1) * DH)
            bias = pick(table_ref[0, h : h + 1, :], index[0])
            bias = bias + pick(table_ref[1, h : h + 1, :], index[1])
            bias = bias + pick(table_ref[2, h : h + 1, :], index[2])
            left = jnp.concatenate(
                [proj_ref[0, rows, cols], spat_ref[0, rows, cols]], axis=1
            )
            right = jnp.concatenate([proj_ref[1, :, cols], spat_ref[1, :, cols]], axis=1)
            scores = mm(left, right, NT) * (DH**-0.5) + bias
            top = jnp.max(scores, axis=-1, keepdims=True)
            raised = jnp.exp(scores - top)
            soft = raised / jnp.sum(raised, axis=-1, keepdims=True)
            soft_ref[h, rows, :] = soft
            att_ref[rows, cols] = mm(soft.astype(BF16), proj_ref[2, :, cols]).astype(BF16)
        return carry

    lax.fori_loop(0, length // block, step, 0)
    mixed_ref[...] = mm(att_ref[...], exit_ref[...]).astype(BF16)


def forward_kernel(
    s_ref,
    x_ref,
    mixed_ref,
    gain_ref,
    shift_ref,
    up_ref,
    hidden_ref,
    down_ref,
    low_ref,
    active_ref,
    slope_ref,
):
    unit, _ = centred(x_ref[...].astype(F32) + mixed_ref[...].astype(F32))
    normed = unit * gain_ref[0:1, :] + shift_ref[0:1, :]
    normed_low = normed.astype(BF16)
    total = None
    for part in range(up_ref.shape[0]):
        upper = mm(normed_low, up_ref[part]) + hidden_ref[part]
        phi = 0.5 * (1.0 + lax.erf(upper * (0.5**0.5)))
        slope_ref[part] = phi + upper * (
            jnp.exp(-0.5 * upper * upper) * (0.5 / jnp.pi) ** 0.5
        )
        active = (upper * phi).astype(BF16)
        active_ref[part] = active
        term = mm(active, down_ref[part])
        total = term if total is None else total + term
    low_ref[...] = total.astype(BF16)


def middle_kernel(
    s_ref,
    x_ref,
    mixed_ref,
    lowered_ref,
    cot_ref,
    gain_ref,
    shift_ref,
    bdown_ref,
    up_ref,
    down_ref,
    slope_ref,
    out_ref,
    hid_ref,
    second_ref,
    dlow_ref,
    dup_ref,
    sums_ref,
):
    unit, _ = centred(x_ref[...].astype(F32) + mixed_ref[...].astype(F32))
    normed = unit * gain_ref[0:1, :] + shift_ref[0:1, :]
    unit2, spread2 = centred(normed + lowered_ref[...].astype(F32) + bdown_ref[...])
    out_ref[...] = (unit2 * gain_ref[1:2, :] + shift_ref[1:2, :]).astype(BF16)
    cot = cot_ref[...].astype(F32)
    second = norm_back(unit2, spread2, cot * gain_ref[1:2, :])
    second_ref[...] = second
    sums_ref[...] = jnp.zeros_like(sums_ref)
    sums_ref[0:1, :] = jnp.sum(cot * unit2, axis=0, keepdims=True)
    sums_ref[1:2, :] = jnp.sum(cot, axis=0, keepdims=True)
    sums_ref[2:3, :] = jnp.sum(second, axis=0, keepdims=True)
    dlow = second.astype(BF16)
    dlow_ref[...] = dlow
    total = None
    for part in range(up_ref.shape[0]):
        dup = (mm(dlow, down_ref[part], NT) * slope_ref[part]).astype(BF16)
        dup_ref[part] = dup
        term = mm(dup, up_ref[part], NT)
        total = term if total is None else total + term
    hid_ref[...] = total.astype(BF16)


def ffn_grad_kernel(
    s_ref,
    x_ref,
    mixed_ref,
    gain_ref,
    shift_ref,
    active_ref,
    dlow_ref,
    dup_ref,
    grad_ref,
):
    unit, _ = centred(x_ref[...].astype(F32) + mixed_ref[...].astype(F32))
    normed_low = (unit * gain_ref[0:1, :] + shift_ref[0:1, :]).astype(BF16)
    width = x_ref.shape[1]
    grad_ref[0:width, :] = mm(normed_low, dup_ref[...], TN).astype(BF16)
    grad_ref[width : 2 * width, :] = mm(active_ref[...], dlow_ref[...], TN).astype(BF16)
    bias = jnp.sum(dup_ref[...].astype(F32), axis=0, keepdims=True)
    grad_ref[2 * width :, :] = jnp.broadcast_to(bias, (16, width)).astype(BF16)


def first_kernel(
    s_ref,
    x_ref,
    mixed_ref,
    second_ref,
    hid_ref,
    gain_ref,
    first_ref,
    dmix_ref,
    sums_ref,
):
    unit, spread = centred(x_ref[...].astype(F32) + mixed_ref[...].astype(F32))
    dnormed = second_ref[...] + hid_ref[...].astype(F32)
    first = norm_back(unit, spread, dnormed * gain_ref[0:1, :])
    first_ref[...] = first
    dmix_ref[...] = first.astype(BF16)
    sums_ref[...] = jnp.zeros_like(sums_ref)
    sums_ref[0:1, :] = jnp.sum(dnormed * unit, axis=0, keepdims=True)
    sums_ref[1:2, :] = jnp.sum(dnormed, axis=0, keepdims=True)


def backward_kernel(
    s_ref,
    dmix_ref,
    first_ref,
    exit_ref,
    soft_ref,
    proj_ref,
    spat_ref,
    w_ref,
    ws_ref,
    dscore_ref,
    dproj_ref,
    dspat_ref,
    dx_ref,
    dsp_ref,
    *,
    heads,
    block,
):
    length = dmix_ref.shape[0]
    scale = DH**-0.5
    datt = mm(dmix_ref[...], exit_ref[...], NT).astype(BF16)
    for h in range(heads):
        cols = slice(h * DH, (h + 1) * DH)
        value = proj_ref[2, :, cols]
        left = jnp.concatenate([proj_ref[0, :, cols], spat_ref[0, :, cols]], axis=1)
        right = jnp.concatenate([proj_ref[1, :, cols], spat_ref[1, :, cols]], axis=1)
        own = datt[:, cols]
        for at in range(0, length, block):
            soft = soft_ref[h, at : at + block, :]
            dsoft = mm(own[at : at + block], value, NT)
            inner = jnp.sum(soft * dsoft, axis=-1, keepdims=True)
            dscore_ref[h, at : at + block, :] = (soft * (dsoft - inner)).astype(BF16)
        dscore = dscore_ref[h]
        dleft = (mm(dscore, right) * scale).astype(BF16)
        dright = (mm(dscore, left, TN) * scale).astype(BF16)
        dproj_ref[0, :, cols] = dleft[:, :DH]
        dspat_ref[0, :, cols] = dleft[:, DH:]
        dproj_ref[1, :, cols] = dright[:, :DH]
        dspat_ref[1, :, cols] = dright[:, DH:]
        dproj_ref[2, :, cols] = mm(soft_ref[h].astype(BF16), own, TN).astype(BF16)
    total = first_ref[...]
    for k in range(3):
        total = total + mm(dproj_ref[k], w_ref[k], NT)
    dx_ref[...] = total.astype(BF16)
    dsp_ref[...] = (mm(dspat_ref[0], ws_ref[0], NT) + mm(dspat_ref[1], ws_ref[1], NT)).astype(BF16)


def attention_grad_kernel(
    s_ref,
    dmix_ref,
    x_ref,
    sp_ref,
    att_ref,
    dscore_ref,
    dproj_ref,
    dspat_ref,
    rowidx_ref,
    colidx_ref,
    wgrad_ref,
    wsgrad_ref,
    exitgrad_ref,
    tables_ref,
    *,
    heads,
):
    x = x_ref[...]
    sp = sp_ref[...]
    length = x.shape[0]
    for k in range(3):
        wgrad_ref[k] = mm(x, dproj_ref[k], TN).astype(BF16)
    for k in range(2):
        wsgrad_ref[k] = mm(sp, dspat_ref[k], TN).astype(BF16)
    exitgrad_ref[...] = mm(att_ref[...], dmix_ref[...], TN).astype(BF16)
    tables_ref[...] = jnp.zeros_like(tables_ref)
    lane = lax.broadcasted_iota(jnp.int32, (1, NBUCK), 1)
    for kind in range(3):
        extent = length if kind == 0 else NBUCK
        own = colidx_ref[:, kind : kind + 1]
        level = lax.broadcasted_iota(jnp.int32, (length, extent), 1)
        chosen = (own == level).astype(BF16)
        place = own - HALF + lax.broadcasted_iota(jnp.int32, (length, NBUCK), 1)
        turn = place & (NBUCK - 1)
        piece = place >> 7
        for h in range(heads):
            spread = mm(dscore_ref[h], chosen)
            window = jnp.zeros((length, NBUCK), F32)
            for q in range(extent // NBUCK):
                part = jnp.take_along_axis(
                    spread[:, q * NBUCK : (q + 1) * NBUCK],
                    turn,
                    axis=1,
                    mode="promise_in_bounds",
                )
                window = window + jnp.where(piece == q, part, 0.0)
            row = jnp.sum(window, axis=0, keepdims=True)
            row = jnp.where((lane > 0) & (lane < NBUCK - 1), row, 0.0)
            least = jnp.sum(jnp.where(level <= own - HALF, spread, 0.0), axis=0, keepdims=True)
            most = jnp.sum(jnp.where(level >= own + HALF - 1, spread, 0.0), axis=0, keepdims=True)
            row = row + jnp.where(lane == 0, jnp.sum(least, axis=1, keepdims=True), 0.0)
            row = row + jnp.where(
                lane == NBUCK - 1, jnp.sum(most, axis=1, keepdims=True), 0.0
            )
            tables_ref[kind * heads + h : kind * heads + h + 1, :] = row


def swap(value, axis):
    return lax.ppermute(value, axis, [(0, 1), (1, 0)])


def shards(
    tokens,
    spatial,
    positions,
    boxes,
    query_key_value_weight,
    w_spatial,
    rel_tables,
    exit_matrix,
    ln_gains,
    ln_shifts,
    up_weight,
    hidden_bias,
    shrink_projection_array,
    b_down,
    cotangent,
):
    heads = rel_tables.shape[2]
    rows = tokens.shape[2]
    width = tokens.shape[3]
    inner = query_key_value_weight.shape[3]
    hidden = up_weight.shape[2]
    length = 4 * rows
    page = lax.axis_index("y")
    core = lax.axis_index("core")
    head = lax.axis_index("head")
    stream = core.reshape(1)

    def to_page(array):
        mine = lax.dynamic_index_in_dim(array, page, 1, keepdims=False)
        other = lax.dynamic_index_in_dim(array, 1 - page, 1, keepdims=False)
        return jnp.stack([mine, swap(other, "y")], axis=1)

    def to_stream(array):
        mine = lax.dynamic_index_in_dim(array, core, 0, keepdims=False)
        other = lax.dynamic_index_in_dim(array, 1 - core, 0, keepdims=False)
        return jnp.concatenate([mine, swap(other, "core")], axis=0).reshape(length, -1)

    x = to_stream(to_page(tokens))
    sp_half = to_page(spatial[None])[0]
    sp = jnp.concatenate([sp_half, swap(sp_half, "core")], axis=0).reshape(length, width)
    places = jnp.concatenate([positions[None], boxes], axis=0)
    places = to_page(places)
    places = jnp.concatenate([places, swap(places, "core")], axis=1).reshape(3, length)
    rowidx = jnp.pad(places, ((0, 5), (0, 0)))
    colidx = rowidx.T
    cot = to_stream(to_page(cotangent))

    own = (True,)
    whole = (False,)
    attention_flops = 2 * length * (width * inner * 6 + heads * length * DH * 3)
    proj, spat, soft, att, mixed_part = kernel_call(
        functools.partial(attention_kernel, heads=heads, block=128),
        stream,
        [
            (x, False),
            (sp, False),
            (query_key_value_weight, True),
            (w_spatial, False),
            (rel_tables, True),
            (rowidx, False),
            (colidx, False),
            (exit_matrix, True),
        ],
        [
            ((3, length, inner), BF16),
            ((2, length, inner), BF16),
            ((heads, length, length), F32),
            ((length, inner), BF16),
            ((length, width), BF16),
        ],
        attention_flops,
    )
    half = length // 2
    mixed_half = mixed_part[:half].astype(F32) + swap(mixed_part[half:], "core").astype(F32)
    mixed_half = lax.psum(mixed_half.astype(BF16), "head")
    mixed = jnp.concatenate([mixed_half, swap(mixed_half, "core")], axis=0)

    up = up_weight[:, None]
    down = shrink_projection_array[:, None]
    hidden_rows = hidden_bias[:, None, None]
    matrix_flops = 2 * length * width * hidden
    low_part, active, slope = kernel_call(
        forward_kernel,
        stream,
        [
            (x, False),
            (mixed, False),
            (ln_gains, True),
            (ln_shifts, True),
            (up, True),
            (hidden_rows, True),
            (down, True),
        ],
        [
            ((length, width), BF16),
            ((1, length, hidden), BF16),
            ((1, length, hidden), F32),
        ],
        2 * matrix_flops,
    )
    lowered = lax.psum(low_part, "head")
    out, hid_part, second, dlow, dup, sums_two = kernel_call(
        middle_kernel,
        stream,
        [
            (x, False),
            (mixed, False),
            (lowered, False),
            (cot, False),
            (ln_gains, True),
            (ln_shifts, True),
            (b_down[:, None], True),
            (up, True),
            (down, True),
            (slope, False),
        ],
        [
            ((length, width), BF16),
            ((length, width), BF16),
            ((length, width), F32),
            ((length, width), BF16),
            ((1, length, hidden), BF16),
            ((8, width), F32),
        ],
        2 * matrix_flops,
    )
    hid = lax.psum(hid_part, "head")
    (ffn_grad,) = kernel_call(
        ffn_grad_kernel,
        stream,
        [
            (x, False),
            (mixed, False),
            (ln_gains, True),
            (ln_shifts, True),
            (active[0], False),
            (dlow, False),
            (dup[0], False),
        ],
        [((2 * width + 16, hidden), BF16)],
        2 * matrix_flops,
    )
    ffn_grad = lax.psum(ffn_grad, ("batch", "y"))
    first, dmix_part, sums_one = kernel_call(
        first_kernel,
        stream,
        [
            (x, False),
            (mixed, False),
            (second, False),
            (hid, False),
            (ln_gains, True),
        ],
        [((length, width), F32), ((length, width), BF16), ((8, width), F32)],
        0,
    )
    other_dmix = swap(dmix_part, "core")
    other_dmix = jnp.concatenate([other_dmix[half:], other_dmix[:half]], axis=0)
    dmix = (first + other_dmix.astype(F32)).astype(BF16)

    first_once = jnp.where(head == 0, first, 0.0)
    dscore, dproj, dspat, dx, dsp = kernel_call(
        functools.partial(backward_kernel, heads=heads, block=128),
        stream,
        [
            (dmix, False),
            (first_once, False),
            (exit_matrix, True),
            (soft, False),
            (proj, False),
            (spat, False),
            (query_key_value_weight, True),
            (w_spatial, False),
        ],
        [
            ((heads, length, length), BF16),
            ((3, length, inner), BF16),
            ((2, length, inner), BF16),
            ((length, width), BF16),
            ((length, width), BF16),
        ],
        2 * length * (width * inner * 6 + heads * length * DH * 6),
    )
    dx_mine, dx_other = dx[:half], swap(dx[half:], "core")
    dsp_mine = (dsp[:half].astype(F32) + swap(dsp[half:], "core").astype(F32)).astype(BF16)
    ends = jnp.stack([dx_mine, dx_other, dsp_mine]).reshape(3, 2, rows, width)
    out_ends = jnp.stack([out[:half], swap(out[half:], "core")]).reshape(2, 2, rows, width)

    def to_owner(array):
        other = swap(array[:, 1], "y")
        return jnp.stack([array[:, 0], other], axis=1)

    def in_place(array, index, axis):
        return jnp.where(index == 0, array, jnp.flip(array, axis))

    ends = lax.psum(to_owner(ends), "head")
    ends = in_place(ends, page, 1)
    grad_tokens = in_place(ends[:2], core, 0).astype(F32)
    grad_spatial = ends[2].astype(F32)
    output = in_place(in_place(to_owner(out_ends), page, 1), core, 0)

    wgrad, wsgrad, exitgrad, tables = kernel_call(
        functools.partial(attention_grad_kernel, heads=heads),
        stream,
        [
            (dmix, False),
            (x, False),
            (sp, False),
            (att, False),
            (dscore, False),
            (dproj, False),
            (dspat, False),
            (rowidx, False),
            (colidx, False),
        ],
        [
            ((3, width, inner), BF16),
            ((2, width, inner), BF16),
            ((inner, width), BF16),
            ((16, NBUCK), F32),
        ],
        2 * length * (width * inner * 6 + heads * length * width),
    )
    part = width // lax.axis_size("head")
    sums = jnp.stack([sums_one[0], sums_two[0], sums_one[1], sums_two[1], sums_two[2]])
    sums = lax.dynamic_slice_in_dim(sums, head * part, part, 1)
    tables = tables[: 3 * heads].reshape(3, heads, NBUCK)
    wsgrad = (wsgrad.astype(F32) + swap(wsgrad, "core").astype(F32)).astype(BF16)
    wgrad, wsgrad, exitgrad, tables, sums = lax.psum(
        (wgrad, wsgrad, exitgrad, tables, sums), ("batch", "y")
    )

    def both(array):
        return in_place(jnp.stack([array, swap(array, "core")]), core, 0)

    grad_qkv = both(wgrad).astype(F32)
    grad_exit = both(exitgrad).astype(F32)
    grad_tables = both(tables)
    sums = both(sums)
    ffn = both(ffn_grad).astype(F32)
    return (
        output,
        grad_tokens,
        grad_spatial,
        grad_qkv,
        wsgrad.astype(F32),
        grad_tables,
        grad_exit,
        sums[:, 0:2],
        sums[:, 2:4],
        ffn[:, :width],
        ffn[:, 2 * width],
        ffn[:, width : 2 * width],
        sums[:, 4],
    )


def solution(mesh):
    devices = mesh.devices
    batch, seq, head = devices.shape
    fine = Mesh(
        devices.reshape(batch, seq // 2, 2, head), ("batch", "y", "core", "head")
    )
    seq_axes = ("y", "core")
    return jax.shard_map(
        shards,
        mesh=fine,
        in_specs=(
            P(None, "batch", seq_axes, None),
            P("batch", seq_axes, None),
            P("batch", seq_axes),
            P(None, "batch", seq_axes),
            P(None, None, None, "head"),
            P(None, None, "head"),
            P(None, None, "head", None),
            P(None, "head", None),
            P(),
            P(),
            P(None, None, "head"),
            P(None, "head"),
            P(None, "head", None),
            P(),
            P(None, "batch", seq_axes, None),
        ),
        out_specs=(
            P(None, "batch", seq_axes, None),
            P(None, "batch", seq_axes, None),
            P("batch", seq_axes, None),
            P(None, None, None, "head"),
            P(None, None, "head"),
            P(None, None, "head", None),
            P(None, "head", None),
            P(None, None, "head"),
            P(None, None, "head"),
            P(None, None, "head"),
            P(None, "head"),
            P(None, "head", None),
            P(None, "head"),
        ),
        check_vma=False,
    )
```

```python
import functools

import jax
import jax.numpy as jnp
from jax import lax
from jax.experimental import pallas as pl
from jax.experimental.pallas import tpu as pltpu
from jax.sharding import Mesh, PartitionSpec as P

DH = 64
NBUCK = 128
HALF = 64
EPSILON = 1e-05
F32 = jnp.float32
BF16 = jnp.bfloat16
VMEM_BYTES = 56 * 1024 * 1024
NN = (((1,), (0,)), ((), ()))
NT = (((1,), (1,)), ((), ()))
TN = (((0,), (0,)), ((), ()))


def mm(left, right, dims=NN):
    return lax.dot_general(left, right, dims, preferred_element_type=F32)


def kernel_call(body, place, operands, outs, flops, scratch=()):
    specs, arrays, moved = [], [], 0
    for array, per_stream in operands:
        if per_stream:
            rest = array.shape[1:]
            specs.append(
                pl.BlockSpec(
                    (None,) + rest, lambda g, s, n=len(rest): (s[0],) + (0,) * n
                )
            )
        else:
            rest = array.shape
            specs.append(pl.BlockSpec(rest, lambda g, s, n=len(rest): (0,) * n))
        arrays.append(array)
        size = array.dtype.itemsize
        for extent in rest:
            size *= extent
        moved += size
    out_specs = [
        pl.BlockSpec(shape, lambda g, s, n=len(shape): (0,) * n) for shape, _ in outs
    ]
    for shape, dtype in outs:
        size = jnp.dtype(dtype).itemsize
        for extent in shape:
            size *= extent
        moved += size
    return pl.pallas_call(
        body,
        out_shape=[jax.ShapeDtypeStruct(shape, dtype) for shape, dtype in outs],
        grid_spec=pltpu.PrefetchScalarGridSpec(
            num_scalar_prefetch=1,
            grid=(1,),
            in_specs=specs,
            out_specs=out_specs,
            scratch_shapes=list(scratch),
        ),
        compiler_params=pltpu.CompilerParams(
            dimension_semantics=("arbitrary",), vmem_limit_bytes=VMEM_BYTES
        ),
        cost_estimate=pl.CostEstimate(
            flops=flops, bytes_accessed=moved, transcendentals=0
        ),
    )(place, *arrays)


def centred(rows):
    centre = rows - jnp.mean(rows, axis=-1, keepdims=True)
    spread = lax.rsqrt(jnp.mean(centre * centre, axis=-1, keepdims=True) + EPSILON)
    return centre * spread, spread


def norm_back(unit, spread, tilted):
    return spread * (
        tilted
        - jnp.mean(tilted, axis=-1, keepdims=True)
        - unit * jnp.mean(tilted * unit, axis=-1, keepdims=True)
    )


def pick(table_row, index):
    width = index.shape[1]
    table = jnp.broadcast_to(table_row, (index.shape[0], NBUCK))
    parts = [
        jnp.take_along_axis(
            table,
            index[:, at : at + NBUCK],
            axis=1,
            mode="promise_in_bounds",
        )
        for at in range(0, width, NBUCK)
    ]
    return jnp.concatenate(parts, axis=1)


def stack_rows(pieces):
    return jnp.concatenate(pieces, axis=0)


def turned(rows, size):
    pieces = [rows[at : at + size] for at in range(0, rows.shape[0], size)]
    return stack_rows([pieces[i ^ 1] for i in range(len(pieces))])


def residual(x_ref, half, mixed_refs):
    rest = mixed_refs[0].shape[0] // 2
    pieces = []
    for y in range(2):
        for c in range(2):
            own = x_ref[y, half, c * rest : (c + 1) * rest, :].astype(F32)
            pieces.append(own + mixed_refs[c][y * rest : (y + 1) * rest, :].astype(F32))
    return stack_rows(pieces)


def quarter(refs, place_ref, b, y, rows, straight):
    near_ref, far_ref = refs
    db = place_ref[1] ^ b
    dy = place_ref[2] ^ y
    near, far = (db, dy) if straight else (dy, db)
    return jnp.where(far == 0, near_ref[near, rows, :], far_ref[near, rows, :])


def attention_kernel(
    p_ref,
    x_ref,
    sp_ref,
    w_ref,
    ws_ref,
    table_ref,
    rowidx_ref,
    colidx_ref,
    proj_ref,
    spat_ref,
    soft_ref,
    own_ref,
    send_ref,
    att_ref,
    *,
    heads,
    block,
):
    width = x_ref.shape[-1]
    x = x_ref[...].reshape(-1, width)
    sp = sp_ref[...].reshape(-1, width)
    for k in range(3):
        proj_ref[k] = mm(x, w_ref[k], NT).astype(BF16)
    for k in range(2):
        spat_ref[k] = mm(sp, ws_ref[k], NT).astype(BF16)
    length = x.shape[0]
    level = lax.broadcasted_iota(jnp.int32, (length, NBUCK), 1)
    chosen = [(colidx_ref[:, kind : kind + 1] == level).astype(BF16) for kind in (1, 2)]
    chosen = jnp.concatenate(chosen, axis=1)

    def step(at, carry):
        rows = pl.ds(pl.multiple_of(at * block, block), block)
        lane = lax.broadcasted_iota(jnp.int32, (block, NBUCK), 1)
        index = jnp.clip(rowidx_ref[0:1, :] - colidx_ref[rows, 0:1], -HALF, HALF - 1) + HALF
        boxes = [
            jnp.clip(lane - colidx_ref[rows, kind : kind + 1], -HALF, HALF - 1) + HALF
            for kind in (1, 2)
        ]
        for h in range(heads):
            cols = slice(h * DH, (h + 1) * DH)
            bias = jnp.concatenate(
                [pick(table_ref[k, h : h + 1, :], boxes[k - 1]) for k in (1, 2)], axis=1
            )
            coarse = bias.astype(BF16)
            fine = (bias - coarse.astype(F32)).astype(BF16)
            left = jnp.concatenate(
                [proj_ref[0, rows, cols], spat_ref[0, rows, cols]], axis=1
            ) * jnp.asarray(DH**-0.5, BF16)
            right = jnp.concatenate([proj_ref[1, :, cols], spat_ref[1, :, cols]], axis=1)
            scores = mm(
                jnp.concatenate([left, coarse, fine], axis=1),
                jnp.concatenate([right, chosen, chosen], axis=1),
                NT,
            ) + pick(table_ref[0, h : h + 1, :], index)
            top = jnp.max(scores, axis=-1, keepdims=True)
            raised = jnp.exp(scores - top)
            soft = raised * (1.0 / jnp.sum(raised, axis=-1, keepdims=True))
            soft_ref[h, rows, :] = soft
            att_ref[rows, cols] = mm(soft.astype(BF16), proj_ref[2, :, cols]).astype(BF16)
        return carry

    lax.fori_loop(0, length // block, step, 0)
    part = length // 4
    own_ref[0:part, :] = att_ref[0:part, :]
    own_ref[part:, :] = att_ref[2 * part : 3 * part, :]
    send_ref[0:part, :] = att_ref[part : 2 * part, :]
    send_ref[part:, :] = att_ref[3 * part :, :]


def mixed_kernel(
    p_ref,
    own_ref,
    recv_ref,
    exit_ref,
    near_ref,
    far_ref,
    keep_ref,
    send_ref,
    partner_ref,
):
    share = exit_ref.shape[0] // 4
    for q in range(4):
        partner_ref[q * share : (q + 1) * share, :] = quarter(
            (near_ref, far_ref), p_ref, q // 2, q % 2, slice(0, share), True
        )
    total = mm(own_ref[...], exit_ref[...]) + mm(recv_ref[...], partner_ref[...])
    rest = total.shape[0] // 4
    for y in range(2):
        at = 2 * y * rest
        keep_ref[y * rest : (y + 1) * rest, :] = total[at : at + rest]
        send_ref[y * rest : (y + 1) * rest, :] = total[at + rest : at + 2 * rest].astype(BF16)


def gelu_parts(upper):
    phi = 0.5 * (1.0 + lax.erf(upper * (0.5**0.5)))
    slope = phi + upper * (jnp.exp(-0.5 * upper * upper) * (0.5 / jnp.pi) ** 0.5)
    return (upper * phi).astype(BF16), slope


def forward_kernel(
    p_ref,
    x_ref,
    mixed0_ref,
    mixed1_ref,
    gain_ref,
    shift_ref,
    up_ref,
    hidden_ref,
    down_ref,
    upn1_ref,
    upf1_ref,
    upn2_ref,
    upf2_ref,
    dnn1_ref,
    dnf1_ref,
    dnn2_ref,
    dnf2_ref,
    low_ref,
    active_ref,
    slope_ref,
    upp_ref,
    downp_ref,
):
    width = x_ref.shape[-1]
    first = upn1_ref.shape[1]
    skip = width // 16
    split = first - skip
    share = width // 4
    piece = dnn1_ref.shape[1]
    for q in range(4):
        b, y, at = q // 2, q % 2, q * share
        upp_ref[at : at + split, :] = quarter(
            (upn1_ref, upf1_ref), p_ref, b, y, slice(skip, first), True
        )
        upp_ref[at + split : at + share, :] = quarter(
            (upn2_ref, upf2_ref), p_ref, b, y, slice(0, share - split), False
        )
        downp_ref[at : at + piece, :] = quarter(
            (dnn1_ref, dnf1_ref), p_ref, b, y, slice(0, piece), True
        )
        downp_ref[at + piece : at + share, :] = quarter(
            (dnn2_ref, dnf2_ref), p_ref, b, y, slice(0, share - piece), False
        )
    extra = upn2_ref[0, share - split : share - split + 16, :].astype(F32)
    partner_bias = extra[0:1] + extra[1:2] + extra[2:3]
    unit, _ = centred(residual(x_ref, 0, (mixed0_ref, mixed1_ref)))
    normed_low = (unit * gain_ref[0:1, :] + shift_ref[0:1, :]).astype(BF16)
    active, slope = gelu_parts(mm(normed_low, up_ref[...]) + hidden_ref[...])
    active_ref[0] = active
    slope_ref[0] = slope
    total = mm(active, down_ref[...])
    active, slope = gelu_parts(mm(normed_low, upp_ref[...]) + partner_bias)
    active_ref[1] = active
    slope_ref[1] = slope
    low_ref[...] = (total + mm(active, downp_ref[...])).astype(BF16)


def other_kernel(
    p_ref,
    x_ref,
    mixed0_ref,
    mixed1_ref,
    gain_ref,
    shift_ref,
    up_ref,
    hidden_ref,
    normed_ref,
    active_ref,
    slope_ref,
):
    unit, _ = centred(residual(x_ref, 1, (mixed0_ref, mixed1_ref)))
    normed_low = (unit * gain_ref[0:1, :] + shift_ref[0:1, :]).astype(BF16)
    normed_ref[...] = normed_low
    active, slope = gelu_parts(mm(normed_low, up_ref[...]) + hidden_ref[...])
    active_ref[...] = active
    slope_ref[...] = slope


def middle_kernel(
    p_ref,
    x_ref,
    mixed0_ref,
    mixed1_ref,
    low_ref,
    lowr_ref,
    cot_ref,
    gain_ref,
    shift_ref,
    bdown_ref,
    up_ref,
    down_ref,
    upp_ref,
    downp_ref,
    slope_ref,
    outk_ref,
    outs_ref,
    hid_ref,
    second_ref,
    normed_ref,
    dlow_ref,
    dlows_ref,
    dup_ref,
    sums_ref,
):
    unit, _ = centred(residual(x_ref, 0, (mixed0_ref, mixed1_ref)))
    normed = unit * gain_ref[0:1, :] + shift_ref[0:1, :]
    normed_ref[...] = normed.astype(BF16)
    length = normed.shape[0]
    least = length // 8
    lowered = low_ref[...].astype(F32) + turned(lowr_ref[...], least).astype(F32)
    unit2, spread2 = centred(normed + lowered + bdown_ref[...])
    out = (unit2 * gain_ref[1:2, :] + shift_ref[1:2, :]).astype(BF16)
    for y in range(2):
        at = 4 * y * least
        outk_ref[y * least : (y + 1) * least, :] = out[at : at + least]
        outs_ref[y * least : (y + 1) * least, :] = out[at + 2 * least : at + 3 * least]
    cot = cot_ref[...].astype(F32)
    second = norm_back(unit2, spread2, cot * gain_ref[1:2, :])
    second_ref[...] = second
    sums_ref[...] = jnp.zeros_like(sums_ref)
    sums_ref[0:1, :] = jnp.sum(cot * unit2, axis=0, keepdims=True)
    sums_ref[1:2, :] = jnp.sum(cot, axis=0, keepdims=True)
    sums_ref[2:3, :] = jnp.sum(second, axis=0, keepdims=True)
    dlow = second.astype(BF16)
    dlow_ref[...] = dlow
    for i in range(4):
        dlows_ref[i * least : (i + 1) * least, :] = dlow[2 * i * least : (2 * i + 1) * least]
    dup = (mm(dlow, down_ref[...], NT) * slope_ref[0]).astype(BF16)
    dup_ref[...] = dup
    total = mm(dup, up_ref[...], NT)
    dup = (mm(dlow, downp_ref[...], NT) * slope_ref[1]).astype(BF16)
    hid_ref[...] = (total + mm(dup, upp_ref[...], NT)).astype(BF16)


def ffn_grad_kernel(
    p_ref,
    normed_ref,
    normedo_ref,
    active_ref,
    activeo_ref,
    dlow_ref,
    dlow0_ref,
    dlow1_ref,
    dup_ref,
    slopeo_ref,
    down_ref,
    upg_ref,
    downg_ref,
    bias_ref,
):
    least = dlow0_ref.shape[0] // 4
    pieces = []
    for i in range(4):
        pieces.append(dlow0_ref[i * least : (i + 1) * least, :])
        pieces.append(dlow1_ref[i * least : (i + 1) * least, :])
    dlowo = stack_rows(pieces)
    dupo = (mm(dlowo, down_ref[...], NT) * slopeo_ref[...]).astype(BF16)
    dup = dup_ref[...]
    upg_ref[...] = (mm(normed_ref[...], dup, TN) + mm(normedo_ref[...], dupo, TN)).astype(BF16)
    downg_ref[...] = (
        mm(active_ref[0], dlow_ref[...], TN) + mm(activeo_ref[...], dlowo, TN)
    ).astype(BF16)
    bias = jnp.sum(dup.astype(F32), axis=0, keepdims=True)
    bias = bias + jnp.sum(dupo.astype(F32), axis=0, keepdims=True)
    bias_ref[...] = jnp.broadcast_to(bias, bias_ref.shape)


def first_kernel(
    p_ref,
    x_ref,
    mixed0_ref,
    mixed1_ref,
    second_ref,
    hid_ref,
    hidr_ref,
    gain_ref,
    first_ref,
    dmix_ref,
    sums_ref,
):
    unit, spread = centred(residual(x_ref, 0, (mixed0_ref, mixed1_ref)))
    hid = hid_ref[...].astype(F32) + turned(hidr_ref[...], hid_ref.shape[0] // 8).astype(F32)
    dnormed = second_ref[...] + hid
    first = norm_back(unit, spread, dnormed * gain_ref[0:1, :])
    first_ref[...] = first
    dmix_ref[...] = first.astype(BF16)
    sums_ref[...] = jnp.zeros_like(sums_ref)
    sums_ref[0:1, :] = jnp.sum(dnormed * unit, axis=0, keepdims=True)
    sums_ref[1:2, :] = jnp.sum(dnormed, axis=0, keepdims=True)


def attended_kernel(
    p_ref,
    dmix_ref,
    dmixr_ref,
    exit_ref,
    exitp_ref,
    sums1_ref,
    sums2_ref,
    own_ref,
    send_ref,
    total_ref,
    pay_ref,
):
    length = dmix_ref.shape[0]
    rest = length // 4
    total = dmix_ref[...].astype(F32) + turned(dmixr_ref[...], rest).astype(F32)
    total = total.astype(BF16)
    total_ref[...] = total
    own_ref[...] = mm(total, exit_ref[...], NT).astype(BF16)
    send_ref[...] = mm(total, exitp_ref[...], NT).astype(BF16)
    pay_ref[0:rest, :] = total[0:rest]
    pay_ref[rest : 2 * rest, :] = total[2 * rest : 3 * rest]
    pay_ref[2 * rest :, :] = jnp.concatenate([sums1_ref[...], sums2_ref[...]], axis=0).astype(BF16)


def backward_kernel(
    p_ref,
    datt_ref,
    dattr_ref,
    first_ref,
    soft_ref,
    proj_ref,
    spat_ref,
    w_ref,
    ws_ref,
    dscore_ref,
    dproj_ref,
    dspat_ref,
    dxk0_ref,
    dxk1_ref,
    dxs0_ref,
    dxs1_ref,
    dsk0_ref,
    dsk1_ref,
    dss0_ref,
    dss1_ref,
    *,
    heads,
    block,
):
    length = 2 * datt_ref.shape[0]
    scale = DH**-0.5
    part = length // 4
    datt = stack_rows(
        [datt_ref[0:part, :], dattr_ref[0:part, :], datt_ref[part:, :], dattr_ref[part:, :]]
    )
    for h in range(heads):
        cols = slice(h * DH, (h + 1) * DH)
        value = proj_ref[2, :, cols]
        left = jnp.concatenate([proj_ref[0, :, cols], spat_ref[0, :, cols]], axis=1)
        right = jnp.concatenate([proj_ref[1, :, cols], spat_ref[1, :, cols]], axis=1)
        own = datt[:, cols]
        for at in range(0, length, block):
            soft = soft_ref[h, at : at + block, :]
            dsoft = mm(own[at : at + block], value, NT)
            inner = jnp.sum(soft * dsoft, axis=-1, keepdims=True)
            dscore_ref[h, at : at + block, :] = (soft * (dsoft - inner)).astype(BF16)
        dscore = dscore_ref[h]
        dleft = (mm(dscore, right) * scale).astype(BF16)
        dright = (mm(dscore, left, TN) * scale).astype(BF16)
        dproj_ref[0, :, cols] = dleft[:, :DH]
        dspat_ref[0, :, cols] = dleft[:, DH:]
        dproj_ref[1, :, cols] = dright[:, :DH]
        dspat_ref[1, :, cols] = dright[:, DH:]
        dproj_ref[2, :, cols] = mm(soft_ref[h].astype(BF16), own, TN).astype(BF16)
    once = (p_ref[3] == 0).astype(F32)
    total = mm(dproj_ref[0], w_ref[0])
    for k in range(1, 3):
        total = total + mm(dproj_ref[k], w_ref[k])
    least = part // 4

    def deal(rows, refs):
        for y in range(2):
            for zh in range(2):
                for c in range(2):
                    for zl in range(2):
                        at = (((y * 2 + zh) * 2 + c) * 2 + zl) * least
                        to = (zh * 2 + y) * least
                        value = rows[at : at + least]
                        if zh == 0 and first_ref is not None and refs[0][0] is dxk0_ref:
                            of = ((y * 2 + c) * 2 + zl) * least
                            value = value + once * first_ref[of : of + least, :]
                        refs[c][zl][to : to + least, :] = value.astype(BF16)

    deal(total, ((dxk0_ref, dxk1_ref), (dxs0_ref, dxs1_ref)))
    total = mm(dspat_ref[0], ws_ref[0]) + mm(dspat_ref[1], ws_ref[1])
    deal(total, ((dsk0_ref, dsk1_ref), (dss0_ref, dss1_ref)))


def attention_grad_kernel(
    p_ref,
    dmix_ref,
    pay_ref,
    payr_ref,
    payc_ref,
    atto_ref,
    atts_ref,
    x_ref,
    sp_ref,
    dscore_ref,
    dproj_ref,
    dspat_ref,
    colidx_ref,
    bup_ref,
    first_ref,
    second_ref,
    *,
    heads,
):
    width = x_ref.shape[-1]
    x = x_ref[...].reshape(-1, width)
    sp = sp_ref[...].reshape(-1, width)
    length = x.shape[0]
    inner = dproj_ref.shape[-1]
    for k in range(3):
        first_ref[k * inner : (k + 1) * inner, :] = mm(dproj_ref[k], x, TN).astype(BF16)
    rest = length // 8
    dmixo = stack_rows(
        [payr_ref[0:rest, :], payc_ref[0:rest, :], payr_ref[rest : 2 * rest, :], payc_ref[rest : 2 * rest, :]]
    )
    second_ref[0:inner, :] = (
        mm(atto_ref[...], dmix_ref[...], TN) + mm(atts_ref[...], dmixo, TN)
    ).astype(BF16)
    for k in range(2):
        second_ref[(k + 1) * inner : (k + 2) * inner, :] = mm(dspat_ref[k], sp, TN).astype(BF16)
    small = pay_ref[2 * rest :, :].astype(F32) + payr_ref[2 * rest :, :].astype(F32)
    lane = lax.broadcasted_iota(jnp.int32, (1, NBUCK), 1)
    found = []
    for kind in range(3):
        extent = length if kind == 0 else NBUCK
        own = colidx_ref[:, kind : kind + 1]
        level = lax.broadcasted_iota(jnp.int32, (length, extent), 1)
        chosen = (own == level).astype(BF16)
        place = own - HALF + lax.broadcasted_iota(jnp.int32, (length, NBUCK), 1)
        turn = place & (NBUCK - 1)
        piece = place >> 7
        for h in range(heads):
            spread = mm(dscore_ref[h], chosen)
            window = jnp.zeros((length, NBUCK), F32)
            for q in range(extent // NBUCK):
                part = jnp.take_along_axis(
                    spread[:, q * NBUCK : (q + 1) * NBUCK],
                    turn,
                    axis=1,
                    mode="promise_in_bounds",
                )
                window = window + jnp.where(piece == q, part, 0.0)
            row = jnp.sum(window, axis=0, keepdims=True)
            row = jnp.where((lane > 0) & (lane < NBUCK - 1), row, 0.0)
            least = jnp.sum(jnp.where(level <= own - HALF, spread, 0.0), axis=0, keepdims=True)
            most = jnp.sum(jnp.where(level >= own + HALF - 1, spread, 0.0), axis=0, keepdims=True)
            row = row + jnp.where(lane == 0, jnp.sum(least, axis=1, keepdims=True), 0.0)
            row = row + jnp.where(
                lane == NBUCK - 1, jnp.sum(most, axis=1, keepdims=True), 0.0
            )
            found.append(row)
    base = 3 * inner
    first_ref[base : base + 16, :] = small.astype(BF16)
    per = width // NBUCK
    found = found + [jnp.zeros((1, NBUCK), F32)] * (-len(found) % per)
    lines = [
        jnp.concatenate(found[at : at + per], axis=1) for at in range(0, len(found), per)
    ]
    lines.append(bup_ref[0:1, :])
    lines = jnp.concatenate(lines + [jnp.zeros((16 - len(lines), width), F32)], axis=0)
    first_ref[base + 16 : base + 32, :] = lines.astype(BF16)


def swap(value, axis, step=1):
    size = lax.axis_size(axis)
    return lax.ppermute(value, axis, [(i, i ^ step) for i in range(size)])


def added(left, right):
    return (left.astype(F32) + right.astype(F32)).astype(BF16)


def summed(straight, crossed):
    steps = [1 << bit for bit in range(lax.axis_size("batch").bit_length() - 1)]
    for step in steps:
        straight = added(straight, swap(straight, "batch", step))
    crossed = added(crossed, swap(crossed, "y"))
    straight = added(straight, swap(straight, "y"))
    for step in steps:
        crossed = added(crossed, swap(crossed, "batch", step))
    return straight, crossed


def in_place(array, index, axis):
    return jnp.where(index == 0, array, jnp.flip(array, axis))


def shards(
    tokens,
    spatial,
    positions,
    boxes,
    query_key_value_weight,
    w_spatial,
    rel_tables,
    exit_matrix,
    ln_gains,
    ln_shifts,
    up_weight,
    hidden_bias,
    shrink_projection_array,
    b_down,
    cotangent,
):
    heads = rel_tables.shape[2]
    rows = tokens.shape[2]
    width = tokens.shape[3]
    inner = query_key_value_weight.shape[3]
    hidden = up_weight.shape[2]
    least = rows // 4
    rest = rows // 2
    length = 4 * rows
    page = lax.axis_index("y")
    core = lax.axis_index("core")
    zh = lax.axis_index("zh")
    zl = lax.axis_index("zl")
    pair = lax.axis_index("batch") & 1
    place = jnp.stack([core, pair, page, zl]).astype(jnp.int32)
    call = functools.partial(kernel_call, place=place)

    def run(body, operands, outs, flops, scratch=()):
        marked = [a if isinstance(a, tuple) else (a, False) for a in operands]
        return kernel_call(body, place, marked, outs, flops, scratch)

    def take(array, index, axis):
        return lax.dynamic_index_in_dim(array, index, axis, keepdims=False)

    def near_first(array, axis):
        shape = array.shape
        array = array.reshape(shape[:axis] + (2, 2, least) + shape[axis + 1 :])
        return in_place(in_place(array, zh, axis), zl, axis + 1)

    def to_stream(array):
        mine, other = take(array, page, 1), take(array, 1 - page, 1)
        return mine, other

    token_blocks = near_first(tokens, 2)
    mine, other = take(token_blocks, page, 1), take(token_blocks, 1 - page, 1)
    far = swap(other, "y")
    both = jnp.stack([mine, far])
    kept, passed = take(both, core, 1), take(both, 1 - core, 1)
    x = jnp.stack([kept, swap(passed, "core")], axis=2).reshape(2, 2, rows, width)

    spatial_blocks = near_first(spatial, 1)
    mine, other = take(spatial_blocks, page, 0), take(spatial_blocks, 1 - page, 0)
    both = jnp.stack([mine, swap(other, "y")])
    sp = jnp.stack([both, swap(both, "core")], axis=2).reshape(2, 2, rows, width)

    places = jnp.concatenate([positions[None], boxes], axis=0)
    places = near_first(places, 2)
    mine, other = take(places, page, 1), take(places, 1 - page, 1)
    both = jnp.stack([mine, swap(other, "y")], axis=1)
    places = jnp.stack([both, swap(both, "core")], axis=3).reshape(3, length)
    rowidx = jnp.pad(places, ((0, 5), (0, 0)))
    colidx = rowidx.T

    mine = pair * 2 + page
    exit_own = take(exit_matrix, core, 0)
    up_own = take(up_weight, core, 0)
    down_own = take(shrink_projection_array, core, 0)
    bias_own = take(hidden_bias, core, 0)
    bias_rows = []
    left_over = bias_own
    for _ in range(3):
        bias_rows.append(left_over.astype(BF16))
        left_over = left_over - bias_rows[-1].astype(F32)
    bias_rows = jnp.pad(jnp.stack(bias_rows), ((0, 13), (0, 0)))
    share = hidden // 4
    exit_share = lax.dynamic_slice_in_dim(exit_own, mine * (inner // 4), inner // 4, 0)
    up_share = lax.dynamic_slice_in_dim(up_own, mine * share, share, 0)
    down_share = lax.dynamic_slice_in_dim(down_own, mine * share, share, 0)
    split = (share + 16 - inner // 4) // 2
    one = swap(jnp.concatenate([exit_share, up_share[:split]]), "zh")
    two = swap(jnp.concatenate([up_share[split:], bias_rows]), "zh")
    three = swap(down_share[: share // 2], "zh")
    four = swap(down_share[share // 2 :], "zh")

    def spread(array, axes):
        near = jnp.stack([array, swap(array, axes[0])])
        return near, swap(near, axes[1])

    up_parts = spread(one, ("batch", "y")) + spread(two, ("y", "batch"))
    down_parts = spread(three, ("batch", "y")) + spread(four, ("y", "batch"))

    cot = cotangent.reshape(2, 2, 2, 2, least, width)
    cot = in_place(take(cot, zh, 2), zl, 2)
    mine, other = take(cot, page, 1), take(cot, 1 - page, 1)
    both = jnp.stack([mine, swap(other, "y")])
    kept, passed = take(both, core, 1), take(both, 1 - core, 1)
    cot = jnp.stack([kept, swap(passed, "core")], axis=1).reshape(2 * rows, width)

    weights = jnp.swapaxes(query_key_value_weight, 2, 3)
    spatial_weights = jnp.swapaxes(w_spatial, 1, 2)
    half = length // 2
    proj, spat, soft, att_own, att_send = run(
        functools.partial(attention_kernel, heads=heads, block=128),
        [
            x,
            sp,
            (weights, True),
            spatial_weights,
            (rel_tables, True),
            rowidx,
            colidx,
        ],
        [
            ((3, length, inner), BF16),
            ((2, length, inner), BF16),
            ((heads, length, length), F32),
            ((half, inner), BF16),
            ((half, inner), BF16),
        ],
        2 * length * (width * inner * 5 + heads * length * DH * 12),
        [pltpu.VMEM((length, inner), BF16)],
    )
    att_recv = swap(att_send, "zh")
    keep, send, exit_partner = run(
        mixed_kernel,
        [att_own, att_recv, (exit_matrix, True), up_parts[0], up_parts[1]],
        [((rows, width), F32), ((rows, width), BF16), ((inner, width), BF16)],
        2 * length * inner * width,
    )
    mixed0 = added(keep, swap(send, "core"))
    far = swap(mixed0, "zl").reshape(2, 2, least, width)
    mixed0 = added(mixed0, jnp.flip(far, 1).reshape(rows, width))
    mixed1 = swap(mixed0, "core")
    mixed_far0 = swap(mixed0, "zh")
    mixed_far1 = swap(mixed_far0, "core")

    gains = (ln_gains, True)
    shifts = (ln_shifts, True)
    up = (up_weight, True)
    down = (shrink_projection_array, True)
    hidden_rows = (hidden_bias[:, None], True)
    matrix_flops = 2 * half * width * hidden
    low, active, slope, up_partner, down_partner = run(
        forward_kernel,
        [x, mixed0, mixed1, gains, shifts, up, hidden_rows, down, *up_parts, *down_parts],
        [
            ((half, width), BF16),
            ((2, half, hidden), BF16),
            ((2, half, hidden), F32),
            ((width, hidden), BF16),
            ((hidden, width), BF16),
        ],
        4 * matrix_flops,
    )
    low_recv = swap(low, "zl")
    normed_far, active_far, slope_far = run(
        other_kernel,
        [x, mixed_far0, mixed_far1, gains, shifts, up, hidden_rows],
        [((half, width), BF16), ((half, hidden), BF16), ((half, hidden), F32)],
        matrix_flops,
    )
    out_keep, out_send, hid, second, normed, dlow, dlow_send, dup, sums_two = run(
        middle_kernel,
        [
            x,
            mixed0,
            mixed1,
            low,
            low_recv,
            cot,
            gains,
            shifts,
            (b_down[:, None], True),
            up,
            down,
            up_partner,
            down_partner,
            slope,
        ],
        [
            ((rest, width), BF16),
            ((rest, width), BF16),
            ((half, width), BF16),
            ((half, width), F32),
            ((half, width), BF16),
            ((half, width), BF16),
            ((rows, width), BF16),
            ((half, hidden), BF16),
            ((8, width), F32),
        ],
        4 * matrix_flops,
    )
    hid_recv = swap(hid, "zl")
    dlow_far0 = swap(dlow_send, "zh")
    dlow_far1 = swap(dlow_far0, "zl")
    first, dmix, sums_one = run(
        first_kernel,
        [x, mixed0, mixed1, second, hid, hid_recv, gains],
        [((half, width), F32), ((half, width), BF16), ((8, width), F32)],
        0,
    )
    datt, datt_send, dmix, pay = run(
        attended_kernel,
        [dmix, swap(dmix, "core"), (exit_matrix, True), exit_partner, sums_one, sums_two],
        [
            ((half, inner), BF16),
            ((half, inner), BF16),
            ((half, width), BF16),
            ((rows + 16, width), BF16),
        ],
        2 * length * inner * width,
    )
    datt_recv = swap(datt_send, "zh")
    pay_recv = swap(pay, "zh")
    pay_core = swap(pay_recv, "core")
    piece = ((rows, width), BF16)
    dscore, dproj, dspat, dxk0, dxk1, dxs0, dxs1, dsk0, dsk1, dss0, dss1 = run(
        functools.partial(backward_kernel, heads=heads, block=128),
        [datt, datt_recv, first, soft, proj, spat, (weights, True), spatial_weights],
        [
            ((heads, length, length), BF16),
            ((3, length, inner), BF16),
            ((2, length, inner), BF16),
        ]
        + [piece] * 8,
        2 * length * (width * inner * 5 + heads * length * DH * 6),
    )

    dso1 = added(dsk1, swap(dss1, "core"))
    dso0 = added(dsk0, swap(dss0, "core"))
    units = (
        (dxk0, dxk1),
        (swap(dxs0, "core"), swap(dxs1, "core")),
        (dso0, dso1),
    )
    ends = []
    for near, far in units:
        total = added(near, swap(far, "zl"))
        ends.append(added(total[:rest], swap(total[rest:], "zh")))
    ends = jnp.stack(ends).reshape(3, 2, least, width)

    def to_owner(array):
        array = jnp.stack([array[:, 0], swap(array[:, 1], "y")], axis=1)
        array = jnp.stack([array, swap(array, "zh")])
        return jnp.stack([array, swap(array, "zl")])

    def in_order(array):
        array = in_place(in_place(array, zl, 0), zh, 1)
        array = in_place(array, page, 3)
        array = array.transpose(2, 3, 1, 0, 4, 5)
        return array.reshape(array.shape[0], 2, rows, width)

    ends = in_order(to_owner(ends))
    grad_tokens = in_place(ends[:2], core, 0).astype(F32)
    grad_spatial = ends[2].astype(F32)
    outs = jnp.stack([out_keep, swap(out_send, "core")]).reshape(2, 2, least, width)
    output = in_place(in_order(to_owner(outs)), core, 0)

    up_grad, down_grad, bias_grad = run(
        ffn_grad_kernel,
        [
            normed,
            normed_far,
            active,
            active_far,
            dlow,
            dlow_far0,
            dlow_far1,
            dup,
            slope_far,
            down,
        ],
        [((width, hidden), BF16), ((hidden, width), BF16), ((8, hidden), F32)],
        5 * matrix_flops,
    )
    up_grad, down_grad = summed(up_grad, down_grad)
    grads_one, grads_two = run(
        functools.partial(attention_grad_kernel, heads=heads),
        [
            dmix,
            pay,
            pay_recv,
            pay_core,
            att_own,
            att_send,
            x,
            sp,
            dscore,
            dproj,
            dspat,
            colidx,
            bias_grad,
        ],
        [((3 * inner + 32, width), BF16), ((3 * inner, width), BF16)],
        2 * length * (width * inner * 6 + heads * length * width),
    )
    grads_one, grads_two = summed(grads_one, grads_two)

    def both_streams(array):
        return in_place(jnp.stack([array, swap(array, "core")]), core, 0).astype(F32)

    grads_one = both_streams(grads_one)
    grads_two = both_streams(grads_two)
    grad_qkv = grads_one[:, : 3 * inner].reshape(2, 3, inner, width).swapaxes(2, 3)
    grad_exit = grads_two[:, :inner]
    grad_spatial_w = grads_two[0, inner:] + grads_two[1, inner:]
    grad_spatial_w = grad_spatial_w.reshape(2, inner, width).swapaxes(1, 2)
    small = grads_one[:, 3 * inner :]
    part = width // (2 * lax.axis_size("zh"))
    sums = lax.dynamic_slice_in_dim(small[:, :16], (2 * zh + zl) * part, part, 2)
    tables = small[:, 16:18].reshape(2, -1, NBUCK)[:, : 3 * heads]
    tables = tables.reshape(2, 3, heads, NBUCK)
    gains_grad = jnp.stack([sums[:, 0], sums[:, 8]], axis=1)
    shifts_grad = jnp.stack([sums[:, 1], sums[:, 9]], axis=1)
    return (
        output,
        grad_tokens,
        grad_spatial,
        grad_qkv,
        grad_spatial_w,
        tables,
        grad_exit,
        gains_grad,
        shifts_grad,
        both_streams(up_grad),
        small[:, 18],
        both_streams(down_grad),
        sums[:, 10],
    )


def solution(mesh):
    batch, seq, head = mesh.devices.shape
    fine = Mesh(
        mesh.devices.reshape(batch, seq // 2, 2, head // 2, 2),
        ("batch", "y", "core", "zh", "zl"),
    )
    seq = ("y", "core")
    head = ("zh", "zl")
    return jax.shard_map(
        shards,
        mesh=fine,
        in_specs=(
            P(None, "batch", seq, None),
            P("batch", seq, None),
            P("batch", seq),
            P(None, "batch", seq),
            P(None, None, None, head),
            P(None, None, head),
            P(None, None, head, None),
            P(None, head, None),
            P(),
            P(),
            P(None, None, head),
            P(None, head),
            P(None, head, None),
            P(),
            P(None, "batch", seq, None),
        ),
        out_specs=(
            P(None, "batch", seq, None),
            P(None, "batch", seq, None),
            P("batch", seq, None),
            P(None, None, None, head),
            P(None, None, head),
            P(None, None, head, None),
            P(None, head, None),
            P(None, None, head),
            P(None, None, head),
            P(None, None, head),
            P(None, head),
            P(None, head, None),
            P(None, head),
        ),
        check_vma=False,
    )
```

```python
import functools

import jax
import jax.numpy as jnp
from jax import lax
from jax.experimental import pallas as pl
from jax.experimental.pallas import tpu as pltpu
from jax.sharding import Mesh, PartitionSpec as P

DH = 64
NBUCK = 128
HALF = 64
EPSILON = 1e-05
F32 = jnp.float32
BF16 = jnp.bfloat16
VMEM_BYTES = 20 * 1024 * 1024
TICK = 0.1
PACK_VMEM = 60 * 1024 * 1024
NN = (((1,), (0,)), ((), ()))
NT = (((1,), (1,)), ((), ()))
TN = (((0,), (0,)), ((), ()))


def mm(left, right, dims=NN):
    return lax.dot_general(left, right, dims, preferred_element_type=F32)


def kernel_call(body, place, operands, outs, us, scratch=(), after=(), vmem=VMEM_BYTES):
    specs, arrays, hows = [], [], []
    for operand in operands:
        array, how = operand if isinstance(operand, tuple) else (operand, None)
        specs.append(pl.BlockSpec(memory_space=pltpu.HBM if how == "any" else pltpu.VMEM))
        arrays.append(array)
        hows.append(how)
    count = len(arrays)
    specs += [pl.BlockSpec(memory_space=pl.ANY)] * len(after)

    def view(s_ref, ref, how):
        if how == "stream":
            return ref.at[s_ref[0]]
        if how is None or how == "any":
            return ref
        return ref.at[tuple(slice(None) if at is None else at for at in how)]

    def kernel(s_ref, *refs):
        given = [view(s_ref, ref, how) for ref, how in zip(refs, hows)]
        body(s_ref, *given, *refs[count + len(after) :])

    return pl.pallas_call(
        kernel,
        out_shape=[jax.ShapeDtypeStruct(out[0], out[1]) for out in outs],
        in_specs=[pl.BlockSpec(memory_space=pltpu.SMEM)] + specs,
        out_specs=[
            pl.BlockSpec(memory_space=pltpu.HBM if len(out) > 2 else pltpu.VMEM) for out in outs
        ],
        scratch_shapes=list(scratch),
        compiler_params=pltpu.CompilerParams(vmem_limit_bytes=vmem),
        cost_estimate=pl.CostEstimate(
            flops=int(us * 1.1e9), bytes_accessed=int(us * 3.5e6), transcendentals=0
        ),
    )(place, *arrays, *after)


def centred(rows):
    centre = rows - jnp.mean(rows, axis=-1, keepdims=True)
    spread = lax.rsqrt(jnp.mean(centre * centre, axis=-1, keepdims=True) + EPSILON)
    return centre * spread, spread


def norm_back(unit, spread, tilted):
    return spread * (
        tilted
        - jnp.mean(tilted, axis=-1, keepdims=True)
        - unit * jnp.mean(tilted * unit, axis=-1, keepdims=True)
    )


def pick(table_row, index):
    width = index.shape[1]
    table = jnp.broadcast_to(table_row, (index.shape[0], NBUCK))
    parts = [
        jnp.take_along_axis(
            table,
            index[:, at : at + NBUCK],
            axis=1,
            mode="promise_in_bounds",
        )
        for at in range(0, width, NBUCK)
    ]
    return jnp.concatenate(parts, axis=1)


def stack_rows(pieces):
    return jnp.concatenate(pieces, axis=0)


def turned(rows, size):
    pieces = [rows[at : at + size] for at in range(0, rows.shape[0], size)]
    return stack_rows([pieces[i ^ 1] for i in range(len(pieces))])


def residual(x_ref, mixed_refs):
    rest = mixed_refs[0].shape[0] // 2
    pieces = []
    for y in range(2):
        for c in range(2):
            own = x_ref[y, c * rest : (c + 1) * rest, :].astype(F32)
            pieces.append(own + mixed_refs[c][y * rest : (y + 1) * rest, :].astype(F32))
    return stack_rows(pieces)


def dealt(rows_ref, side, keep_ref, send_ref):
    half = keep_ref.shape[0]
    keep_ref[...] = rows_ref[pl.ds(pl.multiple_of(side * half, 16), half), :]
    send_ref[...] = rows_ref[pl.ds(pl.multiple_of((1 - side) * half, 16), half), :]


def gathered(place_ref, refs, rows, to_ref):
    size = rows.stop - rows.start
    for turn, ref in enumerate(refs):
        q = (place_ref[1] ^ (turn // 2)) * 2 + (place_ref[2] ^ (turn % 2))
        to_ref[pl.ds(pl.multiple_of(q * size, 16), size), :] = ref[rows, :]


def pack_kernel(
    p_ref,
    tok_ref,
    sp_ref,
    pos_ref,
    box_ref,
    exit_ref,
    up_ref,
    down_ref,
    bias_ref,
    cot_ref,
    far_ref,
    near_ref,
    own_ref,
    ups_ref,
    downs_ref,
    cotfar_ref,
    cotnear_ref,
    cotown_ref,
    posv_ref,
    boxv_ref,
    biasv_ref,
    sems,
):
    c, y, zl, zh = p_ref[0], p_ref[2], p_ref[3], p_ref[4]
    block = zh * 2 + zl
    q = p_ref[1] * 2 + y
    least = tok_ref.shape[3]
    rows = 4 * least
    many = down_ref.shape[1] // 4
    few = exit_ref.shape[1] // 4
    pairs = [(pos_ref, posv_ref), (box_ref, boxv_ref), (bias_ref, biasv_ref)]
    for k in range(4):
        at = block ^ k
        to = k * least
        pairs += [
            (tok_ref.at[1 - c, 1 - y, at], far_ref.at[pl.ds(to, least)]),
            (sp_ref.at[1 - y, at], far_ref.at[pl.ds(rows + to, least)]),
            (tok_ref.at[c, 1 - y, at], far_ref.at[pl.ds(2 * rows + 16 + to, least)]),
            (tok_ref.at[1 - c, y, at], near_ref.at[pl.ds(to, least)]),
            (sp_ref.at[y, at], near_ref.at[pl.ds(rows + to, least)]),
            (tok_ref.at[c, y, at], own_ref.at[pl.ds(to, least)]),
        ]
    pairs += [
        (exit_ref.at[c, pl.ds(pl.multiple_of(q * few, 16), few)], ups_ref.at[pl.ds(many + 16, few)]),
        (up_ref.at[c, pl.ds(pl.multiple_of(q * many, 16), many)], ups_ref.at[pl.ds(0, many)]),
        (down_ref.at[c, pl.ds(pl.multiple_of(q * many, 16), many)], downs_ref),
    ]
    for k in range(2):
        at = zh * 2 + (zl ^ k)
        to = pl.ds(k * least, least)
        pairs += [
            (cot_ref.at[c, 1 - y, at], cotfar_ref.at[0, to]),
            (cot_ref.at[1 - c, 1 - y, at], cotfar_ref.at[1, to]),
            (cot_ref.at[1 - c, y, at], cotnear_ref.at[to]),
            (cot_ref.at[c, y, at], cotown_ref.at[to]),
        ]
    started = [
        pltpu.make_async_copy(source, target, sems.at[n])
        for n, (source, target) in enumerate(pairs)
    ]
    for copy in started:
        copy.start()
    for copy in started[:3]:
        copy.wait()
    lane = lax.broadcasted_iota(jnp.int32, (8, NBUCK), 1)
    width = far_ref.shape[1]
    for page, ref in ((1 - y, far_ref), (y, near_ref)):
        place = posv_ref[pl.ds(page, 1), :]
        lines = [place & 255, place >> 8, boxv_ref[0, pl.ds(page, 1), :], boxv_ref[1, pl.ds(page, 1), :]]
        value = jnp.concatenate(lines + [jnp.zeros((4, NBUCK), jnp.int32)], axis=0)
        crossed = jnp.where(
            (lane & 63) < 32, pltpu.roll(value, NBUCK - 32, 1), pltpu.roll(value, 32, 1)
        )
        value = jnp.where(zl == 0, value, crossed)
        value = jnp.where(zh == 0, value, pltpu.roll(value, 64, 1))
        value = jnp.concatenate([value.astype(F32), jnp.zeros((8, NBUCK), F32)], axis=0)
        ref[2 * rows : 2 * rows + 16, 0:NBUCK] = value.astype(BF16)
        ref[2 * rows : 2 * rows + 16, NBUCK:] = jnp.zeros((16, width - NBUCK), BF16)
    left = biasv_ref[pl.ds(c, 1), :]
    lines = []
    for _ in range(3):
        lines.append(left.astype(BF16).astype(F32))
        left = left - lines[-1]
    lines.append(jnp.zeros((13, left.shape[1]), F32))
    ups_ref[many : many + 16, :] = jnp.concatenate(lines, axis=0).astype(BF16)
    for copy in started[3:]:
        copy.wait()


def indices(ref, least):
    lines = ref[2 * least : 2 * least + 16, 0:NBUCK].astype(F32).astype(jnp.int32)
    place = lines[0:1] + lines[1:2] * 256
    return jnp.concatenate([place, lines[2:4], jnp.zeros((5, NBUCK), jnp.int32)], axis=0)


def two_cores(index0, index1, half):
    lane = lax.broadcasted_iota(jnp.int32, (8, NBUCK), 1)
    if half == 0:
        return jnp.where(lane < 64, index0, pltpu.roll(index1, 64, 1))
    return jnp.where(lane < 64, pltpu.roll(index0, 64, 1), index1)


def arrange(x0_ref, n0_ref, n1_ref, x_ref, sp_ref):
    least = x_ref.shape[1]
    rest = least // 2
    found = []
    index0, index1 = indices(n0_ref, least), indices(n1_ref, least)
    for half in range(2):
        at = half * rest
        x_ref[half, 0:rest, :] = x0_ref[at : at + rest, :]
        x_ref[half, rest:, :] = n1_ref[at : at + rest, :]
        sp_ref[half, 0:rest, :] = n0_ref[least + at : least + at + rest, :]
        sp_ref[half, rest:, :] = n1_ref[least + at : least + at + rest, :]
        found.append(two_cores(index0, index1, half))
    return found


def project(x_ref, sp_ref, w_ref, ws_ref, proj_ref, spat_ref, at):
    width = x_ref.shape[-1]
    x = x_ref[...].reshape(-1, width)
    sp = sp_ref[...].reshape(-1, width)
    rows = slice(at, at + x.shape[0])
    for k in range(3):
        proj_ref[k, rows, :] = mm(x, w_ref[k], NT).astype(BF16)
    for k in range(2):
        spat_ref[k, rows, :] = mm(sp, ws_ref[k], NT).astype(BF16)


def near_kernel(
    p_ref,
    x00_ref,
    n01_ref,
    n00_ref,
    w_ref,
    ws_ref,
    up_hbm,
    down_hbm,
    exit_hbm,
    x_ref,
    sp_ref,
    index_ref,
    proj_ref,
    spat_ref,
    up_ref,
    down_ref,
    exit_ref,
    sems,
):
    fetched = [
        pltpu.make_async_copy(source.at[p_ref[0]], target, sems.at[n])
        for n, (source, target) in enumerate(
            ((exit_hbm, exit_ref), (up_hbm, up_ref), (down_hbm, down_ref))
        )
    ]
    for copy in fetched:
        copy.start()
    found = arrange(x00_ref, n00_ref, n01_ref, x_ref, sp_ref)
    index_ref[...] = jnp.concatenate(found, axis=1)
    project(x_ref, sp_ref, w_ref, ws_ref, proj_ref, spat_ref, 0)
    for copy in fetched:
        copy.wait()


def attention_kernel(
    p_ref,
    n11_ref,
    n10_ref,
    x0_ref,
    sp0_ref,
    index_ref,
    proj0_ref,
    spat0_ref,
    w_ref,
    ws_ref,
    table_ref,
    x_ref,
    sp_ref,
    colidx_ref,
    proj_hbm,
    spat_hbm,
    soft_hbm,
    own_ref,
    send_ref,
    att_ref,
    proj_ref,
    spat_ref,
    soft_ref,
    sems,
    *,
    heads,
    block,
):
    least = x_ref.shape[2]
    near = 2 * least
    x_ref[0] = x0_ref[...]
    sp_ref[0] = sp0_ref[...]
    proj_ref[:, 0:near, :] = proj0_ref[...]
    spat_ref[:, 0:near, :] = spat0_ref[...]
    found = arrange(
        n10_ref.at[2 * least + 16 :], n10_ref, n11_ref, x_ref.at[1], sp_ref.at[1]
    )
    places = jnp.concatenate([index_ref[...]] + found, axis=1)
    colidx_ref[...] = jnp.transpose(places.astype(F32)).astype(jnp.int32)
    project(x_ref.at[1], sp_ref.at[1], w_ref, ws_ref, proj_ref, spat_ref, near)
    length = 2 * near
    stored = [
        pltpu.make_async_copy(proj_ref, proj_hbm, sems.at[0]),
        pltpu.make_async_copy(spat_ref, spat_hbm, sems.at[1]),
    ]
    for copy in stored:
        copy.start()
    level = lax.broadcasted_iota(jnp.int32, (length, NBUCK), 1)
    chosen = [(colidx_ref[:, kind : kind + 1] == level).astype(BF16) for kind in (1, 2)]
    chosen = jnp.concatenate(chosen, axis=1)

    def step(at, carry):
        rows = pl.ds(pl.multiple_of(at * block, block), block)
        lane = lax.broadcasted_iota(jnp.int32, (block, NBUCK), 1)
        index = jnp.clip(places[0:1, :] - colidx_ref[rows, 0:1], -HALF, HALF - 1) + HALF
        boxes = [
            jnp.clip(lane - colidx_ref[rows, kind : kind + 1], -HALF, HALF - 1) + HALF
            for kind in (1, 2)
        ]
        for h in range(heads):
            cols = slice(h * DH, (h + 1) * DH)
            bias = jnp.concatenate(
                [pick(table_ref[k, h : h + 1, :], boxes[k - 1]) for k in (1, 2)], axis=1
            )
            coarse = bias.astype(BF16)
            fine = (bias - coarse.astype(F32)).astype(BF16)
            left = jnp.concatenate(
                [proj_ref[0, rows, cols], spat_ref[0, rows, cols]], axis=1
            ) * jnp.asarray(DH**-0.5, BF16)
            right = jnp.concatenate([proj_ref[1, :, cols], spat_ref[1, :, cols]], axis=1)
            scores = mm(
                jnp.concatenate([left, coarse, fine], axis=1),
                jnp.concatenate([right, chosen, chosen], axis=1),
                NT,
            ) + pick(table_ref[0, h : h + 1, :], index)
            top = jnp.max(scores, axis=-1, keepdims=True)
            raised = jnp.exp(scores - top)
            soft = raised * (1.0 / jnp.sum(raised, axis=-1, keepdims=True))
            soft_ref[h, rows, :] = soft
            att_ref[rows, cols] = mm(soft.astype(BF16), proj_ref[2, :, cols]).astype(BF16)
        saved(at).start()
        return carry

    def saved(at):
        rows = pl.ds(pl.multiple_of(at * block, block), block)
        return pltpu.make_async_copy(
            soft_ref.at[:, rows, :], soft_hbm.at[:, rows, :], sems.at[2 + at]
        )

    lax.fori_loop(0, length // block, step, 0)
    for copy in stored + [saved(at) for at in range(length // block)]:
        copy.wait()
    part = length // 4
    own_ref[0:part, :] = att_ref[0:part, :]
    own_ref[part:, :] = att_ref[2 * part : 3 * part, :]
    send_ref[0:part, :] = att_ref[part : 2 * part, :]
    send_ref[part:, :] = att_ref[3 * part :, :]


def mixed_kernel(
    p_ref,
    own_ref,
    recv_ref,
    exit_ref,
    one0_ref,
    one1_ref,
    one2_ref,
    one3_ref,
    keep_ref,
    send_ref,
    partner_ref,
):
    rows = slice(one0_ref.shape[0] - exit_ref.shape[0] // 4, one0_ref.shape[0])
    gathered(p_ref, (one0_ref, one1_ref, one2_ref, one3_ref), rows, partner_ref)
    total = mm(own_ref[...], exit_ref[...]) + mm(recv_ref[...], partner_ref[...])
    rest = total.shape[0] // 4
    for y in range(2):
        at = 2 * y * rest
        keep_ref[y * rest : (y + 1) * rest, :] = total[at : at + rest]
        send_ref[y * rest : (y + 1) * rest, :] = total[at + rest : at + 2 * rest].astype(BF16)


def gelu_parts(upper):
    phi = 0.5 * (1.0 + lax.erf(upper * (0.5**0.5)))
    slope = phi + upper * (jnp.exp(-0.5 * upper * upper) * (0.5 / jnp.pi) ** 0.5)
    return (upper * phi).astype(BF16), slope


def forward_kernel(
    p_ref,
    x_ref,
    mixed0_ref,
    mixed1_ref,
    gain_ref,
    shift_ref,
    up_ref,
    hidden_ref,
    down_ref,
    one0_ref,
    one1_ref,
    one2_ref,
    one3_ref,
    two0_ref,
    two1_ref,
    two2_ref,
    two3_ref,
    low_ref,
    active_ref,
    slope_ref,
    upp_ref,
    downp_ref,
):
    many = two0_ref.shape[0]
    gathered(p_ref, (one0_ref, one1_ref, one2_ref, one3_ref), slice(0, many), upp_ref)
    gathered(p_ref, (two0_ref, two1_ref, two2_ref, two3_ref), slice(0, many), downp_ref)
    extra = one0_ref[many : many + 16, :].astype(F32)
    partner_bias = extra[0:1] + extra[1:2] + extra[2:3]
    unit, _ = centred(residual(x_ref, (mixed0_ref, mixed1_ref)))
    normed_low = (unit * gain_ref[0:1, :] + shift_ref[0:1, :]).astype(BF16)
    active, slope = gelu_parts(mm(normed_low, up_ref[...]) + hidden_ref[pl.ds(p_ref[0], 1), :])
    active_ref[0] = active
    slope_ref[0] = slope.astype(BF16)
    total = mm(active, down_ref[...])
    active, slope = gelu_parts(mm(normed_low, upp_ref[...]) + partner_bias)
    active_ref[1] = active
    slope_ref[1] = slope.astype(BF16)
    low_ref[...] = (total + mm(active, downp_ref[...])).astype(BF16)


def other_kernel(
    p_ref,
    x_ref,
    mixed0_ref,
    mixed1_ref,
    gain_ref,
    shift_ref,
    up_ref,
    hidden_ref,
    normed_ref,
    active_ref,
    slope_ref,
):
    unit, _ = centred(residual(x_ref, (mixed0_ref, mixed1_ref)))
    normed_low = (unit * gain_ref[0:1, :] + shift_ref[0:1, :]).astype(BF16)
    normed_ref[...] = normed_low
    active, slope = gelu_parts(mm(normed_low, up_ref[...]) + hidden_ref[pl.ds(p_ref[0], 1), :])
    active_ref[...] = active
    slope_ref[...] = slope.astype(BF16)


def middle_kernel(
    p_ref,
    x_ref,
    mixed0_ref,
    mixed1_ref,
    low_ref,
    lowr_ref,
    cot00_ref,
    cot10_ref,
    cot01_ref,
    cot11_ref,
    gain_ref,
    shift_ref,
    bdown_ref,
    up_ref,
    down_ref,
    upp_ref,
    downp_ref,
    slope_ref,
    outk_ref,
    outs_ref,
    hid_ref,
    second_ref,
    normed_ref,
    dlow_ref,
    dlows_ref,
    dup_ref,
    sums_ref,
):
    unit, _ = centred(residual(x_ref, (mixed0_ref, mixed1_ref)))
    normed = unit * gain_ref[0:1, :] + shift_ref[0:1, :]
    normed_ref[...] = normed.astype(BF16)
    length = normed.shape[0]
    least = length // 8
    lowered = low_ref[...].astype(F32) + turned(lowr_ref[...], least).astype(F32)
    unit2, spread2 = centred(normed + lowered + bdown_ref[pl.ds(p_ref[0], 1), :])
    out = (unit2 * gain_ref[1:2, :] + shift_ref[1:2, :]).astype(BF16)
    for y in range(2):
        at = 4 * y * least
        outk_ref[y * least : (y + 1) * least, :] = out[at : at + least]
        outs_ref[y * least : (y + 1) * least, :] = out[at + 2 * least : at + 3 * least]
    cot = stack_rows([cot00_ref[...], cot01_ref[...], cot10_ref[0], cot11_ref[1]]).astype(F32)
    second = norm_back(unit2, spread2, cot * gain_ref[1:2, :])
    second_ref[...] = second
    sums_ref[...] = jnp.zeros_like(sums_ref)
    sums_ref[0:1, :] = jnp.sum(cot * unit2, axis=0, keepdims=True)
    sums_ref[1:2, :] = jnp.sum(cot, axis=0, keepdims=True)
    sums_ref[2:3, :] = jnp.sum(second, axis=0, keepdims=True)
    dlow = second.astype(BF16)
    dlow_ref[...] = dlow
    for i in range(4):
        dlows_ref[i * least : (i + 1) * least, :] = dlow[2 * i * least : (2 * i + 1) * least]
    dup = (mm(dlow, down_ref[...], NT) * slope_ref[0].astype(F32)).astype(BF16)
    dup_ref[...] = dup
    total = mm(dup, up_ref[...], NT)
    dup = (mm(dlow, downp_ref[...], NT) * slope_ref[1].astype(F32)).astype(BF16)
    hid_ref[...] = (total + mm(dup, upp_ref[...], NT)).astype(BF16)


def ffn_grad_kernel(
    p_ref,
    normed_ref,
    normedo_ref,
    active_ref,
    activeo_ref,
    dlow_ref,
    dlow0_ref,
    dlow1_ref,
    dup_ref,
    slopeo_ref,
    down_ref,
    upk_ref,
    ups_ref,
    downk_ref,
    downs_ref,
    bias_ref,
    all_ref,
):
    least = dlow0_ref.shape[0] // 4
    pieces = []
    for i in range(4):
        pieces.append(dlow0_ref[i * least : (i + 1) * least, :])
        pieces.append(dlow1_ref[i * least : (i + 1) * least, :])
    dlowo = stack_rows(pieces)
    dupo = (mm(dlowo, down_ref[...], NT) * slopeo_ref[...].astype(F32)).astype(BF16)
    dup = dup_ref[...]
    all_ref[...] = (mm(normed_ref[...], dup, TN) + mm(normedo_ref[...], dupo, TN)).astype(BF16)
    dealt(all_ref, p_ref[1], upk_ref, ups_ref)
    all_ref[...] = (
        mm(active_ref[...], dlow_ref[...], TN) + mm(activeo_ref[...], dlowo, TN)
    ).astype(BF16)
    dealt(all_ref, p_ref[2], downk_ref, downs_ref)
    bias = jnp.sum(dup.astype(F32), axis=0, keepdims=True)
    bias = bias + jnp.sum(dupo.astype(F32), axis=0, keepdims=True)
    bias_ref[...] = jnp.broadcast_to(bias, bias_ref.shape)


def first_kernel(
    p_ref,
    x_ref,
    mixed0_ref,
    mixed1_ref,
    second_ref,
    hid_ref,
    hidr_ref,
    gain_ref,
    first_ref,
    dmix_ref,
    sums_ref,
):
    unit, spread = centred(residual(x_ref, (mixed0_ref, mixed1_ref)))
    hid = hid_ref[...].astype(F32) + turned(hidr_ref[...], hid_ref.shape[0] // 8).astype(F32)
    dnormed = second_ref[...] + hid
    first = norm_back(unit, spread, dnormed * gain_ref[0:1, :])
    first_ref[...] = first
    dmix_ref[...] = first.astype(BF16)
    sums_ref[...] = jnp.zeros_like(sums_ref)
    sums_ref[0:1, :] = jnp.sum(dnormed * unit, axis=0, keepdims=True)
    sums_ref[1:2, :] = jnp.sum(dnormed, axis=0, keepdims=True)


def attended_kernel(
    p_ref,
    dmix_ref,
    dmixr_ref,
    exit_ref,
    exitp_ref,
    sums1_ref,
    sums2_ref,
    own_ref,
    send_ref,
    total_ref,
    pay_ref,
):
    length = dmix_ref.shape[0]
    rest = length // 4
    total = dmix_ref[...].astype(F32) + turned(dmixr_ref[...], rest).astype(F32)
    total = total.astype(BF16)
    total_ref[...] = total
    own_ref[...] = mm(total, exit_ref[...], NT).astype(BF16)
    send_ref[...] = mm(total, exitp_ref[...], NT).astype(BF16)
    pay_ref[0:rest, :] = total[0:rest]
    pay_ref[rest : 2 * rest, :] = total[2 * rest : 3 * rest]
    pay_ref[2 * rest :, :] = jnp.concatenate([sums1_ref[...], sums2_ref[...]], axis=0).astype(BF16)


def backward_kernel(
    p_ref,
    datt_ref,
    dattr_ref,
    first_ref,
    soft_hbm,
    proj_ref,
    spat_ref,
    w_ref,
    ws_ref,
    dscore_ref,
    dproj_ref,
    dspat_ref,
    dxk0_ref,
    dxk1_ref,
    dxs_ref,
    dsk0_ref,
    dsk1_ref,
    dss_ref,
    soft_ref,
    sems,
    *,
    heads,
    block,
):
    fetched = [
        pltpu.make_async_copy(soft_hbm.at[h], soft_ref.at[h], sems.at[h]) for h in range(heads)
    ]
    for copy in fetched:
        copy.start()
    length = 2 * datt_ref.shape[0]
    scale = DH**-0.5
    part = length // 4
    datt = stack_rows(
        [datt_ref[0:part, :], dattr_ref[0:part, :], datt_ref[part:, :], dattr_ref[part:, :]]
    )
    for h in range(heads):
        cols = slice(h * DH, (h + 1) * DH)
        value = proj_ref[2, :, cols]
        left = jnp.concatenate([proj_ref[0, :, cols], spat_ref[0, :, cols]], axis=1)
        right = jnp.concatenate([proj_ref[1, :, cols], spat_ref[1, :, cols]], axis=1)
        own = datt[:, cols]
        fetched[h].wait()
        for at in range(0, length, block):
            soft = soft_ref[h, at : at + block, :]
            dsoft = mm(own[at : at + block], value, NT)
            inner = jnp.sum(soft * dsoft, axis=-1, keepdims=True)
            dscore_ref[h, at : at + block, :] = (soft * (dsoft - inner)).astype(BF16)
        dscore = dscore_ref[h]
        dleft = (mm(dscore, right) * scale).astype(BF16)
        dright = (mm(dscore, left, TN) * scale).astype(BF16)
        dproj_ref[0, :, cols] = dleft[:, :DH]
        dspat_ref[0, :, cols] = dleft[:, DH:]
        dproj_ref[1, :, cols] = dright[:, :DH]
        dspat_ref[1, :, cols] = dright[:, DH:]
        dproj_ref[2, :, cols] = mm(soft_ref[h].astype(BF16), own, TN).astype(BF16)
    once = (p_ref[3] == 0).astype(F32)
    total = mm(dproj_ref[0], w_ref[0])
    for k in range(1, 3):
        total = total + mm(dproj_ref[k], w_ref[k])
    least = part // 4

    def deal(rows, refs):
        for y in range(2):
            for zh in range(2):
                for c in range(2):
                    for zl in range(2):
                        at = (((y * 2 + zh) * 2 + c) * 2 + zl) * least
                        to = (zh * 2 + y) * least
                        value = rows[at : at + least]
                        if zh == 0 and refs[0][0] is dxk0_ref:
                            of = ((y * 2 + c) * 2 + zl) * least
                            value = value + once * first_ref[of : of + least, :]
                        refs[c][zl][to : to + least, :] = value.astype(BF16)

    deal(total, ((dxk0_ref, dxk1_ref), (dxs_ref.at[0], dxs_ref.at[1])))
    total = mm(dspat_ref[0], ws_ref[0]) + mm(dspat_ref[1], ws_ref[1])
    deal(total, ((dsk0_ref, dsk1_ref), (dss_ref.at[0], dss_ref.at[1])))


def second_grad_kernel(
    p_ref,
    dmix_ref,
    pay_ref,
    payr_ref,
    payc_ref,
    atto_ref,
    atts_ref,
    sp_ref,
    dspat_ref,
    lines_ref,
    keep_ref,
    send_ref,
    second_ref,
):
    width = sp_ref.shape[-1]
    sp = sp_ref[...].reshape(-1, width)
    inner = dspat_ref.shape[-1]
    rest = sp.shape[0] // 8
    dmixo = stack_rows(
        [payr_ref[0:rest, :], payc_ref[0:rest, :], payr_ref[rest : 2 * rest, :], payc_ref[rest : 2 * rest, :]]
    )
    second_ref[0:inner, :] = (
        mm(atto_ref[...], dmix_ref[...], TN) + mm(atts_ref[...], dmixo, TN)
    ).astype(BF16)
    for k in range(2):
        second_ref[(k + 1) * inner : (k + 2) * inner, :] = mm(dspat_ref[k], sp, TN).astype(BF16)
    base = 3 * inner
    small = pay_ref[2 * rest :, :].astype(F32) + payr_ref[2 * rest :, :].astype(F32)
    second_ref[base : base + 16, :] = small.astype(BF16)
    second_ref[base + 16 : base + 32, :] = lines_ref[...].astype(BF16)
    dealt(second_ref, p_ref[2], keep_ref, send_ref)


def first_grad_kernel(
    p_ref,
    x_ref,
    dscore_ref,
    dproj_ref,
    colidx_ref,
    bup_ref,
    keep_ref,
    send_ref,
    lines_ref,
    first_ref,
    *,
    heads,
):
    width = x_ref.shape[-1]
    x = x_ref[...].reshape(-1, width)
    length = x.shape[0]
    inner = dproj_ref.shape[-1]
    for k in range(3):
        first_ref[k * inner : (k + 1) * inner, :] = mm(dproj_ref[k], x, TN).astype(BF16)
    dealt(first_ref, p_ref[1], keep_ref, send_ref)
    lane = lax.broadcasted_iota(jnp.int32, (1, NBUCK), 1)
    found = []
    for kind in range(3):
        extent = length if kind == 0 else NBUCK
        own = colidx_ref[:, kind : kind + 1]
        level = lax.broadcasted_iota(jnp.int32, (length, extent), 1)
        chosen = (own == level).astype(BF16)
        place = own - HALF + lax.broadcasted_iota(jnp.int32, (length, NBUCK), 1)
        turn = place & (NBUCK - 1)
        piece = place >> 7
        for h in range(heads):
            spread = mm(dscore_ref[h], chosen)
            window = jnp.zeros((length, NBUCK), F32)
            for q in range(extent // NBUCK):
                part = jnp.take_along_axis(
                    spread[:, q * NBUCK : (q + 1) * NBUCK],
                    turn,
                    axis=1,
                    mode="promise_in_bounds",
                )
                window = window + jnp.where(piece == q, part, 0.0)
            row = jnp.sum(window, axis=0, keepdims=True)
            row = jnp.where((lane > 0) & (lane < NBUCK - 1), row, 0.0)
            least = jnp.sum(jnp.where(level <= own - HALF, spread, 0.0), axis=0, keepdims=True)
            most = jnp.sum(jnp.where(level >= own + HALF - 1, spread, 0.0), axis=0, keepdims=True)
            row = row + jnp.where(lane == 0, jnp.sum(least, axis=1, keepdims=True), 0.0)
            row = row + jnp.where(
                lane == NBUCK - 1, jnp.sum(most, axis=1, keepdims=True), 0.0
            )
            found.append(row)
    per = width // NBUCK
    found = found + [jnp.zeros((1, NBUCK), F32)] * (-len(found) % per)
    lines = [
        jnp.concatenate(found[at : at + per], axis=1) for at in range(0, len(found), per)
    ]
    lines.append(bup_ref[0:1, :])
    lines_ref[...] = jnp.concatenate(
        lines + [jnp.zeros((16 - len(lines), width), F32)], axis=0
    )


def ends_kernel(
    p_ref,
    w_ref,
    y_ref,
    zhw_ref,
    zlw_ref,
    zzw_ref,
    tok_ref,
    sp_ref,
    event_ref,
):
    c, y, block = p_ref[0], p_ref[2], p_ref[4] * 2 + p_ref[3]
    for turn, ref in enumerate((None, zlw_ref, zhw_ref, zzw_ref)):
        at = block ^ turn
        for far in range(2):
            for unit in range(3):
                if ref is None:
                    value = (y_ref if far else w_ref)[unit]
                else:
                    value = ref[far, unit]
                value = value.astype(F32)
                if unit < 2:
                    tok_ref[c ^ unit, y ^ far, at] = value
                else:
                    sp_ref[y ^ far, at] = value
    event_ref[...] = jnp.zeros_like(event_ref)


def out_kernel(p_ref, w_ref, y_ref, zh_ref, zl_ref, zz_ref, out_ref):
    c, y, block = p_ref[0], p_ref[2], p_ref[4] * 2 + p_ref[3]
    for turn, ref in enumerate((None, zl_ref, zh_ref, zz_ref)):
        at = block ^ turn
        for far in range(2):
            for unit in range(2):
                if ref is None:
                    value = (y_ref if far else w_ref)[unit]
                else:
                    value = ref[far, unit]
                out_ref[c ^ unit, y ^ far, at] = value


def turn_kernel(p_ref, own_ref, far_ref, sum_ref, *, size):
    far = turned(far_ref[...], size).astype(F32)
    sum_ref[...] = (own_ref[...].astype(F32) + far).astype(BF16)


def units_kernel(p_ref, near_ref, far_ref, other_ref, spat_ref, nears_ref, fars_ref):
    nears_ref[0] = other_ref[0]
    fars_ref[0] = other_ref[1]
    nears_ref[1] = (near_ref[...].astype(F32) + spat_ref[0].astype(F32)).astype(BF16)
    fars_ref[1] = (far_ref[...].astype(F32) + spat_ref[1].astype(F32)).astype(BF16)


def fold_kernel(p_ref, own_ref, far_ref, keep_ref, send_ref):
    total = (own_ref[...].astype(F32) + far_ref[...].astype(F32)).astype(BF16)
    half = total.shape[-2] // 2
    keep_ref[...] = total[..., :half, :]
    send_ref[...] = total[..., half:, :]


def ends_first_kernel(p_ref, ownk_ref, ownf_ref, bothk_ref, bothf_ref, mine_ref, other_ref):
    least = mine_ref.shape[1]
    for unit in range(3):
        if unit == 0:
            total = ownk_ref[...].astype(F32) + ownf_ref[...].astype(F32)
        else:
            total = bothk_ref[unit - 1].astype(F32) + bothf_ref[unit - 1].astype(F32)
        total = total.astype(BF16)
        mine_ref[unit] = total[:least]
        other_ref[unit] = total[least:]


def spread_kernel(p_ref, *refs):
    c = p_ref[0]
    event_ref = refs[10]
    for n, out_ref in enumerate(refs[8:10]):
        side = p_ref[1 + n]
        for other in range(2):
            for far in range(2):
                out_ref[c ^ other, side ^ far] = refs[n * 4 + other * 2 + far][...].astype(F32)
    event_ref[...] = jnp.zeros_like(event_ref)


def last_kernel(
    p_ref,
    one0_ref,
    one1_ref,
    one2_ref,
    one3_ref,
    two0_ref,
    two1_ref,
    two2_ref,
    two3_ref,
    qkv_ref,
    spat_ref,
    exit_ref,
    tables_ref,
    gains_ref,
    shifts_ref,
    bup_ref,
    bdown_ref,
    first_ref,
    second_ref,
    *,
    heads,
):
    c, head = p_ref[0], p_ref[4] * 2 + p_ref[3]
    inner = exit_ref.shape[1]
    width = exit_ref.shape[2]
    part = gains_ref.shape[2]
    per = width // NBUCK
    base = 3 * inner
    firsts = ((one0_ref, one1_ref), (one2_ref, one3_ref))
    seconds = ((two0_ref, two1_ref), (two2_ref, two3_ref))

    def whole(halves, side, to_ref):
        size = halves[0].shape[0]
        for far in range(2):
            at = pl.multiple_of((side ^ far) * size, 16)
            to_ref[pl.ds(at, size), :] = halves[far][...].astype(F32)

    for other in range(2):
        s = c ^ other
        whole(firsts[other], p_ref[1], first_ref)
        qkv_ref[s] = first_ref[...]
        whole(seconds[other], p_ref[2], second_ref)
        exit_ref[s] = second_ref[0:inner, :]
        if other:
            spat_ref[...] += second_ref[inner:base, :]
        else:
            spat_ref[...] = second_ref[inner:base, :]
        sums = second_ref[base : base + 16, :]
        cut = sums[:, 0:part]
        for at in range(1, width // part):
            cut = jnp.where(head == at, sums[:, at * part : (at + 1) * part], cut)
        gains_ref[s] = jnp.concatenate([cut[0:1], cut[8:9]], axis=0)
        shifts_ref[s] = jnp.concatenate([cut[1:2], cut[9:10]], axis=0)
        bdown_ref[pl.ds(s, 1), :] = cut[10:11]
        lines = second_ref[base + 16 : base + 32, :]
        for n in range(3 * heads):
            at = (n % per) * NBUCK
            tables_ref[s, n // heads, n % heads : n % heads + 1, :] = lines[
                n // per : n // per + 1, at : at + NBUCK
            ]
        bup_ref[pl.ds(s, 1), :] = lines[2:3]


def swap(value, axis, step=1):
    size = lax.axis_size(axis)
    return lax.ppermute(value, axis, [(i, i ^ step) for i in range(size)])


def swap_both(value):
    size = lax.axis_size("batch") * 2
    return lax.ppermute(value, ("batch", "y"), [(i, i ^ 3) for i in range(size)])


def added(left, right):
    return (left.astype(F32) + right.astype(F32)).astype(BF16)


def batch_steps():
    return [1 << bit for bit in range(lax.axis_size("batch").bit_length() - 1)]


def join(*values):
    return lax.optimization_barrier(values)


def shards(
    tokens,
    spatial,
    positions,
    boxes,
    query_key_value_weight,
    w_spatial,
    rel_tables,
    exit_matrix,
    ln_gains,
    ln_shifts,
    up_weight,
    hidden_bias,
    shrink_projection_array,
    b_down,
    cotangent,
):
    heads = rel_tables.shape[2]
    rows = tokens.shape[2]
    width = tokens.shape[3]
    inner = query_key_value_weight.shape[3]
    hidden = up_weight.shape[2]
    least = rows // 4
    rest = rows // 2
    length = 4 * rows
    half = length // 2
    page = lax.axis_index("y")
    core = lax.axis_index("core")
    zh = lax.axis_index("zh")
    zl = lax.axis_index("zl")
    pair = lax.axis_index("batch") & 1
    place = jnp.stack([core, pair, page, zl, zh]).astype(jnp.int32)

    def run(body, operands, outs, us=TICK, scratch=(), after=(), vmem=VMEM_BYTES):
        return kernel_call(body, place, operands, outs, us, scratch, after, vmem)

    def rows_of(count, dtype=BF16):
        return ((count, width), dtype)

    share = hidden // 4
    anywhere = [
        tokens.reshape(2, 2, 4, least, width),
        spatial.reshape(2, 4, least, width),
        positions,
        boxes,
        exit_matrix,
        up_weight,
        shrink_projection_array,
        hidden_bias,
        cotangent.reshape(2, 2, 4, least, width),
    ]
    far, near, x00, up_part, down_part, cot_far, cot_near, cot00 = run(
        pack_kernel,
        [(array, "any") for array in anywhere],
        [
            rows_of(3 * rows + 16),
            rows_of(2 * rows + 16),
            rows_of(rows),
            rows_of(share + 16 + inner // 4),
            rows_of(share),
            ((2, 2 * least, width), BF16),
            rows_of(2 * least),
            rows_of(2 * least),
        ],
        scratch=[
            pltpu.VMEM(positions.shape, jnp.int32),
            pltpu.VMEM(boxes.shape, jnp.int32),
            pltpu.VMEM(hidden_bias.shape, F32),
            pltpu.SemaphoreType.DMA((38,)),
        ],
        vmem=PACK_VMEM,
    )
    n10 = swap(far, "y")
    n01 = swap(near, "core")
    up_part = swap(up_part, "zh")
    weights = (jnp.swapaxes(query_key_value_weight, 2, 3), "stream")
    spatial_weights = jnp.swapaxes(w_spatial, 1, 2)
    x0, sp0, index0, proj0, spat0, up, down, exit_own = run(
        near_kernel,
        [
            x00,
            n01,
            near,
            weights,
            spatial_weights,
            (up_weight, "any"),
            (shrink_projection_array, "any"),
            (exit_matrix, "any"),
        ],
        [
            ((2, rows, width), BF16),
            ((2, rows, width), BF16),
            ((8, 2 * rows), jnp.int32),
            ((3, 2 * rows, inner), BF16),
            ((2, 2 * rows, inner), BF16),
            ((width, hidden), BF16),
            ((hidden, width), BF16),
            rows_of(inner),
        ],
        scratch=[pltpu.SemaphoreType.DMA((3,))],
    )
    n10, x0, up_part, down_part = join(n10, x0, up_part, down_part)
    n11 = swap(n10, "core")
    ups = [up_part, swap(up_part, "y"), swap(up_part, "batch"), swap_both(up_part)]
    down_part = swap(down_part, "zh")

    x, sp, colidx, proj, spat, soft, att_own, att_send = run(
        functools.partial(attention_kernel, heads=heads, block=128),
        [
            n11,
            n10,
            x0,
            sp0,
            index0,
            proj0,
            spat0,
            weights,
            spatial_weights,
            (rel_tables, "stream"),
        ],
        [
            ((2, 2, rows, width), BF16),
            ((2, 2, rows, width), BF16),
            ((length, 8), jnp.int32),
            ((3, length, inner), BF16, "any"),
            ((2, length, inner), BF16, "any"),
            ((heads, length, length), F32, "any"),
            ((half, inner), BF16),
            ((half, inner), BF16),
        ],
        us=30,
        scratch=[
            pltpu.VMEM((length, inner), BF16),
            pltpu.VMEM((3, length, inner), BF16),
            pltpu.VMEM((2, length, inner), BF16),
            pltpu.VMEM((heads, length, length), F32),
            pltpu.SemaphoreType.DMA((2 + length // 128,)),
        ],
    )
    att_send, att_own, *ups, down_part = join(att_send, att_own, *ups, down_part)
    att_recv = swap(att_send, "zh")
    downs = [down_part, swap(down_part, "y"), swap(down_part, "batch"), swap_both(down_part)]

    keep, send, exit_partner = run(
        mixed_kernel,
        [att_own, att_recv, exit_own, *ups],
        [rows_of(rows, F32), rows_of(rows), rows_of(inner)],
    )
    mixed0 = added(keep, swap(send, "core"))
    mixed_zl = swap(mixed0, "zl")
    (mixed0,) = run(
        functools.partial(turn_kernel, size=least), [mixed0, mixed_zl], [rows_of(rows)]
    )
    mixed0, cot_far, cot_near, *downs = join(mixed0, cot_far, cot_near, *downs)
    mixed1 = swap(mixed0, "core")
    cot10 = swap(cot_far, "y")
    cot01 = swap(cot_near, "core")
    mixed_far0 = swap(mixed0, "zh")

    gains = (ln_gains, "stream")
    shifts = (ln_shifts, "stream")
    x_own = (x, (None, 0, None, None))
    x_far = (x, (None, 1, None, None))
    low, active, slope, up_partner, down_partner = run(
        forward_kernel,
        [x_own, mixed0, mixed1, gains, shifts, up, hidden_bias, down, *ups, *downs],
        [
            rows_of(half),
            ((2, half, hidden), BF16),
            ((2, half, hidden), BF16),
            ((width, hidden), BF16),
            ((hidden, width), BF16),
        ],
    )
    low_recv = swap(low, "zl")
    cot11 = swap(cot10, "core")
    mixed_far1 = swap(mixed_far0, "core")
    normed_far, active_far, slope_far = run(
        other_kernel,
        [x_far, mixed_far0, mixed_far1, gains, shifts, up, hidden_bias],
        [rows_of(half), ((half, hidden), BF16), ((half, hidden), BF16)],
        after=[low],
    )
    out_keep, out_send, hid, second, normed, dlow, dlow_send, dup, sums_two = run(
        middle_kernel,
        [
            x_own,
            mixed0,
            mixed1,
            low,
            low_recv,
            cot00,
            cot10,
            cot01,
            cot11,
            gains,
            shifts,
            b_down,
            up,
            down,
            up_partner,
            down_partner,
            slope,
        ],
        [
            rows_of(rest),
            rows_of(rest),
            rows_of(half),
            rows_of(half, F32),
            rows_of(half),
            rows_of(half),
            rows_of(rows),
            ((half, hidden), BF16),
            rows_of(8, F32),
        ],
        after=[slope_far],
    )
    hid_recv = swap(hid, "zl")
    dlow_far0 = swap(dlow_send, "zh")
    out_core = swap(out_send, "core")
    hid_recv, dlow_far0, out_core = join(hid_recv, dlow_far0, out_core)
    dlow_far1 = swap(dlow_far0, "zl")
    first, dmix, sums_one = run(
        first_kernel,
        [x_own, mixed0, mixed1, second, hid, hid_recv, gains],
        [rows_of(half, F32), rows_of(half), rows_of(8, F32)],
    )
    datt, datt_send, dmix, pay = run(
        attended_kernel,
        [dmix, swap(dmix, "core"), exit_own, exit_partner, sums_one, sums_two],
        [
            ((half, inner), BF16),
            ((half, inner), BF16),
            rows_of(half),
            rows_of(rows + 16),
        ],
    )
    datt_recv = swap(datt_send, "zh")
    up_keep, up_send, down_keep, down_send, bias_grad = run(
        ffn_grad_kernel,
        [
            normed,
            normed_far,
            (active, (0, None, None)),
            active_far,
            dlow,
            dlow_far0,
            dlow_far1,
            dup,
            slope_far,
            down,
        ],
        [
            ((width // 2, hidden), BF16),
            ((width // 2, hidden), BF16),
            rows_of(hidden // 2),
            rows_of(hidden // 2),
            ((8, hidden), F32),
        ],
        us=30,
        scratch=[pltpu.VMEM((width, hidden), BF16)],
        after=[datt],
    )
    datt_recv, up_send, down_send, pay = join(datt_recv, up_send, down_send, pay)
    pay_recv = swap(pay, "zh")
    up_recv = swap(up_send, "batch")
    down_recv = swap(down_send, "y")
    piece = rows_of(rows)
    dscore, dproj, dspat, dxk0, dxk1, dxs, dsk0, dsk1, dss = run(
        functools.partial(backward_kernel, heads=heads, block=128),
        [datt, datt_recv, first, (soft, "any"), proj, spat, weights, spatial_weights],
        [
            ((heads, length, length), BF16),
            ((3, length, inner), BF16),
            ((2, length, inner), BF16),
            piece,
            piece,
            ((2, rows, width), BF16),
            piece,
            piece,
            ((2, rows, width), BF16),
        ],
        us=30,
        scratch=[pltpu.VMEM((heads, length, length), F32), pltpu.SemaphoreType.DMA((heads,))],
        after=[bias_grad],
    )

    dxk1, dxs, dss = join(dxk1, dxs, dss)
    own_far = swap(dxk1, "zl")
    dxs, dss = swap(dxs, "core"), swap(dss, "core")
    near, far = run(
        units_kernel,
        [dsk0, dsk1, dxs, dss],
        [((2, rows, width), BF16), ((2, rows, width), BF16)],
    )
    far, own_far, up_recv, down_recv, pay_recv = join(
        far, own_far, up_recv, down_recv, pay_recv
    )
    both_far = swap(far, "zl")
    up_half = added(up_keep, up_recv)
    down_half = added(down_keep, down_recv)
    up_other = swap(up_half, "y")
    down_other = swap(down_half, "batch")
    own_keep, own_send = run(fold_kernel, [dxk0, own_far], [rows_of(rest), rows_of(rest)])
    own_zh = swap(own_send, "zh")
    one_keep, one_send, lines = run(
        functools.partial(first_grad_kernel, heads=heads),
        [x, dscore, dproj, colidx, bias_grad],
        [rows_of(3 * inner // 2), rows_of(3 * inner // 2), rows_of(16, F32)],
        scratch=[pltpu.VMEM((3 * inner, width), BF16)],
        after=[own_send],
    )
    both_far, own_zh, lines = join(both_far, own_zh, lines)
    both_keep, both_send = run(
        fold_kernel, [near, both_far], [((2, rest, width), BF16), ((2, rest, width), BF16)]
    )
    both_zh = swap(both_send, "zh")
    pay_core = swap(pay_recv, "core")
    base = 3 * inner + 32
    two_keep, two_send = run(
        second_grad_kernel,
        [dmix, pay, pay_recv, pay_core, att_own, att_send, sp, dspat, lines],
        [rows_of(base // 2), rows_of(base // 2)],
        scratch=[pltpu.VMEM((base, width), BF16)],
        after=[both_send],
    )
    steps = batch_steps()[1:]

    def total(left, right):
        left = added(left, right)
        for step in steps:
            left = added(left, swap(left, "batch", step))
        return left

    up_other, down_other, two_keep = join(up_other, down_other, two_keep)
    up_half = total(up_half, up_other)
    down_half = total(down_half, down_other)
    up_far = swap(up_half, "batch")
    down_far = swap(down_half, "y")
    both_zh, one_send, two_send, up_half, down_half = join(
        both_zh, one_send, two_send, up_half, down_half
    )
    mine, other = run(
        ends_first_kernel,
        [own_keep, own_zh, both_keep, both_zh],
        [((3, least, width), BF16), ((3, least, width), BF16)],
    )
    got = swap(other, "y")
    got, up_far, down_far, one_send, two_send, out_core = join(
        got, up_far, down_far, one_send, two_send, out_core
    )
    pages = jnp.stack([mine, got])
    pages_zh = swap(pages, "zh")
    pages_zl = swap(pages, "zl")
    one_recv = swap(one_send, "batch")
    two_recv = swap(two_send, "y")
    halves = [up_half, up_far, down_half, down_far]
    others = [swap(value, "core") for value in halves]
    grad_up, grad_down, spread_event = run(
        spread_kernel,
        halves[:2] + others[:2] + halves[2:] + others[2:],
        [
            ((2, 2, width // 2, hidden), F32),
            ((2, 2, hidden // 2, width), F32),
            ((8, NBUCK), F32),
        ],
    )
    one_recv, two_recv, pages_zl, spread_event = join(one_recv, two_recv, pages_zl, spread_event)
    one_half = added(one_keep, one_recv)
    two_half = added(two_keep, two_recv)
    one_other = swap(one_half, "y")
    two_other = swap(two_half, "batch")
    pages_zh, out_core = join(pages_zh, out_core)
    pages_zz = swap(pages_zh, "zl")
    outs = jnp.stack([out_keep, out_core]).reshape(2, 2, least, width)
    out_y = swap(outs[:, 1], "y")
    one_other, two_other, out_y, pages_zz = join(one_other, two_other, out_y, pages_zz)
    one_half = total(one_half, one_other)
    two_half = total(two_half, two_other)
    one_far = swap(one_half, "batch")
    two_far = swap(two_half, "y")
    out_pages = jnp.stack([outs[:, 0], out_y])
    out_zh = swap(out_pages, "zh")
    out_zl = swap(out_pages, "zl")
    grad_tokens, grad_spatial, ends_event = run(
        ends_kernel,
        [mine, got, pages_zh, pages_zl, pages_zz],
        [((2, 2, 4, least, width), F32), ((2, 4, least, width), F32), ((8, NBUCK), F32)],
        after=[one_half, two_half],
    )
    out_zh, out_zl, one_far, two_far, ends_event = join(
        out_zh, out_zl, one_far, two_far, ends_event
    )
    out_zz = swap(out_zh, "zl")
    halves = [one_half, one_far, two_half, two_far]
    others = [swap(value, "core") for value in halves]
    part = width // (2 * lax.axis_size("zh"))
    grad_qkv, grad_spatial_w, grad_exit, tables, gains_grad, shifts_grad, grad_b_up, grad_b_down = run(
        functools.partial(last_kernel, heads=heads),
        halves[:2] + others[:2] + halves[2:] + others[2:],
        [
            ((2, 3 * inner, width), F32),
            rows_of(2 * inner, F32),
            ((2, inner, width), F32),
            ((2, 3, heads, NBUCK), F32),
            ((2, 2, part), F32),
            ((2, 2, part), F32),
            ((2, hidden), F32),
            ((2, part), F32),
        ],
        scratch=[pltpu.VMEM((3 * inner, width), F32), pltpu.VMEM((base, width), F32)],
        after=[spread_event, ends_event],
    )
    (output,) = run(
        out_kernel,
        [outs[:, 0], out_y, out_zh, out_zl, out_zz],
        [((2, 2, 4, least, width), BF16)],
    )
    return (
        output.reshape(tokens.shape),
        grad_tokens.reshape(tokens.shape),
        grad_spatial.reshape(spatial.shape),
        grad_qkv.reshape(2, 3, inner, width).swapaxes(2, 3),
        grad_spatial_w.reshape(2, inner, width).swapaxes(1, 2),
        tables,
        grad_exit,
        gains_grad,
        shifts_grad,
        grad_up.reshape(2, width, hidden),
        grad_b_up,
        grad_down.reshape(2, hidden, width),
        grad_b_down,
    )


def solution(mesh):
    batch, seq, head = mesh.devices.shape
    fine = Mesh(
        mesh.devices.reshape(batch, seq // 2, 2, head // 2, 2),
        ("batch", "y", "core", "zh", "zl"),
    )
    seq = ("y", "core")
    head = ("zh", "zl")
    return jax.shard_map(
        shards,
        mesh=fine,
        in_specs=(
            P(None, "batch", seq, None),
            P("batch", seq, None),
            P("batch", seq),
            P(None, "batch", seq),
            P(None, None, None, head),
            P(None, None, head),
            P(None, None, head, None),
            P(None, head, None),
            P(),
            P(),
            P(None, None, head),
            P(None, head),
            P(None, head, None),
            P(),
            P(None, "batch", seq, None),
        ),
        out_specs=(
            P(None, "batch", seq, None),
            P(None, "batch", seq, None),
            P("batch", seq, None),
            P(None, None, None, head),
            P(None, None, head),
            P(None, None, head, None),
            P(None, head, None),
            P(None, None, head),
            P(None, None, head),
            P(None, None, head),
            P(None, head),
            P(None, head, None),
            P(None, head),
        ),
        check_vma=False,
    )
```

```python
import functools

import jax
import jax.numpy as jnp
from jax import lax
from jax.experimental import pallas as pl
from jax.experimental.pallas import tpu as pltpu
from jax.sharding import Mesh, PartitionSpec as P

DH = 64
NBUCK = 128
HALF = 64
EPSILON = 1e-05
F32 = jnp.float32
BF16 = jnp.bfloat16
VMEM_BYTES = 20 * 1024 * 1024
TICK = 0.1
PACK_VMEM = 60 * 1024 * 1024
NN = (((1,), (0,)), ((), ()))
NT = (((1,), (1,)), ((), ()))
TN = (((0,), (0,)), ((), ()))


def mm(left, right, dims=NN):
    return lax.dot_general(left, right, dims, preferred_element_type=F32)


def kernel_call(body, place, operands, outs, us, scratch=(), after=(), vmem=VMEM_BYTES):
    specs, arrays, hows = [], [], []
    for operand in operands:
        array, how = operand if isinstance(operand, tuple) else (operand, None)
        specs.append(pl.BlockSpec(memory_space=pltpu.HBM if how == "any" else pltpu.VMEM))
        arrays.append(array)
        hows.append(how)
    count = len(arrays)
    specs += [pl.BlockSpec(memory_space=pl.ANY)] * len(after)

    def view(s_ref, ref, how):
        if how == "stream":
            return ref.at[s_ref[0]]
        if how is None or how == "any":
            return ref
        return ref.at[tuple(slice(None) if at is None else at for at in how)]

    def kernel(s_ref, *refs):
        given = [view(s_ref, ref, how) for ref, how in zip(refs, hows)]
        body(s_ref, *given, *refs[count + len(after) :])

    return pl.pallas_call(
        kernel,
        out_shape=[jax.ShapeDtypeStruct(out[0], out[1]) for out in outs],
        in_specs=[pl.BlockSpec(memory_space=pltpu.SMEM)] + specs,
        out_specs=[
            pl.BlockSpec(memory_space=pltpu.HBM if len(out) > 2 else pltpu.VMEM) for out in outs
        ],
        scratch_shapes=list(scratch),
        compiler_params=pltpu.CompilerParams(vmem_limit_bytes=vmem),
        cost_estimate=pl.CostEstimate(
            flops=int(us * 1.1e9), bytes_accessed=int(us * 3.5e6), transcendentals=0
        ),
    )(place, *arrays, *after)


def centred(rows):
    centre = rows - jnp.mean(rows, axis=-1, keepdims=True)
    spread = lax.rsqrt(jnp.mean(centre * centre, axis=-1, keepdims=True) + EPSILON)
    return centre * spread, spread


def norm_back(unit, spread, tilted):
    return spread * (
        tilted
        - jnp.mean(tilted, axis=-1, keepdims=True)
        - unit * jnp.mean(tilted * unit, axis=-1, keepdims=True)
    )


def pick(table_row, index):
    width = index.shape[1]
    table = jnp.broadcast_to(table_row, (index.shape[0], NBUCK))
    parts = [
        jnp.take_along_axis(
            table,
            index[:, at : at + NBUCK],
            axis=1,
            mode="promise_in_bounds",
        )
        for at in range(0, width, NBUCK)
    ]
    return jnp.concatenate(parts, axis=1)


def stack_rows(pieces):
    return jnp.concatenate(pieces, axis=0)


def turned(rows, size):
    pieces = [rows[at : at + size] for at in range(0, rows.shape[0], size)]
    return stack_rows([pieces[i ^ 1] for i in range(len(pieces))])


def residual(x_ref, mixed_refs):
    rest = mixed_refs[0].shape[0] // 2
    pieces = []
    for y in range(2):
        for c in range(2):
            own = x_ref[y, c * rest : (c + 1) * rest, :].astype(F32)
            pieces.append(own + mixed_refs[c][y * rest : (y + 1) * rest, :].astype(F32))
    return stack_rows(pieces)


def dealt(rows_ref, side, keep_ref, send_ref):
    half = keep_ref.shape[0]
    keep_ref[...] = rows_ref[pl.ds(pl.multiple_of(side * half, 16), half), :]
    send_ref[...] = rows_ref[pl.ds(pl.multiple_of((1 - side) * half, 16), half), :]


def gathered(place_ref, refs, rows, to_ref):
    size = rows.stop - rows.start
    for turn, ref in enumerate(refs):
        q = (place_ref[1] ^ (turn // 2)) * 2 + (place_ref[2] ^ (turn % 2))
        to_ref[pl.ds(pl.multiple_of(q * size, 16), size), :] = ref[rows, :]


def pack_kernel(
    p_ref,
    tok_ref,
    sp_ref,
    pos_ref,
    box_ref,
    exit_ref,
    up_ref,
    down_ref,
    bias_ref,
    cot_ref,
    far_ref,
    near_ref,
    own_ref,
    ups_ref,
    downs_ref,
    cotfar_ref,
    cotnear_ref,
    cotown_ref,
    posv_ref,
    boxv_ref,
    biasv_ref,
    sems,
):
    c, y, zl, zh = p_ref[0], p_ref[2], p_ref[3], p_ref[4]
    block = zh * 2 + zl
    q = p_ref[1] * 2 + y
    least = tok_ref.shape[3]
    rows = 4 * least
    many = down_ref.shape[1] // 4
    few = exit_ref.shape[1] // 4
    pairs = [(pos_ref, posv_ref), (box_ref, boxv_ref), (bias_ref, biasv_ref)]
    for k in range(4):
        at = block ^ k
        to = k * least
        pairs += [
            (tok_ref.at[1 - c, 1 - y, at], far_ref.at[pl.ds(to, least)]),
            (sp_ref.at[1 - y, at], far_ref.at[pl.ds(rows + to, least)]),
            (tok_ref.at[c, 1 - y, at], far_ref.at[pl.ds(2 * rows + 16 + to, least)]),
            (tok_ref.at[1 - c, y, at], near_ref.at[pl.ds(to, least)]),
            (sp_ref.at[y, at], near_ref.at[pl.ds(rows + to, least)]),
            (tok_ref.at[c, y, at], own_ref.at[pl.ds(to, least)]),
        ]
    pairs += [
        (exit_ref.at[c, pl.ds(pl.multiple_of(q * few, 16), few)], ups_ref.at[pl.ds(many + 16, few)]),
        (up_ref.at[c, pl.ds(pl.multiple_of(q * many, 16), many)], ups_ref.at[pl.ds(0, many)]),
        (down_ref.at[c, pl.ds(pl.multiple_of(q * many, 16), many)], downs_ref),
    ]
    for k in range(4):
        at = block ^ k
        to = pl.ds(k * least, least)
        pairs += [
            (cot_ref.at[c, 1 - y, at], cotfar_ref.at[0, to]),
            (cot_ref.at[1 - c, 1 - y, at], cotfar_ref.at[1, to]),
            (cot_ref.at[1 - c, y, at], cotnear_ref.at[to]),
            (cot_ref.at[c, y, at], cotown_ref.at[to]),
        ]
    started = [
        pltpu.make_async_copy(source, target, sems.at[n])
        for n, (source, target) in enumerate(pairs)
    ]
    for copy in started:
        copy.start()
    for copy in started[:3]:
        copy.wait()
    lane = lax.broadcasted_iota(jnp.int32, (8, NBUCK), 1)
    width = far_ref.shape[1]
    for page, ref in ((1 - y, far_ref), (y, near_ref)):
        place = posv_ref[pl.ds(page, 1), :]
        lines = [place & 255, place >> 8, boxv_ref[0, pl.ds(page, 1), :], boxv_ref[1, pl.ds(page, 1), :]]
        value = jnp.concatenate(lines + [jnp.zeros((4, NBUCK), jnp.int32)], axis=0)
        crossed = jnp.where(
            (lane & 63) < 32, pltpu.roll(value, NBUCK - 32, 1), pltpu.roll(value, 32, 1)
        )
        value = jnp.where(zl == 0, value, crossed)
        value = jnp.where(zh == 0, value, pltpu.roll(value, 64, 1))
        value = jnp.concatenate([value.astype(F32), jnp.zeros((8, NBUCK), F32)], axis=0)
        ref[2 * rows : 2 * rows + 16, 0:NBUCK] = value.astype(BF16)
        ref[2 * rows : 2 * rows + 16, NBUCK:] = jnp.zeros((16, width - NBUCK), BF16)
    left = biasv_ref[pl.ds(c, 1), :]
    lines = []
    for _ in range(3):
        lines.append(left.astype(BF16).astype(F32))
        left = left - lines[-1]
    lines.append(jnp.zeros((13, left.shape[1]), F32))
    ups_ref[many : many + 16, :] = jnp.concatenate(lines, axis=0).astype(BF16)
    for copy in started[3:]:
        copy.wait()


def indices(ref, least):
    lines = ref[2 * least : 2 * least + 16, 0:NBUCK].astype(F32).astype(jnp.int32)
    place = lines[0:1] + lines[1:2] * 256
    return jnp.concatenate([place, lines[2:4], jnp.zeros((5, NBUCK), jnp.int32)], axis=0)


def two_cores(index0, index1, half):
    lane = lax.broadcasted_iota(jnp.int32, (8, NBUCK), 1)
    if half == 0:
        return jnp.where(lane < 64, index0, pltpu.roll(index1, 64, 1))
    return jnp.where(lane < 64, pltpu.roll(index0, 64, 1), index1)


def arrange(x0_ref, n0_ref, n1_ref, x_ref, sp_ref):
    least = x_ref.shape[1]
    rest = least // 2
    found = []
    index0, index1 = indices(n0_ref, least), indices(n1_ref, least)
    for half in range(2):
        at = half * rest
        x_ref[half, 0:rest, :] = x0_ref[at : at + rest, :]
        x_ref[half, rest:, :] = n1_ref[at : at + rest, :]
        sp_ref[half, 0:rest, :] = n0_ref[least + at : least + at + rest, :]
        sp_ref[half, rest:, :] = n1_ref[least + at : least + at + rest, :]
        found.append(two_cores(index0, index1, half))
    return found


def project(x_ref, sp_ref, w_ref, ws_ref, proj_ref, spat_ref, at):
    width = x_ref.shape[-1]
    x = x_ref[...].reshape(-1, width)
    sp = sp_ref[...].reshape(-1, width)
    rows = slice(at, at + x.shape[0])
    for k in range(3):
        proj_ref[k, rows, :] = mm(x, w_ref[k], NT).astype(BF16)
    for k in range(2):
        spat_ref[k, rows, :] = mm(sp, ws_ref[k], NT).astype(BF16)


def near_kernel(
    p_ref,
    x00_ref,
    n01_ref,
    n00_ref,
    w_ref,
    ws_ref,
    up_hbm,
    down_hbm,
    exit_hbm,
    x_ref,
    sp_ref,
    index_ref,
    proj_ref,
    spat_ref,
    up_ref,
    down_ref,
    exit_ref,
    sems,
):
    fetched = [
        pltpu.make_async_copy(source.at[p_ref[0]], target, sems.at[n])
        for n, (source, target) in enumerate(
            ((exit_hbm, exit_ref), (up_hbm, up_ref), (down_hbm, down_ref))
        )
    ]
    for copy in fetched:
        copy.start()
    found = arrange(x00_ref, n00_ref, n01_ref, x_ref, sp_ref)
    index_ref[...] = jnp.concatenate(found, axis=1)
    project(x_ref, sp_ref, w_ref, ws_ref, proj_ref, spat_ref, 0)
    for copy in fetched:
        copy.wait()


def attention_kernel(
    p_ref,
    n11_ref,
    n10_ref,
    x0_ref,
    sp0_ref,
    index_ref,
    proj0_ref,
    spat0_ref,
    w_ref,
    ws_ref,
    table_ref,
    x_ref,
    sp_ref,
    colidx_ref,
    proj_hbm,
    spat_hbm,
    soft_hbm,
    own_ref,
    send_ref,
    att_ref,
    proj_ref,
    spat_ref,
    soft_ref,
    sems,
    *,
    heads,
    block,
):
    least = x_ref.shape[2]
    near = 2 * least
    x_ref[0] = x0_ref[...]
    sp_ref[0] = sp0_ref[...]
    proj_ref[:, 0:near, :] = proj0_ref[...]
    spat_ref[:, 0:near, :] = spat0_ref[...]
    found = arrange(
        n10_ref.at[2 * least + 16 :], n10_ref, n11_ref, x_ref.at[1], sp_ref.at[1]
    )
    places = jnp.concatenate([index_ref[...]] + found, axis=1)
    colidx_ref[...] = jnp.transpose(places.astype(F32)).astype(jnp.int32)
    project(x_ref.at[1], sp_ref.at[1], w_ref, ws_ref, proj_ref, spat_ref, near)
    length = 2 * near
    stored = [
        pltpu.make_async_copy(proj_ref, proj_hbm, sems.at[0]),
        pltpu.make_async_copy(spat_ref, spat_hbm, sems.at[1]),
    ]
    for copy in stored:
        copy.start()
    level = lax.broadcasted_iota(jnp.int32, (length, NBUCK), 1)
    chosen = [(colidx_ref[:, kind : kind + 1] == level).astype(BF16) for kind in (1, 2)]
    chosen = jnp.concatenate(chosen, axis=1)

    def step(at, carry):
        rows = pl.ds(pl.multiple_of(at * block, block), block)
        lane = lax.broadcasted_iota(jnp.int32, (block, NBUCK), 1)
        index = jnp.clip(places[0:1, :] - colidx_ref[rows, 0:1], -HALF, HALF - 1) + HALF
        boxes = [
            jnp.clip(lane - colidx_ref[rows, kind : kind + 1], -HALF, HALF - 1) + HALF
            for kind in (1, 2)
        ]
        for h in range(heads):
            cols = slice(h * DH, (h + 1) * DH)
            bias = jnp.concatenate(
                [pick(table_ref[k, h : h + 1, :], boxes[k - 1]) for k in (1, 2)], axis=1
            )
            coarse = bias.astype(BF16)
            fine = (bias - coarse.astype(F32)).astype(BF16)
            left = jnp.concatenate(
                [proj_ref[0, rows, cols], spat_ref[0, rows, cols]], axis=1
            ) * jnp.asarray(DH**-0.5, BF16)
            right = jnp.concatenate([proj_ref[1, :, cols], spat_ref[1, :, cols]], axis=1)
            scores = mm(
                jnp.concatenate([left, coarse, fine], axis=1),
                jnp.concatenate([right, chosen, chosen], axis=1),
                NT,
            ) + pick(table_ref[0, h : h + 1, :], index)
            top = jnp.max(scores, axis=-1, keepdims=True)
            raised = jnp.exp(scores - top)
            soft = raised * (1.0 / jnp.sum(raised, axis=-1, keepdims=True))
            soft_ref[h, rows, :] = soft
            att_ref[rows, cols] = mm(soft.astype(BF16), proj_ref[2, :, cols]).astype(BF16)
        saved(at).start()
        return carry

    def saved(at):
        rows = pl.ds(pl.multiple_of(at * block, block), block)
        return pltpu.make_async_copy(
            soft_ref.at[:, rows, :], soft_hbm.at[:, rows, :], sems.at[2 + at]
        )

    lax.fori_loop(0, length // block, step, 0)
    for copy in stored + [saved(at) for at in range(length // block)]:
        copy.wait()
    part = length // 4
    own_ref[0:part, :] = att_ref[0:part, :]
    own_ref[part:, :] = att_ref[2 * part : 3 * part, :]
    send_ref[0:part, :] = att_ref[part : 2 * part, :]
    send_ref[part:, :] = att_ref[3 * part :, :]


def mixed_kernel(
    p_ref,
    own_ref,
    recv_ref,
    exit_ref,
    one0_ref,
    one1_ref,
    one2_ref,
    one3_ref,
    keep_ref,
    send_ref,
    partner_ref,
):
    rows = slice(one0_ref.shape[0] - exit_ref.shape[0] // 4, one0_ref.shape[0])
    gathered(p_ref, (one0_ref, one1_ref, one2_ref, one3_ref), rows, partner_ref)
    total = mm(own_ref[...], exit_ref[...]) + mm(recv_ref[...], partner_ref[...])
    rest = total.shape[0] // 4
    for y in range(2):
        at = 2 * y * rest
        keep_ref[y * rest : (y + 1) * rest, :] = total[at : at + rest]
        send_ref[y * rest : (y + 1) * rest, :] = total[at + rest : at + 2 * rest].astype(BF16)


def gelu_parts(upper):
    phi = 0.5 * (1.0 + lax.erf(upper * (0.5**0.5)))
    slope = phi + upper * (jnp.exp(-0.5 * upper * upper) * (0.5 / jnp.pi) ** 0.5)
    return (upper * phi).astype(BF16), slope


def forward_kernel(
    p_ref,
    x_ref,
    mixed0_ref,
    mixed1_ref,
    gain_ref,
    shift_ref,
    up_ref,
    hidden_ref,
    down_ref,
    one0_ref,
    one1_ref,
    one2_ref,
    one3_ref,
    two0_ref,
    two1_ref,
    two2_ref,
    two3_ref,
    low_ref,
    normed_ref,
    active_ref,
    slope_ref,
    upp_ref,
    downp_ref,
):
    many = two0_ref.shape[0]
    gathered(p_ref, (one0_ref, one1_ref, one2_ref, one3_ref), slice(0, many), upp_ref)
    gathered(p_ref, (two0_ref, two1_ref, two2_ref, two3_ref), slice(0, many), downp_ref)
    extra = one0_ref[many : many + 16, :].astype(F32)
    partner_bias = extra[0:1] + extra[1:2] + extra[2:3]
    unit, _ = centred(residual(x_ref, (mixed0_ref, mixed1_ref)))
    normed_low = (unit * gain_ref[0:1, :] + shift_ref[0:1, :]).astype(BF16)
    normed_ref[...] = normed_low
    active, slope = gelu_parts(mm(normed_low, up_ref[...]) + hidden_ref[pl.ds(p_ref[0], 1), :])
    active_ref[0] = active
    slope_ref[0] = slope.astype(BF16)
    total = mm(active, down_ref[...])
    active, slope = gelu_parts(mm(normed_low, upp_ref[...]) + partner_bias)
    active_ref[1] = active
    slope_ref[1] = slope.astype(BF16)
    low_ref[...] = (total + mm(active, downp_ref[...])).astype(BF16)


def other_kernel(
    p_ref,
    normed_ref,
    up_ref,
    hidden_ref,
    active_ref,
    slope_ref,
):
    active, slope = gelu_parts(
        mm(normed_ref[...], up_ref[...]) + hidden_ref[pl.ds(p_ref[0], 1), :]
    )
    active_ref[...] = active
    slope_ref[...] = slope.astype(BF16)


def first_norm_kernel(p_ref, x_ref, mixed0_ref, mixed1_ref, gain_ref, shift_ref, normed_ref):
    unit, _ = centred(residual(x_ref, (mixed0_ref, mixed1_ref)))
    normed_ref[...] = (unit * gain_ref[0:1, :] + shift_ref[0:1, :]).astype(BF16)


def lowered_kernel(p_ref, own_ref, far_ref, low0_ref, low1_ref):
    least = own_ref.shape[0] // 8
    total = own_ref[...].astype(F32) + turned(far_ref[...], least).astype(F32)
    total = total.astype(BF16)
    for i in range(4):
        low0_ref[i * least : (i + 1) * least, :] = total[2 * i * least : (2 * i + 1) * least]
        low1_ref[i * least : (i + 1) * least, :] = total[(2 * i + 1) * least : (2 * i + 2) * least]


def final_kernel(
    p_ref,
    x_ref,
    mixed0_ref,
    mixed1_ref,
    low0_ref,
    low1_ref,
    cot00_ref,
    cot10_ref,
    cot01_ref,
    cot11_ref,
    gain_ref,
    shift_ref,
    bdown_ref,
    outk_ref,
    outs_ref,
    second_ref,
    dlow_ref,
    sums_ref,
):
    unit, _ = centred(residual(x_ref, (mixed0_ref, mixed1_ref)))
    normed = unit * gain_ref[0:1, :] + shift_ref[0:1, :]
    least = low0_ref.shape[0] // 4
    pieces = []
    for i in range(4):
        pieces.append(low0_ref[i * least : (i + 1) * least, :])
        pieces.append(low1_ref[i * least : (i + 1) * least, :])
    lowered = stack_rows(pieces).astype(F32)
    unit2, spread2 = centred(normed + lowered + bdown_ref[pl.ds(p_ref[0], 1), :])
    out = (unit2 * gain_ref[1:2, :] + shift_ref[1:2, :]).astype(BF16)
    for y in range(2):
        at = 4 * y * least
        outk_ref[y] = out[at : at + 2 * least]
        outs_ref[y] = out[at + 2 * least : at + 4 * least]
    cot = stack_rows([cot00_ref[...], cot01_ref[...], cot10_ref[...], cot11_ref[...]]).astype(F32)
    second = norm_back(unit2, spread2, cot * gain_ref[1:2, :])
    second_ref[...] = second
    dlow_ref[...] = second.astype(BF16)
    sums_ref[...] = jnp.zeros_like(sums_ref)
    sums_ref[0:1, :] = jnp.sum(cot * unit2, axis=0, keepdims=True)
    sums_ref[1:2, :] = jnp.sum(cot, axis=0, keepdims=True)
    sums_ref[2:3, :] = jnp.sum(second, axis=0, keepdims=True)


def middle_kernel(
    p_ref,
    dlow_ref,
    up_ref,
    down_ref,
    upp_ref,
    downp_ref,
    slope_ref,
    hid_ref,
    dup_ref,
):
    dlow = dlow_ref[...]
    dup = (mm(dlow, down_ref[...], NT) * slope_ref[0].astype(F32)).astype(BF16)
    dup_ref[...] = dup
    total = mm(dup, up_ref[...], NT)
    dup = (mm(dlow, downp_ref[...], NT) * slope_ref[1].astype(F32)).astype(BF16)
    hid_ref[...] = (total + mm(dup, upp_ref[...], NT)).astype(BF16)


def ffn_grad_kernel(
    p_ref,
    normed_ref,
    normedo_ref,
    active_ref,
    activeo_ref,
    dlow_ref,
    dlowo_ref,
    dup_ref,
    slopeo_ref,
    down_ref,
    upk_ref,
    ups_ref,
    downk_ref,
    downs_ref,
    bias_ref,
    all_ref,
):
    dlowo = dlowo_ref[...]
    dupo = (mm(dlowo, down_ref[...], NT) * slopeo_ref[...].astype(F32)).astype(BF16)
    dup = dup_ref[...]
    all_ref[...] = (mm(normed_ref[...], dup, TN) + mm(normedo_ref[...], dupo, TN)).astype(BF16)
    dealt(all_ref, p_ref[1], upk_ref, ups_ref)
    all_ref[...] = (
        mm(active_ref[...], dlow_ref[...], TN) + mm(activeo_ref[...], dlowo, TN)
    ).astype(BF16)
    dealt(all_ref, p_ref[2], downk_ref, downs_ref)
    bias = jnp.sum(dup.astype(F32), axis=0, keepdims=True)
    bias = bias + jnp.sum(dupo.astype(F32), axis=0, keepdims=True)
    bias_ref[...] = jnp.broadcast_to(bias, bias_ref.shape)


def first_kernel(
    p_ref,
    x_ref,
    mixed0_ref,
    mixed1_ref,
    second_ref,
    hid_ref,
    hidr_ref,
    gain_ref,
    first_ref,
    dmix_ref,
    sums_ref,
):
    unit, spread = centred(residual(x_ref, (mixed0_ref, mixed1_ref)))
    hid = hid_ref[...].astype(F32) + turned(hidr_ref[...], hid_ref.shape[0] // 8).astype(F32)
    dnormed = second_ref[...] + hid
    first = norm_back(unit, spread, dnormed * gain_ref[0:1, :])
    first_ref[...] = first
    dmix_ref[...] = first.astype(BF16)
    sums_ref[...] = jnp.zeros_like(sums_ref)
    sums_ref[0:1, :] = jnp.sum(dnormed * unit, axis=0, keepdims=True)
    sums_ref[1:2, :] = jnp.sum(dnormed, axis=0, keepdims=True)


def attended_kernel(
    p_ref,
    dmix_ref,
    dmixr_ref,
    exit_ref,
    exitp_ref,
    sums1_ref,
    sums2_ref,
    own_ref,
    send_ref,
    total_ref,
    pay_ref,
):
    length = dmix_ref.shape[0]
    rest = length // 4
    total = dmix_ref[...].astype(F32) + turned(dmixr_ref[...], rest).astype(F32)
    total = total.astype(BF16)
    total_ref[...] = total
    own_ref[...] = mm(total, exit_ref[...], NT).astype(BF16)
    send_ref[...] = mm(total, exitp_ref[...], NT).astype(BF16)
    least = rest // 2
    pay_ref[0:least, :] = total[0:least]
    pay_ref[least:rest, :] = total[2 * rest : 2 * rest + least]
    pay_ref[rest:, :] = jnp.concatenate([sums1_ref[...], sums2_ref[...]], axis=0).astype(BF16)


def backward_kernel(
    p_ref,
    datt_ref,
    dattr_ref,
    first_ref,
    soft_hbm,
    proj_ref,
    spat_ref,
    w_ref,
    ws_ref,
    dscore_ref,
    dproj_ref,
    dspat_ref,
    dxk0_ref,
    dxk1_ref,
    dxs_ref,
    dsk0_ref,
    dsk1_ref,
    dss_ref,
    soft_ref,
    sems,
    *,
    heads,
    block,
):
    fetched = [
        pltpu.make_async_copy(soft_hbm.at[h], soft_ref.at[h], sems.at[h]) for h in range(heads)
    ]
    for copy in fetched:
        copy.start()
    length = 2 * datt_ref.shape[0]
    scale = DH**-0.5
    part = length // 4
    datt = stack_rows(
        [datt_ref[0:part, :], dattr_ref[0:part, :], datt_ref[part:, :], dattr_ref[part:, :]]
    )
    for h in range(heads):
        cols = slice(h * DH, (h + 1) * DH)
        value = proj_ref[2, :, cols]
        left = jnp.concatenate([proj_ref[0, :, cols], spat_ref[0, :, cols]], axis=1)
        right = jnp.concatenate([proj_ref[1, :, cols], spat_ref[1, :, cols]], axis=1)
        own = datt[:, cols]
        fetched[h].wait()
        for at in range(0, length, block):
            soft = soft_ref[h, at : at + block, :]
            dsoft = mm(own[at : at + block], value, NT)
            inner = jnp.sum(soft * dsoft, axis=-1, keepdims=True)
            dscore_ref[h, at : at + block, :] = (soft * (dsoft - inner)).astype(BF16)
        dscore = dscore_ref[h]
        dleft = (mm(dscore, right) * scale).astype(BF16)
        dright = (mm(dscore, left, TN) * scale).astype(BF16)
        dproj_ref[0, :, cols] = dleft[:, :DH]
        dspat_ref[0, :, cols] = dleft[:, DH:]
        dproj_ref[1, :, cols] = dright[:, :DH]
        dspat_ref[1, :, cols] = dright[:, DH:]
        dproj_ref[2, :, cols] = mm(soft_ref[h].astype(BF16), own, TN).astype(BF16)
    once = (p_ref[3] == 0).astype(F32)
    total = mm(dproj_ref[0], w_ref[0])
    for k in range(1, 3):
        total = total + mm(dproj_ref[k], w_ref[k])
    least = part // 4

    def deal(rows, refs):
        for y in range(2):
            for zh in range(2):
                for c in range(2):
                    for zl in range(2):
                        at = (((y * 2 + zh) * 2 + c) * 2 + zl) * least
                        to = (zh * 2 + y) * least
                        value = rows[at : at + least]
                        if zh == 0 and refs[0][0] is dxk0_ref:
                            of = ((y * 2 + c) * 2 + zl) * least
                            value = value + once * first_ref[of : of + least, :]
                        refs[c][zl][to : to + least, :] = value.astype(BF16)

    deal(total, ((dxk0_ref, dxk1_ref), (dxs_ref.at[0], dxs_ref.at[1])))
    total = mm(dspat_ref[0], ws_ref[0]) + mm(dspat_ref[1], ws_ref[1])
    deal(total, ((dsk0_ref, dsk1_ref), (dss_ref.at[0], dss_ref.at[1])))


def second_grad_kernel(
    p_ref,
    dmix_ref,
    pay_ref,
    payr_ref,
    payl_ref,
    payc_ref,
    paylc_ref,
    atto_ref,
    atts_ref,
    sp_ref,
    dspat_ref,
    lines_ref,
    keep_ref,
    send_ref,
    second_ref,
):
    width = sp_ref.shape[-1]
    sp = sp_ref[...].reshape(-1, width)
    inner = dspat_ref.shape[-1]
    least = sp.shape[0] // 16
    rest = 2 * least
    dmixo = stack_rows(
        [
            ref[y * least : (y + 1) * least, :]
            for y in range(2)
            for ref in (payr_ref, payl_ref, payc_ref, paylc_ref)
        ]
    )
    second_ref[0:inner, :] = (
        mm(atto_ref[...], dmix_ref[...], TN) + mm(atts_ref[...], dmixo, TN)
    ).astype(BF16)
    for k in range(2):
        second_ref[(k + 1) * inner : (k + 2) * inner, :] = mm(dspat_ref[k], sp, TN).astype(BF16)
    base = 3 * inner
    small = pay_ref[rest:, :].astype(F32) + payr_ref[rest:, :].astype(F32)
    second_ref[base : base + 16, :] = small.astype(BF16)
    second_ref[base + 16 : base + 32, :] = lines_ref[...].astype(BF16)
    dealt(second_ref, p_ref[2], keep_ref, send_ref)


def first_grad_kernel(
    p_ref,
    x_ref,
    dscore_ref,
    dproj_ref,
    colidx_ref,
    bup_ref,
    keep_ref,
    send_ref,
    lines_ref,
    first_ref,
    *,
    heads,
):
    width = x_ref.shape[-1]
    x = x_ref[...].reshape(-1, width)
    length = x.shape[0]
    inner = dproj_ref.shape[-1]
    for k in range(3):
        first_ref[k * inner : (k + 1) * inner, :] = mm(dproj_ref[k], x, TN).astype(BF16)
    dealt(first_ref, p_ref[1], keep_ref, send_ref)
    lane = lax.broadcasted_iota(jnp.int32, (1, NBUCK), 1)
    found = []
    for kind in range(3):
        extent = length if kind == 0 else NBUCK
        own = colidx_ref[:, kind : kind + 1]
        level = lax.broadcasted_iota(jnp.int32, (length, extent), 1)
        chosen = (own == level).astype(BF16)
        place = own - HALF + lax.broadcasted_iota(jnp.int32, (length, NBUCK), 1)
        turn = place & (NBUCK - 1)
        piece = place >> 7
        for h in range(heads):
            spread = mm(dscore_ref[h], chosen)
            window = jnp.zeros((length, NBUCK), F32)
            for q in range(extent // NBUCK):
                part = jnp.take_along_axis(
                    spread[:, q * NBUCK : (q + 1) * NBUCK],
                    turn,
                    axis=1,
                    mode="promise_in_bounds",
                )
                window = window + jnp.where(piece == q, part, 0.0)
            row = jnp.sum(window, axis=0, keepdims=True)
            row = jnp.where((lane > 0) & (lane < NBUCK - 1), row, 0.0)
            least = jnp.sum(jnp.where(level <= own - HALF, spread, 0.0), axis=0, keepdims=True)
            most = jnp.sum(jnp.where(level >= own + HALF - 1, spread, 0.0), axis=0, keepdims=True)
            row = row + jnp.where(lane == 0, jnp.sum(least, axis=1, keepdims=True), 0.0)
            row = row + jnp.where(
                lane == NBUCK - 1, jnp.sum(most, axis=1, keepdims=True), 0.0
            )
            found.append(row)
    per = width // NBUCK
    found = found + [jnp.zeros((1, NBUCK), F32)] * (-len(found) % per)
    lines = [
        jnp.concatenate(found[at : at + per], axis=1) for at in range(0, len(found), per)
    ]
    lines.append(bup_ref[0:1, :])
    lines_ref[...] = jnp.concatenate(
        lines + [jnp.zeros((16 - len(lines), width), F32)], axis=0
    )


def ends_kernel(
    p_ref,
    w_ref,
    y_ref,
    zhw_ref,
    zlw_ref,
    zzw_ref,
    tok_ref,
    sp_ref,
    event_ref,
):
    c, y, block = p_ref[0], p_ref[2], p_ref[4] * 2 + p_ref[3]
    for turn, ref in enumerate((None, zlw_ref, zhw_ref, zzw_ref)):
        at = block ^ turn
        for far in range(2):
            for unit in range(3):
                if ref is None:
                    value = (y_ref if far else w_ref)[unit]
                else:
                    value = ref[far, unit]
                value = value.astype(F32)
                if unit < 2:
                    tok_ref[c ^ unit, y ^ far, at] = value
                else:
                    sp_ref[y ^ far, at] = value
    event_ref[...] = jnp.zeros_like(event_ref)


def out_kernel(p_ref, *refs):
    c, y, block = p_ref[0], p_ref[2], p_ref[4] * 2 + p_ref[3]
    out_ref, event_ref = refs[8:]
    least = out_ref.shape[3]
    for half in range(2):
        for far in range(2):
            for unit in range(2):
                ref = refs[half * 4 + far * 2 + unit]
                for turn in range(2):
                    at = block ^ (half * 2 + turn)
                    out_ref[c ^ unit, y ^ far, at] = ref[turn * least : (turn + 1) * least, :]
    event_ref[...] = jnp.zeros_like(event_ref)


def turn_kernel(p_ref, own_ref, far_ref, sum_ref, *, size):
    far = turned(far_ref[...], size).astype(F32)
    sum_ref[...] = (own_ref[...].astype(F32) + far).astype(BF16)


def plus_kernel(p_ref, *refs):
    count = len(refs) // 3
    for n in range(count):
        total = refs[2 * n][...].astype(F32) + refs[2 * n + 1][...].astype(F32)
        refs[2 * count + n][...] = total.astype(BF16)


def units_kernel(
    p_ref, own0_ref, own1_ref, other_ref, near_ref, far_ref, spat_ref, nears_ref, fars_ref
):
    nears_ref[0] = own0_ref[...]
    fars_ref[0] = own1_ref[...]
    nears_ref[1] = other_ref[0]
    fars_ref[1] = other_ref[1]
    nears_ref[2] = (near_ref[...].astype(F32) + spat_ref[0].astype(F32)).astype(BF16)
    fars_ref[2] = (far_ref[...].astype(F32) + spat_ref[1].astype(F32)).astype(BF16)


def fold_kernel(p_ref, own_ref, far_ref, keep_ref, send_ref):
    total = (own_ref[...].astype(F32) + far_ref[...].astype(F32)).astype(BF16)
    half = total.shape[-2] // 2
    keep_ref[...] = total[..., :half, :]
    send_ref[...] = total[..., half:, :]


def ends_first_kernel(p_ref, keep_ref, far_ref, mine_ref, other_ref):
    least = mine_ref.shape[1]
    total = (keep_ref[...].astype(F32) + far_ref[...].astype(F32)).astype(BF16)
    mine_ref[...] = total[:, :least]
    other_ref[...] = total[:, least:]


def spread_kernel(p_ref, *refs):
    c = p_ref[0]
    event_ref = refs[10]
    for n, out_ref in enumerate(refs[8:10]):
        side = p_ref[1 + n]
        for other in range(2):
            for far in range(2):
                out_ref[c ^ other, side ^ far] = refs[n * 4 + other * 2 + far][...].astype(F32)
    event_ref[...] = jnp.zeros_like(event_ref)


def last_kernel(
    p_ref,
    one0_ref,
    one1_ref,
    one2_ref,
    one3_ref,
    two0_ref,
    two1_ref,
    two2_ref,
    two3_ref,
    qkv_ref,
    spat_ref,
    exit_ref,
    tables_ref,
    gains_ref,
    shifts_ref,
    bup_ref,
    bdown_ref,
    first_ref,
    second_ref,
    *,
    heads,
):
    c, head = p_ref[0], p_ref[4] * 2 + p_ref[3]
    inner = exit_ref.shape[1]
    width = exit_ref.shape[2]
    part = gains_ref.shape[2]
    per = width // NBUCK
    base = 3 * inner
    firsts = ((one0_ref, one1_ref), (one2_ref, one3_ref))
    seconds = ((two0_ref, two1_ref), (two2_ref, two3_ref))

    def whole(halves, side, to_ref):
        size = halves[0].shape[0]
        for far in range(2):
            at = pl.multiple_of((side ^ far) * size, 16)
            to_ref[pl.ds(at, size), :] = halves[far][...].astype(F32)

    for other in range(2):
        s = c ^ other
        whole(firsts[other], p_ref[1], first_ref)
        qkv_ref[s] = first_ref[...]
        whole(seconds[other], p_ref[2], second_ref)
        exit_ref[s] = second_ref[0:inner, :]
        if other:
            spat_ref[...] += second_ref[inner:base, :]
        else:
            spat_ref[...] = second_ref[inner:base, :]
        sums = second_ref[base : base + 16, :]
        cut = sums[:, 0:part]
        for at in range(1, width // part):
            cut = jnp.where(head == at, sums[:, at * part : (at + 1) * part], cut)
        gains_ref[s] = jnp.concatenate([cut[0:1], cut[8:9]], axis=0)
        shifts_ref[s] = jnp.concatenate([cut[1:2], cut[9:10]], axis=0)
        bdown_ref[pl.ds(s, 1), :] = cut[10:11]
        lines = second_ref[base + 16 : base + 32, :]
        for n in range(3 * heads):
            at = (n % per) * NBUCK
            tables_ref[s, n // heads, n % heads : n % heads + 1, :] = lines[
                n // per : n // per + 1, at : at + NBUCK
            ]
        bup_ref[pl.ds(s, 1), :] = lines[2:3]


def swap(value, axis, step=1):
    size = lax.axis_size(axis)
    return lax.ppermute(value, axis, [(i, i ^ step) for i in range(size)])


def swap_both(value):
    size = lax.axis_size("batch") * 2
    return lax.ppermute(value, ("batch", "y"), [(i, i ^ 3) for i in range(size)])


def added(left, right):
    return (left.astype(F32) + right.astype(F32)).astype(BF16)


def batch_steps():
    return [1 << bit for bit in range(lax.axis_size("batch").bit_length() - 1)]


def join(*values):
    return lax.optimization_barrier(values)


def shards(
    tokens,
    spatial,
    positions,
    boxes,
    query_key_value_weight,
    w_spatial,
    rel_tables,
    exit_matrix,
    ln_gains,
    ln_shifts,
    up_weight,
    hidden_bias,
    shrink_projection_array,
    b_down,
    cotangent,
):
    heads = rel_tables.shape[2]
    rows = tokens.shape[2]
    width = tokens.shape[3]
    inner = query_key_value_weight.shape[3]
    hidden = up_weight.shape[2]
    least = rows // 4
    rest = rows // 2
    length = 4 * rows
    half = length // 2
    page = lax.axis_index("y")
    core = lax.axis_index("core")
    zh = lax.axis_index("zh")
    zl = lax.axis_index("zl")
    pair = lax.axis_index("batch") & 1
    place = jnp.stack([core, pair, page, zl, zh]).astype(jnp.int32)

    def run(body, operands, outs, us=TICK, scratch=(), after=(), vmem=VMEM_BYTES):
        return kernel_call(body, place, operands, outs, us, scratch, after, vmem)

    def rows_of(count, dtype=BF16):
        return ((count, width), dtype)

    share = hidden // 4
    anywhere = [
        tokens.reshape(2, 2, 4, least, width),
        spatial.reshape(2, 4, least, width),
        positions,
        boxes,
        exit_matrix,
        up_weight,
        shrink_projection_array,
        hidden_bias,
        cotangent.reshape(2, 2, 4, least, width),
    ]
    far, near, x00, up_part, down_part, cot_far, cot_near, cot00 = run(
        pack_kernel,
        [(array, "any") for array in anywhere],
        [
            rows_of(3 * rows + 16),
            rows_of(2 * rows + 16),
            rows_of(rows),
            rows_of(share + 16 + inner // 4),
            rows_of(share),
            ((2, rows, width), BF16),
            rows_of(rows),
            rows_of(rows),
        ],
        scratch=[
            pltpu.VMEM(positions.shape, jnp.int32),
            pltpu.VMEM(boxes.shape, jnp.int32),
            pltpu.VMEM(hidden_bias.shape, F32),
            pltpu.SemaphoreType.DMA((46,)),
        ],
        vmem=PACK_VMEM,
    )
    n10 = swap(far, "y")
    n01 = swap(near, "core")
    up_part = swap(up_part, "zh")
    weights = (jnp.swapaxes(query_key_value_weight, 2, 3), "stream")
    spatial_weights = jnp.swapaxes(w_spatial, 1, 2)
    x0, sp0, index0, proj0, spat0, up, down, exit_own = run(
        near_kernel,
        [
            x00,
            n01,
            near,
            weights,
            spatial_weights,
            (up_weight, "any"),
            (shrink_projection_array, "any"),
            (exit_matrix, "any"),
        ],
        [
            ((2, rows, width), BF16),
            ((2, rows, width), BF16),
            ((8, 2 * rows), jnp.int32),
            ((3, 2 * rows, inner), BF16),
            ((2, 2 * rows, inner), BF16),
            ((width, hidden), BF16),
            ((hidden, width), BF16),
            rows_of(inner),
        ],
        scratch=[pltpu.SemaphoreType.DMA((3,))],
    )
    n10, x0, up_part, down_part = join(n10, x0, up_part, down_part)
    n11 = swap(n10, "core")
    ups = [up_part, swap(up_part, "y"), swap(up_part, "batch"), swap_both(up_part)]
    down_part = swap(down_part, "zh")

    x, sp, colidx, proj, spat, soft, att_own, att_send = run(
        functools.partial(attention_kernel, heads=heads, block=128),
        [
            n11,
            n10,
            x0,
            sp0,
            index0,
            proj0,
            spat0,
            weights,
            spatial_weights,
            (rel_tables, "stream"),
        ],
        [
            ((2, 2, rows, width), BF16),
            ((2, 2, rows, width), BF16),
            ((length, 8), jnp.int32),
            ((3, length, inner), BF16, "any"),
            ((2, length, inner), BF16, "any"),
            ((heads, length, length), F32, "any"),
            ((half, inner), BF16),
            ((half, inner), BF16),
        ],
        us=30,
        scratch=[
            pltpu.VMEM((length, inner), BF16),
            pltpu.VMEM((3, length, inner), BF16),
            pltpu.VMEM((2, length, inner), BF16),
            pltpu.VMEM((heads, length, length), F32),
            pltpu.SemaphoreType.DMA((2 + length // 128,)),
        ],
    )
    att_recv = swap(att_send, "zh")
    att_own, down_part, *ups = join(att_own, down_part, *ups)
    downs = [down_part, swap(down_part, "y"), swap(down_part, "batch"), swap_both(down_part)]

    keep, send, exit_partner = run(
        mixed_kernel,
        [att_own, att_recv, exit_own, *ups],
        [rows_of(rows, F32), rows_of(rows), rows_of(inner)],
    )
    (mixed0,) = run(
        plus_kernel, [keep, swap(send, "core")], [rows_of(rows)], after=downs[1:3]
    )
    mixed_zl = swap(mixed0, "zl")
    (mixed0,) = run(
        functools.partial(turn_kernel, size=least), [mixed0, mixed_zl], [rows_of(rows)]
    )
    mixed1 = swap(mixed0, "core")
    mixed_far0 = swap(mixed0, "zh")
    mixed1, cot_far, cot_near, *downs = join(mixed1, cot_far, cot_near, *downs)
    cot10 = swap(cot_far, "y")
    cot01 = swap(cot_near, "core")

    gains = (ln_gains, "stream")
    shifts = (ln_shifts, "stream")
    x_own = (x, (None, 0, None, None))
    x_far = (x, (None, 1, None, None))
    low, normed, active, slope, up_partner, down_partner = run(
        forward_kernel,
        [x_own, mixed0, mixed1, gains, shifts, up, hidden_bias, down, *ups, *downs],
        [
            rows_of(half),
            rows_of(half),
            ((2, half, hidden), BF16),
            ((2, half, hidden), BF16),
            ((width, hidden), BF16),
            ((hidden, width), BF16),
        ],
    )
    low_recv = swap(low, "zl")
    mixed_far0, cot10, low = join(mixed_far0, cot10, low)
    mixed_far1 = swap(mixed_far0, "core")
    cot11 = swap(cot10, "core")
    (normed_far,) = run(
        first_norm_kernel,
        [x_far, mixed_far0, mixed_far1, gains, shifts],
        [rows_of(half)],
        after=[low],
    )
    active_far, slope_far = run(
        other_kernel,
        [normed_far, up, hidden_bias],
        [((half, hidden), BF16), ((half, hidden), BF16)],
    )
    low0, low1 = run(
        lowered_kernel, [low, low_recv], [rows_of(rows), rows_of(rows)], after=[slope_far, cot11]
    )
    far_low0 = swap(low0, "zh")

    def finish(x_half, pieces, part, after=()):
        rows_part = slice(part * rest, (part + 1) * rest)
        cots = [
            cot00[rows_part],
            cot10[0, rows_part],
            cot01[rows_part],
            cot11[1, rows_part],
        ]
        return run(
            final_kernel,
            [x_half, *pieces, *cots, gains, shifts, b_down],
            [
                ((2, rest, width), BF16),
                ((2, rest, width), BF16),
                rows_of(half, F32),
                rows_of(half),
                rows_of(8, F32),
            ],
            after=after,
        )

    out_keep, out_send, second, dlow, sums_two = finish(x_own, [mixed0, mixed1, low0, low1], 0)
    hid, dup = run(
        middle_kernel,
        [dlow, up, down, up_partner, down_partner, slope],
        [rows_of(half), ((half, hidden), BF16)],
    )
    hid_recv = swap(hid, "zl")
    out_core = swap(out_send, "core")
    out_y = swap(jnp.stack([out_keep[1], out_core[1]]), "y")
    hid_recv, far_low0, out_y = join(hid_recv, far_low0, out_y)
    far_low1 = swap(far_low0, "zl")
    first, dmix, sums_one = run(
        first_kernel,
        [x_own, mixed0, mixed1, second, hid, hid_recv, gains],
        [rows_of(half, F32), rows_of(half), rows_of(8, F32)],
    )
    dmix_core = swap(dmix, "core")
    datt, datt_send, dmix, pay = run(
        attended_kernel,
        [dmix, dmix_core, exit_own, exit_partner, sums_one, sums_two],
        [
            ((half, inner), BF16),
            ((half, inner), BF16),
            rows_of(half),
            rows_of(rest + 16),
        ],
    )
    datt_recv = swap(datt_send, "zh")
    far_keep, far_send, _, dlow_far, _ = finish(
        x_far, [mixed_far0, mixed_far1, far_low0, far_low1], 1, [datt]
    )
    up_keep, up_send, down_keep, down_send, bias_grad = run(
        ffn_grad_kernel,
        [
            normed,
            normed_far,
            (active, (0, None, None)),
            active_far,
            dlow,
            dlow_far,
            dup,
            slope_far,
            down,
        ],
        [
            ((width // 2, hidden), BF16),
            ((width // 2, hidden), BF16),
            rows_of(hidden // 2),
            rows_of(hidden // 2),
            ((8, hidden), F32),
        ],
        us=30,
        scratch=[pltpu.VMEM((width, hidden), BF16)],
        after=[datt],
    )
    up_recv = swap(up_send, "batch")
    down_recv = swap(down_send, "y")
    datt_recv, pay = join(datt_recv, pay)
    pay_recv = swap(pay, "zh")
    piece = rows_of(rows)
    dscore, dproj, dspat, dxk0, dxk1, dxs, dsk0, dsk1, dss = run(
        functools.partial(backward_kernel, heads=heads, block=128),
        [datt, datt_recv, first, (soft, "any"), proj, spat, weights, spatial_weights],
        [
            ((heads, length, length), BF16),
            ((3, length, inner), BF16),
            ((2, length, inner), BF16),
            piece,
            piece,
            ((2, rows, width), BF16),
            piece,
            piece,
            ((2, rows, width), BF16),
        ],
        us=30,
        scratch=[pltpu.VMEM((heads, length, length), F32), pltpu.SemaphoreType.DMA((heads,))],
        after=[bias_grad],
    )

    steps = batch_steps()[1:]

    def plus(pairs, after=(), over_batch=False):
        sums = run(
            plus_kernel,
            [array for pair_of in pairs for array in pair_of],
            [(left.shape, BF16) for left, _ in pairs],
            after=after,
        )
        if over_batch:
            for step in steps:
                sums = [added(value, swap(value, "batch", step)) for value in sums]
        return sums

    dxk1, dxs, dss, pay_recv = join(dxk1, dxs, dss, pay_recv)
    dxs, dss = swap(dxs, "core"), swap(dss, "core")
    near, far = run(
        units_kernel,
        [dxk0, dxk1, dxs, dsk0, dsk1, dss],
        [((3, rows, width), BF16), ((3, rows, width), BF16)],
    )
    far_zl = swap(far, "zl")
    up_half, down_half = plus([(up_keep, up_recv), (down_keep, down_recv)], after=[far])
    up_other = swap(up_half, "y")
    down_other = swap(down_half, "batch")
    pay_zl = swap(join(pay_recv, far)[0], "zl")
    one_keep, one_send, lines = run(
        functools.partial(first_grad_kernel, heads=heads),
        [x, dscore, dproj, colidx, bias_grad],
        [rows_of(3 * inner // 2), rows_of(3 * inner // 2), rows_of(16, F32)],
        scratch=[pltpu.VMEM((3 * inner, width), BF16)],
        after=[up_half],
    )
    keep, send = run(
        fold_kernel,
        [near, far_zl],
        [((3, rest, width), BF16), ((3, rest, width), BF16)],
        after=[lines],
    )
    send_zh = swap(send, "zh")
    up_half, down_half = plus(
        [(up_half, up_other), (down_half, down_other)], after=[send], over_batch=True
    )
    up_far = swap(up_half, "batch")
    down_far = swap(down_half, "y")
    mine, other = run(
        ends_first_kernel,
        [keep, send_zh],
        [((3, least, width), BF16), ((3, least, width), BF16)],
        after=[up_half],
    )
    got = swap(other, "y")
    pay_recv, pay_zl, far_send, mine = join(pay_recv, pay_zl, far_send, mine)
    pay_core, pay_zlcore = swap(pay_recv, "core"), swap(pay_zl, "core")
    far_core = swap(far_send, "core")
    base = 3 * inner + 32
    two_keep, two_send = run(
        second_grad_kernel,
        [dmix, pay, pay_recv, pay_zl, pay_core, pay_zlcore, att_own, att_send, sp, dspat, lines],
        [rows_of(base // 2), rows_of(base // 2)],
        scratch=[pltpu.VMEM((base, width), BF16)],
        after=[mine, up_far, down_far],
    )
    one_send, two_send, got, two_keep = join(one_send, two_send, got, two_keep)
    one_recv = swap(one_send, "batch")
    two_recv = swap(two_send, "y")
    pages = jnp.stack([mine, got])
    pages_zh = swap(pages, "zh")
    pages_zl = swap(pages, "zl")
    one_half, two_half = plus([(one_keep, one_recv), (two_keep, two_recv)], after=[pages])
    one_other = swap(one_half, "y")
    two_other = swap(two_half, "batch")
    far_y = swap(jnp.stack([far_keep[1], far_core[1]]), "y")
    halves = [up_half, up_far, down_half, down_far]
    others = [swap(value, "core") for value in halves]
    grad_up, grad_down, spread_event = run(
        spread_kernel,
        halves[:2] + others[:2] + halves[2:] + others[2:],
        [
            ((2, 2, width // 2, hidden), F32),
            ((2, 2, hidden // 2, width), F32),
            ((8, NBUCK), F32),
        ],
        after=[one_half],
    )
    one_half, two_half = plus(
        [(one_half, one_other), (two_half, two_other)], after=[spread_event], over_batch=True
    )
    one_far = swap(one_half, "batch")
    two_far = swap(two_half, "y")
    pages_zh, one_half = join(pages_zh, one_half)
    pages_zz = swap(pages_zh, "zl")
    grad_tokens, grad_spatial, ends_event = run(
        ends_kernel,
        [mine, got, pages_zh, pages_zl, pages_zz],
        [((2, 2, 4, least, width), F32), ((2, 4, least, width), F32), ((8, NBUCK), F32)],
        after=[one_half],
    )
    output, out_event = run(
        out_kernel,
        [
            out_keep[0],
            out_core[0],
            out_y[0],
            out_y[1],
            far_keep[0],
            far_core[0],
            far_y[0],
            far_y[1],
        ],
        [((2, 2, 4, least, width), BF16), ((8, NBUCK), F32)],
        after=[one_half],
    )
    one_far, two_far, out_event, ends_event = join(one_far, two_far, out_event, ends_event)
    halves = [one_half, one_far, two_half, two_far]
    others = [swap(value, "core") for value in halves]
    part = width // (2 * lax.axis_size("zh"))
    grad_qkv, grad_spatial_w, grad_exit, tables, gains_grad, shifts_grad, grad_b_up, grad_b_down = run(
        functools.partial(last_kernel, heads=heads),
        halves[:2] + others[:2] + halves[2:] + others[2:],
        [
            ((2, 3 * inner, width), F32),
            rows_of(2 * inner, F32),
            ((2, inner, width), F32),
            ((2, 3, heads, NBUCK), F32),
            ((2, 2, part), F32),
            ((2, 2, part), F32),
            ((2, hidden), F32),
            ((2, part), F32),
        ],
        scratch=[pltpu.VMEM((3 * inner, width), F32), pltpu.VMEM((base, width), F32)],
        after=[spread_event, out_event, ends_event],
    )
    return (
        output.reshape(tokens.shape),
        grad_tokens.reshape(tokens.shape),
        grad_spatial.reshape(spatial.shape),
        grad_qkv.reshape(2, 3, inner, width).swapaxes(2, 3),
        grad_spatial_w.reshape(2, inner, width).swapaxes(1, 2),
        tables,
        grad_exit,
        gains_grad,
        shifts_grad,
        grad_up.reshape(2, width, hidden),
        grad_b_up,
        grad_down.reshape(2, hidden, width),
        grad_b_down,
    )


def solution(mesh):
    batch, seq, head = mesh.devices.shape
    fine = Mesh(
        mesh.devices.reshape(batch, seq // 2, 2, head // 2, 2),
        ("batch", "y", "core", "zh", "zl"),
    )
    seq = ("y", "core")
    head = ("zh", "zl")
    return jax.shard_map(
        shards,
        mesh=fine,
        in_specs=(
            P(None, "batch", seq, None),
            P("batch", seq, None),
            P("batch", seq),
            P(None, "batch", seq),
            P(None, None, None, head),
            P(None, None, head),
            P(None, None, head, None),
            P(None, head, None),
            P(),
            P(),
            P(None, None, head),
            P(None, head),
            P(None, head, None),
            P(),
            P(None, "batch", seq, None),
        ),
        out_specs=(
            P(None, "batch", seq, None),
            P(None, "batch", seq, None),
            P("batch", seq, None),
            P(None, None, None, head),
            P(None, None, head),
            P(None, None, head, None),
            P(None, head, None),
            P(None, None, head),
            P(None, None, head),
            P(None, None, head),
            P(None, head),
            P(None, head, None),
            P(None, head),
        ),
        check_vma=False,
    )
```

```python
import functools

import jax
import jax.numpy as jnp
from jax import lax
from jax.experimental import pallas as pl
from jax.experimental.pallas import tpu as pltpu
from jax.sharding import Mesh, PartitionSpec as P

DH = 64
NBUCK = 128
HALF = 64
EPSILON = 1e-05
F32 = jnp.float32
BF16 = jnp.bfloat16
VMEM_BYTES = 20 * 1024 * 1024
TICK = 0.1
PACK_VMEM = 60 * 1024 * 1024
NN = (((1,), (0,)), ((), ()))
NT = (((1,), (1,)), ((), ()))
TN = (((0,), (0,)), ((), ()))


def mm(left, right, dims=NN):
    return lax.dot_general(left, right, dims, preferred_element_type=F32)


def kernel_call(body, place, operands, outs, us, scratch=(), after=(), vmem=VMEM_BYTES):
    specs, arrays, hows = [], [], []
    for operand in operands:
        array, how = operand if isinstance(operand, tuple) else (operand, None)
        specs.append(pl.BlockSpec(memory_space=pltpu.HBM if how == "any" else pltpu.VMEM))
        arrays.append(array)
        hows.append(how)
    count = len(arrays)
    specs += [pl.BlockSpec(memory_space=pl.ANY)] * len(after)

    def view(s_ref, ref, how):
        if how == "stream":
            return ref.at[s_ref[0]]
        if how is None or how == "any":
            return ref
        return ref.at[tuple(slice(None) if at is None else at for at in how)]

    def kernel(s_ref, *refs):
        given = [view(s_ref, ref, how) for ref, how in zip(refs, hows)]
        body(s_ref, *given, *refs[count + len(after) :])

    return pl.pallas_call(
        kernel,
        out_shape=[jax.ShapeDtypeStruct(out[0], out[1]) for out in outs],
        in_specs=[pl.BlockSpec(memory_space=pltpu.SMEM)] + specs,
        out_specs=[
            pl.BlockSpec(memory_space=pltpu.HBM if len(out) > 2 else pltpu.VMEM) for out in outs
        ],
        scratch_shapes=list(scratch),
        compiler_params=pltpu.CompilerParams(vmem_limit_bytes=vmem),
        cost_estimate=pl.CostEstimate(
            flops=int(us * 1.1e9), bytes_accessed=int(us * 3.5e6), transcendentals=0
        ),
    )(place, *arrays, *after)


def centred(rows):
    centre = rows - jnp.mean(rows, axis=-1, keepdims=True)
    spread = lax.rsqrt(jnp.mean(centre * centre, axis=-1, keepdims=True) + EPSILON)
    return centre * spread, spread


def norm_back(unit, spread, tilted):
    return spread * (
        tilted
        - jnp.mean(tilted, axis=-1, keepdims=True)
        - unit * jnp.mean(tilted * unit, axis=-1, keepdims=True)
    )


def pick(table_row, index):
    width = index.shape[1]
    table = jnp.broadcast_to(table_row, (index.shape[0], NBUCK))
    parts = [
        jnp.take_along_axis(
            table,
            index[:, at : at + NBUCK],
            axis=1,
            mode="promise_in_bounds",
        )
        for at in range(0, width, NBUCK)
    ]
    return jnp.concatenate(parts, axis=1)


def stack_rows(pieces):
    return jnp.concatenate(pieces, axis=0)


def turned(rows, size):
    pieces = [rows[at : at + size] for at in range(0, rows.shape[0], size)]
    return stack_rows([pieces[i ^ 1] for i in range(len(pieces))])


def residual(x_ref, mixed_refs):
    rest = mixed_refs[0].shape[0] // 2
    pieces = []
    for y in range(2):
        for c in range(2):
            own = x_ref[y, c * rest : (c + 1) * rest, :].astype(F32)
            pieces.append(own + mixed_refs[c][y * rest : (y + 1) * rest, :].astype(F32))
    return stack_rows(pieces)


def dealt(rows_ref, side, keep_ref, send_ref):
    half = keep_ref.shape[0]
    keep_ref[...] = rows_ref[pl.ds(pl.multiple_of(side * half, 16), half), :]
    send_ref[...] = rows_ref[pl.ds(pl.multiple_of((1 - side) * half, 16), half), :]


def gathered(place_ref, refs, rows, to_ref):
    size = rows.stop - rows.start
    for turn, ref in enumerate(refs):
        q = (place_ref[1] ^ (turn // 2)) * 2 + (place_ref[2] ^ (turn % 2))
        to_ref[pl.ds(pl.multiple_of(q * size, 16), size), :] = ref[rows, :]


def copied(pairs, sems):
    started = [
        pltpu.make_async_copy(source, target, sems.at[n])
        for n, (source, target) in enumerate(pairs)
    ]
    for copy in started:
        copy.start()
    return started


def share_kernel(p_ref, exit_ref, up_ref, down_ref, bias_ref, ups_ref, downs_ref, biasv_ref, sems):
    c = p_ref[0]
    q = p_ref[1] * 2 + p_ref[2]
    many = down_ref.shape[1] // 4
    few = exit_ref.shape[1] // 4
    started = copied(
        [
            (bias_ref, biasv_ref),
            (up_ref.at[c, pl.ds(pl.multiple_of(q * many, 16), many)], ups_ref.at[pl.ds(0, many)]),
            (
                exit_ref.at[c, pl.ds(pl.multiple_of(q * few, 16), few)],
                ups_ref.at[pl.ds(many + 16, few)],
            ),
            (down_ref.at[c, pl.ds(pl.multiple_of(q * many, 16), many)], downs_ref),
        ],
        sems,
    )
    started[0].wait()
    left = biasv_ref[pl.ds(c, 1), :]
    lines = []
    for _ in range(3):
        lines.append(left.astype(BF16).astype(F32))
        left = left - lines[-1]
    lines.append(jnp.zeros((13, left.shape[1]), F32))
    ups_ref[many : many + 16, :] = jnp.concatenate(lines, axis=0).astype(BF16)
    for copy in started[1:]:
        copy.wait()


def pack_kernel(
    p_ref,
    tok_ref,
    sp_ref,
    pos_ref,
    box_ref,
    far0_ref,
    far1_ref,
    far2_ref,
    near_ref,
    own_ref,
    posv_ref,
    boxv_ref,
    sems,
):
    c, y, zl, zh = p_ref[0], p_ref[2], p_ref[3], p_ref[4]
    block = zh * 2 + zl
    least = tok_ref.shape[3]
    rows = 4 * least
    pairs = [(pos_ref, posv_ref), (box_ref, boxv_ref)]
    for k in range(4):
        at = block ^ k
        to = pl.ds(k * least, least)
        pairs += [
            (tok_ref.at[1 - c, 1 - y, at], far0_ref.at[to]),
            (sp_ref.at[1 - y, at], far1_ref.at[to]),
            (tok_ref.at[c, 1 - y, at], far2_ref.at[to]),
            (tok_ref.at[1 - c, y, at], near_ref.at[to]),
            (sp_ref.at[y, at], near_ref.at[pl.ds(rows + k * least, least)]),
            (tok_ref.at[c, y, at], own_ref.at[to]),
        ]
    started = copied(pairs, sems)
    for copy in started[:2]:
        copy.wait()
    lane = lax.broadcasted_iota(jnp.int32, (8, NBUCK), 1)
    width = far0_ref.shape[1]
    for page, ref, at in ((1 - y, far0_ref, rows), (y, near_ref, 2 * rows)):
        place = posv_ref[pl.ds(page, 1), :]
        lines = [
            place & 255,
            place >> 8,
            boxv_ref[0, pl.ds(page, 1), :],
            boxv_ref[1, pl.ds(page, 1), :],
        ]
        value = jnp.concatenate(lines + [jnp.zeros((4, NBUCK), jnp.int32)], axis=0)
        crossed = jnp.where(
            (lane & 63) < 32, pltpu.roll(value, NBUCK - 32, 1), pltpu.roll(value, 32, 1)
        )
        value = jnp.where(zl == 0, value, crossed)
        value = jnp.where(zh == 0, value, pltpu.roll(value, 64, 1))
        value = jnp.concatenate([value.astype(F32), jnp.zeros((8, NBUCK), F32)], axis=0)
        ref[at : at + 16, 0:NBUCK] = value.astype(BF16)
        ref[at : at + 16, NBUCK:] = jnp.zeros((16, width - NBUCK), BF16)
    for copy in started[2:]:
        copy.wait()


def cotangent_kernel(p_ref, cot_ref, far_ref, near_ref, own_ref, sems):
    c, y, block = p_ref[0], p_ref[2], p_ref[4] * 2 + p_ref[3]
    least = cot_ref.shape[3]
    pairs = []
    for k in range(4):
        at = block ^ k
        to = pl.ds(k * least, least)
        pairs += [
            (cot_ref.at[c, 1 - y, at], far_ref.at[0, to]),
            (cot_ref.at[1 - c, 1 - y, at], far_ref.at[1, to]),
            (cot_ref.at[1 - c, y, at], near_ref.at[to]),
            (cot_ref.at[c, y, at], own_ref.at[to]),
        ]
    for copy in copied(pairs, sems):
        copy.wait()


def indices(ref, at):
    lines = ref[at : at + 16, 0:NBUCK].astype(F32).astype(jnp.int32)
    place = lines[0:1] + lines[1:2] * 256
    return jnp.concatenate([place, lines[2:4], jnp.zeros((5, NBUCK), jnp.int32)], axis=0)


def two_cores(index0, index1, half):
    lane = lax.broadcasted_iota(jnp.int32, (8, NBUCK), 1)
    if half == 0:
        return jnp.where(lane < 64, index0, pltpu.roll(index1, 64, 1))
    return jnp.where(lane < 64, pltpu.roll(index0, 64, 1), index1)


def arrange(x0_ref, x1_ref, s0_ref, s1_ref, i0_ref, i1_ref, at, x_ref, sp_ref):
    least = x_ref.shape[1]
    rest = least // 2
    found = []
    index0, index1 = indices(i0_ref, at), indices(i1_ref, at)
    for half in range(2):
        at = half * rest
        x_ref[half, 0:rest, :] = x0_ref[at : at + rest, :]
        x_ref[half, rest:, :] = x1_ref[at : at + rest, :]
        sp_ref[half, 0:rest, :] = s0_ref[at : at + rest, :]
        sp_ref[half, rest:, :] = s1_ref[at : at + rest, :]
        found.append(two_cores(index0, index1, half))
    return found


def project(x_ref, sp_ref, w_ref, ws_ref, proj_ref, spat_ref, at):
    width = x_ref.shape[-1]
    x = x_ref[...].reshape(-1, width)
    sp = sp_ref[...].reshape(-1, width)
    rows = slice(at, at + x.shape[0])
    for k in range(3):
        proj_ref[k, rows, :] = mm(x, w_ref[k], NT).astype(BF16)
    for k in range(2):
        spat_ref[k, rows, :] = mm(sp, ws_ref[k], NT).astype(BF16)


def near_kernel(
    p_ref,
    x00_ref,
    n01_ref,
    n00_ref,
    w_ref,
    ws_ref,
    up_hbm,
    down_hbm,
    exit_hbm,
    x_ref,
    sp_ref,
    index_ref,
    proj_ref,
    spat_ref,
    up_ref,
    down_ref,
    exit_ref,
    sems,
):
    fetched = [
        pltpu.make_async_copy(source.at[p_ref[0]], target, sems.at[n])
        for n, (source, target) in enumerate(
            ((exit_hbm, exit_ref), (up_hbm, up_ref), (down_hbm, down_ref))
        )
    ]
    for copy in fetched:
        copy.start()
    least = x_ref.shape[1]
    found = arrange(
        x00_ref,
        n01_ref,
        n00_ref.at[least:],
        n01_ref.at[least:],
        n00_ref,
        n01_ref,
        2 * least,
        x_ref,
        sp_ref,
    )
    index_ref[...] = jnp.concatenate(found, axis=1)
    project(x_ref, sp_ref, w_ref, ws_ref, proj_ref, spat_ref, 0)
    for copy in fetched:
        copy.wait()


def attention_kernel(
    p_ref,
    x10_ref,
    x11_ref,
    s10_ref,
    s11_ref,
    i10_ref,
    x0_ref,
    sp0_ref,
    index_ref,
    proj0_ref,
    spat0_ref,
    w_ref,
    ws_ref,
    table_ref,
    x_ref,
    sp_ref,
    colidx_ref,
    proj_hbm,
    spat_hbm,
    soft_hbm,
    own_ref,
    send_ref,
    att_ref,
    proj_ref,
    spat_ref,
    soft_ref,
    sems,
    *,
    heads,
):
    least = x_ref.shape[2]
    near = 2 * least
    x_ref[0] = x0_ref[...]
    sp_ref[0] = sp0_ref[...]
    proj_ref[:, 0:near, :] = proj0_ref[...]
    spat_ref[:, 0:near, :] = spat0_ref[...]
    found = arrange(
        x10_ref, x11_ref, s10_ref, s11_ref, i10_ref, x11_ref, least, x_ref.at[1], sp_ref.at[1]
    )
    places = jnp.concatenate([index_ref[...]] + found, axis=1)
    colidx_ref[...] = jnp.transpose(places.astype(F32)).astype(jnp.int32)
    project(x_ref.at[1], sp_ref.at[1], w_ref, ws_ref, proj_ref, spat_ref, near)
    length = 2 * near
    stored = [
        pltpu.make_async_copy(proj_ref, proj_hbm, sems.at[0]),
        pltpu.make_async_copy(spat_ref, spat_hbm, sems.at[1]),
    ]
    for copy in stored:
        copy.start()
    level = lax.broadcasted_iota(jnp.int32, (length, NBUCK), 1)
    chosen = [(colidx_ref[:, kind : kind + 1] == level).astype(BF16) for kind in (1, 2)]
    chosen = jnp.concatenate(chosen, axis=1)

    lane = lax.broadcasted_iota(jnp.int32, (length, NBUCK), 1)
    boxes = [
        jnp.clip(lane - colidx_ref[:, kind : kind + 1], -HALF, HALF - 1) + HALF
        for kind in (1, 2)
    ]
    index = jnp.clip(places[0:1, :] - colidx_ref[:, 0:1], -HALF, HALF - 1) + HALF
    for h in range(heads):
        cols = slice(h * DH, (h + 1) * DH)
        bias = jnp.concatenate(
            [pick(table_ref[k, h : h + 1, :], boxes[k - 1]) for k in (1, 2)], axis=1
        )
        coarse = bias.astype(BF16)
        fine = (bias - coarse.astype(F32)).astype(BF16)
        left = jnp.concatenate(
            [proj_ref[0, :, cols], spat_ref[0, :, cols]], axis=1
        ) * jnp.asarray(DH**-0.5, BF16)
        right = jnp.concatenate([proj_ref[1, :, cols], spat_ref[1, :, cols]], axis=1)
        scores = mm(
            jnp.concatenate([left, coarse, fine], axis=1),
            jnp.concatenate([right, chosen, chosen], axis=1),
            NT,
        ) + pick(table_ref[0, h : h + 1, :], index)
        top = jnp.max(scores, axis=-1, keepdims=True)
        raised = jnp.exp(scores - top)
        soft = raised * (1.0 / jnp.sum(raised, axis=-1, keepdims=True))
        soft_ref[h] = soft
        stored.append(pltpu.make_async_copy(soft_ref.at[h], soft_hbm.at[h], sems.at[2 + h]))
        stored[-1].start()
        att_ref[:, cols] = mm(soft.astype(BF16), proj_ref[2, :, cols]).astype(BF16)
    for copy in stored:
        copy.wait()
    part = length // 4
    own_ref[0:part, :] = att_ref[0:part, :]
    own_ref[part:, :] = att_ref[2 * part : 3 * part, :]
    send_ref[0:part, :] = att_ref[part : 2 * part, :]
    send_ref[part:, :] = att_ref[3 * part :, :]


def mixed_kernel(
    p_ref,
    own_ref,
    recv_ref,
    exit_ref,
    one0_ref,
    one1_ref,
    one2_ref,
    one3_ref,
    keep_ref,
    send_ref,
    partner_ref,
):
    rows = slice(one0_ref.shape[0] - exit_ref.shape[0] // 4, one0_ref.shape[0])
    gathered(p_ref, (one0_ref, one1_ref, one2_ref, one3_ref), rows, partner_ref)
    total = mm(own_ref[...], exit_ref[...]) + mm(recv_ref[...], partner_ref[...])
    rest = total.shape[0] // 4
    for y in range(2):
        at = 2 * y * rest
        keep_ref[y * rest : (y + 1) * rest, :] = total[at : at + rest]
        send_ref[y * rest : (y + 1) * rest, :] = total[at + rest : at + 2 * rest].astype(BF16)


def gelu_parts(upper):
    phi = 0.5 * (1.0 + lax.erf(upper * (0.5**0.5)))
    slope = phi + upper * (jnp.exp(-0.5 * upper * upper) * (0.5 / jnp.pi) ** 0.5)
    return (upper * phi).astype(BF16), slope


def forward_kernel(
    p_ref,
    x_ref,
    mixed0_ref,
    mixed1_ref,
    gain_ref,
    shift_ref,
    up_ref,
    hidden_ref,
    down_ref,
    one0_ref,
    one1_ref,
    one2_ref,
    one3_ref,
    two0_ref,
    two1_ref,
    two2_ref,
    two3_ref,
    low_ref,
    normed_ref,
    active_ref,
    slope_ref,
    upp_ref,
    downp_ref,
):
    many = two0_ref.shape[0]
    gathered(p_ref, (one0_ref, one1_ref, one2_ref, one3_ref), slice(0, many), upp_ref)
    gathered(p_ref, (two0_ref, two1_ref, two2_ref, two3_ref), slice(0, many), downp_ref)
    extra = one0_ref[many : many + 16, :].astype(F32)
    partner_bias = extra[0:1] + extra[1:2] + extra[2:3]
    unit, _ = centred(residual(x_ref, (mixed0_ref, mixed1_ref)))
    normed_low = (unit * gain_ref[0:1, :] + shift_ref[0:1, :]).astype(BF16)
    normed_ref[...] = normed_low
    active, slope = gelu_parts(mm(normed_low, up_ref[...]) + hidden_ref[pl.ds(p_ref[0], 1), :])
    active_ref[0] = active
    slope_ref[0] = slope.astype(BF16)
    total = mm(active, down_ref[...])
    active, slope = gelu_parts(mm(normed_low, upp_ref[...]) + partner_bias)
    active_ref[1] = active
    slope_ref[1] = slope.astype(BF16)
    low_ref[...] = (total + mm(active, downp_ref[...])).astype(BF16)


def other_kernel(
    p_ref,
    normed_ref,
    up_ref,
    hidden_ref,
    active_ref,
    slope_ref,
):
    active, slope = gelu_parts(
        mm(normed_ref[...], up_ref[...]) + hidden_ref[pl.ds(p_ref[0], 1), :]
    )
    active_ref[...] = active
    slope_ref[...] = slope.astype(BF16)


def first_norm_kernel(p_ref, x_ref, mixed0_ref, mixed1_ref, gain_ref, shift_ref, normed_ref):
    unit, _ = centred(residual(x_ref, (mixed0_ref, mixed1_ref)))
    normed_ref[...] = (unit * gain_ref[0:1, :] + shift_ref[0:1, :]).astype(BF16)


def lowered_kernel(p_ref, own_ref, far_ref, low0_ref, low1_ref):
    least = own_ref.shape[0] // 8
    total = own_ref[...].astype(F32) + turned(far_ref[...], least).astype(F32)
    total = total.astype(BF16)
    for i in range(4):
        low0_ref[i * least : (i + 1) * least, :] = total[2 * i * least : (2 * i + 1) * least]
        low1_ref[i * least : (i + 1) * least, :] = total[(2 * i + 1) * least : (2 * i + 2) * least]


def final_kernel(
    p_ref,
    x_ref,
    mixed0_ref,
    mixed1_ref,
    low0_ref,
    low1_ref,
    cot00_ref,
    cot10_ref,
    cot01_ref,
    cot11_ref,
    gain_ref,
    shift_ref,
    bdown_ref,
    outk_ref,
    outs_ref,
    second_ref,
    dlow_ref,
    sums_ref,
):
    unit, _ = centred(residual(x_ref, (mixed0_ref, mixed1_ref)))
    normed = unit * gain_ref[0:1, :] + shift_ref[0:1, :]
    least = low0_ref.shape[0] // 4
    pieces = []
    for i in range(4):
        pieces.append(low0_ref[i * least : (i + 1) * least, :])
        pieces.append(low1_ref[i * least : (i + 1) * least, :])
    lowered = stack_rows(pieces).astype(F32)
    unit2, spread2 = centred(normed + lowered + bdown_ref[pl.ds(p_ref[0], 1), :])
    out = (unit2 * gain_ref[1:2, :] + shift_ref[1:2, :]).astype(BF16)
    for y in range(2):
        at = 4 * y * least
        outk_ref[y] = out[at : at + 2 * least]
        outs_ref[y] = out[at + 2 * least : at + 4 * least]
    cot = stack_rows([cot00_ref[...], cot01_ref[...], cot10_ref[...], cot11_ref[...]]).astype(F32)
    second = norm_back(unit2, spread2, cot * gain_ref[1:2, :])
    second_ref[...] = second
    dlow_ref[...] = second.astype(BF16)
    sums_ref[...] = jnp.zeros_like(sums_ref)
    sums_ref[0:1, :] = jnp.sum(cot * unit2, axis=0, keepdims=True)
    sums_ref[1:2, :] = jnp.sum(cot, axis=0, keepdims=True)
    sums_ref[2:3, :] = jnp.sum(second, axis=0, keepdims=True)


def middle_kernel(
    p_ref,
    dlow_ref,
    up_ref,
    down_ref,
    upp_ref,
    downp_ref,
    slope_ref,
    hid_ref,
    dup_ref,
):
    dlow = dlow_ref[...]
    dup = (mm(dlow, down_ref[...], NT) * slope_ref[0].astype(F32)).astype(BF16)
    dup_ref[...] = dup
    total = mm(dup, up_ref[...], NT)
    dup = (mm(dlow, downp_ref[...], NT) * slope_ref[1].astype(F32)).astype(BF16)
    hid_ref[...] = (total + mm(dup, upp_ref[...], NT)).astype(BF16)


def ffn_grad_kernel(
    p_ref,
    normed_ref,
    normedo_ref,
    active_ref,
    activeo_ref,
    dlow_ref,
    dlowo_ref,
    dup_ref,
    slopeo_ref,
    down_ref,
    upk_ref,
    ups_ref,
    downk_ref,
    downs_ref,
    bias_ref,
    all_ref,
):
    dlowo = dlowo_ref[...]
    dupo = (mm(dlowo, down_ref[...], NT) * slopeo_ref[...].astype(F32)).astype(BF16)
    dup = dup_ref[...]
    all_ref[...] = (mm(normed_ref[...], dup, TN) + mm(normedo_ref[...], dupo, TN)).astype(BF16)
    dealt(all_ref, p_ref[1], upk_ref, ups_ref)
    all_ref[...] = (
        mm(active_ref[...], dlow_ref[...], TN) + mm(activeo_ref[...], dlowo, TN)
    ).astype(BF16)
    dealt(all_ref, p_ref[2], downk_ref, downs_ref)
    bias = jnp.sum(dup.astype(F32), axis=0, keepdims=True)
    bias = bias + jnp.sum(dupo.astype(F32), axis=0, keepdims=True)
    bias_ref[...] = jnp.broadcast_to(bias, bias_ref.shape)


def first_kernel(
    p_ref,
    x_ref,
    mixed0_ref,
    mixed1_ref,
    second_ref,
    hid_ref,
    hidr_ref,
    gain_ref,
    first_ref,
    dmix_ref,
    sums_ref,
):
    unit, spread = centred(residual(x_ref, (mixed0_ref, mixed1_ref)))
    hid = hid_ref[...].astype(F32) + turned(hidr_ref[...], hid_ref.shape[0] // 8).astype(F32)
    dnormed = second_ref[...] + hid
    first = norm_back(unit, spread, dnormed * gain_ref[0:1, :])
    first_ref[...] = first
    dmix_ref[...] = first.astype(BF16)
    sums_ref[...] = jnp.zeros_like(sums_ref)
    sums_ref[0:1, :] = jnp.sum(dnormed * unit, axis=0, keepdims=True)
    sums_ref[1:2, :] = jnp.sum(dnormed, axis=0, keepdims=True)


def attended_kernel(
    p_ref,
    dmix_ref,
    dmixr_ref,
    exit_ref,
    exitp_ref,
    sums1_ref,
    sums2_ref,
    own_ref,
    send_ref,
    total_ref,
    pay_ref,
):
    length = dmix_ref.shape[0]
    rest = length // 4
    total = dmix_ref[...].astype(F32) + turned(dmixr_ref[...], rest).astype(F32)
    total = total.astype(BF16)
    total_ref[...] = total
    own_ref[...] = mm(total, exit_ref[...], NT).astype(BF16)
    send_ref[...] = mm(total, exitp_ref[...], NT).astype(BF16)
    least = rest // 2
    pay_ref[0:least, :] = total[0:least]
    pay_ref[least:rest, :] = total[2 * rest : 2 * rest + least]
    pay_ref[rest:, :] = jnp.concatenate([sums1_ref[...], sums2_ref[...]], axis=0).astype(BF16)


def backward_kernel(
    p_ref,
    datt_ref,
    dattr_ref,
    first_ref,
    soft_hbm,
    proj_ref,
    spat_ref,
    w_ref,
    ws_ref,
    dscore_ref,
    dproj_ref,
    dspat_ref,
    dxk0_ref,
    dxk1_ref,
    dxs_ref,
    dsk0_ref,
    dsk1_ref,
    dss_ref,
    soft_ref,
    sems,
    *,
    heads,
    block,
):
    fetched = [
        pltpu.make_async_copy(soft_hbm.at[h], soft_ref.at[h], sems.at[h]) for h in range(heads)
    ]
    for copy in fetched:
        copy.start()
    length = 2 * datt_ref.shape[0]
    scale = DH**-0.5
    part = length // 4
    datt = stack_rows(
        [datt_ref[0:part, :], dattr_ref[0:part, :], datt_ref[part:, :], dattr_ref[part:, :]]
    )
    for h in range(heads):
        cols = slice(h * DH, (h + 1) * DH)
        value = proj_ref[2, :, cols]
        left = jnp.concatenate([proj_ref[0, :, cols], spat_ref[0, :, cols]], axis=1)
        right = jnp.concatenate([proj_ref[1, :, cols], spat_ref[1, :, cols]], axis=1)
        own = datt[:, cols]
        fetched[h].wait()
        for at in range(0, length, block):
            soft = soft_ref[h, at : at + block, :]
            dsoft = mm(own[at : at + block], value, NT)
            inner = jnp.sum(soft * dsoft, axis=-1, keepdims=True)
            dscore_ref[h, at : at + block, :] = (soft * (dsoft - inner)).astype(BF16)
        dscore = dscore_ref[h]
        dleft = (mm(dscore, right) * scale).astype(BF16)
        dright = (mm(dscore, left, TN) * scale).astype(BF16)
        dproj_ref[0, :, cols] = dleft[:, :DH]
        dspat_ref[0, :, cols] = dleft[:, DH:]
        dproj_ref[1, :, cols] = dright[:, :DH]
        dspat_ref[1, :, cols] = dright[:, DH:]
        dproj_ref[2, :, cols] = mm(soft_ref[h].astype(BF16), own, TN).astype(BF16)
    once = (p_ref[3] == 0).astype(F32)
    total = mm(dproj_ref[0], w_ref[0])
    for k in range(1, 3):
        total = total + mm(dproj_ref[k], w_ref[k])
    least = part // 4

    def deal(rows, refs):
        for y in range(2):
            for zh in range(2):
                for c in range(2):
                    for zl in range(2):
                        at = (((y * 2 + zh) * 2 + c) * 2 + zl) * least
                        to = (zh * 2 + y) * least
                        value = rows[at : at + least]
                        if zh == 0 and refs[0][0] is dxk0_ref:
                            of = ((y * 2 + c) * 2 + zl) * least
                            value = value + once * first_ref[of : of + least, :]
                        refs[c][zl][to : to + least, :] = value.astype(BF16)

    deal(total, ((dxk0_ref, dxk1_ref), (dxs_ref.at[0], dxs_ref.at[1])))
    total = mm(dspat_ref[0], ws_ref[0]) + mm(dspat_ref[1], ws_ref[1])
    deal(total, ((dsk0_ref, dsk1_ref), (dss_ref.at[0], dss_ref.at[1])))


def spatial_grad_kernel(p_ref, sp_ref, dspat_ref, keep_ref, send_ref):
    sp = sp_ref[...].reshape(-1, sp_ref.shape[-1])
    keep_ref[...] = mm(dspat_ref[p_ref[0]], sp, TN).astype(BF16)
    send_ref[...] = mm(dspat_ref[1 - p_ref[0]], sp, TN).astype(BF16)


def second_grad_kernel(
    p_ref,
    dmix_ref,
    pay_ref,
    payr_ref,
    payl_ref,
    payc_ref,
    paylc_ref,
    atto_ref,
    atts_ref,
    rest_ref,
    spk_ref,
    spr_ref,
    lines_ref,
    keep_ref,
    send_ref,
    second_ref,
):
    inner = spk_ref.shape[0]
    length = dmix_ref.shape[0]
    least = length // 8
    rest = 2 * least
    dmixo = stack_rows(
        [
            ref[y * least : (y + 1) * least, :]
            for y in range(2)
            for ref in (payr_ref, payl_ref, payc_ref, paylc_ref)
        ]
    )
    base = rest_ref.shape[0]
    second_ref[0:base, :] = rest_ref[...]
    second_ref[base : base + inner, :] = (
        mm(atto_ref[...], dmix_ref[...], TN) + mm(atts_ref[...], dmixo, TN)
    ).astype(BF16)
    base += inner
    second_ref[base : base + inner, :] = (
        spk_ref[...].astype(F32) + spr_ref[...].astype(F32)
    ).astype(BF16)
    base += inner
    small = pay_ref[rest:, :].astype(F32) + payr_ref[rest:, :].astype(F32)
    second_ref[base : base + 16, :] = small.astype(BF16)
    second_ref[base + 16 : base + 32, :] = lines_ref[...].astype(BF16)
    dealt(second_ref, p_ref[2], keep_ref, send_ref)


def first_grad_kernel(
    p_ref,
    x_ref,
    dscore_ref,
    dproj_ref,
    colidx_ref,
    bup_ref,
    keep_ref,
    send_ref,
    rest_ref,
    lines_ref,
    first_ref,
    *,
    heads,
):
    width = x_ref.shape[-1]
    x = x_ref[...].reshape(-1, width)
    length = x.shape[0]
    inner = dproj_ref.shape[-1]
    for k in range(3):
        first_ref[k * inner : (k + 1) * inner, :] = mm(dproj_ref[k], x, TN).astype(BF16)
    dealt(first_ref, p_ref[1], keep_ref, send_ref)
    rest_ref[...] = first_ref[2 * keep_ref.shape[0] :, :]
    lane = lax.broadcasted_iota(jnp.int32, (1, NBUCK), 1)
    found = []
    for kind in range(3):
        extent = length if kind == 0 else NBUCK
        own = colidx_ref[:, kind : kind + 1]
        level = lax.broadcasted_iota(jnp.int32, (length, extent), 1)
        chosen = (own == level).astype(BF16)
        place = own - HALF + lax.broadcasted_iota(jnp.int32, (length, NBUCK), 1)
        turn = place & (NBUCK - 1)
        piece = place >> 7
        for h in range(heads):
            spread = mm(dscore_ref[h], chosen)
            window = jnp.zeros((length, NBUCK), F32)
            for q in range(extent // NBUCK):
                part = jnp.take_along_axis(
                    spread[:, q * NBUCK : (q + 1) * NBUCK],
                    turn,
                    axis=1,
                    mode="promise_in_bounds",
                )
                window = window + jnp.where(piece == q, part, 0.0)
            row = jnp.sum(window, axis=0, keepdims=True)
            row = jnp.where((lane > 0) & (lane < NBUCK - 1), row, 0.0)
            least = jnp.sum(jnp.where(level <= own - HALF, spread, 0.0), axis=0, keepdims=True)
            most = jnp.sum(jnp.where(level >= own + HALF - 1, spread, 0.0), axis=0, keepdims=True)
            row = row + jnp.where(lane == 0, jnp.sum(least, axis=1, keepdims=True), 0.0)
            row = row + jnp.where(
                lane == NBUCK - 1, jnp.sum(most, axis=1, keepdims=True), 0.0
            )
            found.append(row)
    per = width // NBUCK
    found = found + [jnp.zeros((1, NBUCK), F32)] * (-len(found) % per)
    lines = [
        jnp.concatenate(found[at : at + per], axis=1) for at in range(0, len(found), per)
    ]
    lines.append(bup_ref[0:1, :])
    lines_ref[...] = jnp.concatenate(
        lines + [jnp.zeros((16 - len(lines), width), F32)], axis=0
    )


def ends_kernel(
    p_ref,
    w_ref,
    y_ref,
    zhw_ref,
    zlw_ref,
    zzw_ref,
    tok_ref,
    sp_ref,
    event_ref,
):
    c, y, block = p_ref[0], p_ref[2], p_ref[4] * 2 + p_ref[3]
    for turn, ref in enumerate((None, zlw_ref, zhw_ref, zzw_ref)):
        at = block ^ turn
        for far in range(2):
            for unit in range(3):
                if ref is None:
                    value = (y_ref if far else w_ref)[unit]
                else:
                    value = ref[far, unit]
                value = value.astype(F32)
                if unit < 2:
                    tok_ref[c ^ unit, y ^ far, at] = value
                else:
                    sp_ref[y ^ far, at] = value
    event_ref[...] = jnp.zeros_like(event_ref)


def out_kernel(p_ref, *refs):
    c, y, block = p_ref[0], p_ref[2], p_ref[4] * 2 + p_ref[3]
    out_ref, event_ref = refs[8:]
    least = out_ref.shape[3]
    for half in range(2):
        for far in range(2):
            for unit in range(2):
                ref = refs[half * 4 + far * 2 + unit]
                for turn in range(2):
                    at = block ^ (half * 2 + turn)
                    out_ref[c ^ unit, y ^ far, at] = ref[turn * least : (turn + 1) * least, :]
    event_ref[...] = jnp.zeros_like(event_ref)


def turn_kernel(p_ref, own_ref, far_ref, sum_ref, *, size):
    far = turned(far_ref[...], size).astype(F32)
    sum_ref[...] = (own_ref[...].astype(F32) + far).astype(BF16)


def plus_kernel(p_ref, *refs):
    count = len(refs) // 3
    for n in range(count):
        total = refs[2 * n][...].astype(F32) + refs[2 * n + 1][...].astype(F32)
        refs[2 * count + n][...] = total.astype(BF16)


def units_kernel(
    p_ref, own0_ref, own1_ref, other_ref, near_ref, far_ref, spat_ref, nears_ref, fars_ref
):
    nears_ref[0] = own0_ref[...]
    fars_ref[0] = own1_ref[...]
    nears_ref[1] = other_ref[0]
    fars_ref[1] = other_ref[1]
    nears_ref[2] = (near_ref[...].astype(F32) + spat_ref[0].astype(F32)).astype(BF16)
    fars_ref[2] = (far_ref[...].astype(F32) + spat_ref[1].astype(F32)).astype(BF16)


def fold_kernel(p_ref, own_ref, far_ref, keep_ref, send_ref):
    total = (own_ref[...].astype(F32) + far_ref[...].astype(F32)).astype(BF16)
    half = total.shape[-2] // 2
    keep_ref[...] = total[..., :half, :]
    send_ref[...] = total[..., half:, :]


def ends_first_kernel(p_ref, keep_ref, far_ref, mine_ref, other_ref):
    least = mine_ref.shape[1]
    total = (keep_ref[...].astype(F32) + far_ref[...].astype(F32)).astype(BF16)
    mine_ref[...] = total[:, :least]
    other_ref[...] = total[:, least:]


def spread_kernel(p_ref, *refs):
    c = p_ref[0]
    event_ref = refs[10]
    for n, out_ref in enumerate(refs[8:10]):
        side = p_ref[1 + n]
        for other in range(2):
            for far in range(2):
                out_ref[c ^ other, side ^ far] = refs[n * 4 + other * 2 + far][...].astype(F32)
    event_ref[...] = jnp.zeros_like(event_ref)


def last_kernel(
    p_ref,
    one0_ref,
    one1_ref,
    one2_ref,
    one3_ref,
    two0_ref,
    two1_ref,
    two2_ref,
    two3_ref,
    qkv_ref,
    spat_ref,
    exit_ref,
    tables_ref,
    gains_ref,
    shifts_ref,
    bup_ref,
    bdown_ref,
    second_ref,
    *,
    heads,
):
    c, head = p_ref[0], p_ref[4] * 2 + p_ref[3]
    inner = exit_ref.shape[1]
    width = exit_ref.shape[2]
    part = gains_ref.shape[2]
    per = width // NBUCK
    firsts = ((one0_ref, one1_ref), (one2_ref, one3_ref))
    seconds = ((two0_ref, two1_ref), (two2_ref, two3_ref))
    for other in range(2):
        s = c ^ other
        for far in range(2):
            size = one0_ref.shape[0]
            at = pl.multiple_of((p_ref[1] ^ far) * size, 16)
            qkv_ref[s, pl.ds(at, size), :] = firsts[other][far][...].astype(F32)
            size = two0_ref.shape[0]
            at = pl.multiple_of((p_ref[2] ^ far) * size, 16)
            second_ref[pl.ds(at, size), :] = seconds[other][far][...].astype(F32)
        base = 3 * inner - 2 * one0_ref.shape[0]
        qkv_ref[s, 2 * one0_ref.shape[0] :, :] = second_ref[0:base, :]
        exit_ref[s] = second_ref[base : base + inner, :]
        base += inner
        spat_ref[s] = second_ref[base : base + inner, :]
        base += inner
        sums = second_ref[base : base + 16, :]
        cut = sums[:, 0:part]
        for at in range(1, width // part):
            cut = jnp.where(head == at, sums[:, at * part : (at + 1) * part], cut)
        gains_ref[s] = jnp.concatenate([cut[0:1], cut[8:9]], axis=0)
        shifts_ref[s] = jnp.concatenate([cut[1:2], cut[9:10]], axis=0)
        bdown_ref[pl.ds(s, 1), :] = cut[10:11]
        lines = second_ref[base + 16 : base + 32, :]
        for n in range(3 * heads):
            at = (n % per) * NBUCK
            tables_ref[n // heads, n % heads, pl.ds(s, 1), :] = lines[
                n // per : n // per + 1, at : at + NBUCK
            ]
        bup_ref[pl.ds(s, 1), :] = lines[2:3]


def swap(value, axis, step=1):
    size = lax.axis_size(axis)
    return lax.ppermute(value, axis, [(i, i ^ step) for i in range(size)])


def swap_both(value):
    size = lax.axis_size("batch") * 2
    return lax.ppermute(value, ("batch", "y"), [(i, i ^ 3) for i in range(size)])


def added(left, right):
    return (left.astype(F32) + right.astype(F32)).astype(BF16)


def batch_steps():
    return [1 << bit for bit in range(lax.axis_size("batch").bit_length() - 1)]


def join(*values):
    return lax.optimization_barrier(values)


def shards(
    tokens,
    spatial,
    positions,
    boxes,
    query_key_value_weight,
    w_spatial,
    rel_tables,
    exit_matrix,
    ln_gains,
    ln_shifts,
    up_weight,
    hidden_bias,
    shrink_projection_array,
    b_down,
    cotangent,
):
    heads = rel_tables.shape[2]
    rows = tokens.shape[2]
    width = tokens.shape[3]
    inner = query_key_value_weight.shape[3]
    hidden = up_weight.shape[2]
    least = rows // 4
    rest = rows // 2
    length = 4 * rows
    half = length // 2
    page = lax.axis_index("y")
    core = lax.axis_index("core")
    zh = lax.axis_index("zh")
    zl = lax.axis_index("zl")
    pair = lax.axis_index("batch") & 1
    place = jnp.stack([core, pair, page, zl, zh]).astype(jnp.int32)

    def run(body, operands, outs, us=TICK, scratch=(), after=(), vmem=VMEM_BYTES):
        return kernel_call(body, place, operands, outs, us, scratch, after, vmem)

    def rows_of(count, dtype=BF16):
        return ((count, width), dtype)

    share = hidden // 4
    up_part, down_part = run(
        share_kernel,
        [
            (exit_matrix, "any"),
            (up_weight, "any"),
            (shrink_projection_array, "any"),
            (hidden_bias, "any"),
        ],
        [rows_of(share + 16 + inner // 4), rows_of(share)],
        scratch=[pltpu.VMEM(hidden_bias.shape, F32), pltpu.SemaphoreType.DMA((4,))],
        vmem=PACK_VMEM,
    )
    up_part = swap(up_part, "zh")
    far0, far1, far2, near, x00 = run(
        pack_kernel,
        [
            (tokens.reshape(2, 2, 4, least, width), "any"),
            (spatial.reshape(2, 4, least, width), "any"),
            (positions, "any"),
            (boxes, "any"),
        ],
        [
            rows_of(rows + 16),
            rows_of(rows),
            rows_of(rows),
            rows_of(2 * rows + 16),
            rows_of(rows),
        ],
        us=30,
        scratch=[
            pltpu.VMEM(positions.shape, jnp.int32),
            pltpu.VMEM(boxes.shape, jnp.int32),
            pltpu.SemaphoreType.DMA((26,)),
        ],
        vmem=PACK_VMEM,
        after=[down_part],
    )
    i10, s10, x10 = swap(far0, "y"), swap(far1, "y"), swap(far2, "y")
    cot_far, cot_near, cot00 = run(
        cotangent_kernel,
        [(cotangent.reshape(2, 2, 4, least, width), "any")],
        [((2, rows, width), BF16), rows_of(rows), rows_of(rows)],
        scratch=[pltpu.SemaphoreType.DMA((16,))],
        vmem=PACK_VMEM,
        after=[x00],
    )
    n01 = swap(near, "core")
    weights = (jnp.swapaxes(query_key_value_weight, 2, 3), "stream")
    spatial_weights = jnp.swapaxes(w_spatial, 1, 2)
    x0, sp0, index0, proj0, spat0, up, down, exit_own = run(
        near_kernel,
        [
            x00,
            n01,
            near,
            weights,
            spatial_weights,
            (up_weight, "any"),
            (shrink_projection_array, "any"),
            (exit_matrix, "any"),
        ],
        [
            ((2, rows, width), BF16),
            ((2, rows, width), BF16),
            ((8, 2 * rows), jnp.int32),
            ((3, 2 * rows, inner), BF16),
            ((2, 2 * rows, inner), BF16),
            ((width, hidden), BF16),
            ((hidden, width), BF16),
            rows_of(inner),
        ],
        scratch=[pltpu.SemaphoreType.DMA((3,))],
        after=[cot00],
    )
    i10, s10, x10, x0, up_part, down_part = join(i10, s10, x10, x0, up_part, down_part)
    x11, s11 = swap(i10, "core"), swap(s10, "core")
    ups = [up_part, swap(up_part, "y"), swap(up_part, "batch"), swap_both(up_part)]
    down_part = swap(down_part, "zh")

    x, sp, colidx, proj, spat, soft, att_own, att_send = run(
        functools.partial(attention_kernel, heads=heads),
        [
            x10,
            x11,
            s10,
            s11,
            i10,
            x0,
            sp0,
            index0,
            proj0,
            spat0,
            weights,
            spatial_weights,
            (rel_tables, "stream"),
        ],
        [
            ((2, 2, rows, width), BF16),
            ((2, 2, rows, width), BF16),
            ((length, 8), jnp.int32),
            ((3, length, inner), BF16, "any"),
            ((2, length, inner), BF16, "any"),
            ((heads, length, length), F32, "any"),
            ((half, inner), BF16),
            ((half, inner), BF16),
        ],
        us=30,
        scratch=[
            pltpu.VMEM((length, inner), BF16),
            pltpu.VMEM((3, length, inner), BF16),
            pltpu.VMEM((2, length, inner), BF16),
            pltpu.VMEM((heads, length, length), F32),
            pltpu.SemaphoreType.DMA((2 + heads,)),
        ],
    )
    att_recv = swap(att_send, "zh")
    att_own, down_part, *ups = join(att_own, down_part, *ups)
    downs = [down_part, swap(down_part, "y"), swap(down_part, "batch"), swap_both(down_part)]

    keep, send, exit_partner = run(
        mixed_kernel,
        [att_own, att_recv, exit_own, *ups],
        [rows_of(rows, F32), rows_of(rows), rows_of(inner)],
    )
    (mixed0,) = run(
        plus_kernel, [keep, swap(send, "core")], [rows_of(rows)], after=downs[1:3]
    )
    mixed_zl = swap(mixed0, "zl")
    (mixed0,) = run(
        functools.partial(turn_kernel, size=least), [mixed0, mixed_zl], [rows_of(rows)]
    )
    mixed1 = swap(mixed0, "core")
    mixed_far0 = swap(mixed0, "zh")
    mixed1, *downs = join(mixed1, *downs)

    gains = (ln_gains, "stream")
    shifts = (ln_shifts, "stream")
    x_own = (x, (None, 0, None, None))
    x_far = (x, (None, 1, None, None))
    low, normed, active, slope, up_partner, down_partner = run(
        forward_kernel,
        [x_own, mixed0, mixed1, gains, shifts, up, hidden_bias, down, *ups, *downs],
        [
            rows_of(half),
            rows_of(half),
            ((2, half, hidden), BF16),
            ((2, half, hidden), BF16),
            ((width, hidden), BF16),
            ((hidden, width), BF16),
        ],
    )
    low_recv = swap(low, "zl")
    cot_far, cot_near, low = join(cot_far, cot_near, low)
    cot10 = swap(cot_far, "y")
    cot01 = swap(cot_near, "core")
    mixed_far1 = swap(mixed_far0, "core")
    cot11 = swap(cot10, "core")
    (normed_far,) = run(
        first_norm_kernel,
        [x_far, mixed_far0, mixed_far1, gains, shifts],
        [rows_of(half)],
        after=[low],
    )
    active_far, slope_far = run(
        other_kernel,
        [normed_far, up, hidden_bias],
        [((half, hidden), BF16), ((half, hidden), BF16)],
    )
    low0, low1 = run(
        lowered_kernel, [low, low_recv], [rows_of(rows), rows_of(rows)], after=[slope_far]
    )
    far_low0 = swap(low0, "zh")

    def finish(x_half, pieces, part, after=()):
        rows_part = slice(part * rest, (part + 1) * rest)
        cots = [
            cot00[rows_part],
            cot10[0, rows_part],
            cot01[rows_part],
            cot11[1, rows_part],
        ]
        return run(
            final_kernel,
            [x_half, *pieces, *cots, gains, shifts, b_down],
            [
                ((2, rest, width), BF16),
                ((2, rest, width), BF16),
                rows_of(half, F32),
                rows_of(half),
                rows_of(8, F32),
            ],
            after=after,
        )

    out_keep, out_send, second, dlow, sums_two = finish(x_own, [mixed0, mixed1, low0, low1], 0)
    hid, dup = run(
        middle_kernel,
        [dlow, up, down, up_partner, down_partner, slope],
        [rows_of(half), ((half, hidden), BF16)],
    )
    hid_recv = swap(hid, "zl")
    out_core = swap(out_send, "core")
    out_y = swap(jnp.stack([out_keep[1], out_core[1]]), "y")
    hid_recv, far_low0, out_y = join(hid_recv, far_low0, out_y)
    far_low1 = swap(far_low0, "zl")
    first, dmix, sums_one = run(
        first_kernel,
        [x_own, mixed0, mixed1, second, hid, hid_recv, gains],
        [rows_of(half, F32), rows_of(half), rows_of(8, F32)],
    )
    dmix_core = swap(dmix, "core")
    datt, datt_send, dmix, pay = run(
        attended_kernel,
        [dmix, dmix_core, exit_own, exit_partner, sums_one, sums_two],
        [
            ((half, inner), BF16),
            ((half, inner), BF16),
            rows_of(half),
            rows_of(rest + 16),
        ],
    )
    datt_recv = swap(datt_send, "zh")
    far_keep, far_send, _, dlow_far, _ = finish(
        x_far, [mixed_far0, mixed_far1, far_low0, far_low1], 1, [datt]
    )
    up_keep, up_send, down_keep, down_send, bias_grad = run(
        ffn_grad_kernel,
        [
            normed,
            normed_far,
            (active, (0, None, None)),
            active_far,
            dlow,
            dlow_far,
            dup,
            slope_far,
            down,
        ],
        [
            ((width // 2, hidden), BF16),
            ((width // 2, hidden), BF16),
            rows_of(hidden // 2),
            rows_of(hidden // 2),
            ((8, hidden), F32),
        ],
        us=30,
        scratch=[pltpu.VMEM((width, hidden), BF16)],
        after=[datt],
    )
    up_recv = swap(up_send, "batch")
    down_recv = swap(down_send, "y")
    datt_recv, pay = join(datt_recv, pay)
    pay_recv = swap(pay, "zh")
    piece = rows_of(rows)
    dscore, dproj, dspat, dxk0, dxk1, dxs, dsk0, dsk1, dss = run(
        functools.partial(backward_kernel, heads=heads, block=128),
        [datt, datt_recv, first, (soft, "any"), proj, spat, weights, spatial_weights],
        [
            ((heads, length, length), BF16),
            ((3, length, inner), BF16),
            ((2, length, inner), BF16),
            piece,
            piece,
            ((2, rows, width), BF16),
            piece,
            piece,
            ((2, rows, width), BF16),
        ],
        us=30,
        scratch=[pltpu.VMEM((heads, length, length), F32), pltpu.SemaphoreType.DMA((heads,))],
        after=[bias_grad],
    )

    steps = batch_steps()[1:]

    def plus(pairs, after=(), over_batch=False):
        sums = run(
            plus_kernel,
            [array for pair_of in pairs for array in pair_of],
            [(left.shape, BF16) for left, _ in pairs],
            after=after,
        )
        if over_batch:
            for step in steps:
                sums = [added(value, swap(value, "batch", step)) for value in sums]
        return sums

    dxk1, dxs, dss, pay_recv = join(dxk1, dxs, dss, pay_recv)
    dxs, dss = swap(dxs, "core"), swap(dss, "core")
    near, far = run(
        units_kernel,
        [dxk0, dxk1, dxs, dsk0, dsk1, dss],
        [((3, rows, width), BF16), ((3, rows, width), BF16)],
    )
    far_zl = swap(far, "zl")
    up_half, down_half = plus([(up_keep, up_recv), (down_keep, down_recv)], after=[far])
    up_other = swap(up_half, "y")
    down_other = swap(down_half, "batch")
    pay_zl = swap(join(pay_recv, far)[0], "zl")
    few = inner // 2
    main = 3 * inner - few
    sp_keep, sp_send = run(
        spatial_grad_kernel, [sp, dspat], [rows_of(inner), rows_of(inner)], after=[up_half]
    )
    sp_recv = swap(sp_send, "core")
    one_keep, one_send, value_rest, lines = run(
        functools.partial(first_grad_kernel, heads=heads),
        [x, dscore, dproj, colidx, bias_grad],
        [rows_of(main // 2), rows_of(main // 2), rows_of(few), rows_of(16, F32)],
        scratch=[pltpu.VMEM((3 * inner, width), BF16)],
        after=[sp_keep],
    )
    keep, send = run(
        fold_kernel,
        [near, far_zl],
        [((3, rest, width), BF16), ((3, rest, width), BF16)],
        after=[lines],
    )
    send_zh = swap(send, "zh")
    up_half, down_half = plus(
        [(up_half, up_other), (down_half, down_other)], after=[send], over_batch=True
    )
    up_far = swap(up_half, "batch")
    down_far = swap(down_half, "y")
    mine, other = run(
        ends_first_kernel,
        [keep, send_zh],
        [((3, least, width), BF16), ((3, least, width), BF16)],
        after=[up_half],
    )
    got = swap(other, "y")
    pay_recv, pay_zl, far_send, mine = join(pay_recv, pay_zl, far_send, mine)
    pay_core, pay_zlcore = swap(pay_recv, "core"), swap(pay_zl, "core")
    far_core = swap(far_send, "core")
    base = few + 2 * inner + 32
    two_keep, two_send = run(
        second_grad_kernel,
        [
            dmix,
            pay,
            pay_recv,
            pay_zl,
            pay_core,
            pay_zlcore,
            att_own,
            att_send,
            value_rest,
            sp_keep,
            sp_recv,
            lines,
        ],
        [rows_of(base // 2), rows_of(base // 2)],
        scratch=[pltpu.VMEM((base, width), BF16)],
        after=[mine, up_far, down_far],
    )
    one_send, two_send, got, two_keep = join(one_send, two_send, got, two_keep)
    one_recv = swap(one_send, "batch")
    two_recv = swap(two_send, "y")
    pages = jnp.stack([mine, got])
    pages_zh = swap(pages, "zh")
    pages_zl = swap(pages, "zl")
    one_half, two_half = plus([(one_keep, one_recv), (two_keep, two_recv)], after=[pages])
    one_other = swap(one_half, "y")
    two_other = swap(two_half, "batch")
    far_y = swap(jnp.stack([far_keep[1], far_core[1]]), "y")
    halves = [up_half, up_far, down_half, down_far]
    others = [swap(value, "core") for value in halves]
    grad_up, grad_down, spread_event = run(
        spread_kernel,
        halves[:2] + others[:2] + halves[2:] + others[2:],
        [
            ((2, 2, width // 2, hidden), F32),
            ((2, 2, hidden // 2, width), F32),
            ((8, NBUCK), F32),
        ],
        after=[one_half],
    )
    pages_zz = swap(pages_zh, "zl")
    one_half, two_half = plus(
        [(one_half, one_other), (two_half, two_other)],
        after=[spread_event, pages_zz],
        over_batch=True,
    )
    one_far = swap(one_half, "batch")
    two_far = swap(two_half, "y")
    grad_tokens, grad_spatial, ends_event = run(
        ends_kernel,
        [mine, got, pages_zh, pages_zl, pages_zz],
        [((2, 2, 4, least, width), F32), ((2, 4, least, width), F32), ((8, NBUCK), F32)],
        after=[one_half],
    )
    output, out_event = run(
        out_kernel,
        [
            out_keep[0],
            out_core[0],
            out_y[0],
            out_y[1],
            far_keep[0],
            far_core[0],
            far_y[0],
            far_y[1],
        ],
        [((2, 2, 4, least, width), BF16), ((8, NBUCK), F32)],
        after=[one_half],
    )
    one_far, two_far, out_event, ends_event = join(one_far, two_far, out_event, ends_event)
    halves = [one_half, one_far, two_half, two_far]
    others = [swap(value, "core") for value in halves]
    part = width // (2 * lax.axis_size("zh"))
    grad_qkv, grad_spatial_w, grad_exit, tables, gains_grad, shifts_grad, grad_b_up, grad_b_down = run(
        functools.partial(last_kernel, heads=heads),
        halves[:2] + others[:2] + halves[2:] + others[2:],
        [
            ((2, 3 * inner, width), F32),
            ((2, inner, width), F32),
            ((2, inner, width), F32),
            ((3, heads, 2, NBUCK), F32),
            ((2, 2, part), F32),
            ((2, 2, part), F32),
            ((2, hidden), F32),
            ((2, part), F32),
        ],
        scratch=[pltpu.VMEM((base, width), F32)],
        after=[spread_event, out_event, ends_event],
    )
    return (
        output.reshape(tokens.shape),
        grad_tokens.reshape(tokens.shape),
        grad_spatial.reshape(spatial.shape),
        grad_qkv.reshape(2, 3, inner, width).swapaxes(2, 3),
        grad_spatial_w.reshape(2, inner, width).swapaxes(1, 2),
        tables.transpose(2, 0, 1, 3),
        grad_exit,
        gains_grad,
        shifts_grad,
        grad_up.reshape(2, width, hidden),
        grad_b_up,
        grad_down.reshape(2, hidden, width),
        grad_b_down,
    )


def solution(mesh):
    batch, seq, head = mesh.devices.shape
    fine = Mesh(
        mesh.devices.reshape(batch, seq // 2, 2, head // 2, 2),
        ("batch", "y", "core", "zh", "zl"),
    )
    seq = ("y", "core")
    head = ("zh", "zl")
    return jax.shard_map(
        shards,
        mesh=fine,
        in_specs=(
            P(None, "batch", seq, None),
            P("batch", seq, None),
            P("batch", seq),
            P(None, "batch", seq),
            P(None, None, None, head),
            P(None, None, head),
            P(None, None, head, None),
            P(None, head, None),
            P(),
            P(),
            P(None, None, head),
            P(None, head),
            P(None, head, None),
            P(),
            P(None, "batch", seq, None),
        ),
        out_specs=(
            P(None, "batch", seq, None),
            P(None, "batch", seq, None),
            P("batch", seq, None),
            P(None, None, None, head),
            P(None, None, head),
            P(None, None, head, None),
            P(None, head, None),
            P(None, None, head),
            P(None, None, head),
            P(None, None, head),
            P(None, head),
            P(None, head, None),
            P(None, head),
        ),
        check_vma=False,
    )
```

```python
import functools

import jax
import jax.numpy as jnp
from jax import lax
from jax.experimental import pallas as pl
from jax.experimental.pallas import tpu as pltpu
from jax.sharding import Mesh, PartitionSpec as P

DH = 64
NBUCK = 128
HALF = 64
EPSILON = 1e-05
F32 = jnp.float32
BF16 = jnp.bfloat16
VMEM_BYTES = 20 * 1024 * 1024
TICK = 0.1
PACK_VMEM = 60 * 1024 * 1024
NN = (((1,), (0,)), ((), ()))
NT = (((1,), (1,)), ((), ()))
TN = (((0,), (0,)), ((), ()))


def mm(left, right, dims=NN):
    return lax.dot_general(left, right, dims, preferred_element_type=F32)


def kernel_call(body, place, operands, outs, us, scratch=(), after=(), vmem=VMEM_BYTES):
    specs, arrays, hows = [], [], []
    for operand in operands:
        array, how = operand if isinstance(operand, tuple) else (operand, None)
        specs.append(pl.BlockSpec(memory_space=pltpu.HBM if how == "any" else pltpu.VMEM))
        arrays.append(array)
        hows.append(how)
    count = len(arrays)
    specs += [pl.BlockSpec(memory_space=pl.ANY)] * len(after)

    def view(s_ref, ref, how):
        if how == "stream":
            return ref.at[s_ref[0]]
        if how is None or how == "any":
            return ref
        return ref.at[tuple(slice(None) if at is None else at for at in how)]

    def kernel(s_ref, *refs):
        given = [view(s_ref, ref, how) for ref, how in zip(refs, hows)]
        body(s_ref, *given, *refs[count + len(after) :])

    return pl.pallas_call(
        kernel,
        out_shape=[jax.ShapeDtypeStruct(out[0], out[1]) for out in outs],
        in_specs=[pl.BlockSpec(memory_space=pltpu.SMEM)] + specs,
        out_specs=[
            pl.BlockSpec(memory_space=pltpu.HBM if len(out) > 2 else pltpu.VMEM) for out in outs
        ],
        scratch_shapes=list(scratch),
        compiler_params=pltpu.CompilerParams(vmem_limit_bytes=vmem),
        cost_estimate=pl.CostEstimate(
            flops=int(us * 1.1e9), bytes_accessed=int(us * 3.5e6), transcendentals=0
        ),
    )(place, *arrays, *after)


def centred(rows):
    centre = rows - jnp.mean(rows, axis=-1, keepdims=True)
    spread = lax.rsqrt(jnp.mean(centre * centre, axis=-1, keepdims=True) + EPSILON)
    return centre * spread, spread


def norm_back(unit, spread, tilted):
    return spread * (
        tilted
        - jnp.mean(tilted, axis=-1, keepdims=True)
        - unit * jnp.mean(tilted * unit, axis=-1, keepdims=True)
    )


def pick(table_row, index):
    width = index.shape[1]
    table = jnp.broadcast_to(table_row, (index.shape[0], NBUCK))
    parts = [
        jnp.take_along_axis(
            table,
            index[:, at : at + NBUCK],
            axis=1,
            mode="promise_in_bounds",
        )
        for at in range(0, width, NBUCK)
    ]
    return jnp.concatenate(parts, axis=1)


def stack_rows(pieces):
    return jnp.concatenate(pieces, axis=0)


def turned(rows, size):
    pieces = [rows[at : at + size] for at in range(0, rows.shape[0], size)]
    return stack_rows([pieces[i ^ 1] for i in range(len(pieces))])


def residual(x_ref, mixed_refs):
    rest = mixed_refs[0].shape[0] // 2
    pieces = []
    for y in range(2):
        for c in range(2):
            own = x_ref[y, c * rest : (c + 1) * rest, :].astype(F32)
            pieces.append(own + mixed_refs[c][y * rest : (y + 1) * rest, :].astype(F32))
    return stack_rows(pieces)


def dealt(rows_ref, side, keep_ref, send_ref):
    half = keep_ref.shape[0]
    keep_ref[...] = rows_ref[pl.ds(pl.multiple_of(side * half, 16), half), :]
    send_ref[...] = rows_ref[pl.ds(pl.multiple_of((1 - side) * half, 16), half), :]


def gathered(place_ref, refs, rows, to_ref):
    size = rows.stop - rows.start
    for turn, ref in enumerate(refs):
        q = (place_ref[1] ^ (turn // 2)) * 2 + (place_ref[2] ^ (turn % 2))
        to_ref[pl.ds(pl.multiple_of(q * size, 16), size), :] = ref[rows, :]


def copied(pairs, sems):
    started = [
        pltpu.make_async_copy(source, target, sems.at[n])
        for n, (source, target) in enumerate(pairs)
    ]
    for copy in started:
        copy.start()
    return started


def pack_kernel(
    p_ref,
    tok_ref,
    sp_ref,
    pos_ref,
    box_ref,
    exit_ref,
    up_ref,
    down_ref,
    bias_ref,
    far0_ref,
    far1_ref,
    far2_ref,
    near_ref,
    own_ref,
    ups_ref,
    downs_ref,
    posv_ref,
    boxv_ref,
    biasv_ref,
    sems,
):
    c, y, zl, zh = p_ref[0], p_ref[2], p_ref[3], p_ref[4]
    block = zh * 2 + zl
    least = tok_ref.shape[3]
    rows = 4 * least
    q = p_ref[1] * 2 + y
    many = down_ref.shape[1] // 4
    few = exit_ref.shape[1] // 4
    pairs = [
        (pos_ref, posv_ref),
        (box_ref, boxv_ref),
        (bias_ref, biasv_ref),
        (up_ref.at[c, pl.ds(pl.multiple_of(q * many, 16), many)], ups_ref.at[pl.ds(0, many)]),
        (
            exit_ref.at[c, pl.ds(pl.multiple_of(q * few, 16), few)],
            ups_ref.at[pl.ds(many + 16, few)],
        ),
        (down_ref.at[c, pl.ds(pl.multiple_of(q * many, 16), many)], downs_ref),
    ]
    for k in range(4):
        at = block ^ k
        to = pl.ds(k * least, least)
        pairs += [
            (tok_ref.at[1 - c, 1 - y, at], far0_ref.at[to]),
            (sp_ref.at[1 - y, at], far1_ref.at[to]),
            (tok_ref.at[c, 1 - y, at], far2_ref.at[to]),
            (tok_ref.at[1 - c, y, at], near_ref.at[to]),
            (sp_ref.at[y, at], near_ref.at[pl.ds(rows + k * least, least)]),
            (tok_ref.at[c, y, at], own_ref.at[to]),
        ]
    started = copied(pairs, sems)
    for copy in started[:3]:
        copy.wait()
    left = biasv_ref[pl.ds(c, 1), :]
    lines = []
    for _ in range(3):
        lines.append(left.astype(BF16).astype(F32))
        left = left - lines[-1]
    lines.append(jnp.zeros((13, left.shape[1]), F32))
    ups_ref[many : many + 16, :] = jnp.concatenate(lines, axis=0).astype(BF16)
    lane = lax.broadcasted_iota(jnp.int32, (8, NBUCK), 1)
    width = far0_ref.shape[1]
    for page, ref, at in ((1 - y, far0_ref, rows), (y, near_ref, 2 * rows)):
        place = posv_ref[pl.ds(page, 1), :]
        lines = [
            place & 255,
            place >> 8,
            boxv_ref[0, pl.ds(page, 1), :],
            boxv_ref[1, pl.ds(page, 1), :],
        ]
        value = jnp.concatenate(lines + [jnp.zeros((4, NBUCK), jnp.int32)], axis=0)
        crossed = jnp.where(
            (lane & 63) < 32, pltpu.roll(value, NBUCK - 32, 1), pltpu.roll(value, 32, 1)
        )
        value = jnp.where(zl == 0, value, crossed)
        value = jnp.where(zh == 0, value, pltpu.roll(value, 64, 1))
        value = jnp.concatenate([value.astype(F32), jnp.zeros((8, NBUCK), F32)], axis=0)
        ref[at : at + 16, 0:NBUCK] = value.astype(BF16)
        ref[at : at + 16, NBUCK:] = jnp.zeros((16, width - NBUCK), BF16)
    for copy in started[3:]:
        copy.wait()


def cotangent_kernel(p_ref, cot_ref, far_ref, near_ref, own_ref, sems):
    c, y, block = p_ref[0], p_ref[2], p_ref[4] * 2 + p_ref[3]
    least = cot_ref.shape[3]
    pairs = []
    for k in range(4):
        at = block ^ k
        to = pl.ds(k * least, least)
        pairs += [
            (cot_ref.at[c, 1 - y, at], far_ref.at[0, to]),
            (cot_ref.at[1 - c, 1 - y, at], far_ref.at[1, to]),
            (cot_ref.at[1 - c, y, at], near_ref.at[to]),
            (cot_ref.at[c, y, at], own_ref.at[to]),
        ]
    for copy in copied(pairs, sems):
        copy.wait()


def indices(ref, at):
    lines = ref[at : at + 16, 0:NBUCK].astype(F32).astype(jnp.int32)
    place = lines[0:1] + lines[1:2] * 256
    return jnp.concatenate([place, lines[2:4], jnp.zeros((5, NBUCK), jnp.int32)], axis=0)


def two_cores(index0, index1, half):
    lane = lax.broadcasted_iota(jnp.int32, (8, NBUCK), 1)
    if half == 0:
        return jnp.where(lane < 64, index0, pltpu.roll(index1, 64, 1))
    return jnp.where(lane < 64, pltpu.roll(index0, 64, 1), index1)


def arrange(x0_ref, x1_ref, s0_ref, s1_ref, i0_ref, i1_ref, at, x_ref, sp_ref):
    least = x_ref.shape[1]
    rest = least // 2
    found = []
    index0, index1 = indices(i0_ref, at), indices(i1_ref, at)
    for half in range(2):
        at = half * rest
        x_ref[half, 0:rest, :] = x0_ref[at : at + rest, :]
        x_ref[half, rest:, :] = x1_ref[at : at + rest, :]
        sp_ref[half, 0:rest, :] = s0_ref[at : at + rest, :]
        sp_ref[half, rest:, :] = s1_ref[at : at + rest, :]
        found.append(two_cores(index0, index1, half))
    return found


def project(x_ref, sp_ref, w_ref, ws_ref, proj_ref, spat_ref, at):
    width = x_ref.shape[-1]
    x = x_ref[...].reshape(-1, width)
    sp = sp_ref[...].reshape(-1, width)
    rows = slice(at, at + x.shape[0])
    for k in range(3):
        proj_ref[k, rows, :] = mm(x, w_ref[k], NT).astype(BF16)
    for k in range(2):
        spat_ref[k, rows, :] = mm(sp, ws_ref[k], NT).astype(BF16)


def near_kernel(
    p_ref,
    x00_ref,
    n01_ref,
    n00_ref,
    w_ref,
    ws_ref,
    up_hbm,
    down_hbm,
    exit_hbm,
    x_ref,
    sp_ref,
    index_ref,
    proj_ref,
    spat_ref,
    up_ref,
    down_ref,
    exit_ref,
    sems,
):
    fetched = [
        pltpu.make_async_copy(source.at[p_ref[0]], target, sems.at[n])
        for n, (source, target) in enumerate(
            ((exit_hbm, exit_ref), (up_hbm, up_ref), (down_hbm, down_ref))
        )
    ]
    for copy in fetched:
        copy.start()
    least = x_ref.shape[1]
    found = arrange(
        x00_ref,
        n01_ref,
        n00_ref.at[least:],
        n01_ref.at[least:],
        n00_ref,
        n01_ref,
        2 * least,
        x_ref,
        sp_ref,
    )
    index_ref[...] = jnp.concatenate(found, axis=1)
    project(x_ref, sp_ref, w_ref, ws_ref, proj_ref, spat_ref, 0)
    for copy in fetched:
        copy.wait()


def attention_kernel(
    p_ref,
    x10_ref,
    x11_ref,
    s10_ref,
    s11_ref,
    i10_ref,
    x0_ref,
    sp0_ref,
    index_ref,
    proj0_ref,
    spat0_ref,
    w_ref,
    ws_ref,
    table_ref,
    x_ref,
    sp_ref,
    colidx_ref,
    proj_hbm,
    spat_hbm,
    soft_hbm,
    own_ref,
    send_ref,
    att_ref,
    proj_ref,
    spat_ref,
    soft_ref,
    sems,
    *,
    heads,
):
    least = x_ref.shape[2]
    near = 2 * least
    x_ref[0] = x0_ref[...]
    sp_ref[0] = sp0_ref[...]
    proj_ref[:, 0:near, :] = proj0_ref[...]
    spat_ref[:, 0:near, :] = spat0_ref[...]
    found = arrange(
        x10_ref, x11_ref, s10_ref, s11_ref, i10_ref, x11_ref, least, x_ref.at[1], sp_ref.at[1]
    )
    places = jnp.concatenate([index_ref[...]] + found, axis=1)
    colidx_ref[...] = jnp.transpose(places.astype(F32)).astype(jnp.int32)
    project(x_ref.at[1], sp_ref.at[1], w_ref, ws_ref, proj_ref, spat_ref, near)
    length = 2 * near
    stored = [
        pltpu.make_async_copy(proj_ref, proj_hbm, sems.at[0]),
        pltpu.make_async_copy(spat_ref, spat_hbm, sems.at[1]),
    ]
    for copy in stored:
        copy.start()
    level = lax.broadcasted_iota(jnp.int32, (length, NBUCK), 1)
    chosen = [(colidx_ref[:, kind : kind + 1] == level).astype(BF16) for kind in (1, 2)]
    chosen = jnp.concatenate(chosen, axis=1)

    lane = lax.broadcasted_iota(jnp.int32, (length, NBUCK), 1)
    boxes = [
        jnp.clip(lane - colidx_ref[:, kind : kind + 1], -HALF, HALF - 1) + HALF
        for kind in (1, 2)
    ]
    index = jnp.clip(places[0:1, :] - colidx_ref[:, 0:1], -HALF, HALF - 1) + HALF
    for h in range(heads):
        cols = slice(h * DH, (h + 1) * DH)
        bias = jnp.concatenate(
            [pick(table_ref[k, h : h + 1, :], boxes[k - 1]) for k in (1, 2)], axis=1
        )
        coarse = bias.astype(BF16)
        fine = (bias - coarse.astype(F32)).astype(BF16)
        left = jnp.concatenate(
            [proj_ref[0, :, cols], spat_ref[0, :, cols]], axis=1
        ) * jnp.asarray(DH**-0.5, BF16)
        right = jnp.concatenate([proj_ref[1, :, cols], spat_ref[1, :, cols]], axis=1)
        scores = mm(
            jnp.concatenate([left, coarse, fine], axis=1),
            jnp.concatenate([right, chosen, chosen], axis=1),
            NT,
        ) + pick(table_ref[0, h : h + 1, :], index)
        top = jnp.max(scores, axis=-1, keepdims=True)
        raised = jnp.exp(scores - top)
        soft = raised * (1.0 / jnp.sum(raised, axis=-1, keepdims=True))
        soft_ref[h] = soft
        stored.append(pltpu.make_async_copy(soft_ref.at[h], soft_hbm.at[h], sems.at[2 + h]))
        stored[-1].start()
        att_ref[:, cols] = mm(soft.astype(BF16), proj_ref[2, :, cols]).astype(BF16)
    for copy in stored:
        copy.wait()
    part = length // 4
    own_ref[0:part, :] = att_ref[0:part, :]
    own_ref[part:, :] = att_ref[2 * part : 3 * part, :]
    send_ref[0:part, :] = att_ref[part : 2 * part, :]
    send_ref[part:, :] = att_ref[3 * part :, :]


def mixed_kernel(
    p_ref,
    own_ref,
    recv_ref,
    exit_ref,
    one0_ref,
    one1_ref,
    one2_ref,
    one3_ref,
    keep_ref,
    send_ref,
    partner_ref,
):
    rows = slice(one0_ref.shape[0] - exit_ref.shape[0] // 4, one0_ref.shape[0])
    gathered(p_ref, (one0_ref, one1_ref, one2_ref, one3_ref), rows, partner_ref)
    total = mm(own_ref[...], exit_ref[...]) + mm(recv_ref[...], partner_ref[...])
    rest = total.shape[0] // 4
    for y in range(2):
        at = 2 * y * rest
        keep_ref[y * rest : (y + 1) * rest, :] = total[at : at + rest]
        send_ref[y * rest : (y + 1) * rest, :] = total[at + rest : at + 2 * rest].astype(BF16)


def gelu_parts(upper):
    phi = 0.5 * (1.0 + lax.erf(upper * (0.5**0.5)))
    slope = phi + upper * (jnp.exp(-0.5 * upper * upper) * (0.5 / jnp.pi) ** 0.5)
    return (upper * phi).astype(BF16), slope


def forward_kernel(
    p_ref,
    x_ref,
    mixed0_ref,
    mixed1_ref,
    gain_ref,
    shift_ref,
    up_ref,
    hidden_ref,
    down_ref,
    one0_ref,
    one1_ref,
    one2_ref,
    one3_ref,
    two0_ref,
    two1_ref,
    two2_ref,
    two3_ref,
    low_ref,
    normed_ref,
    active_ref,
    slope_ref,
    upp_ref,
    downp_ref,
):
    many = two0_ref.shape[0]
    gathered(p_ref, (one0_ref, one1_ref, one2_ref, one3_ref), slice(0, many), upp_ref)
    gathered(p_ref, (two0_ref, two1_ref, two2_ref, two3_ref), slice(0, many), downp_ref)
    extra = one0_ref[many : many + 16, :].astype(F32)
    partner_bias = extra[0:1] + extra[1:2] + extra[2:3]
    unit, _ = centred(residual(x_ref, (mixed0_ref, mixed1_ref)))
    normed_low = (unit * gain_ref[0:1, :] + shift_ref[0:1, :]).astype(BF16)
    normed_ref[...] = normed_low
    active, slope = gelu_parts(mm(normed_low, up_ref[...]) + hidden_ref[pl.ds(p_ref[0], 1), :])
    active_ref[0] = active
    slope_ref[0] = slope.astype(BF16)
    total = mm(active, down_ref[...])
    active, slope = gelu_parts(mm(normed_low, upp_ref[...]) + partner_bias)
    active_ref[1] = active
    slope_ref[1] = slope.astype(BF16)
    low_ref[...] = (total + mm(active, downp_ref[...])).astype(BF16)


def other_kernel(
    p_ref,
    normed_ref,
    up_ref,
    hidden_ref,
    active_ref,
    slope_ref,
):
    active, slope = gelu_parts(
        mm(normed_ref[...], up_ref[...]) + hidden_ref[pl.ds(p_ref[0], 1), :]
    )
    active_ref[...] = active
    slope_ref[...] = slope.astype(BF16)


def first_norm_kernel(p_ref, x_ref, mixed0_ref, mixed1_ref, gain_ref, shift_ref, normed_ref):
    unit, _ = centred(residual(x_ref, (mixed0_ref, mixed1_ref)))
    normed_ref[...] = (unit * gain_ref[0:1, :] + shift_ref[0:1, :]).astype(BF16)


def lowered_kernel(p_ref, own_ref, far_ref, low0_ref, low1_ref):
    least = own_ref.shape[0] // 8
    total = own_ref[...].astype(F32) + turned(far_ref[...], least).astype(F32)
    total = total.astype(BF16)
    for i in range(4):
        low0_ref[i * least : (i + 1) * least, :] = total[2 * i * least : (2 * i + 1) * least]
        low1_ref[i * least : (i + 1) * least, :] = total[(2 * i + 1) * least : (2 * i + 2) * least]


def final_kernel(
    p_ref,
    x_ref,
    mixed0_ref,
    mixed1_ref,
    low0_ref,
    low1_ref,
    cot00_ref,
    cot10_ref,
    cot01_ref,
    cot11_ref,
    gain_ref,
    shift_ref,
    bdown_ref,
    outk_ref,
    outs_ref,
    second_ref,
    dlow_ref,
    sums_ref,
):
    unit, _ = centred(residual(x_ref, (mixed0_ref, mixed1_ref)))
    normed = unit * gain_ref[0:1, :] + shift_ref[0:1, :]
    least = low0_ref.shape[0] // 4
    pieces = []
    for i in range(4):
        pieces.append(low0_ref[i * least : (i + 1) * least, :])
        pieces.append(low1_ref[i * least : (i + 1) * least, :])
    lowered = stack_rows(pieces).astype(F32)
    unit2, spread2 = centred(normed + lowered + bdown_ref[pl.ds(p_ref[0], 1), :])
    out = (unit2 * gain_ref[1:2, :] + shift_ref[1:2, :]).astype(BF16)
    for y in range(2):
        at = 4 * y * least
        outk_ref[y] = out[at : at + 2 * least]
        outs_ref[y] = out[at + 2 * least : at + 4 * least]
    cot = stack_rows([cot00_ref[...], cot01_ref[...], cot10_ref[...], cot11_ref[...]]).astype(F32)
    second = norm_back(unit2, spread2, cot * gain_ref[1:2, :])
    second_ref[...] = second
    dlow_ref[...] = second.astype(BF16)
    sums_ref[...] = jnp.zeros_like(sums_ref)
    sums_ref[0:1, :] = jnp.sum(cot * unit2, axis=0, keepdims=True)
    sums_ref[1:2, :] = jnp.sum(cot, axis=0, keepdims=True)
    sums_ref[2:3, :] = jnp.sum(second, axis=0, keepdims=True)


def middle_kernel(
    p_ref,
    dlow_ref,
    up_ref,
    down_ref,
    upp_ref,
    downp_ref,
    slope_ref,
    hid_ref,
    dup_ref,
):
    dlow = dlow_ref[...]
    dup = (mm(dlow, down_ref[...], NT) * slope_ref[0].astype(F32)).astype(BF16)
    dup_ref[...] = dup
    total = mm(dup, up_ref[...], NT)
    dup = (mm(dlow, downp_ref[...], NT) * slope_ref[1].astype(F32)).astype(BF16)
    hid_ref[...] = (total + mm(dup, upp_ref[...], NT)).astype(BF16)


def ffn_grad_kernel(
    p_ref,
    normed_ref,
    normedo_ref,
    active_ref,
    activeo_ref,
    dlow_ref,
    dlowo_ref,
    dup_ref,
    slopeo_ref,
    down_ref,
    upk_ref,
    ups_ref,
    downk_ref,
    downs_ref,
    bias_ref,
    all_ref,
):
    dlowo = dlowo_ref[...]
    dupo = (mm(dlowo, down_ref[...], NT) * slopeo_ref[...].astype(F32)).astype(BF16)
    dup = dup_ref[...]
    all_ref[...] = (mm(normed_ref[...], dup, TN) + mm(normedo_ref[...], dupo, TN)).astype(BF16)
    dealt(all_ref, p_ref[1], upk_ref, ups_ref)
    all_ref[...] = (
        mm(active_ref[...], dlow_ref[...], TN) + mm(activeo_ref[...], dlowo, TN)
    ).astype(BF16)
    dealt(all_ref, p_ref[2], downk_ref, downs_ref)
    bias = jnp.sum(dup.astype(F32), axis=0, keepdims=True)
    bias = bias + jnp.sum(dupo.astype(F32), axis=0, keepdims=True)
    bias_ref[...] = jnp.broadcast_to(bias, bias_ref.shape)


def first_kernel(
    p_ref,
    x_ref,
    mixed0_ref,
    mixed1_ref,
    second_ref,
    hid_ref,
    hidr_ref,
    gain_ref,
    first_ref,
    dmix_ref,
    sums_ref,
):
    unit, spread = centred(residual(x_ref, (mixed0_ref, mixed1_ref)))
    hid = hid_ref[...].astype(F32) + turned(hidr_ref[...], hid_ref.shape[0] // 8).astype(F32)
    dnormed = second_ref[...] + hid
    first = norm_back(unit, spread, dnormed * gain_ref[0:1, :])
    first_ref[...] = first
    dmix_ref[...] = first.astype(BF16)
    sums_ref[...] = jnp.zeros_like(sums_ref)
    sums_ref[0:1, :] = jnp.sum(dnormed * unit, axis=0, keepdims=True)
    sums_ref[1:2, :] = jnp.sum(dnormed, axis=0, keepdims=True)


def attended_kernel(
    p_ref,
    dmix_ref,
    dmixr_ref,
    exit_ref,
    exitp_ref,
    sums1_ref,
    sums2_ref,
    own_ref,
    send_ref,
    total_ref,
    pay_ref,
):
    length = dmix_ref.shape[0]
    rest = length // 4
    total = dmix_ref[...].astype(F32) + turned(dmixr_ref[...], rest).astype(F32)
    total = total.astype(BF16)
    total_ref[...] = total
    own_ref[...] = mm(total, exit_ref[...], NT).astype(BF16)
    send_ref[...] = mm(total, exitp_ref[...], NT).astype(BF16)
    least = rest // 2
    pay_ref[0:least, :] = total[0:least]
    pay_ref[least:rest, :] = total[2 * rest : 2 * rest + least]
    pay_ref[rest:, :] = jnp.concatenate([sums1_ref[...], sums2_ref[...]], axis=0).astype(BF16)


def backward_kernel(
    p_ref,
    datt_ref,
    dattr_ref,
    first_ref,
    soft_hbm,
    proj_ref,
    spat_ref,
    w_ref,
    ws_ref,
    dscore_ref,
    dproj_ref,
    dspat_ref,
    dxk0_ref,
    dxk1_ref,
    dxs_ref,
    dsk0_ref,
    dsk1_ref,
    dss_ref,
    soft_ref,
    sems,
    *,
    heads,
    block,
):
    fetched = [
        pltpu.make_async_copy(soft_hbm.at[h], soft_ref.at[h], sems.at[h]) for h in range(heads)
    ]
    for copy in fetched:
        copy.start()
    length = 2 * datt_ref.shape[0]
    scale = DH**-0.5
    part = length // 4
    datt = stack_rows(
        [datt_ref[0:part, :], dattr_ref[0:part, :], datt_ref[part:, :], dattr_ref[part:, :]]
    )
    for h in range(heads):
        cols = slice(h * DH, (h + 1) * DH)
        value = proj_ref[2, :, cols]
        left = jnp.concatenate([proj_ref[0, :, cols], spat_ref[0, :, cols]], axis=1)
        right = jnp.concatenate([proj_ref[1, :, cols], spat_ref[1, :, cols]], axis=1)
        own = datt[:, cols]
        fetched[h].wait()
        for at in range(0, length, block):
            soft = soft_ref[h, at : at + block, :]
            dsoft = mm(own[at : at + block], value, NT)
            inner = jnp.sum(soft * dsoft, axis=-1, keepdims=True)
            dscore_ref[h, at : at + block, :] = (soft * (dsoft - inner)).astype(BF16)
        dscore = dscore_ref[h]
        dleft = (mm(dscore, right) * scale).astype(BF16)
        dright = (mm(dscore, left, TN) * scale).astype(BF16)
        dproj_ref[0, :, cols] = dleft[:, :DH]
        dspat_ref[0, :, cols] = dleft[:, DH:]
        dproj_ref[1, :, cols] = dright[:, :DH]
        dspat_ref[1, :, cols] = dright[:, DH:]
        dproj_ref[2, :, cols] = mm(soft_ref[h].astype(BF16), own, TN).astype(BF16)
    once = (p_ref[3] == 0).astype(F32)
    total = mm(dproj_ref[0], w_ref[0])
    for k in range(1, 3):
        total = total + mm(dproj_ref[k], w_ref[k])
    least = part // 4

    def deal(rows, refs):
        for y in range(2):
            for zh in range(2):
                for c in range(2):
                    for zl in range(2):
                        at = (((y * 2 + zh) * 2 + c) * 2 + zl) * least
                        to = (zh * 2 + y) * least
                        value = rows[at : at + least]
                        if zh == 0 and refs[0][0] is dxk0_ref:
                            of = ((y * 2 + c) * 2 + zl) * least
                            value = value + once * first_ref[of : of + least, :]
                        refs[c][zl][to : to + least, :] = value.astype(BF16)

    deal(total, ((dxk0_ref, dxk1_ref), (dxs_ref.at[0], dxs_ref.at[1])))
    total = mm(dspat_ref[0], ws_ref[0]) + mm(dspat_ref[1], ws_ref[1])
    deal(total, ((dsk0_ref, dsk1_ref), (dss_ref.at[0], dss_ref.at[1])))


def spatial_grad_kernel(p_ref, sp_ref, dspat_ref, keep_ref, send_ref):
    sp = sp_ref[...].reshape(-1, sp_ref.shape[-1])
    keep_ref[...] = mm(dspat_ref[p_ref[0]], sp, TN).astype(BF16)
    send_ref[...] = mm(dspat_ref[1 - p_ref[0]], sp, TN).astype(BF16)


def second_grad_kernel(
    p_ref,
    dmix_ref,
    pay_ref,
    payr_ref,
    payl_ref,
    payc_ref,
    paylc_ref,
    atto_ref,
    atts_ref,
    rest_ref,
    spk_ref,
    spr_ref,
    lines_ref,
    keep_ref,
    send_ref,
    second_ref,
):
    inner = spk_ref.shape[0]
    length = dmix_ref.shape[0]
    least = length // 8
    rest = 2 * least
    dmixo = stack_rows(
        [
            ref[y * least : (y + 1) * least, :]
            for y in range(2)
            for ref in (payr_ref, payl_ref, payc_ref, paylc_ref)
        ]
    )
    base = rest_ref.shape[0]
    second_ref[0:base, :] = rest_ref[...]
    second_ref[base : base + inner, :] = (
        mm(atto_ref[...], dmix_ref[...], TN) + mm(atts_ref[...], dmixo, TN)
    ).astype(BF16)
    base += inner
    second_ref[base : base + inner, :] = (
        spk_ref[...].astype(F32) + spr_ref[...].astype(F32)
    ).astype(BF16)
    base += inner
    small = pay_ref[rest:, :].astype(F32) + payr_ref[rest:, :].astype(F32)
    second_ref[base : base + 16, :] = small.astype(BF16)
    second_ref[base + 16 : base + 32, :] = lines_ref[...].astype(BF16)
    dealt(second_ref, p_ref[2], keep_ref, send_ref)


def first_grad_kernel(
    p_ref,
    x_ref,
    dscore_ref,
    dproj_ref,
    colidx_ref,
    bup_ref,
    keep_ref,
    send_ref,
    rest_ref,
    lines_ref,
    first_ref,
    *,
    heads,
):
    width = x_ref.shape[-1]
    x = x_ref[...].reshape(-1, width)
    length = x.shape[0]
    inner = dproj_ref.shape[-1]
    for k in range(3):
        first_ref[k * inner : (k + 1) * inner, :] = mm(dproj_ref[k], x, TN).astype(BF16)
    dealt(first_ref, p_ref[1], keep_ref, send_ref)
    rest_ref[...] = first_ref[2 * keep_ref.shape[0] :, :]
    lane = lax.broadcasted_iota(jnp.int32, (1, NBUCK), 1)
    found = []
    for kind in range(3):
        extent = length if kind == 0 else NBUCK
        own = colidx_ref[:, kind : kind + 1]
        level = lax.broadcasted_iota(jnp.int32, (length, extent), 1)
        chosen = (own == level).astype(BF16)
        place = own - HALF + lax.broadcasted_iota(jnp.int32, (length, NBUCK), 1)
        turn = place & (NBUCK - 1)
        piece = place >> 7
        for h in range(heads):
            spread = mm(dscore_ref[h], chosen)
            window = jnp.zeros((length, NBUCK), F32)
            for q in range(extent // NBUCK):
                part = jnp.take_along_axis(
                    spread[:, q * NBUCK : (q + 1) * NBUCK],
                    turn,
                    axis=1,
                    mode="promise_in_bounds",
                )
                window = window + jnp.where(piece == q, part, 0.0)
            row = jnp.sum(window, axis=0, keepdims=True)
            row = jnp.where((lane > 0) & (lane < NBUCK - 1), row, 0.0)
            least = jnp.sum(jnp.where(level <= own - HALF, spread, 0.0), axis=0, keepdims=True)
            most = jnp.sum(jnp.where(level >= own + HALF - 1, spread, 0.0), axis=0, keepdims=True)
            row = row + jnp.where(lane == 0, jnp.sum(least, axis=1, keepdims=True), 0.0)
            row = row + jnp.where(
                lane == NBUCK - 1, jnp.sum(most, axis=1, keepdims=True), 0.0
            )
            found.append(row)
    per = width // NBUCK
    found = found + [jnp.zeros((1, NBUCK), F32)] * (-len(found) % per)
    lines = [
        jnp.concatenate(found[at : at + per], axis=1) for at in range(0, len(found), per)
    ]
    lines.append(bup_ref[0:1, :])
    lines_ref[...] = jnp.concatenate(
        lines + [jnp.zeros((16 - len(lines), width), F32)], axis=0
    )


def ends_kernel(
    p_ref,
    w_ref,
    y_ref,
    zhw_ref,
    zlw_ref,
    zzw_ref,
    tok_ref,
    sp_ref,
    event_ref,
):
    c, y, block = p_ref[0], p_ref[2], p_ref[4] * 2 + p_ref[3]
    for turn, ref in enumerate((None, zlw_ref, zhw_ref, zzw_ref)):
        at = block ^ turn
        for far in range(2):
            for unit in range(3):
                if ref is None:
                    value = (y_ref if far else w_ref)[unit]
                else:
                    value = ref[far, unit]
                value = value.astype(F32)
                if unit < 2:
                    tok_ref[c ^ unit, y ^ far, at] = value
                else:
                    sp_ref[y ^ far, at] = value
    event_ref[...] = jnp.zeros_like(event_ref)


def out_kernel(p_ref, *refs):
    c, y, block = p_ref[0], p_ref[2], p_ref[4] * 2 + p_ref[3]
    out_ref, event_ref = refs[8:]
    least = out_ref.shape[3]
    for half in range(2):
        for far in range(2):
            for unit in range(2):
                ref = refs[half * 4 + far * 2 + unit]
                for turn in range(2):
                    at = block ^ (half * 2 + turn)
                    out_ref[c ^ unit, y ^ far, at] = ref[turn * least : (turn + 1) * least, :]
    event_ref[...] = jnp.zeros_like(event_ref)


def turn_kernel(p_ref, own_ref, far_ref, sum_ref, *, size):
    far = turned(far_ref[...], size).astype(F32)
    sum_ref[...] = (own_ref[...].astype(F32) + far).astype(BF16)


def plus_kernel(p_ref, *refs):
    count = len(refs) // 3
    for n in range(count):
        total = refs[2 * n][...].astype(F32) + refs[2 * n + 1][...].astype(F32)
        refs[2 * count + n][...] = total.astype(BF16)


def units_kernel(
    p_ref, own0_ref, own1_ref, other_ref, near_ref, far_ref, spat_ref, nears_ref, fars_ref
):
    nears_ref[0] = own0_ref[...]
    fars_ref[0] = own1_ref[...]
    nears_ref[1] = other_ref[0]
    fars_ref[1] = other_ref[1]
    nears_ref[2] = (near_ref[...].astype(F32) + spat_ref[0].astype(F32)).astype(BF16)
    fars_ref[2] = (far_ref[...].astype(F32) + spat_ref[1].astype(F32)).astype(BF16)


def fold_kernel(p_ref, own_ref, far_ref, keep_ref, send_ref):
    total = (own_ref[...].astype(F32) + far_ref[...].astype(F32)).astype(BF16)
    half = total.shape[-2] // 2
    keep_ref[...] = total[..., :half, :]
    send_ref[...] = total[..., half:, :]


def ends_first_kernel(p_ref, keep_ref, far_ref, mine_ref, other_ref):
    least = mine_ref.shape[1]
    total = (keep_ref[...].astype(F32) + far_ref[...].astype(F32)).astype(BF16)
    mine_ref[...] = total[:, :least]
    other_ref[...] = total[:, least:]


def spread_kernel(p_ref, *refs):
    c = p_ref[0]
    event_ref = refs[10]
    for n, out_ref in enumerate(refs[8:10]):
        side = p_ref[1 + n]
        for other in range(2):
            for far in range(2):
                out_ref[c ^ other, side ^ far] = refs[n * 4 + other * 2 + far][...].astype(F32)
    event_ref[...] = jnp.zeros_like(event_ref)


def last_kernel(
    p_ref,
    one0_ref,
    one1_ref,
    one2_ref,
    one3_ref,
    two0_ref,
    two1_ref,
    two2_ref,
    two3_ref,
    qkv_ref,
    spat_ref,
    exit_ref,
    tables_ref,
    gains_ref,
    shifts_ref,
    bup_ref,
    bdown_ref,
    second_ref,
    *,
    heads,
):
    c, head = p_ref[0], p_ref[4] * 2 + p_ref[3]
    inner = exit_ref.shape[1]
    width = exit_ref.shape[2]
    part = gains_ref.shape[2]
    per = width // NBUCK
    firsts = ((one0_ref, one1_ref), (one2_ref, one3_ref))
    seconds = ((two0_ref, two1_ref), (two2_ref, two3_ref))
    for other in range(2):
        s = c ^ other
        for far in range(2):
            size = one0_ref.shape[0]
            at = pl.multiple_of((p_ref[1] ^ far) * size, 16)
            qkv_ref[s, pl.ds(at, size), :] = firsts[other][far][...].astype(F32)
            size = two0_ref.shape[0]
            at = pl.multiple_of((p_ref[2] ^ far) * size, 16)
            second_ref[pl.ds(at, size), :] = seconds[other][far][...].astype(F32)
        base = 3 * inner - 2 * one0_ref.shape[0]
        qkv_ref[s, 2 * one0_ref.shape[0] :, :] = second_ref[0:base, :]
        exit_ref[s] = second_ref[base : base + inner, :]
        base += inner
        spat_ref[s] = second_ref[base : base + inner, :]
        base += inner
        sums = second_ref[base : base + 16, :]
        cut = sums[:, 0:part]
        for at in range(1, width // part):
            cut = jnp.where(head == at, sums[:, at * part : (at + 1) * part], cut)
        gains_ref[s] = jnp.concatenate([cut[0:1], cut[8:9]], axis=0)
        shifts_ref[s] = jnp.concatenate([cut[1:2], cut[9:10]], axis=0)
        bdown_ref[pl.ds(s, 1), :] = cut[10:11]
        lines = second_ref[base + 16 : base + 32, :]
        for n in range(3 * heads):
            at = (n % per) * NBUCK
            tables_ref[n // heads, n % heads, pl.ds(s, 1), :] = lines[
                n // per : n // per + 1, at : at + NBUCK
            ]
        bup_ref[pl.ds(s, 1), :] = lines[2:3]


def swap(value, axis, step=1):
    size = lax.axis_size(axis)
    return lax.ppermute(value, axis, [(i, i ^ step) for i in range(size)])


def swap_both(value):
    size = lax.axis_size("batch") * 2
    return lax.ppermute(value, ("batch", "y"), [(i, i ^ 3) for i in range(size)])


def added(left, right):
    return (left.astype(F32) + right.astype(F32)).astype(BF16)


def batch_steps():
    return [1 << bit for bit in range(lax.axis_size("batch").bit_length() - 1)]


def join(*values):
    return lax.optimization_barrier(values)


def shards(
    tokens,
    spatial,
    positions,
    boxes,
    query_key_value_weight,
    w_spatial,
    rel_tables,
    exit_matrix,
    ln_gains,
    ln_shifts,
    up_weight,
    hidden_bias,
    shrink_projection_array,
    b_down,
    cotangent,
):
    heads = rel_tables.shape[2]
    rows = tokens.shape[2]
    width = tokens.shape[3]
    inner = query_key_value_weight.shape[3]
    hidden = up_weight.shape[2]
    least = rows // 4
    rest = rows // 2
    length = 4 * rows
    half = length // 2
    page = lax.axis_index("y")
    core = lax.axis_index("core")
    zh = lax.axis_index("zh")
    zl = lax.axis_index("zl")
    pair = lax.axis_index("batch") & 1
    place = jnp.stack([core, pair, page, zl, zh]).astype(jnp.int32)

    def run(body, operands, outs, us=TICK, scratch=(), after=(), vmem=VMEM_BYTES):
        return kernel_call(body, place, operands, outs, us, scratch, after, vmem)

    def rows_of(count, dtype=BF16):
        return ((count, width), dtype)

    share = hidden // 4
    far0, far1, far2, near, x00, up_part, down_part = run(
        pack_kernel,
        [
            (tokens.reshape(2, 2, 4, least, width), "any"),
            (spatial.reshape(2, 4, least, width), "any"),
            (positions, "any"),
            (boxes, "any"),
            (exit_matrix, "any"),
            (up_weight, "any"),
            (shrink_projection_array, "any"),
            (hidden_bias, "any"),
        ],
        [
            rows_of(rows + 16),
            rows_of(rows),
            rows_of(rows),
            rows_of(2 * rows + 16),
            rows_of(rows),
            rows_of(share + 16 + inner // 4),
            rows_of(share),
        ],
        scratch=[
            pltpu.VMEM(positions.shape, jnp.int32),
            pltpu.VMEM(boxes.shape, jnp.int32),
            pltpu.VMEM(hidden_bias.shape, F32),
            pltpu.SemaphoreType.DMA((30,)),
        ],
        vmem=PACK_VMEM,
    )
    up_part = swap(up_part, "zh")
    i10, s10, x10 = swap(far0, "y"), swap(far1, "y"), swap(far2, "y")
    cot_far, cot_near, cot00 = run(
        cotangent_kernel,
        [(cotangent.reshape(2, 2, 4, least, width), "any")],
        [((2, rows, width), BF16), rows_of(rows), rows_of(rows)],
        scratch=[pltpu.SemaphoreType.DMA((16,))],
        vmem=PACK_VMEM,
        after=[x00],
    )
    n01 = swap(near, "core")
    weights = (jnp.swapaxes(query_key_value_weight, 2, 3), "stream")
    spatial_weights = jnp.swapaxes(w_spatial, 1, 2)
    x0, sp0, index0, proj0, spat0, up, down, exit_own = run(
        near_kernel,
        [
            x00,
            n01,
            near,
            weights,
            spatial_weights,
            (up_weight, "any"),
            (shrink_projection_array, "any"),
            (exit_matrix, "any"),
        ],
        [
            ((2, rows, width), BF16),
            ((2, rows, width), BF16),
            ((8, 2 * rows), jnp.int32),
            ((3, 2 * rows, inner), BF16),
            ((2, 2 * rows, inner), BF16),
            ((width, hidden), BF16),
            ((hidden, width), BF16),
            rows_of(inner),
        ],
        scratch=[pltpu.SemaphoreType.DMA((3,))],
        after=[cot00],
    )
    i10, s10, x10, x0, up_part, down_part = join(i10, s10, x10, x0, up_part, down_part)
    x11, s11 = swap(i10, "core"), swap(s10, "core")
    ups = [up_part, swap(up_part, "y"), swap(up_part, "batch"), swap_both(up_part)]
    down_part = swap(down_part, "zh")

    x, sp, colidx, proj, spat, soft, att_own, att_send = run(
        functools.partial(attention_kernel, heads=heads),
        [
            x10,
            x11,
            s10,
            s11,
            i10,
            x0,
            sp0,
            index0,
            proj0,
            spat0,
            weights,
            spatial_weights,
            (rel_tables, "stream"),
        ],
        [
            ((2, 2, rows, width), BF16),
            ((2, 2, rows, width), BF16),
            ((length, 8), jnp.int32),
            ((3, length, inner), BF16, "any"),
            ((2, length, inner), BF16, "any"),
            ((heads, length, length), F32, "any"),
            ((half, inner), BF16),
            ((half, inner), BF16),
        ],
        us=30,
        scratch=[
            pltpu.VMEM((length, inner), BF16),
            pltpu.VMEM((3, length, inner), BF16),
            pltpu.VMEM((2, length, inner), BF16),
            pltpu.VMEM((heads, length, length), F32),
            pltpu.SemaphoreType.DMA((2 + heads,)),
        ],
    )
    att_recv = swap(att_send, "zh")
    att_own, down_part, *ups = join(att_own, down_part, *ups)
    downs = [down_part, swap(down_part, "y"), swap(down_part, "batch"), swap_both(down_part)]

    keep, send, exit_partner = run(
        mixed_kernel,
        [att_own, att_recv, exit_own, *ups],
        [rows_of(rows, F32), rows_of(rows), rows_of(inner)],
    )
    (mixed0,) = run(
        plus_kernel, [keep, swap(send, "core")], [rows_of(rows)], after=downs[1:3]
    )
    mixed_zl = swap(mixed0, "zl")
    (mixed0,) = run(
        functools.partial(turn_kernel, size=least), [mixed0, mixed_zl], [rows_of(rows)]
    )
    mixed1 = swap(mixed0, "core")
    mixed_far0 = swap(mixed0, "zh")
    mixed1, *downs = join(mixed1, *downs)

    gains = (ln_gains, "stream")
    shifts = (ln_shifts, "stream")
    x_own = (x, (None, 0, None, None))
    x_far = (x, (None, 1, None, None))
    low, normed, active, slope, up_partner, down_partner = run(
        forward_kernel,
        [x_own, mixed0, mixed1, gains, shifts, up, hidden_bias, down, *ups, *downs],
        [
            rows_of(half),
            rows_of(half),
            ((2, half, hidden), BF16),
            ((2, half, hidden), BF16),
            ((width, hidden), BF16),
            ((hidden, width), BF16),
        ],
    )
    low_recv = swap(low, "zl")
    cot_far, cot_near, low = join(cot_far, cot_near, low)
    cot10 = swap(cot_far, "y")
    cot01 = swap(cot_near, "core")
    mixed_far1 = swap(mixed_far0, "core")
    cot11 = swap(cot10, "core")
    (normed_far,) = run(
        first_norm_kernel,
        [x_far, mixed_far0, mixed_far1, gains, shifts],
        [rows_of(half)],
        after=[low],
    )
    active_far, slope_far = run(
        other_kernel,
        [normed_far, up, hidden_bias],
        [((half, hidden), BF16), ((half, hidden), BF16)],
    )
    low0, low1 = run(
        lowered_kernel, [low, low_recv], [rows_of(rows), rows_of(rows)], after=[slope_far]
    )
    far_low0 = swap(low0, "zh")

    def finish(x_half, pieces, part, after=()):
        rows_part = slice(part * rest, (part + 1) * rest)
        cots = [
            cot00[rows_part],
            cot10[0, rows_part],
            cot01[rows_part],
            cot11[1, rows_part],
        ]
        return run(
            final_kernel,
            [x_half, *pieces, *cots, gains, shifts, b_down],
            [
                ((2, rest, width), BF16),
                ((2, rest, width), BF16),
                rows_of(half, F32),
                rows_of(half),
                rows_of(8, F32),
            ],
            after=after,
        )

    out_keep, out_send, second, dlow, sums_two = finish(x_own, [mixed0, mixed1, low0, low1], 0)
    hid, dup = run(
        middle_kernel,
        [dlow, up, down, up_partner, down_partner, slope],
        [rows_of(half), ((half, hidden), BF16)],
    )
    hid_recv = swap(hid, "zl")
    out_core = swap(out_send, "core")
    out_y = swap(jnp.stack([out_keep[1], out_core[1]]), "y")
    hid_recv, far_low0, out_y = join(hid_recv, far_low0, out_y)
    far_low1 = swap(far_low0, "zl")
    first, dmix, sums_one = run(
        first_kernel,
        [x_own, mixed0, mixed1, second, hid, hid_recv, gains],
        [rows_of(half, F32), rows_of(half), rows_of(8, F32)],
    )
    dmix_core = swap(dmix, "core")
    datt, datt_send, dmix, pay = run(
        attended_kernel,
        [dmix, dmix_core, exit_own, exit_partner, sums_one, sums_two],
        [
            ((half, inner), BF16),
            ((half, inner), BF16),
            rows_of(half),
            rows_of(rest + 16),
        ],
    )
    datt_recv = swap(datt_send, "zh")
    far_keep, far_send, _, dlow_far, _ = finish(
        x_far, [mixed_far0, mixed_far1, far_low0, far_low1], 1, [datt]
    )
    up_keep, up_send, down_keep, down_send, bias_grad = run(
        ffn_grad_kernel,
        [
            normed,
            normed_far,
            (active, (0, None, None)),
            active_far,
            dlow,
            dlow_far,
            dup,
            slope_far,
            down,
        ],
        [
            ((width // 2, hidden), BF16),
            ((width // 2, hidden), BF16),
            rows_of(hidden // 2),
            rows_of(hidden // 2),
            ((8, hidden), F32),
        ],
        us=30,
        scratch=[pltpu.VMEM((width, hidden), BF16)],
        after=[datt],
    )
    up_recv = swap(up_send, "batch")
    down_recv = swap(down_send, "y")
    datt_recv, pay = join(datt_recv, pay)
    pay_recv = swap(pay, "zh")
    piece = rows_of(rows)
    dscore, dproj, dspat, dxk0, dxk1, dxs, dsk0, dsk1, dss = run(
        functools.partial(backward_kernel, heads=heads, block=128),
        [datt, datt_recv, first, (soft, "any"), proj, spat, weights, spatial_weights],
        [
            ((heads, length, length), BF16),
            ((3, length, inner), BF16),
            ((2, length, inner), BF16),
            piece,
            piece,
            ((2, rows, width), BF16),
            piece,
            piece,
            ((2, rows, width), BF16),
        ],
        us=30,
        scratch=[pltpu.VMEM((heads, length, length), F32), pltpu.SemaphoreType.DMA((heads,))],
        after=[bias_grad],
    )

    steps = batch_steps()[1:]

    def plus(pairs, after=(), over_batch=False):
        sums = run(
            plus_kernel,
            [array for pair_of in pairs for array in pair_of],
            [(left.shape, BF16) for left, _ in pairs],
            after=after,
        )
        if over_batch:
            for step in steps:
                sums = [added(value, swap(value, "batch", step)) for value in sums]
        return sums

    dxk1, dxs, dss, pay_recv = join(dxk1, dxs, dss, pay_recv)
    dxs, dss = swap(dxs, "core"), swap(dss, "core")
    near, far = run(
        units_kernel,
        [dxk0, dxk1, dxs, dsk0, dsk1, dss],
        [((3, rows, width), BF16), ((3, rows, width), BF16)],
    )
    far_zl = swap(far, "zl")
    up_half, down_half = plus([(up_keep, up_recv), (down_keep, down_recv)], after=[far])
    up_other = swap(up_half, "y")
    down_other = swap(down_half, "batch")
    pay_zl = swap(join(pay_recv, far)[0], "zl")
    few = inner // 2
    main = 3 * inner - few
    sp_keep, sp_send = run(
        spatial_grad_kernel, [sp, dspat], [rows_of(inner), rows_of(inner)], after=[up_half]
    )
    sp_recv = swap(sp_send, "core")
    one_keep, one_send, value_rest, lines = run(
        functools.partial(first_grad_kernel, heads=heads),
        [x, dscore, dproj, colidx, bias_grad],
        [rows_of(main // 2), rows_of(main // 2), rows_of(few), rows_of(16, F32)],
        scratch=[pltpu.VMEM((3 * inner, width), BF16)],
        after=[sp_keep],
    )
    keep, send = run(
        fold_kernel,
        [near, far_zl],
        [((3, rest, width), BF16), ((3, rest, width), BF16)],
        after=[lines],
    )
    send_zh = swap(send, "zh")
    up_half, down_half = plus(
        [(up_half, up_other), (down_half, down_other)], after=[send], over_batch=True
    )
    up_far = swap(up_half, "batch")
    down_far = swap(down_half, "y")
    mine, other = run(
        ends_first_kernel,
        [keep, send_zh],
        [((3, least, width), BF16), ((3, least, width), BF16)],
        after=[up_half],
    )
    got = swap(other, "y")
    pay_recv, pay_zl, far_send, mine = join(pay_recv, pay_zl, far_send, mine)
    pay_core, pay_zlcore = swap(pay_recv, "core"), swap(pay_zl, "core")
    far_core = swap(far_send, "core")
    base = few + 2 * inner + 32
    two_keep, two_send = run(
        second_grad_kernel,
        [
            dmix,
            pay,
            pay_recv,
            pay_zl,
            pay_core,
            pay_zlcore,
            att_own,
            att_send,
            value_rest,
            sp_keep,
            sp_recv,
            lines,
        ],
        [rows_of(base // 2), rows_of(base // 2)],
        scratch=[pltpu.VMEM((base, width), BF16)],
        after=[mine, up_far, down_far],
    )
    one_send, two_send, got, two_keep = join(one_send, two_send, got, two_keep)
    one_recv = swap(one_send, "batch")
    two_recv = swap(two_send, "y")
    pages = jnp.stack([mine, got])
    pages_zh = swap(pages, "zh")
    pages_zl = swap(pages, "zl")
    *halves, pages = join(up_half, up_far, down_half, down_far, pages)
    others = [swap(value, "core") for value in halves]
    grad_up, grad_down, spread_event = run(
        spread_kernel,
        halves[:2] + others[:2] + halves[2:] + others[2:],
        [
            ((2, 2, width // 2, hidden), F32),
            ((2, 2, hidden // 2, width), F32),
            ((8, NBUCK), F32),
        ],
        after=[pages],
    )
    one_half, two_half = plus(
        [(one_keep, one_recv), (two_keep, two_recv)], after=[spread_event]
    )
    one_other = swap(one_half, "y")
    two_other = swap(two_half, "batch")
    far_y = swap(jnp.stack([far_keep[1], far_core[1]]), "y")
    pages_zh, pages_zl = join(pages_zh, pages_zl)
    pages_zz = swap(pages_zh, "zl")
    one_half, two_half = plus(
        [(one_half, one_other), (two_half, two_other)],
        after=[pages_zz],
        over_batch=True,
    )
    one_far = swap(one_half, "batch")
    two_far = swap(two_half, "y")
    grad_tokens, grad_spatial, ends_event = run(
        ends_kernel,
        [mine, got, pages_zh, pages_zl, pages_zz],
        [((2, 2, 4, least, width), F32), ((2, 4, least, width), F32), ((8, NBUCK), F32)],
        after=[one_half],
    )
    output, out_event = run(
        out_kernel,
        [
            out_keep[0],
            out_core[0],
            out_y[0],
            out_y[1],
            far_keep[0],
            far_core[0],
            far_y[0],
            far_y[1],
        ],
        [((2, 2, 4, least, width), BF16), ((8, NBUCK), F32)],
        after=[one_half],
    )
    one_far, two_far, out_event, ends_event = join(one_far, two_far, out_event, ends_event)
    halves = [one_half, one_far, two_half, two_far]
    others = [swap(value, "core") for value in halves]
    part = width // (2 * lax.axis_size("zh"))
    grad_qkv, grad_spatial_w, grad_exit, tables, gains_grad, shifts_grad, grad_b_up, grad_b_down = run(
        functools.partial(last_kernel, heads=heads),
        halves[:2] + others[:2] + halves[2:] + others[2:],
        [
            ((2, 3 * inner, width), F32),
            ((2, inner, width), F32),
            ((2, inner, width), F32),
            ((3, heads, 2, NBUCK), F32),
            ((2, 2, part), F32),
            ((2, 2, part), F32),
            ((2, hidden), F32),
            ((2, part), F32),
        ],
        scratch=[pltpu.VMEM((base, width), F32)],
        after=[spread_event, out_event, ends_event],
    )
    return (
        output.reshape(tokens.shape),
        grad_tokens.reshape(tokens.shape),
        grad_spatial.reshape(spatial.shape),
        grad_qkv.reshape(2, 3, inner, width).swapaxes(2, 3),
        grad_spatial_w.reshape(2, inner, width).swapaxes(1, 2),
        tables.transpose(2, 0, 1, 3),
        grad_exit,
        gains_grad,
        shifts_grad,
        grad_up.reshape(2, width, hidden),
        grad_b_up,
        grad_down.reshape(2, hidden, width),
        grad_b_down,
    )


def solution(mesh):
    batch, seq, head = mesh.devices.shape
    fine = Mesh(
        mesh.devices.reshape(batch, seq // 2, 2, head // 2, 2),
        ("batch", "y", "core", "zh", "zl"),
    )
    seq = ("y", "core")
    head = ("zh", "zl")
    return jax.shard_map(
        shards,
        mesh=fine,
        in_specs=(
            P(None, "batch", seq, None),
            P("batch", seq, None),
            P("batch", seq),
            P(None, "batch", seq),
            P(None, None, None, head),
            P(None, None, head),
            P(None, None, head, None),
            P(None, head, None),
            P(),
            P(),
            P(None, None, head),
            P(None, head),
            P(None, head, None),
            P(),
            P(None, "batch", seq, None),
        ),
        out_specs=(
            P(None, "batch", seq, None),
            P(None, "batch", seq, None),
            P("batch", seq, None),
            P(None, None, None, head),
            P(None, None, head),
            P(None, None, head, None),
            P(None, head, None),
            P(None, None, head),
            P(None, None, head),
            P(None, None, head),
            P(None, head),
            P(None, head, None),
            P(None, head),
        ),
        check_vma=False,
    )
```

```python
import functools

import jax
import jax.numpy as jnp
from jax import lax
from jax.experimental import pallas as pl
from jax.experimental.pallas import tpu as pltpu
from jax.sharding import Mesh, PartitionSpec as P

DH = 64
NBUCK = 128
HALF = 64
EPSILON = 1e-05
F32 = jnp.float32
BF16 = jnp.bfloat16
VMEM_BYTES = 20 * 1024 * 1024
TICK = 0.1
PACK_VMEM = 60 * 1024 * 1024
NN = (((1,), (0,)), ((), ()))
NT = (((1,), (1,)), ((), ()))
TN = (((0,), (0,)), ((), ()))


def mm(left, right, dims=NN):
    return lax.dot_general(left, right, dims, preferred_element_type=F32)


def kernel_call(body, place, operands, outs, us, scratch=(), after=(), vmem=VMEM_BYTES):
    specs, arrays, hows = [], [], []
    for operand in operands:
        array, how = operand if isinstance(operand, tuple) else (operand, None)
        specs.append(pl.BlockSpec(memory_space=pltpu.HBM if how == "any" else pltpu.VMEM))
        arrays.append(array)
        hows.append(how)
    count = len(arrays)
    specs += [pl.BlockSpec(memory_space=pl.ANY)] * len(after)

    def view(s_ref, ref, how):
        if how == "stream":
            return ref.at[s_ref[0]]
        if how is None or how == "any":
            return ref
        return ref.at[tuple(slice(None) if at is None else at for at in how)]

    def kernel(s_ref, *refs):
        given = [view(s_ref, ref, how) for ref, how in zip(refs, hows)]
        body(s_ref, *given, *refs[count + len(after) :])

    return pl.pallas_call(
        kernel,
        out_shape=[jax.ShapeDtypeStruct(out[0], out[1]) for out in outs],
        in_specs=[pl.BlockSpec(memory_space=pltpu.SMEM)] + specs,
        out_specs=[
            pl.BlockSpec(memory_space=pltpu.HBM if len(out) > 2 else pltpu.VMEM) for out in outs
        ],
        scratch_shapes=list(scratch),
        compiler_params=pltpu.CompilerParams(vmem_limit_bytes=vmem),
        cost_estimate=pl.CostEstimate(
            flops=int(us * 1.1e9), bytes_accessed=int(us * 3.5e6), transcendentals=0
        ),
    )(place, *arrays, *after)


def centred(rows):
    centre = rows - jnp.mean(rows, axis=-1, keepdims=True)
    spread = lax.rsqrt(jnp.mean(centre * centre, axis=-1, keepdims=True) + EPSILON)
    return centre * spread, spread


def norm_back(unit, spread, tilted):
    return spread * (
        tilted
        - jnp.mean(tilted, axis=-1, keepdims=True)
        - unit * jnp.mean(tilted * unit, axis=-1, keepdims=True)
    )


def pick(table_row, index):
    width = index.shape[1]
    table = jnp.broadcast_to(table_row, (index.shape[0], NBUCK))
    parts = [
        jnp.take_along_axis(
            table,
            index[:, at : at + NBUCK],
            axis=1,
            mode="promise_in_bounds",
        )
        for at in range(0, width, NBUCK)
    ]
    return jnp.concatenate(parts, axis=1)


def stack_rows(pieces):
    return jnp.concatenate(pieces, axis=0)


def turned(rows, size):
    pieces = [rows[at : at + size] for at in range(0, rows.shape[0], size)]
    return stack_rows([pieces[i ^ 1] for i in range(len(pieces))])


def residual(x_ref, mixed_refs):
    rest = mixed_refs[0].shape[0] // 2
    pieces = []
    for y in range(2):
        for c in range(2):
            own = x_ref[y, c * rest : (c + 1) * rest, :].astype(F32)
            pieces.append(own + mixed_refs[c][y * rest : (y + 1) * rest, :].astype(F32))
    return stack_rows(pieces)


def dealt(rows_ref, side, keep_ref, send_ref):
    half = keep_ref.shape[0]
    keep_ref[...] = rows_ref[pl.ds(pl.multiple_of(side * half, 16), half), :]
    send_ref[...] = rows_ref[pl.ds(pl.multiple_of((1 - side) * half, 16), half), :]


def gathered(place_ref, refs, rows, to_ref):
    size = rows.stop - rows.start
    for turn, ref in enumerate(refs):
        q = (place_ref[1] ^ (turn // 2)) * 2 + (place_ref[2] ^ (turn % 2))
        to_ref[pl.ds(pl.multiple_of(q * size, 16), size), :] = ref[rows, :]


def copied(pairs, sems):
    started = [
        pltpu.make_async_copy(source, target, sems.at[n])
        for n, (source, target) in enumerate(pairs)
    ]
    for copy in started:
        copy.start()
    return started


def pack_kernel(
    p_ref,
    tok_ref,
    sp_ref,
    pos_ref,
    box_ref,
    exit_ref,
    up_ref,
    down_ref,
    bias_ref,
    far0_ref,
    far1_ref,
    far2_ref,
    near_ref,
    own_ref,
    ups_ref,
    downs_ref,
    posv_ref,
    boxv_ref,
    biasv_ref,
    sems,
):
    c, y, zl, zh = p_ref[0], p_ref[2], p_ref[3], p_ref[4]
    block = zh * 2 + zl
    least = tok_ref.shape[3]
    rows = 4 * least
    q = p_ref[1] * 2 + y
    many = down_ref.shape[1] // 4
    few = exit_ref.shape[1] // 4
    pairs = [
        (pos_ref, posv_ref),
        (box_ref, boxv_ref),
        (bias_ref, biasv_ref),
        (up_ref.at[c, pl.ds(pl.multiple_of(q * many, 16), many)], ups_ref.at[pl.ds(0, many)]),
        (
            exit_ref.at[c, pl.ds(pl.multiple_of(q * few, 16), few)],
            ups_ref.at[pl.ds(many + 16, few)],
        ),
        (down_ref.at[c, pl.ds(pl.multiple_of(q * many, 16), many)], downs_ref),
    ]
    for k in range(4):
        at = block ^ k
        to = pl.ds(k * least, least)
        pairs += [
            (tok_ref.at[1 - c, 1 - y, at], far0_ref.at[to]),
            (sp_ref.at[1 - y, at], far1_ref.at[to]),
            (tok_ref.at[c, 1 - y, at], far2_ref.at[to]),
            (tok_ref.at[1 - c, y, at], near_ref.at[to]),
            (sp_ref.at[y, at], near_ref.at[pl.ds(rows + k * least, least)]),
            (tok_ref.at[c, y, at], own_ref.at[to]),
        ]
    started = copied(pairs, sems)
    for copy in started[:3]:
        copy.wait()
    left = biasv_ref[pl.ds(c, 1), :]
    lines = []
    for _ in range(3):
        lines.append(left.astype(BF16).astype(F32))
        left = left - lines[-1]
    lines.append(jnp.zeros((13, left.shape[1]), F32))
    ups_ref[many : many + 16, :] = jnp.concatenate(lines, axis=0).astype(BF16)
    lane = lax.broadcasted_iota(jnp.int32, (8, NBUCK), 1)
    width = far0_ref.shape[1]
    for page, ref, at in ((1 - y, far0_ref, rows), (y, near_ref, 2 * rows)):
        place = posv_ref[pl.ds(page, 1), :]
        lines = [
            place & 255,
            place >> 8,
            boxv_ref[0, pl.ds(page, 1), :],
            boxv_ref[1, pl.ds(page, 1), :],
        ]
        value = jnp.concatenate(lines + [jnp.zeros((4, NBUCK), jnp.int32)], axis=0)
        crossed = jnp.where(
            (lane & 63) < 32, pltpu.roll(value, NBUCK - 32, 1), pltpu.roll(value, 32, 1)
        )
        value = jnp.where(zl == 0, value, crossed)
        value = jnp.where(zh == 0, value, pltpu.roll(value, 64, 1))
        value = jnp.concatenate([value.astype(F32), jnp.zeros((8, NBUCK), F32)], axis=0)
        ref[at : at + 16, 0:NBUCK] = value.astype(BF16)
        ref[at : at + 16, NBUCK:] = jnp.zeros((16, width - NBUCK), BF16)
    for copy in started[3:]:
        copy.wait()


def cotangent_kernel(p_ref, cot_ref, far_ref, near_ref, own_ref, sems):
    c, y, block = p_ref[0], p_ref[2], p_ref[4] * 2 + p_ref[3]
    least = cot_ref.shape[3]
    pairs = []
    for k in range(4):
        at = block ^ k
        to = pl.ds(k * least, least)
        pairs += [
            (cot_ref.at[c, 1 - y, at], far_ref.at[0, to]),
            (cot_ref.at[1 - c, 1 - y, at], far_ref.at[1, to]),
            (cot_ref.at[1 - c, y, at], near_ref.at[to]),
            (cot_ref.at[c, y, at], own_ref.at[to]),
        ]
    for copy in copied(pairs, sems):
        copy.wait()


def indices(ref, at):
    lines = ref[at : at + 16, 0:NBUCK].astype(F32).astype(jnp.int32)
    place = lines[0:1] + lines[1:2] * 256
    return jnp.concatenate([place, lines[2:4], jnp.zeros((5, NBUCK), jnp.int32)], axis=0)


def two_cores(index0, index1, half):
    lane = lax.broadcasted_iota(jnp.int32, (8, NBUCK), 1)
    if half == 0:
        return jnp.where(lane < 64, index0, pltpu.roll(index1, 64, 1))
    return jnp.where(lane < 64, pltpu.roll(index0, 64, 1), index1)


def arrange(x0_ref, x1_ref, s0_ref, s1_ref, i0_ref, i1_ref, at, x_ref, sp_ref):
    least = x_ref.shape[1]
    rest = least // 2
    found = []
    index0, index1 = indices(i0_ref, at), indices(i1_ref, at)
    for half in range(2):
        at = half * rest
        x_ref[half, 0:rest, :] = x0_ref[at : at + rest, :]
        x_ref[half, rest:, :] = x1_ref[at : at + rest, :]
        sp_ref[half, 0:rest, :] = s0_ref[at : at + rest, :]
        sp_ref[half, rest:, :] = s1_ref[at : at + rest, :]
        found.append(two_cores(index0, index1, half))
    return found


def project(x_ref, sp_ref, w_ref, ws_ref, proj_ref, spat_ref, at):
    width = x_ref.shape[-1]
    x = x_ref[...].reshape(-1, width)
    sp = sp_ref[...].reshape(-1, width)
    rows = slice(at, at + x.shape[0])
    for k in range(3):
        proj_ref[k, rows, :] = mm(x, w_ref[k], NT).astype(BF16)
    for k in range(2):
        spat_ref[k, rows, :] = mm(sp, ws_ref[k], NT).astype(BF16)


def near_kernel(
    p_ref,
    x00_ref,
    n01_ref,
    n00_ref,
    w_ref,
    ws_ref,
    up_hbm,
    down_hbm,
    exit_hbm,
    x_ref,
    sp_ref,
    index_ref,
    proj_ref,
    spat_ref,
    up_ref,
    down_ref,
    exit_ref,
    sems,
):
    fetched = [
        pltpu.make_async_copy(source.at[p_ref[0]], target, sems.at[n])
        for n, (source, target) in enumerate(
            ((exit_hbm, exit_ref), (up_hbm, up_ref), (down_hbm, down_ref))
        )
    ]
    for copy in fetched:
        copy.start()
    least = x_ref.shape[1]
    found = arrange(
        x00_ref,
        n01_ref,
        n00_ref.at[least:],
        n01_ref.at[least:],
        n00_ref,
        n01_ref,
        2 * least,
        x_ref,
        sp_ref,
    )
    index_ref[...] = jnp.concatenate(found, axis=1)
    project(x_ref, sp_ref, w_ref, ws_ref, proj_ref, spat_ref, 0)
    for copy in fetched:
        copy.wait()


def attention_kernel(
    p_ref,
    x10_ref,
    x11_ref,
    s10_ref,
    s11_ref,
    i10_ref,
    x0_ref,
    sp0_ref,
    index_ref,
    proj0_ref,
    spat0_ref,
    w_ref,
    ws_ref,
    table_ref,
    x_ref,
    sp_ref,
    colidx_ref,
    proj_hbm,
    spat_hbm,
    soft_hbm,
    own_ref,
    send_ref,
    att_ref,
    proj_ref,
    spat_ref,
    soft_ref,
    sems,
    *,
    heads,
):
    least = x_ref.shape[2]
    near = 2 * least
    x_ref[0] = x0_ref[...]
    sp_ref[0] = sp0_ref[...]
    proj_ref[:, 0:near, :] = proj0_ref[...]
    spat_ref[:, 0:near, :] = spat0_ref[...]
    found = arrange(
        x10_ref, x11_ref, s10_ref, s11_ref, i10_ref, x11_ref, least, x_ref.at[1], sp_ref.at[1]
    )
    places = jnp.concatenate([index_ref[...]] + found, axis=1)
    colidx_ref[...] = jnp.transpose(places.astype(F32)).astype(jnp.int32)
    project(x_ref.at[1], sp_ref.at[1], w_ref, ws_ref, proj_ref, spat_ref, near)
    length = 2 * near
    stored = [
        pltpu.make_async_copy(proj_ref, proj_hbm, sems.at[0]),
        pltpu.make_async_copy(spat_ref, spat_hbm, sems.at[1]),
    ]
    for copy in stored:
        copy.start()
    level = lax.broadcasted_iota(jnp.int32, (length, NBUCK), 1)
    chosen = [(colidx_ref[:, kind : kind + 1] == level).astype(BF16) for kind in (1, 2)]
    chosen = jnp.concatenate(chosen, axis=1)

    lane = lax.broadcasted_iota(jnp.int32, (length, NBUCK), 1)
    boxes = [
        jnp.clip(lane - colidx_ref[:, kind : kind + 1], -HALF, HALF - 1) + HALF
        for kind in (1, 2)
    ]
    index = jnp.clip(places[0:1, :] - colidx_ref[:, 0:1], -HALF, HALF - 1) + HALF
    for h in range(heads):
        cols = slice(h * DH, (h + 1) * DH)
        bias = jnp.concatenate(
            [pick(table_ref[k, h : h + 1, :], boxes[k - 1]) for k in (1, 2)], axis=1
        )
        coarse = bias.astype(BF16)
        fine = (bias - coarse.astype(F32)).astype(BF16)
        left = jnp.concatenate(
            [proj_ref[0, :, cols], spat_ref[0, :, cols]], axis=1
        ) * jnp.asarray(DH**-0.5, BF16)
        right = jnp.concatenate([proj_ref[1, :, cols], spat_ref[1, :, cols]], axis=1)
        scores = mm(
            jnp.concatenate([left, coarse, fine], axis=1),
            jnp.concatenate([right, chosen, chosen], axis=1),
            NT,
        ) + pick(table_ref[0, h : h + 1, :], index)
        top = jnp.max(scores, axis=-1, keepdims=True)
        raised = jnp.exp(scores - top)
        soft = raised * (1.0 / jnp.sum(raised, axis=-1, keepdims=True))
        soft_ref[h] = soft
        stored.append(pltpu.make_async_copy(soft_ref.at[h], soft_hbm.at[h], sems.at[2 + h]))
        stored[-1].start()
        att_ref[:, cols] = mm(soft.astype(BF16), proj_ref[2, :, cols]).astype(BF16)
    for copy in stored:
        copy.wait()
    part = length // 4
    own_ref[0:part, :] = att_ref[0:part, :]
    own_ref[part:, :] = att_ref[2 * part : 3 * part, :]
    send_ref[0:part, :] = att_ref[part : 2 * part, :]
    send_ref[part:, :] = att_ref[3 * part :, :]


def mixed_kernel(
    p_ref,
    own_ref,
    recv_ref,
    exit_ref,
    one0_ref,
    one1_ref,
    one2_ref,
    one3_ref,
    keep_ref,
    send_ref,
    partner_ref,
):
    rows = slice(one0_ref.shape[0] - exit_ref.shape[0] // 4, one0_ref.shape[0])
    gathered(p_ref, (one0_ref, one1_ref, one2_ref, one3_ref), rows, partner_ref)
    total = mm(own_ref[...], exit_ref[...]) + mm(recv_ref[...], partner_ref[...])
    rest = total.shape[0] // 4
    for y in range(2):
        at = 2 * y * rest
        keep_ref[y * rest : (y + 1) * rest, :] = total[at : at + rest]
        send_ref[y * rest : (y + 1) * rest, :] = total[at + rest : at + 2 * rest].astype(BF16)


def gelu_parts(upper):
    phi = 0.5 * (1.0 + lax.erf(upper * (0.5**0.5)))
    slope = phi + upper * (jnp.exp(-0.5 * upper * upper) * (0.5 / jnp.pi) ** 0.5)
    return (upper * phi).astype(BF16), slope


def forward_kernel(
    p_ref,
    x_ref,
    mixed0_ref,
    mixed1_ref,
    gain_ref,
    shift_ref,
    up_ref,
    hidden_ref,
    down_ref,
    one0_ref,
    one1_ref,
    one2_ref,
    one3_ref,
    two0_ref,
    two1_ref,
    two2_ref,
    two3_ref,
    low_ref,
    normed_ref,
    active_ref,
    slope_ref,
    upp_ref,
    downp_ref,
):
    many = two0_ref.shape[0]
    gathered(p_ref, (one0_ref, one1_ref, one2_ref, one3_ref), slice(0, many), upp_ref)
    gathered(p_ref, (two0_ref, two1_ref, two2_ref, two3_ref), slice(0, many), downp_ref)
    extra = one0_ref[many : many + 16, :].astype(F32)
    partner_bias = extra[0:1] + extra[1:2] + extra[2:3]
    unit, _ = centred(residual(x_ref, (mixed0_ref, mixed1_ref)))
    normed_low = (unit * gain_ref[0:1, :] + shift_ref[0:1, :]).astype(BF16)
    normed_ref[...] = normed_low
    active, slope = gelu_parts(mm(normed_low, up_ref[...]) + hidden_ref[pl.ds(p_ref[0], 1), :])
    active_ref[0] = active
    slope_ref[0] = slope.astype(BF16)
    total = mm(active, down_ref[...])
    active, slope = gelu_parts(mm(normed_low, upp_ref[...]) + partner_bias)
    active_ref[1] = active
    slope_ref[1] = slope.astype(BF16)
    low_ref[...] = (total + mm(active, downp_ref[...])).astype(BF16)


def other_kernel(
    p_ref,
    normed_ref,
    up_ref,
    hidden_ref,
    active_ref,
    slope_ref,
):
    active, slope = gelu_parts(
        mm(normed_ref[...], up_ref[...]) + hidden_ref[pl.ds(p_ref[0], 1), :]
    )
    active_ref[...] = active
    slope_ref[...] = slope.astype(BF16)


def first_norm_kernel(p_ref, x_ref, mixed0_ref, mixed1_ref, gain_ref, shift_ref, normed_ref):
    unit, _ = centred(residual(x_ref, (mixed0_ref, mixed1_ref)))
    normed_ref[...] = (unit * gain_ref[0:1, :] + shift_ref[0:1, :]).astype(BF16)


def lowered_kernel(p_ref, own_ref, far_ref, low0_ref, low1_ref):
    least = own_ref.shape[0] // 8
    total = own_ref[...].astype(F32) + turned(far_ref[...], least).astype(F32)
    total = total.astype(BF16)
    for i in range(4):
        low0_ref[i * least : (i + 1) * least, :] = total[2 * i * least : (2 * i + 1) * least]
        low1_ref[i * least : (i + 1) * least, :] = total[(2 * i + 1) * least : (2 * i + 2) * least]


def final_kernel(
    p_ref,
    x_ref,
    mixed0_ref,
    mixed1_ref,
    low0_ref,
    low1_ref,
    cot00_ref,
    cot10_ref,
    cot01_ref,
    cot11_ref,
    gain_ref,
    shift_ref,
    bdown_ref,
    outk_ref,
    outs_ref,
    second_ref,
    dlow_ref,
    sums_ref,
):
    unit, _ = centred(residual(x_ref, (mixed0_ref, mixed1_ref)))
    normed = unit * gain_ref[0:1, :] + shift_ref[0:1, :]
    least = low0_ref.shape[0] // 4
    pieces = []
    for i in range(4):
        pieces.append(low0_ref[i * least : (i + 1) * least, :])
        pieces.append(low1_ref[i * least : (i + 1) * least, :])
    lowered = stack_rows(pieces).astype(F32)
    unit2, spread2 = centred(normed + lowered + bdown_ref[pl.ds(p_ref[0], 1), :])
    out = (unit2 * gain_ref[1:2, :] + shift_ref[1:2, :]).astype(BF16)
    for y in range(2):
        at = 4 * y * least
        outk_ref[y] = out[at : at + 2 * least]
        outs_ref[y] = out[at + 2 * least : at + 4 * least]
    cot = stack_rows([cot00_ref[...], cot01_ref[...], cot10_ref[...], cot11_ref[...]]).astype(F32)
    second = norm_back(unit2, spread2, cot * gain_ref[1:2, :])
    second_ref[...] = second
    dlow_ref[...] = second.astype(BF16)
    sums_ref[...] = jnp.zeros_like(sums_ref)
    sums_ref[0:1, :] = jnp.sum(cot * unit2, axis=0, keepdims=True)
    sums_ref[1:2, :] = jnp.sum(cot, axis=0, keepdims=True)
    sums_ref[2:3, :] = jnp.sum(second, axis=0, keepdims=True)


def middle_kernel(
    p_ref,
    dlow_ref,
    up_ref,
    down_ref,
    upp_ref,
    downp_ref,
    slope_ref,
    hid_ref,
    dup_ref,
):
    dlow = dlow_ref[...]
    dup = (mm(dlow, down_ref[...], NT) * slope_ref[0].astype(F32)).astype(BF16)
    dup_ref[...] = dup
    total = mm(dup, up_ref[...], NT)
    dup = (mm(dlow, downp_ref[...], NT) * slope_ref[1].astype(F32)).astype(BF16)
    hid_ref[...] = (total + mm(dup, upp_ref[...], NT)).astype(BF16)


def ffn_own_kernel(p_ref, normed_ref, active_ref, dlow_ref, dup_ref, up_ref, down_ref, bias_ref):
    dup = dup_ref[...]
    up_ref[...] = mm(normed_ref[...], dup, TN)
    down_ref[...] = mm(active_ref[...], dlow_ref[...], TN)
    bias = jnp.sum(dup.astype(F32), axis=0, keepdims=True)
    bias_ref[...] = jnp.broadcast_to(bias, bias_ref.shape)


def ffn_grad_kernel(
    p_ref,
    upa_ref,
    downa_ref,
    biasa_ref,
    normedo_ref,
    activeo_ref,
    dlowo_ref,
    slopeo_ref,
    down_ref,
    upk_ref,
    ups_ref,
    downk_ref,
    downs_ref,
    bias_ref,
    all_ref,
):
    dlowo = dlowo_ref[...]
    dupo = (mm(dlowo, down_ref[...], NT) * slopeo_ref[...].astype(F32)).astype(BF16)
    all_ref[...] = (upa_ref[...] + mm(normedo_ref[...], dupo, TN)).astype(BF16)
    dealt(all_ref, p_ref[1], upk_ref, ups_ref)
    all_ref[...] = (downa_ref[...] + mm(activeo_ref[...], dlowo, TN)).astype(BF16)
    dealt(all_ref, p_ref[2], downk_ref, downs_ref)
    bias = jnp.sum(dupo.astype(F32), axis=0, keepdims=True)
    bias_ref[...] = biasa_ref[...] + jnp.broadcast_to(bias, bias_ref.shape)


def first_kernel(
    p_ref,
    x_ref,
    mixed0_ref,
    mixed1_ref,
    second_ref,
    hid_ref,
    hidr_ref,
    gain_ref,
    first_ref,
    dmix_ref,
    sums_ref,
):
    unit, spread = centred(residual(x_ref, (mixed0_ref, mixed1_ref)))
    hid = hid_ref[...].astype(F32) + turned(hidr_ref[...], hid_ref.shape[0] // 8).astype(F32)
    dnormed = second_ref[...] + hid
    first = norm_back(unit, spread, dnormed * gain_ref[0:1, :])
    first_ref[...] = first
    dmix_ref[...] = first.astype(BF16)
    sums_ref[...] = jnp.zeros_like(sums_ref)
    sums_ref[0:1, :] = jnp.sum(dnormed * unit, axis=0, keepdims=True)
    sums_ref[1:2, :] = jnp.sum(dnormed, axis=0, keepdims=True)


def attended_kernel(
    p_ref,
    dmix_ref,
    dmixr_ref,
    exit_ref,
    exitp_ref,
    sums1_ref,
    sums2_ref,
    own_ref,
    send_ref,
    total_ref,
    pay_ref,
):
    length = dmix_ref.shape[0]
    rest = length // 4
    total = dmix_ref[...].astype(F32) + turned(dmixr_ref[...], rest).astype(F32)
    total = total.astype(BF16)
    total_ref[...] = total
    own_ref[...] = mm(total, exit_ref[...], NT).astype(BF16)
    send_ref[...] = mm(total, exitp_ref[...], NT).astype(BF16)
    least = rest // 2
    pay_ref[0:least, :] = total[0:least]
    pay_ref[least:rest, :] = total[2 * rest : 2 * rest + least]
    pay_ref[rest:, :] = jnp.concatenate([sums1_ref[...], sums2_ref[...]], axis=0).astype(BF16)


def backward_kernel(
    p_ref,
    datt_ref,
    dattr_ref,
    first_ref,
    soft_hbm,
    proj_ref,
    spat_ref,
    w_ref,
    ws_ref,
    dscore_ref,
    dproj_ref,
    dspat_ref,
    dxk0_ref,
    dxk1_ref,
    dxs_ref,
    dsk0_ref,
    dsk1_ref,
    dss_ref,
    soft_ref,
    sems,
    *,
    heads,
    block,
):
    fetched = [
        pltpu.make_async_copy(soft_hbm.at[h], soft_ref.at[h], sems.at[h]) for h in range(heads)
    ]
    for copy in fetched:
        copy.start()
    length = 2 * datt_ref.shape[0]
    scale = DH**-0.5
    part = length // 4
    datt = stack_rows(
        [datt_ref[0:part, :], dattr_ref[0:part, :], datt_ref[part:, :], dattr_ref[part:, :]]
    )
    for h in range(heads):
        cols = slice(h * DH, (h + 1) * DH)
        value = proj_ref[2, :, cols]
        left = jnp.concatenate([proj_ref[0, :, cols], spat_ref[0, :, cols]], axis=1)
        right = jnp.concatenate([proj_ref[1, :, cols], spat_ref[1, :, cols]], axis=1)
        own = datt[:, cols]
        fetched[h].wait()
        for at in range(0, length, block):
            soft = soft_ref[h, at : at + block, :]
            dsoft = mm(own[at : at + block], value, NT)
            inner = jnp.sum(soft * dsoft, axis=-1, keepdims=True)
            dscore_ref[h, at : at + block, :] = (soft * (dsoft - inner)).astype(BF16)
        dscore = dscore_ref[h]
        dleft = (mm(dscore, right) * scale).astype(BF16)
        dright = (mm(dscore, left, TN) * scale).astype(BF16)
        dproj_ref[0, :, cols] = dleft[:, :DH]
        dspat_ref[0, :, cols] = dleft[:, DH:]
        dproj_ref[1, :, cols] = dright[:, :DH]
        dspat_ref[1, :, cols] = dright[:, DH:]
        dproj_ref[2, :, cols] = mm(soft_ref[h].astype(BF16), own, TN).astype(BF16)
    once = (p_ref[3] == 0).astype(F32)
    total = mm(dproj_ref[0], w_ref[0])
    for k in range(1, 3):
        total = total + mm(dproj_ref[k], w_ref[k])
    least = part // 4

    def deal(rows, refs):
        for y in range(2):
            for zh in range(2):
                for c in range(2):
                    for zl in range(2):
                        at = (((y * 2 + zh) * 2 + c) * 2 + zl) * least
                        to = (zh * 2 + y) * least
                        value = rows[at : at + least]
                        if zh == 0 and refs[0][0] is dxk0_ref:
                            of = ((y * 2 + c) * 2 + zl) * least
                            value = value + once * first_ref[of : of + least, :]
                        refs[c][zl][to : to + least, :] = value.astype(BF16)

    deal(total, ((dxk0_ref, dxk1_ref), (dxs_ref.at[0], dxs_ref.at[1])))
    total = mm(dspat_ref[0], ws_ref[0]) + mm(dspat_ref[1], ws_ref[1])
    deal(total, ((dsk0_ref, dsk1_ref), (dss_ref.at[0], dss_ref.at[1])))


def spatial_grad_kernel(p_ref, sp_ref, dspat_ref, keep_ref, send_ref):
    sp = sp_ref[...].reshape(-1, sp_ref.shape[-1])
    keep_ref[...] = mm(dspat_ref[p_ref[0]], sp, TN).astype(BF16)
    send_ref[...] = mm(dspat_ref[1 - p_ref[0]], sp, TN).astype(BF16)


def second_grad_kernel(
    p_ref,
    dmix_ref,
    pay_ref,
    payr_ref,
    payl_ref,
    payc_ref,
    paylc_ref,
    atto_ref,
    atts_ref,
    rest_ref,
    spk_ref,
    spr_ref,
    lines_ref,
    keep_ref,
    send_ref,
    second_ref,
):
    inner = spk_ref.shape[0]
    length = dmix_ref.shape[0]
    least = length // 8
    rest = 2 * least
    dmixo = stack_rows(
        [
            ref[y * least : (y + 1) * least, :]
            for y in range(2)
            for ref in (payr_ref, payl_ref, payc_ref, paylc_ref)
        ]
    )
    base = rest_ref.shape[0]
    second_ref[0:base, :] = rest_ref[...]
    second_ref[base : base + inner, :] = (
        mm(atto_ref[...], dmix_ref[...], TN) + mm(atts_ref[...], dmixo, TN)
    ).astype(BF16)
    base += inner
    second_ref[base : base + inner, :] = (
        spk_ref[...].astype(F32) + spr_ref[...].astype(F32)
    ).astype(BF16)
    base += inner
    small = pay_ref[rest:, :].astype(F32) + payr_ref[rest:, :].astype(F32)
    second_ref[base : base + 16, :] = small.astype(BF16)
    second_ref[base + 16 : base + 32, :] = lines_ref[...].astype(BF16)
    dealt(second_ref, p_ref[2], keep_ref, send_ref)


def first_grad_kernel(
    p_ref,
    x_ref,
    dscore_ref,
    dproj_ref,
    colidx_ref,
    bup_ref,
    keep_ref,
    send_ref,
    rest_ref,
    lines_ref,
    first_ref,
    *,
    heads,
):
    width = x_ref.shape[-1]
    x = x_ref[...].reshape(-1, width)
    length = x.shape[0]
    inner = dproj_ref.shape[-1]
    for k in range(3):
        first_ref[k * inner : (k + 1) * inner, :] = mm(dproj_ref[k], x, TN).astype(BF16)
    dealt(first_ref, p_ref[1], keep_ref, send_ref)
    rest_ref[...] = first_ref[2 * keep_ref.shape[0] :, :]
    lane = lax.broadcasted_iota(jnp.int32, (1, NBUCK), 1)
    found = []
    for kind in range(3):
        extent = length if kind == 0 else NBUCK
        own = colidx_ref[:, kind : kind + 1]
        level = lax.broadcasted_iota(jnp.int32, (length, extent), 1)
        chosen = (own == level).astype(BF16)
        place = own - HALF + lax.broadcasted_iota(jnp.int32, (length, NBUCK), 1)
        turn = place & (NBUCK - 1)
        piece = place >> 7
        for h in range(heads):
            spread = mm(dscore_ref[h], chosen)
            window = jnp.zeros((length, NBUCK), F32)
            for q in range(extent // NBUCK):
                part = jnp.take_along_axis(
                    spread[:, q * NBUCK : (q + 1) * NBUCK],
                    turn,
                    axis=1,
                    mode="promise_in_bounds",
                )
                window = window + jnp.where(piece == q, part, 0.0)
            row = jnp.sum(window, axis=0, keepdims=True)
            row = jnp.where((lane > 0) & (lane < NBUCK - 1), row, 0.0)
            least = jnp.sum(jnp.where(level <= own - HALF, spread, 0.0), axis=0, keepdims=True)
            most = jnp.sum(jnp.where(level >= own + HALF - 1, spread, 0.0), axis=0, keepdims=True)
            row = row + jnp.where(lane == 0, jnp.sum(least, axis=1, keepdims=True), 0.0)
            row = row + jnp.where(
                lane == NBUCK - 1, jnp.sum(most, axis=1, keepdims=True), 0.0
            )
            found.append(row)
    per = width // NBUCK
    found = found + [jnp.zeros((1, NBUCK), F32)] * (-len(found) % per)
    lines = [
        jnp.concatenate(found[at : at + per], axis=1) for at in range(0, len(found), per)
    ]
    lines.append(bup_ref[0:1, :])
    lines_ref[...] = jnp.concatenate(
        lines + [jnp.zeros((16 - len(lines), width), F32)], axis=0
    )


def ends_kernel(
    p_ref,
    w_ref,
    y_ref,
    zhw_ref,
    zlw_ref,
    zzw_ref,
    tok_ref,
    sp_ref,
    event_ref,
):
    c, y, block = p_ref[0], p_ref[2], p_ref[4] * 2 + p_ref[3]
    for turn, ref in enumerate((None, zlw_ref, zhw_ref, zzw_ref)):
        at = block ^ turn
        for far in range(2):
            for unit in range(3):
                if ref is None:
                    value = (y_ref if far else w_ref)[unit]
                else:
                    value = ref[far, unit]
                value = value.astype(F32)
                if unit < 2:
                    tok_ref[c ^ unit, y ^ far, at] = value
                else:
                    sp_ref[y ^ far, at] = value
    event_ref[...] = jnp.zeros_like(event_ref)


def out_kernel(p_ref, *refs):
    c, y, block = p_ref[0], p_ref[2], p_ref[4] * 2 + p_ref[3]
    out_ref, event_ref = refs[8:]
    least = out_ref.shape[3]
    for half in range(2):
        for far in range(2):
            for unit in range(2):
                ref = refs[half * 4 + far * 2 + unit]
                for turn in range(2):
                    at = block ^ (half * 2 + turn)
                    out_ref[c ^ unit, y ^ far, at] = ref[turn * least : (turn + 1) * least, :]
    event_ref[...] = jnp.zeros_like(event_ref)


def turn_kernel(p_ref, own_ref, far_ref, sum_ref, *, size):
    far = turned(far_ref[...], size).astype(F32)
    sum_ref[...] = (own_ref[...].astype(F32) + far).astype(BF16)


def plus_kernel(p_ref, *refs):
    count = len(refs) // 3
    for n in range(count):
        total = refs[2 * n][...].astype(F32) + refs[2 * n + 1][...].astype(F32)
        refs[2 * count + n][...] = total.astype(BF16)


def units_kernel(
    p_ref, own0_ref, own1_ref, other_ref, near_ref, far_ref, spat_ref, nears_ref, fars_ref
):
    nears_ref[0] = own0_ref[...]
    fars_ref[0] = own1_ref[...]
    nears_ref[1] = other_ref[0]
    fars_ref[1] = other_ref[1]
    nears_ref[2] = (near_ref[...].astype(F32) + spat_ref[0].astype(F32)).astype(BF16)
    fars_ref[2] = (far_ref[...].astype(F32) + spat_ref[1].astype(F32)).astype(BF16)


def fold_kernel(p_ref, own_ref, far_ref, keep_ref, send_ref):
    total = (own_ref[...].astype(F32) + far_ref[...].astype(F32)).astype(BF16)
    half = total.shape[-2] // 2
    keep_ref[...] = total[..., :half, :]
    send_ref[...] = total[..., half:, :]


def ends_first_kernel(p_ref, keep_ref, far_ref, mine_ref, other_ref):
    least = mine_ref.shape[1]
    total = (keep_ref[...].astype(F32) + far_ref[...].astype(F32)).astype(BF16)
    mine_ref[...] = total[:, :least]
    other_ref[...] = total[:, least:]


def spread_kernel(p_ref, *refs):
    c = p_ref[0]
    event_ref = refs[10]
    for n, out_ref in enumerate(refs[8:10]):
        side = p_ref[1 + n]
        for other in range(2):
            for far in range(2):
                out_ref[c ^ other, side ^ far] = refs[n * 4 + other * 2 + far][...].astype(F32)
    event_ref[...] = jnp.zeros_like(event_ref)


def last_kernel(
    p_ref,
    one0_ref,
    one1_ref,
    one2_ref,
    one3_ref,
    two0_ref,
    two1_ref,
    two2_ref,
    two3_ref,
    qkv_ref,
    spat_ref,
    exit_ref,
    tables_ref,
    gains_ref,
    shifts_ref,
    bup_ref,
    bdown_ref,
    second_ref,
    *,
    heads,
):
    c, head = p_ref[0], p_ref[4] * 2 + p_ref[3]
    inner = exit_ref.shape[1]
    width = exit_ref.shape[2]
    part = gains_ref.shape[2]
    per = width // NBUCK
    firsts = ((one0_ref, one1_ref), (one2_ref, one3_ref))
    seconds = ((two0_ref, two1_ref), (two2_ref, two3_ref))
    for other in range(2):
        s = c ^ other
        for far in range(2):
            size = one0_ref.shape[0]
            at = pl.multiple_of((p_ref[1] ^ far) * size, 16)
            qkv_ref[s, pl.ds(at, size), :] = firsts[other][far][...].astype(F32)
            size = two0_ref.shape[0]
            at = pl.multiple_of((p_ref[2] ^ far) * size, 16)
            second_ref[pl.ds(at, size), :] = seconds[other][far][...].astype(F32)
        base = 3 * inner - 2 * one0_ref.shape[0]
        qkv_ref[s, 2 * one0_ref.shape[0] :, :] = second_ref[0:base, :]
        exit_ref[s] = second_ref[base : base + inner, :]
        base += inner
        spat_ref[s] = second_ref[base : base + inner, :]
        base += inner
        sums = second_ref[base : base + 16, :]
        cut = sums[:, 0:part]
        for at in range(1, width // part):
            cut = jnp.where(head == at, sums[:, at * part : (at + 1) * part], cut)
        gains_ref[s] = jnp.concatenate([cut[0:1], cut[8:9]], axis=0)
        shifts_ref[s] = jnp.concatenate([cut[1:2], cut[9:10]], axis=0)
        bdown_ref[pl.ds(s, 1), :] = cut[10:11]
        lines = second_ref[base + 16 : base + 32, :]
        for n in range(3 * heads):
            at = (n % per) * NBUCK
            tables_ref[n // heads, n % heads, pl.ds(s, 1), :] = lines[
                n // per : n // per + 1, at : at + NBUCK
            ]
        bup_ref[pl.ds(s, 1), :] = lines[2:3]


def swap(value, axis, step=1):
    size = lax.axis_size(axis)
    return lax.ppermute(value, axis, [(i, i ^ step) for i in range(size)])


def swap_both(value):
    size = lax.axis_size("batch") * 2
    return lax.ppermute(value, ("batch", "y"), [(i, i ^ 3) for i in range(size)])


def added(left, right):
    return (left.astype(F32) + right.astype(F32)).astype(BF16)


def batch_steps():
    return [1 << bit for bit in range(lax.axis_size("batch").bit_length() - 1)]


def join(*values):
    return lax.optimization_barrier(values)


def shards(
    tokens,
    spatial,
    positions,
    boxes,
    query_key_value_weight,
    w_spatial,
    rel_tables,
    exit_matrix,
    ln_gains,
    ln_shifts,
    up_weight,
    hidden_bias,
    shrink_projection_array,
    b_down,
    cotangent,
):
    heads = rel_tables.shape[2]
    rows = tokens.shape[2]
    width = tokens.shape[3]
    inner = query_key_value_weight.shape[3]
    hidden = up_weight.shape[2]
    least = rows // 4
    rest = rows // 2
    length = 4 * rows
    half = length // 2
    page = lax.axis_index("y")
    core = lax.axis_index("core")
    zh = lax.axis_index("zh")
    zl = lax.axis_index("zl")
    pair = lax.axis_index("batch") & 1
    place = jnp.stack([core, pair, page, zl, zh]).astype(jnp.int32)

    def run(body, operands, outs, us=TICK, scratch=(), after=(), vmem=VMEM_BYTES):
        return kernel_call(body, place, operands, outs, us, scratch, after, vmem)

    def rows_of(count, dtype=BF16):
        return ((count, width), dtype)

    share = hidden // 4
    far0, far1, far2, near, x00, up_part, down_part = run(
        pack_kernel,
        [
            (tokens.reshape(2, 2, 4, least, width), "any"),
            (spatial.reshape(2, 4, least, width), "any"),
            (positions, "any"),
            (boxes, "any"),
            (exit_matrix, "any"),
            (up_weight, "any"),
            (shrink_projection_array, "any"),
            (hidden_bias, "any"),
        ],
        [
            rows_of(rows + 16),
            rows_of(rows),
            rows_of(rows),
            rows_of(2 * rows + 16),
            rows_of(rows),
            rows_of(share + 16 + inner // 4),
            rows_of(share),
        ],
        scratch=[
            pltpu.VMEM(positions.shape, jnp.int32),
            pltpu.VMEM(boxes.shape, jnp.int32),
            pltpu.VMEM(hidden_bias.shape, F32),
            pltpu.SemaphoreType.DMA((30,)),
        ],
        vmem=PACK_VMEM,
    )
    up_part = swap(up_part, "zh")
    i10, s10, x10 = swap(far0, "y"), swap(far1, "y"), swap(far2, "y")
    cot_far, cot_near, cot00 = run(
        cotangent_kernel,
        [(cotangent.reshape(2, 2, 4, least, width), "any")],
        [((2, rows, width), BF16), rows_of(rows), rows_of(rows)],
        scratch=[pltpu.SemaphoreType.DMA((16,))],
        vmem=PACK_VMEM,
        after=[x00],
    )
    n01 = swap(near, "core")
    weights = (jnp.swapaxes(query_key_value_weight, 2, 3), "stream")
    spatial_weights = jnp.swapaxes(w_spatial, 1, 2)
    x0, sp0, index0, proj0, spat0, up, down, exit_own = run(
        near_kernel,
        [
            x00,
            n01,
            near,
            weights,
            spatial_weights,
            (up_weight, "any"),
            (shrink_projection_array, "any"),
            (exit_matrix, "any"),
        ],
        [
            ((2, rows, width), BF16),
            ((2, rows, width), BF16),
            ((8, 2 * rows), jnp.int32),
            ((3, 2 * rows, inner), BF16),
            ((2, 2 * rows, inner), BF16),
            ((width, hidden), BF16),
            ((hidden, width), BF16),
            rows_of(inner),
        ],
        scratch=[pltpu.SemaphoreType.DMA((3,))],
        after=[cot00],
    )
    i10, s10, x10, x0, up_part, down_part = join(i10, s10, x10, x0, up_part, down_part)
    x11, s11 = swap(i10, "core"), swap(s10, "core")
    ups = [up_part, swap(up_part, "y"), swap(up_part, "batch"), swap_both(up_part)]
    down_part = swap(down_part, "zh")

    x, sp, colidx, proj, spat, soft, att_own, att_send = run(
        functools.partial(attention_kernel, heads=heads),
        [
            x10,
            x11,
            s10,
            s11,
            i10,
            x0,
            sp0,
            index0,
            proj0,
            spat0,
            weights,
            spatial_weights,
            (rel_tables, "stream"),
        ],
        [
            ((2, 2, rows, width), BF16),
            ((2, 2, rows, width), BF16),
            ((length, 8), jnp.int32),
            ((3, length, inner), BF16, "any"),
            ((2, length, inner), BF16, "any"),
            ((heads, length, length), F32, "any"),
            ((half, inner), BF16),
            ((half, inner), BF16),
        ],
        us=30,
        scratch=[
            pltpu.VMEM((length, inner), BF16),
            pltpu.VMEM((3, length, inner), BF16),
            pltpu.VMEM((2, length, inner), BF16),
            pltpu.VMEM((heads, length, length), F32),
            pltpu.SemaphoreType.DMA((2 + heads,)),
        ],
    )
    att_recv = swap(att_send, "zh")
    att_own, down_part, *ups = join(att_own, down_part, *ups)
    downs = [down_part, swap(down_part, "y"), swap(down_part, "batch"), swap_both(down_part)]

    keep, send, exit_partner = run(
        mixed_kernel,
        [att_own, att_recv, exit_own, *ups],
        [rows_of(rows, F32), rows_of(rows), rows_of(inner)],
    )
    (mixed0,) = run(
        plus_kernel, [keep, swap(send, "core")], [rows_of(rows)], after=downs[1:3]
    )
    mixed_zl = swap(mixed0, "zl")
    (mixed0,) = run(
        functools.partial(turn_kernel, size=least), [mixed0, mixed_zl], [rows_of(rows)]
    )
    mixed1 = swap(mixed0, "core")
    mixed_far0 = swap(mixed0, "zh")
    mixed1, *downs = join(mixed1, *downs)

    gains = (ln_gains, "stream")
    shifts = (ln_shifts, "stream")
    x_own = (x, (None, 0, None, None))
    x_far = (x, (None, 1, None, None))
    low, normed, active, slope, up_partner, down_partner = run(
        forward_kernel,
        [x_own, mixed0, mixed1, gains, shifts, up, hidden_bias, down, *ups, *downs],
        [
            rows_of(half),
            rows_of(half),
            ((2, half, hidden), BF16),
            ((2, half, hidden), BF16),
            ((width, hidden), BF16),
            ((hidden, width), BF16),
        ],
    )
    low_recv = swap(low, "zl")
    cot_far, cot_near, mixed0 = join(cot_far, cot_near, mixed0)
    cot10 = swap(cot_far, "y")
    cot01 = swap(cot_near, "core")
    mixed_far1 = swap(mixed_far0, "core")
    cot11 = swap(cot10, "core")
    (normed_far,) = run(
        first_norm_kernel,
        [x_far, mixed_far0, mixed_far1, gains, shifts],
        [rows_of(half)],
        after=[low],
    )
    active_far, slope_far = run(
        other_kernel,
        [normed_far, up, hidden_bias],
        [((half, hidden), BF16), ((half, hidden), BF16)],
    )
    low0, low1 = run(
        lowered_kernel, [low, low_recv], [rows_of(rows), rows_of(rows)], after=[slope_far]
    )
    far_low0 = swap(low0, "zh")

    def finish(x_half, pieces, part, after=()):
        rows_part = slice(part * rest, (part + 1) * rest)
        cots = [
            cot00[rows_part],
            cot10[0, rows_part],
            cot01[rows_part],
            cot11[1, rows_part],
        ]
        return run(
            final_kernel,
            [x_half, *pieces, *cots, gains, shifts, b_down],
            [
                ((2, rest, width), BF16),
                ((2, rest, width), BF16),
                rows_of(half, F32),
                rows_of(half),
                rows_of(8, F32),
            ],
            after=after,
        )

    out_keep, out_send, second, dlow, sums_two = finish(x_own, [mixed0, mixed1, low0, low1], 0)
    hid, dup = run(
        middle_kernel,
        [dlow, up, down, up_partner, down_partner, slope],
        [rows_of(half), ((half, hidden), BF16)],
    )
    hid_recv = swap(hid, "zl")
    up_own, down_own, bias_own = run(
        ffn_own_kernel,
        [normed, (active, (0, None, None)), dlow, dup],
        [((width, hidden), F32), rows_of(hidden, F32), ((8, hidden), F32)],
        after=[hid],
    )
    out_core = swap(out_send, "core")
    out_y = swap(jnp.stack([out_keep[1], out_core[1]]), "y")
    hid_recv, far_low0, out_y = join(hid_recv, far_low0, out_y)
    far_low1 = swap(far_low0, "zl")
    first, dmix, sums_one = run(
        first_kernel,
        [x_own, mixed0, mixed1, second, hid, hid_recv, gains],
        [rows_of(half, F32), rows_of(half), rows_of(8, F32)],
        after=[bias_own],
    )
    dmix_core = swap(dmix, "core")
    datt, datt_send, dmix, pay = run(
        attended_kernel,
        [dmix, dmix_core, exit_own, exit_partner, sums_one, sums_two],
        [
            ((half, inner), BF16),
            ((half, inner), BF16),
            rows_of(half),
            rows_of(rest + 16),
        ],
    )
    datt_recv = swap(datt_send, "zh")
    far_keep, far_send, _, dlow_far, _ = finish(
        x_far, [mixed_far0, mixed_far1, far_low0, far_low1], 1, [datt]
    )
    up_keep, up_send, down_keep, down_send, bias_grad = run(
        ffn_grad_kernel,
        [
            up_own,
            down_own,
            bias_own,
            normed_far,
            active_far,
            dlow_far,
            slope_far,
            down,
        ],
        [
            ((width // 2, hidden), BF16),
            ((width // 2, hidden), BF16),
            rows_of(hidden // 2),
            rows_of(hidden // 2),
            ((8, hidden), F32),
        ],
        us=30,
        scratch=[pltpu.VMEM((width, hidden), BF16)],
        after=[datt],
    )
    up_recv = swap(up_send, "batch")
    down_recv = swap(down_send, "y")
    datt_recv, pay = join(datt_recv, pay)
    pay_recv = swap(pay, "zh")
    piece = rows_of(rows)
    dscore, dproj, dspat, dxk0, dxk1, dxs, dsk0, dsk1, dss = run(
        functools.partial(backward_kernel, heads=heads, block=128),
        [datt, datt_recv, first, (soft, "any"), proj, spat, weights, spatial_weights],
        [
            ((heads, length, length), BF16),
            ((3, length, inner), BF16),
            ((2, length, inner), BF16),
            piece,
            piece,
            ((2, rows, width), BF16),
            piece,
            piece,
            ((2, rows, width), BF16),
        ],
        us=30,
        scratch=[pltpu.VMEM((heads, length, length), F32), pltpu.SemaphoreType.DMA((heads,))],
        after=[bias_grad],
    )

    steps = batch_steps()[1:]

    def plus(pairs, after=(), over_batch=False):
        sums = run(
            plus_kernel,
            [array for pair_of in pairs for array in pair_of],
            [(left.shape, BF16) for left, _ in pairs],
            after=after,
        )
        if over_batch:
            for step in steps:
                sums = [added(value, swap(value, "batch", step)) for value in sums]
        return sums

    dxk1, dxs, dss, pay_recv = join(dxk1, dxs, dss, pay_recv)
    dxs, dss = swap(dxs, "core"), swap(dss, "core")
    near, far = run(
        units_kernel,
        [dxk0, dxk1, dxs, dsk0, dsk1, dss],
        [((3, rows, width), BF16), ((3, rows, width), BF16)],
    )
    far_zl = swap(far, "zl")
    up_half, down_half = plus([(up_keep, up_recv), (down_keep, down_recv)], after=[far])
    up_other = swap(up_half, "y")
    down_other = swap(down_half, "batch")
    pay_zl = swap(join(pay_recv, far)[0], "zl")
    few = inner // 2
    main = 3 * inner - few
    sp_keep, sp_send = run(
        spatial_grad_kernel, [sp, dspat], [rows_of(inner), rows_of(inner)], after=[up_half]
    )
    sp_recv = swap(sp_send, "core")
    one_keep, one_send, value_rest, lines = run(
        functools.partial(first_grad_kernel, heads=heads),
        [x, dscore, dproj, colidx, bias_grad],
        [rows_of(main // 2), rows_of(main // 2), rows_of(few), rows_of(16, F32)],
        scratch=[pltpu.VMEM((3 * inner, width), BF16)],
        after=[sp_keep],
    )
    keep, send = run(
        fold_kernel,
        [near, far_zl],
        [((3, rest, width), BF16), ((3, rest, width), BF16)],
        after=[lines],
    )
    send_zh = swap(send, "zh")
    up_half, down_half = plus(
        [(up_half, up_other), (down_half, down_other)], after=[send], over_batch=True
    )
    up_far = swap(up_half, "batch")
    down_far = swap(down_half, "y")
    mine, other = run(
        ends_first_kernel,
        [keep, send_zh],
        [((3, least, width), BF16), ((3, least, width), BF16)],
        after=[up_half],
    )
    got = swap(other, "y")
    pay_recv, pay_zl, far_send, mine = join(pay_recv, pay_zl, far_send, mine)
    pay_core, pay_zlcore = swap(pay_recv, "core"), swap(pay_zl, "core")
    far_core = swap(far_send, "core")
    base = few + 2 * inner + 32
    two_keep, two_send = run(
        second_grad_kernel,
        [
            dmix,
            pay,
            pay_recv,
            pay_zl,
            pay_core,
            pay_zlcore,
            att_own,
            att_send,
            value_rest,
            sp_keep,
            sp_recv,
            lines,
        ],
        [rows_of(base // 2), rows_of(base // 2)],
        scratch=[pltpu.VMEM((base, width), BF16)],
        after=[mine, up_far, down_far],
    )
    one_send, two_send, got, two_keep = join(one_send, two_send, got, two_keep)
    one_recv = swap(one_send, "batch")
    two_recv = swap(two_send, "y")
    pages = jnp.stack([mine, got])
    pages_zh = swap(pages, "zh")
    pages_zl = swap(pages, "zl")
    *halves, pages = join(up_half, up_far, down_half, down_far, pages)
    others = [swap(value, "core") for value in halves]
    grad_up, grad_down, spread_event = run(
        spread_kernel,
        halves[:2] + others[:2] + halves[2:] + others[2:],
        [
            ((2, 2, width // 2, hidden), F32),
            ((2, 2, hidden // 2, width), F32),
            ((8, NBUCK), F32),
        ],
        after=[pages],
    )
    one_half, two_half = plus(
        [(one_keep, one_recv), (two_keep, two_recv)], after=[spread_event]
    )
    one_other = swap(one_half, "y")
    two_other = swap(two_half, "batch")
    far_y = swap(jnp.stack([far_keep[1], far_core[1]]), "y")
    pages_zh, pages_zl = join(pages_zh, pages_zl)
    pages_zz = swap(pages_zh, "zl")
    one_half, two_half = plus(
        [(one_half, one_other), (two_half, two_other)],
        after=[pages_zz],
        over_batch=True,
    )
    one_far = swap(one_half, "batch")
    two_far = swap(two_half, "y")
    grad_tokens, grad_spatial, ends_event = run(
        ends_kernel,
        [mine, got, pages_zh, pages_zl, pages_zz],
        [((2, 2, 4, least, width), F32), ((2, 4, least, width), F32), ((8, NBUCK), F32)],
        after=[one_half],
    )
    output, out_event = run(
        out_kernel,
        [
            out_keep[0],
            out_core[0],
            out_y[0],
            out_y[1],
            far_keep[0],
            far_core[0],
            far_y[0],
            far_y[1],
        ],
        [((2, 2, 4, least, width), BF16), ((8, NBUCK), F32)],
        after=[one_half],
    )
    one_far, two_far, out_event, ends_event = join(one_far, two_far, out_event, ends_event)
    halves = [one_half, one_far, two_half, two_far]
    others = [swap(value, "core") for value in halves]
    part = width // (2 * lax.axis_size("zh"))
    grad_qkv, grad_spatial_w, grad_exit, tables, gains_grad, shifts_grad, grad_b_up, grad_b_down = run(
        functools.partial(last_kernel, heads=heads),
        halves[:2] + others[:2] + halves[2:] + others[2:],
        [
            ((2, 3 * inner, width), F32),
            ((2, inner, width), F32),
            ((2, inner, width), F32),
            ((3, heads, 2, NBUCK), F32),
            ((2, 2, part), F32),
            ((2, 2, part), F32),
            ((2, hidden), F32),
            ((2, part), F32),
        ],
        scratch=[pltpu.VMEM((base, width), F32)],
        after=[spread_event, out_event, ends_event],
    )
    return (
        output.reshape(tokens.shape),
        grad_tokens.reshape(tokens.shape),
        grad_spatial.reshape(spatial.shape),
        grad_qkv.reshape(2, 3, inner, width).swapaxes(2, 3),
        grad_spatial_w.reshape(2, inner, width).swapaxes(1, 2),
        tables.transpose(2, 0, 1, 3),
        grad_exit,
        gains_grad,
        shifts_grad,
        grad_up.reshape(2, width, hidden),
        grad_b_up,
        grad_down.reshape(2, hidden, width),
        grad_b_down,
    )


def solution(mesh):
    batch, seq, head = mesh.devices.shape
    fine = Mesh(
        mesh.devices.reshape(batch, seq // 2, 2, head // 2, 2),
        ("batch", "y", "core", "zh", "zl"),
    )
    seq = ("y", "core")
    head = ("zh", "zl")
    return jax.shard_map(
        shards,
        mesh=fine,
        in_specs=(
            P(None, "batch", seq, None),
            P("batch", seq, None),
            P("batch", seq),
            P(None, "batch", seq),
            P(None, None, None, head),
            P(None, None, head),
            P(None, None, head, None),
            P(None, head, None),
            P(),
            P(),
            P(None, None, head),
            P(None, head),
            P(None, head, None),
            P(),
            P(None, "batch", seq, None),
        ),
        out_specs=(
            P(None, "batch", seq, None),
            P(None, "batch", seq, None),
            P("batch", seq, None),
            P(None, None, None, head),
            P(None, None, head),
            P(None, None, head, None),
            P(None, head, None),
            P(None, None, head),
            P(None, None, head),
            P(None, None, head),
            P(None, head),
            P(None, head, None),
            P(None, head),
        ),
        check_vma=False,
    )
```

```python
import functools

import jax
import jax.numpy as jnp
from jax import lax
from jax.experimental import pallas as pl
from jax.experimental.pallas import tpu as pltpu
from jax.sharding import Mesh, PartitionSpec as P

DH = 64
NBUCK = 128
HALF = 64
EPSILON = 1e-05
F32 = jnp.float32
BF16 = jnp.bfloat16
VMEM_BYTES = 20 * 1024 * 1024
TIMES = (
    0.1, 2, 0.02, 30.0, 0.1, 0.1, 0.1, 0.1, 4, 0.1, 0.02,
    0.1, 0.1, 0.1, 0.1, 0.1, 8, 30.0, 30.0, 0.1, 0.1, 30,
    0.1, 0.1, 8, 0.1, 0.1, 0.1, 0.5, 0.1, 0.1, 0.1, 0.1,
)
PACK_VMEM = 60 * 1024 * 1024
NN = (((1,), (0,)), ((), ()))
NT = (((1,), (1,)), ((), ()))
TN = (((0,), (0,)), ((), ()))


def mm(left, right, dims=NN):
    return lax.dot_general(left, right, dims, preferred_element_type=F32)


def kernel_call(body, place, operands, outs, us, scratch=(), after=(), vmem=VMEM_BYTES):
    specs, arrays, hows = [], [], []
    for operand in operands:
        array, how = operand if isinstance(operand, tuple) else (operand, None)
        specs.append(pl.BlockSpec(memory_space=pltpu.HBM if how == "any" else pltpu.VMEM))
        arrays.append(array)
        hows.append(how)
    count = len(arrays)
    specs += [pl.BlockSpec(memory_space=pl.ANY)] * len(after)

    def view(s_ref, ref, how):
        if how == "stream":
            return ref.at[s_ref[0]]
        if how is None or how == "any":
            return ref
        return ref.at[tuple(slice(None) if at is None else at for at in how)]

    def kernel(s_ref, *refs):
        given = [view(s_ref, ref, how) for ref, how in zip(refs, hows)]
        body(s_ref, *given, *refs[count + len(after) :])

    return pl.pallas_call(
        kernel,
        out_shape=[jax.ShapeDtypeStruct(out[0], out[1]) for out in outs],
        in_specs=[pl.BlockSpec(memory_space=pltpu.SMEM)] + specs,
        out_specs=[
            pl.BlockSpec(memory_space=pltpu.HBM if len(out) > 2 else pltpu.VMEM) for out in outs
        ],
        scratch_shapes=list(scratch),
        compiler_params=pltpu.CompilerParams(vmem_limit_bytes=vmem),
        cost_estimate=pl.CostEstimate(
            flops=int(us * 1.1e9), bytes_accessed=int(us * 3.5e6), transcendentals=0
        ),
    )(place, *arrays, *after)


def centred(rows):
    centre = rows - jnp.mean(rows, axis=-1, keepdims=True)
    spread = lax.rsqrt(jnp.mean(centre * centre, axis=-1, keepdims=True) + EPSILON)
    return centre * spread, spread


def norm_back(unit, spread, tilted):
    return spread * (
        tilted
        - jnp.mean(tilted, axis=-1, keepdims=True)
        - unit * jnp.mean(tilted * unit, axis=-1, keepdims=True)
    )


def pick(table_row, index):
    width = index.shape[1]
    table = jnp.broadcast_to(table_row, (index.shape[0], NBUCK))
    parts = [
        jnp.take_along_axis(
            table,
            index[:, at : at + NBUCK],
            axis=1,
            mode="promise_in_bounds",
        )
        for at in range(0, width, NBUCK)
    ]
    return jnp.concatenate(parts, axis=1)


def stack_rows(pieces):
    return jnp.concatenate(pieces, axis=0)


def turned(rows, size):
    pieces = [rows[at : at + size] for at in range(0, rows.shape[0], size)]
    return stack_rows([pieces[i ^ 1] for i in range(len(pieces))])


def residual(x_ref, mixed_refs):
    rest = mixed_refs[0].shape[0] // 2
    pieces = []
    for y in range(2):
        for c in range(2):
            own = x_ref[y, c * rest : (c + 1) * rest, :].astype(F32)
            pieces.append(own + mixed_refs[c][y * rest : (y + 1) * rest, :].astype(F32))
    return stack_rows(pieces)


def dealt(rows_ref, side, keep_ref, send_ref):
    half = keep_ref.shape[0]
    keep_ref[...] = rows_ref[pl.ds(pl.multiple_of(side * half, 16), half), :]
    send_ref[...] = rows_ref[pl.ds(pl.multiple_of((1 - side) * half, 16), half), :]


def gathered(place_ref, refs, rows, to_ref):
    size = rows.stop - rows.start
    for turn, ref in enumerate(refs):
        q = (place_ref[1] ^ (turn // 2)) * 2 + (place_ref[2] ^ (turn % 2))
        to_ref[pl.ds(pl.multiple_of(q * size, 16), size), :] = ref[rows, :]


def copied(pairs, sems):
    started = [
        pltpu.make_async_copy(source, target, sems.at[n])
        for n, (source, target) in enumerate(pairs)
    ]
    for copy in started:
        copy.start()
    return started


def pack_kernel(
    p_ref,
    tok_ref,
    sp_ref,
    pos_ref,
    box_ref,
    exit_ref,
    up_ref,
    down_ref,
    bias_ref,
    far0_ref,
    far1_ref,
    far2_ref,
    near_ref,
    own_ref,
    ups_ref,
    downs_ref,
    posv_ref,
    boxv_ref,
    biasv_ref,
    sems,
):
    c, y, zl, zh = p_ref[0], p_ref[2], p_ref[3], p_ref[4]
    block = zh * 2 + zl
    least = tok_ref.shape[3]
    rows = 4 * least
    q = p_ref[1] * 2 + y
    many = down_ref.shape[1] // 4
    few = exit_ref.shape[1] // 4
    pairs = [
        (pos_ref, posv_ref),
        (box_ref, boxv_ref),
        (bias_ref, biasv_ref),
        (up_ref.at[c, pl.ds(pl.multiple_of(q * many, 16), many)], ups_ref.at[pl.ds(0, many)]),
        (
            exit_ref.at[c, pl.ds(pl.multiple_of(q * few, 16), few)],
            ups_ref.at[pl.ds(many + 16, few)],
        ),
        (down_ref.at[c, pl.ds(pl.multiple_of(q * many, 16), many)], downs_ref),
    ]
    for k in range(4):
        at = block ^ k
        to = pl.ds(k * least, least)
        pairs += [
            (tok_ref.at[1 - c, 1 - y, at], far0_ref.at[to]),
            (sp_ref.at[1 - y, at], far1_ref.at[to]),
            (tok_ref.at[c, 1 - y, at], far2_ref.at[to]),
            (tok_ref.at[1 - c, y, at], near_ref.at[to]),
            (sp_ref.at[y, at], near_ref.at[pl.ds(rows + k * least, least)]),
            (tok_ref.at[c, y, at], own_ref.at[to]),
        ]
    started = copied(pairs, sems)
    for copy in started[:3]:
        copy.wait()
    left = biasv_ref[pl.ds(c, 1), :]
    lines = []
    for _ in range(3):
        lines.append(left.astype(BF16).astype(F32))
        left = left - lines[-1]
    lines.append(jnp.zeros((13, left.shape[1]), F32))
    ups_ref[many : many + 16, :] = jnp.concatenate(lines, axis=0).astype(BF16)
    lane = lax.broadcasted_iota(jnp.int32, (8, NBUCK), 1)
    width = far0_ref.shape[1]
    for page, ref, at in ((1 - y, far0_ref, rows), (y, near_ref, 2 * rows)):
        place = posv_ref[pl.ds(page, 1), :]
        lines = [
            place & 255,
            place >> 8,
            boxv_ref[0, pl.ds(page, 1), :],
            boxv_ref[1, pl.ds(page, 1), :],
        ]
        value = jnp.concatenate(lines + [jnp.zeros((4, NBUCK), jnp.int32)], axis=0)
        crossed = jnp.where(
            (lane & 63) < 32, pltpu.roll(value, NBUCK - 32, 1), pltpu.roll(value, 32, 1)
        )
        value = jnp.where(zl == 0, value, crossed)
        value = jnp.where(zh == 0, value, pltpu.roll(value, 64, 1))
        value = jnp.concatenate([value.astype(F32), jnp.zeros((8, NBUCK), F32)], axis=0)
        ref[at : at + 16, 0:NBUCK] = value.astype(BF16)
        ref[at : at + 16, NBUCK:] = jnp.zeros((16, width - NBUCK), BF16)
    for copy in started[3:]:
        copy.wait()


def cotangent_kernel(p_ref, cot_ref, far_ref, near_ref, own_ref, sems):
    c, y, block = p_ref[0], p_ref[2], p_ref[4] * 2 + p_ref[3]
    least = cot_ref.shape[3]
    pairs = []
    for k in range(4):
        at = block ^ k
        to = pl.ds(k * least, least)
        pairs += [
            (cot_ref.at[c, 1 - y, at], far_ref.at[0, to]),
            (cot_ref.at[1 - c, 1 - y, at], far_ref.at[1, to]),
            (cot_ref.at[1 - c, y, at], near_ref.at[to]),
            (cot_ref.at[c, y, at], own_ref.at[to]),
        ]
    for copy in copied(pairs, sems):
        copy.wait()


def indices(ref, at):
    lines = ref[at : at + 16, 0:NBUCK].astype(F32).astype(jnp.int32)
    place = lines[0:1] + lines[1:2] * 256
    return jnp.concatenate([place, lines[2:4], jnp.zeros((5, NBUCK), jnp.int32)], axis=0)


def two_cores(index0, index1, half):
    lane = lax.broadcasted_iota(jnp.int32, (8, NBUCK), 1)
    if half == 0:
        return jnp.where(lane < 64, index0, pltpu.roll(index1, 64, 1))
    return jnp.where(lane < 64, pltpu.roll(index0, 64, 1), index1)


def arrange(x0_ref, x1_ref, s0_ref, s1_ref, i0_ref, i1_ref, at, x_ref, sp_ref):
    least = x_ref.shape[1]
    rest = least // 2
    found = []
    index0, index1 = indices(i0_ref, at), indices(i1_ref, at)
    for half in range(2):
        at = half * rest
        x_ref[half, 0:rest, :] = x0_ref[at : at + rest, :]
        x_ref[half, rest:, :] = x1_ref[at : at + rest, :]
        sp_ref[half, 0:rest, :] = s0_ref[at : at + rest, :]
        sp_ref[half, rest:, :] = s1_ref[at : at + rest, :]
        found.append(two_cores(index0, index1, half))
    return found


def project(x_ref, sp_ref, w_ref, ws_ref, proj_ref, spat_ref, at):
    width = x_ref.shape[-1]
    x = x_ref[...].reshape(-1, width)
    sp = sp_ref[...].reshape(-1, width)
    rows = slice(at, at + x.shape[0])
    for k in range(3):
        proj_ref[k, rows, :] = mm(x, w_ref[k], NT).astype(BF16)
    for k in range(2):
        spat_ref[k, rows, :] = mm(sp, ws_ref[k], NT).astype(BF16)


def near_kernel(
    p_ref,
    x00_ref,
    n01_ref,
    n00_ref,
    w_ref,
    ws_ref,
    up_hbm,
    down_hbm,
    exit_hbm,
    x_ref,
    sp_ref,
    index_ref,
    proj_ref,
    spat_ref,
    up_ref,
    down_ref,
    exit_ref,
    sems,
):
    fetched = [
        pltpu.make_async_copy(source.at[p_ref[0]], target, sems.at[n])
        for n, (source, target) in enumerate(
            ((exit_hbm, exit_ref), (up_hbm, up_ref), (down_hbm, down_ref))
        )
    ]
    for copy in fetched:
        copy.start()
    least = x_ref.shape[1]
    found = arrange(
        x00_ref,
        n01_ref,
        n00_ref.at[least:],
        n01_ref.at[least:],
        n00_ref,
        n01_ref,
        2 * least,
        x_ref,
        sp_ref,
    )
    index_ref[...] = jnp.concatenate(found, axis=1)
    project(x_ref, sp_ref, w_ref, ws_ref, proj_ref, spat_ref, 0)
    for copy in fetched:
        copy.wait()


def attention_kernel(
    p_ref,
    x10_ref,
    x11_ref,
    s10_ref,
    s11_ref,
    i10_ref,
    x0_ref,
    sp0_ref,
    index_ref,
    proj0_ref,
    spat0_ref,
    w_ref,
    ws_ref,
    table_ref,
    x_ref,
    sp_ref,
    colidx_ref,
    proj_hbm,
    spat_hbm,
    soft_hbm,
    own_ref,
    send_ref,
    att_ref,
    proj_ref,
    spat_ref,
    soft_ref,
    sems,
    *,
    heads,
):
    least = x_ref.shape[2]
    near = 2 * least
    x_ref[0] = x0_ref[...]
    sp_ref[0] = sp0_ref[...]
    proj_ref[:, 0:near, :] = proj0_ref[...]
    spat_ref[:, 0:near, :] = spat0_ref[...]
    found = arrange(
        x10_ref, x11_ref, s10_ref, s11_ref, i10_ref, x11_ref, least, x_ref.at[1], sp_ref.at[1]
    )
    places = jnp.concatenate([index_ref[...]] + found, axis=1)
    colidx_ref[...] = jnp.transpose(places.astype(F32)).astype(jnp.int32)
    project(x_ref.at[1], sp_ref.at[1], w_ref, ws_ref, proj_ref, spat_ref, near)
    length = 2 * near
    stored = [
        pltpu.make_async_copy(proj_ref, proj_hbm, sems.at[0]),
        pltpu.make_async_copy(spat_ref, spat_hbm, sems.at[1]),
    ]
    for copy in stored:
        copy.start()
    level = lax.broadcasted_iota(jnp.int32, (length, NBUCK), 1)
    chosen = [(colidx_ref[:, kind : kind + 1] == level).astype(BF16) for kind in (1, 2)]
    chosen = jnp.concatenate(chosen, axis=1)

    lane = lax.broadcasted_iota(jnp.int32, (length, NBUCK), 1)
    boxes = [
        jnp.clip(lane - colidx_ref[:, kind : kind + 1], -HALF, HALF - 1) + HALF
        for kind in (1, 2)
    ]
    index = jnp.clip(places[0:1, :] - colidx_ref[:, 0:1], -HALF, HALF - 1) + HALF
    for h in range(heads):
        cols = slice(h * DH, (h + 1) * DH)
        bias = jnp.concatenate(
            [pick(table_ref[k, h : h + 1, :], boxes[k - 1]) for k in (1, 2)], axis=1
        )
        coarse = bias.astype(BF16)
        fine = (bias - coarse.astype(F32)).astype(BF16)
        left = jnp.concatenate(
            [proj_ref[0, :, cols], spat_ref[0, :, cols]], axis=1
        ) * jnp.asarray(DH**-0.5, BF16)
        right = jnp.concatenate([proj_ref[1, :, cols], spat_ref[1, :, cols]], axis=1)
        scores = mm(
            jnp.concatenate([left, coarse, fine], axis=1),
            jnp.concatenate([right, chosen, chosen], axis=1),
            NT,
        ) + pick(table_ref[0, h : h + 1, :], index)
        top = jnp.max(scores, axis=-1, keepdims=True)
        raised = jnp.exp(scores - top)
        soft = raised * (1.0 / jnp.sum(raised, axis=-1, keepdims=True))
        soft_ref[h] = soft
        stored.append(pltpu.make_async_copy(soft_ref.at[h], soft_hbm.at[h], sems.at[2 + h]))
        stored[-1].start()
        att_ref[:, cols] = mm(soft.astype(BF16), proj_ref[2, :, cols]).astype(BF16)
    for copy in stored:
        copy.wait()
    part = length // 4
    own_ref[0:part, :] = att_ref[0:part, :]
    own_ref[part:, :] = att_ref[2 * part : 3 * part, :]
    send_ref[0:part, :] = att_ref[part : 2 * part, :]
    send_ref[part:, :] = att_ref[3 * part :, :]


def mixed_kernel(
    p_ref,
    own_ref,
    recv_ref,
    exit_ref,
    one0_ref,
    one1_ref,
    one2_ref,
    one3_ref,
    keep_ref,
    send_ref,
    partner_ref,
):
    rows = slice(one0_ref.shape[0] - exit_ref.shape[0] // 4, one0_ref.shape[0])
    gathered(p_ref, (one0_ref, one1_ref, one2_ref, one3_ref), rows, partner_ref)
    total = mm(own_ref[...], exit_ref[...]) + mm(recv_ref[...], partner_ref[...])
    rest = total.shape[0] // 4
    for y in range(2):
        at = 2 * y * rest
        keep_ref[y * rest : (y + 1) * rest, :] = total[at : at + rest]
        send_ref[y * rest : (y + 1) * rest, :] = total[at + rest : at + 2 * rest].astype(BF16)


def gelu_parts(upper):
    phi = 0.5 * (1.0 + lax.erf(upper * (0.5**0.5)))
    slope = phi + upper * (jnp.exp(-0.5 * upper * upper) * (0.5 / jnp.pi) ** 0.5)
    return (upper * phi).astype(BF16), slope


def forward_kernel(
    p_ref,
    x_ref,
    mixed0_ref,
    mixed1_ref,
    gain_ref,
    shift_ref,
    up_ref,
    hidden_ref,
    down_ref,
    one0_ref,
    one1_ref,
    one2_ref,
    one3_ref,
    two0_ref,
    two1_ref,
    two2_ref,
    two3_ref,
    low_ref,
    normed_ref,
    active_ref,
    slope_ref,
    upp_ref,
    downp_ref,
):
    many = two0_ref.shape[0]
    gathered(p_ref, (one0_ref, one1_ref, one2_ref, one3_ref), slice(0, many), upp_ref)
    gathered(p_ref, (two0_ref, two1_ref, two2_ref, two3_ref), slice(0, many), downp_ref)
    extra = one0_ref[many : many + 16, :].astype(F32)
    partner_bias = extra[0:1] + extra[1:2] + extra[2:3]
    unit, _ = centred(residual(x_ref, (mixed0_ref, mixed1_ref)))
    normed_low = (unit * gain_ref[0:1, :] + shift_ref[0:1, :]).astype(BF16)
    normed_ref[...] = normed_low
    active, slope = gelu_parts(mm(normed_low, up_ref[...]) + hidden_ref[pl.ds(p_ref[0], 1), :])
    active_ref[0] = active
    slope_ref[0] = slope.astype(BF16)
    total = mm(active, down_ref[...])
    active, slope = gelu_parts(mm(normed_low, upp_ref[...]) + partner_bias)
    active_ref[1] = active
    slope_ref[1] = slope.astype(BF16)
    low_ref[...] = (total + mm(active, downp_ref[...])).astype(BF16)


def other_kernel(
    p_ref,
    normed_ref,
    up_ref,
    hidden_ref,
    active_ref,
    slope_ref,
):
    active, slope = gelu_parts(
        mm(normed_ref[...], up_ref[...]) + hidden_ref[pl.ds(p_ref[0], 1), :]
    )
    active_ref[...] = active
    slope_ref[...] = slope.astype(BF16)


def first_norm_kernel(p_ref, x_ref, mixed0_ref, mixed1_ref, gain_ref, shift_ref, normed_ref):
    unit, _ = centred(residual(x_ref, (mixed0_ref, mixed1_ref)))
    normed_ref[...] = (unit * gain_ref[0:1, :] + shift_ref[0:1, :]).astype(BF16)


def lowered_kernel(p_ref, own_ref, far_ref, low0_ref, low1_ref):
    least = own_ref.shape[0] // 8
    total = own_ref[...].astype(F32) + turned(far_ref[...], least).astype(F32)
    total = total.astype(BF16)
    for i in range(4):
        low0_ref[i * least : (i + 1) * least, :] = total[2 * i * least : (2 * i + 1) * least]
        low1_ref[i * least : (i + 1) * least, :] = total[(2 * i + 1) * least : (2 * i + 2) * least]


def final_kernel(
    p_ref,
    x_ref,
    mixed0_ref,
    mixed1_ref,
    low0_ref,
    low1_ref,
    cot00_ref,
    cot10_ref,
    cot01_ref,
    cot11_ref,
    gain_ref,
    shift_ref,
    bdown_ref,
    outk_ref,
    outs_ref,
    second_ref,
    dlow_ref,
    sums_ref,
):
    unit, _ = centred(residual(x_ref, (mixed0_ref, mixed1_ref)))
    normed = unit * gain_ref[0:1, :] + shift_ref[0:1, :]
    least = low0_ref.shape[0] // 4
    pieces = []
    for i in range(4):
        pieces.append(low0_ref[i * least : (i + 1) * least, :])
        pieces.append(low1_ref[i * least : (i + 1) * least, :])
    lowered = stack_rows(pieces).astype(F32)
    unit2, spread2 = centred(normed + lowered + bdown_ref[pl.ds(p_ref[0], 1), :])
    out = (unit2 * gain_ref[1:2, :] + shift_ref[1:2, :]).astype(BF16)
    for y in range(2):
        at = 4 * y * least
        outk_ref[y] = out[at : at + 2 * least]
        outs_ref[y] = out[at + 2 * least : at + 4 * least]
    cot = stack_rows([cot00_ref[...], cot01_ref[...], cot10_ref[...], cot11_ref[...]]).astype(F32)
    second = norm_back(unit2, spread2, cot * gain_ref[1:2, :])
    second_ref[...] = second
    dlow_ref[...] = second.astype(BF16)
    sums_ref[...] = jnp.zeros_like(sums_ref)
    sums_ref[0:1, :] = jnp.sum(cot * unit2, axis=0, keepdims=True)
    sums_ref[1:2, :] = jnp.sum(cot, axis=0, keepdims=True)
    sums_ref[2:3, :] = jnp.sum(second, axis=0, keepdims=True)


def middle_kernel(
    p_ref,
    dlow_ref,
    up_ref,
    down_ref,
    upp_ref,
    downp_ref,
    slope_ref,
    hid_ref,
    dup_ref,
):
    dlow = dlow_ref[...]
    dup = (mm(dlow, down_ref[...], NT) * slope_ref[0].astype(F32)).astype(BF16)
    dup_ref[...] = dup
    total = mm(dup, up_ref[...], NT)
    dup = (mm(dlow, downp_ref[...], NT) * slope_ref[1].astype(F32)).astype(BF16)
    hid_ref[...] = (total + mm(dup, upp_ref[...], NT)).astype(BF16)


def ffn_own_kernel(p_ref, normed_ref, active_ref, dlow_ref, dup_ref, up_ref, down_ref, bias_ref):
    dup = dup_ref[...]
    up_ref[...] = mm(normed_ref[...], dup, TN)
    down_ref[...] = mm(active_ref[...], dlow_ref[...], TN)
    bias = jnp.sum(dup.astype(F32), axis=0, keepdims=True)
    bias_ref[...] = jnp.broadcast_to(bias, bias_ref.shape)


def ffn_grad_kernel(
    p_ref,
    upa_ref,
    downa_ref,
    biasa_ref,
    normedo_ref,
    activeo_ref,
    dlowo_ref,
    slopeo_ref,
    down_ref,
    upk_ref,
    ups_ref,
    downk_ref,
    downs_ref,
    bias_ref,
    all_ref,
):
    dlowo = dlowo_ref[...]
    dupo = (mm(dlowo, down_ref[...], NT) * slopeo_ref[...].astype(F32)).astype(BF16)
    all_ref[...] = (upa_ref[...] + mm(normedo_ref[...], dupo, TN)).astype(BF16)
    dealt(all_ref, p_ref[1], upk_ref, ups_ref)
    all_ref[...] = (downa_ref[...] + mm(activeo_ref[...], dlowo, TN)).astype(BF16)
    dealt(all_ref, p_ref[2], downk_ref, downs_ref)
    bias = jnp.sum(dupo.astype(F32), axis=0, keepdims=True)
    bias_ref[...] = biasa_ref[...] + jnp.broadcast_to(bias, bias_ref.shape)


def first_kernel(
    p_ref,
    x_ref,
    mixed0_ref,
    mixed1_ref,
    second_ref,
    hid_ref,
    hidr_ref,
    gain_ref,
    first_ref,
    dmix_ref,
    sums_ref,
):
    unit, spread = centred(residual(x_ref, (mixed0_ref, mixed1_ref)))
    hid = hid_ref[...].astype(F32) + turned(hidr_ref[...], hid_ref.shape[0] // 8).astype(F32)
    dnormed = second_ref[...] + hid
    first = norm_back(unit, spread, dnormed * gain_ref[0:1, :])
    first_ref[...] = first
    dmix_ref[...] = first.astype(BF16)
    sums_ref[...] = jnp.zeros_like(sums_ref)
    sums_ref[0:1, :] = jnp.sum(dnormed * unit, axis=0, keepdims=True)
    sums_ref[1:2, :] = jnp.sum(dnormed, axis=0, keepdims=True)


def attended_kernel(
    p_ref,
    dmix_ref,
    dmixr_ref,
    exit_ref,
    exitp_ref,
    sums1_ref,
    sums2_ref,
    own_ref,
    send_ref,
    total_ref,
    pay_ref,
):
    length = dmix_ref.shape[0]
    rest = length // 4
    total = dmix_ref[...].astype(F32) + turned(dmixr_ref[...], rest).astype(F32)
    total = total.astype(BF16)
    total_ref[...] = total
    own_ref[...] = mm(total, exit_ref[...], NT).astype(BF16)
    send_ref[...] = mm(total, exitp_ref[...], NT).astype(BF16)
    least = rest // 2
    pay_ref[0:least, :] = total[0:least]
    pay_ref[least:rest, :] = total[2 * rest : 2 * rest + least]
    pay_ref[rest:, :] = jnp.concatenate([sums1_ref[...], sums2_ref[...]], axis=0).astype(BF16)


def backward_kernel(
    p_ref,
    datt_ref,
    dattr_ref,
    first_ref,
    soft_hbm,
    proj_ref,
    spat_ref,
    w_ref,
    ws_ref,
    dscore_ref,
    dproj_ref,
    dspat_ref,
    dxk0_ref,
    dxk1_ref,
    dxs_ref,
    dsk0_ref,
    dsk1_ref,
    dss_ref,
    soft_ref,
    sems,
    *,
    heads,
    block,
):
    fetched = [
        pltpu.make_async_copy(soft_hbm.at[h], soft_ref.at[h], sems.at[h]) for h in range(heads)
    ]
    for copy in fetched:
        copy.start()
    length = 2 * datt_ref.shape[0]
    scale = DH**-0.5
    part = length // 4
    datt = stack_rows(
        [datt_ref[0:part, :], dattr_ref[0:part, :], datt_ref[part:, :], dattr_ref[part:, :]]
    )
    for h in range(heads):
        cols = slice(h * DH, (h + 1) * DH)
        value = proj_ref[2, :, cols]
        left = jnp.concatenate([proj_ref[0, :, cols], spat_ref[0, :, cols]], axis=1)
        right = jnp.concatenate([proj_ref[1, :, cols], spat_ref[1, :, cols]], axis=1)
        own = datt[:, cols]
        fetched[h].wait()
        for at in range(0, length, block):
            soft = soft_ref[h, at : at + block, :]
            dsoft = mm(own[at : at + block], value, NT)
            inner = jnp.sum(soft * dsoft, axis=-1, keepdims=True)
            dscore_ref[h, at : at + block, :] = (soft * (dsoft - inner)).astype(BF16)
        dscore = dscore_ref[h]
        dleft = (mm(dscore, right) * scale).astype(BF16)
        dright = (mm(dscore, left, TN) * scale).astype(BF16)
        dproj_ref[0, :, cols] = dleft[:, :DH]
        dspat_ref[0, :, cols] = dleft[:, DH:]
        dproj_ref[1, :, cols] = dright[:, :DH]
        dspat_ref[1, :, cols] = dright[:, DH:]
        dproj_ref[2, :, cols] = mm(soft_ref[h].astype(BF16), own, TN).astype(BF16)
    once = (p_ref[3] == 0).astype(F32)
    total = mm(dproj_ref[0], w_ref[0])
    for k in range(1, 3):
        total = total + mm(dproj_ref[k], w_ref[k])
    least = part // 4

    def deal(rows, refs):
        for y in range(2):
            for zh in range(2):
                for c in range(2):
                    for zl in range(2):
                        at = (((y * 2 + zh) * 2 + c) * 2 + zl) * least
                        to = (zh * 2 + y) * least
                        value = rows[at : at + least]
                        if zh == 0 and refs[0][0] is dxk0_ref:
                            of = ((y * 2 + c) * 2 + zl) * least
                            value = value + once * first_ref[of : of + least, :]
                        refs[c][zl][to : to + least, :] = value.astype(BF16)

    deal(total, ((dxk0_ref, dxk1_ref), (dxs_ref.at[0], dxs_ref.at[1])))
    total = mm(dspat_ref[0], ws_ref[0]) + mm(dspat_ref[1], ws_ref[1])
    deal(total, ((dsk0_ref, dsk1_ref), (dss_ref.at[0], dss_ref.at[1])))


def spatial_grad_kernel(p_ref, sp_ref, dspat_ref, keep_ref, send_ref):
    sp = sp_ref[...].reshape(-1, sp_ref.shape[-1])
    keep_ref[...] = mm(dspat_ref[p_ref[0]], sp, TN).astype(BF16)
    send_ref[...] = mm(dspat_ref[1 - p_ref[0]], sp, TN).astype(BF16)


def second_grad_kernel(
    p_ref,
    dmix_ref,
    pay_ref,
    payr_ref,
    payl_ref,
    payc_ref,
    paylc_ref,
    atto_ref,
    atts_ref,
    rest_ref,
    spk_ref,
    spr_ref,
    lines_ref,
    keep_ref,
    send_ref,
    second_ref,
):
    inner = spk_ref.shape[0]
    length = dmix_ref.shape[0]
    least = length // 8
    rest = 2 * least
    dmixo = stack_rows(
        [
            ref[y * least : (y + 1) * least, :]
            for y in range(2)
            for ref in (payr_ref, payl_ref, payc_ref, paylc_ref)
        ]
    )
    base = rest_ref.shape[0]
    second_ref[0:base, :] = rest_ref[...]
    second_ref[base : base + inner, :] = (
        mm(atto_ref[...], dmix_ref[...], TN) + mm(atts_ref[...], dmixo, TN)
    ).astype(BF16)
    base += inner
    second_ref[base : base + inner, :] = (
        spk_ref[...].astype(F32) + spr_ref[...].astype(F32)
    ).astype(BF16)
    base += inner
    small = pay_ref[rest:, :].astype(F32) + payr_ref[rest:, :].astype(F32)
    second_ref[base : base + 16, :] = small.astype(BF16)
    second_ref[base + 16 : base + 32, :] = lines_ref[...].astype(BF16)
    dealt(second_ref, p_ref[2], keep_ref, send_ref)


def first_grad_kernel(
    p_ref,
    x_ref,
    dscore_ref,
    dproj_ref,
    colidx_ref,
    bup_ref,
    keep_ref,
    send_ref,
    rest_ref,
    lines_ref,
    first_ref,
    *,
    heads,
):
    width = x_ref.shape[-1]
    x = x_ref[...].reshape(-1, width)
    length = x.shape[0]
    inner = dproj_ref.shape[-1]
    for k in range(3):
        first_ref[k * inner : (k + 1) * inner, :] = mm(dproj_ref[k], x, TN).astype(BF16)
    dealt(first_ref, p_ref[1], keep_ref, send_ref)
    rest_ref[...] = first_ref[2 * keep_ref.shape[0] :, :]
    lane = lax.broadcasted_iota(jnp.int32, (1, NBUCK), 1)
    found = []
    for kind in range(3):
        extent = length if kind == 0 else NBUCK
        own = colidx_ref[:, kind : kind + 1]
        level = lax.broadcasted_iota(jnp.int32, (length, extent), 1)
        chosen = (own == level).astype(BF16)
        place = own - HALF + lax.broadcasted_iota(jnp.int32, (length, NBUCK), 1)
        turn = place & (NBUCK - 1)
        piece = place >> 7
        for h in range(heads):
            spread = mm(dscore_ref[h], chosen)
            window = jnp.zeros((length, NBUCK), F32)
            for q in range(extent // NBUCK):
                part = jnp.take_along_axis(
                    spread[:, q * NBUCK : (q + 1) * NBUCK],
                    turn,
                    axis=1,
                    mode="promise_in_bounds",
                )
                window = window + jnp.where(piece == q, part, 0.0)
            row = jnp.sum(window, axis=0, keepdims=True)
            row = jnp.where((lane > 0) & (lane < NBUCK - 1), row, 0.0)
            least = jnp.sum(jnp.where(level <= own - HALF, spread, 0.0), axis=0, keepdims=True)
            most = jnp.sum(jnp.where(level >= own + HALF - 1, spread, 0.0), axis=0, keepdims=True)
            row = row + jnp.where(lane == 0, jnp.sum(least, axis=1, keepdims=True), 0.0)
            row = row + jnp.where(
                lane == NBUCK - 1, jnp.sum(most, axis=1, keepdims=True), 0.0
            )
            found.append(row)
    per = width // NBUCK
    found = found + [jnp.zeros((1, NBUCK), F32)] * (-len(found) % per)
    lines = [
        jnp.concatenate(found[at : at + per], axis=1) for at in range(0, len(found), per)
    ]
    lines.append(bup_ref[0:1, :])
    lines_ref[...] = jnp.concatenate(
        lines + [jnp.zeros((16 - len(lines), width), F32)], axis=0
    )


def ends_kernel(
    p_ref,
    w_ref,
    y_ref,
    zhw_ref,
    zlw_ref,
    zzw_ref,
    tok_ref,
    sp_ref,
    event_ref,
):
    c, y, block = p_ref[0], p_ref[2], p_ref[4] * 2 + p_ref[3]
    for turn, ref in enumerate((None, zlw_ref, zhw_ref, zzw_ref)):
        at = block ^ turn
        for far in range(2):
            for unit in range(3):
                if ref is None:
                    value = (y_ref if far else w_ref)[unit]
                else:
                    value = ref[far, unit]
                value = value.astype(F32)
                if unit < 2:
                    tok_ref[c ^ unit, y ^ far, at] = value
                else:
                    sp_ref[y ^ far, at] = value
    event_ref[...] = jnp.zeros_like(event_ref)


def out_kernel(p_ref, *refs):
    c, y, block = p_ref[0], p_ref[2], p_ref[4] * 2 + p_ref[3]
    out_ref, event_ref = refs[8:]
    least = out_ref.shape[3]
    for half in range(2):
        for far in range(2):
            for unit in range(2):
                ref = refs[half * 4 + far * 2 + unit]
                for turn in range(2):
                    at = block ^ (half * 2 + turn)
                    out_ref[c ^ unit, y ^ far, at] = ref[turn * least : (turn + 1) * least, :]
    event_ref[...] = jnp.zeros_like(event_ref)


def turn_kernel(p_ref, own_ref, far_ref, sum_ref, *, size):
    far = turned(far_ref[...], size).astype(F32)
    sum_ref[...] = (own_ref[...].astype(F32) + far).astype(BF16)


def plus_kernel(p_ref, *refs):
    count = len(refs) // 3
    for n in range(count):
        total = refs[2 * n][...].astype(F32) + refs[2 * n + 1][...].astype(F32)
        refs[2 * count + n][...] = total.astype(BF16)


def units_kernel(
    p_ref, own0_ref, own1_ref, other_ref, near_ref, far_ref, spat_ref, nears_ref, fars_ref
):
    nears_ref[0] = own0_ref[...]
    fars_ref[0] = own1_ref[...]
    nears_ref[1] = other_ref[0]
    fars_ref[1] = other_ref[1]
    nears_ref[2] = (near_ref[...].astype(F32) + spat_ref[0].astype(F32)).astype(BF16)
    fars_ref[2] = (far_ref[...].astype(F32) + spat_ref[1].astype(F32)).astype(BF16)


def fold_kernel(p_ref, own_ref, far_ref, keep_ref, send_ref):
    total = (own_ref[...].astype(F32) + far_ref[...].astype(F32)).astype(BF16)
    half = total.shape[-2] // 2
    keep_ref[...] = total[..., :half, :]
    send_ref[...] = total[..., half:, :]


def ends_first_kernel(p_ref, keep_ref, far_ref, mine_ref, other_ref):
    least = mine_ref.shape[1]
    total = (keep_ref[...].astype(F32) + far_ref[...].astype(F32)).astype(BF16)
    mine_ref[...] = total[:, :least]
    other_ref[...] = total[:, least:]


def spread_kernel(p_ref, *refs):
    c = p_ref[0]
    event_ref = refs[10]
    for n, out_ref in enumerate(refs[8:10]):
        side = p_ref[1 + n]
        for other in range(2):
            for far in range(2):
                out_ref[c ^ other, side ^ far] = refs[n * 4 + other * 2 + far][...].astype(F32)
    event_ref[...] = jnp.zeros_like(event_ref)


def last_kernel(
    p_ref,
    one0_ref,
    one1_ref,
    one2_ref,
    one3_ref,
    two0_ref,
    two1_ref,
    two2_ref,
    two3_ref,
    qkv_ref,
    spat_ref,
    exit_ref,
    tables_ref,
    gains_ref,
    shifts_ref,
    bup_ref,
    bdown_ref,
    second_ref,
    *,
    heads,
):
    c, head = p_ref[0], p_ref[4] * 2 + p_ref[3]
    inner = exit_ref.shape[1]
    width = exit_ref.shape[2]
    part = gains_ref.shape[2]
    per = width // NBUCK
    firsts = ((one0_ref, one1_ref), (one2_ref, one3_ref))
    seconds = ((two0_ref, two1_ref), (two2_ref, two3_ref))
    for other in range(2):
        s = c ^ other
        for far in range(2):
            size = one0_ref.shape[0]
            at = pl.multiple_of((p_ref[1] ^ far) * size, 16)
            qkv_ref[s, pl.ds(at, size), :] = firsts[other][far][...].astype(F32)
            size = two0_ref.shape[0]
            at = pl.multiple_of((p_ref[2] ^ far) * size, 16)
            second_ref[pl.ds(at, size), :] = seconds[other][far][...].astype(F32)
        base = 3 * inner - 2 * one0_ref.shape[0]
        qkv_ref[s, 2 * one0_ref.shape[0] :, :] = second_ref[0:base, :]
        exit_ref[s] = second_ref[base : base + inner, :]
        base += inner
        spat_ref[s] = second_ref[base : base + inner, :]
        base += inner
        sums = second_ref[base : base + 16, :]
        cut = sums[:, 0:part]
        for at in range(1, width // part):
            cut = jnp.where(head == at, sums[:, at * part : (at + 1) * part], cut)
        gains_ref[s] = jnp.concatenate([cut[0:1], cut[8:9]], axis=0)
        shifts_ref[s] = jnp.concatenate([cut[1:2], cut[9:10]], axis=0)
        bdown_ref[pl.ds(s, 1), :] = cut[10:11]
        lines = second_ref[base + 16 : base + 32, :]
        for n in range(3 * heads):
            at = (n % per) * NBUCK
            tables_ref[n // heads, n % heads, pl.ds(s, 1), :] = lines[
                n // per : n // per + 1, at : at + NBUCK
            ]
        bup_ref[pl.ds(s, 1), :] = lines[2:3]


def swap(value, axis, step=1):
    size = lax.axis_size(axis)
    return lax.ppermute(value, axis, [(i, i ^ step) for i in range(size)])


def swap_both(value):
    size = lax.axis_size("batch") * 2
    return lax.ppermute(value, ("batch", "y"), [(i, i ^ 3) for i in range(size)])


def added(left, right):
    return (left.astype(F32) + right.astype(F32)).astype(BF16)


def batch_steps():
    return [1 << bit for bit in range(lax.axis_size("batch").bit_length() - 1)]


def join(*values):
    return lax.optimization_barrier(values)


def shards(
    tokens,
    spatial,
    positions,
    boxes,
    query_key_value_weight,
    w_spatial,
    rel_tables,
    exit_matrix,
    ln_gains,
    ln_shifts,
    up_weight,
    hidden_bias,
    shrink_projection_array,
    b_down,
    cotangent,
):
    heads = rel_tables.shape[2]
    rows = tokens.shape[2]
    width = tokens.shape[3]
    inner = query_key_value_weight.shape[3]
    hidden = up_weight.shape[2]
    least = rows // 4
    rest = rows // 2
    length = 4 * rows
    half = length // 2
    page = lax.axis_index("y")
    core = lax.axis_index("core")
    zh = lax.axis_index("zh")
    zl = lax.axis_index("zl")
    pair = lax.axis_index("batch") & 1
    place = jnp.stack([core, pair, page, zl, zh]).astype(jnp.int32)

    times = iter(TIMES)

    def run(body, operands, outs, scratch=(), after=(), vmem=VMEM_BYTES):
        return kernel_call(body, place, operands, outs, next(times), scratch, after, vmem)

    def rows_of(count, dtype=BF16):
        return ((count, width), dtype)

    share = hidden // 4
    far0, far1, far2, near, x00, up_part, down_part = run(
        pack_kernel,
        [
            (tokens.reshape(2, 2, 4, least, width), "any"),
            (spatial.reshape(2, 4, least, width), "any"),
            (positions, "any"),
            (boxes, "any"),
            (exit_matrix, "any"),
            (up_weight, "any"),
            (shrink_projection_array, "any"),
            (hidden_bias, "any"),
        ],
        [
            rows_of(rows + 16),
            rows_of(rows),
            rows_of(rows),
            rows_of(2 * rows + 16),
            rows_of(rows),
            rows_of(share + 16 + inner // 4),
            rows_of(share),
        ],
        scratch=[
            pltpu.VMEM(positions.shape, jnp.int32),
            pltpu.VMEM(boxes.shape, jnp.int32),
            pltpu.VMEM(hidden_bias.shape, F32),
            pltpu.SemaphoreType.DMA((30,)),
        ],
        vmem=PACK_VMEM,
    )
    up_part = swap(up_part, "zh")
    i10, s10, x10 = swap(far0, "y"), swap(far1, "y"), swap(far2, "y")
    cot_far, cot_near, cot00 = run(
        cotangent_kernel,
        [(cotangent.reshape(2, 2, 4, least, width), "any")],
        [((2, rows, width), BF16), rows_of(rows), rows_of(rows)],
        scratch=[pltpu.SemaphoreType.DMA((16,))],
        vmem=PACK_VMEM,
        after=[x00],
    )
    n01 = swap(near, "core")
    weights = (jnp.swapaxes(query_key_value_weight, 2, 3), "stream")
    spatial_weights = jnp.swapaxes(w_spatial, 1, 2)
    x0, sp0, index0, proj0, spat0, up, down, exit_own = run(
        near_kernel,
        [
            x00,
            n01,
            near,
            weights,
            spatial_weights,
            (up_weight, "any"),
            (shrink_projection_array, "any"),
            (exit_matrix, "any"),
        ],
        [
            ((2, rows, width), BF16),
            ((2, rows, width), BF16),
            ((8, 2 * rows), jnp.int32),
            ((3, 2 * rows, inner), BF16),
            ((2, 2 * rows, inner), BF16),
            ((width, hidden), BF16),
            ((hidden, width), BF16),
            rows_of(inner),
        ],
        scratch=[pltpu.SemaphoreType.DMA((3,))],
        after=[cot00],
    )
    i10, s10, x10, x0, up_part, down_part = join(i10, s10, x10, x0, up_part, down_part)
    x11, s11 = swap(i10, "core"), swap(s10, "core")
    ups = [up_part, swap(up_part, "y"), swap(up_part, "batch"), swap_both(up_part)]
    down_part = swap(down_part, "zh")

    x, sp, colidx, proj, spat, soft, att_own, att_send = run(
        functools.partial(attention_kernel, heads=heads),
        [
            x10,
            x11,
            s10,
            s11,
            i10,
            x0,
            sp0,
            index0,
            proj0,
            spat0,
            weights,
            spatial_weights,
            (rel_tables, "stream"),
        ],
        [
            ((2, 2, rows, width), BF16),
            ((2, 2, rows, width), BF16),
            ((length, 8), jnp.int32),
            ((3, length, inner), BF16, "any"),
            ((2, length, inner), BF16, "any"),
            ((heads, length, length), F32, "any"),
            ((half, inner), BF16),
            ((half, inner), BF16),
        ],
        scratch=[
            pltpu.VMEM((length, inner), BF16),
            pltpu.VMEM((3, length, inner), BF16),
            pltpu.VMEM((2, length, inner), BF16),
            pltpu.VMEM((heads, length, length), F32),
            pltpu.SemaphoreType.DMA((2 + heads,)),
        ],
    )
    att_recv = swap(att_send, "zh")
    att_own, down_part, *ups = join(att_own, down_part, *ups)
    downs = [down_part, swap(down_part, "y"), swap(down_part, "batch"), swap_both(down_part)]

    keep, send, exit_partner = run(
        mixed_kernel,
        [att_own, att_recv, exit_own, *ups],
        [rows_of(rows, F32), rows_of(rows), rows_of(inner)],
    )
    (mixed0,) = run(
        plus_kernel, [keep, swap(send, "core")], [rows_of(rows)], after=downs[1:3]
    )
    mixed_zl = swap(mixed0, "zl")
    (mixed0,) = run(
        functools.partial(turn_kernel, size=least), [mixed0, mixed_zl], [rows_of(rows)]
    )
    mixed1 = swap(mixed0, "core")
    mixed_far0 = swap(mixed0, "zh")
    mixed1, *downs = join(mixed1, *downs)

    gains = (ln_gains, "stream")
    shifts = (ln_shifts, "stream")
    x_own = (x, (None, 0, None, None))
    x_far = (x, (None, 1, None, None))
    low, normed, active, slope, up_partner, down_partner = run(
        forward_kernel,
        [x_own, mixed0, mixed1, gains, shifts, up, hidden_bias, down, *ups, *downs],
        [
            rows_of(half),
            rows_of(half),
            ((2, half, hidden), BF16),
            ((2, half, hidden), BF16),
            ((width, hidden), BF16),
            ((hidden, width), BF16),
        ],
    )
    low_recv = swap(low, "zl")
    cot_far, cot_near, mixed0 = join(cot_far, cot_near, mixed0)
    cot10 = swap(cot_far, "y")
    cot01 = swap(cot_near, "core")
    mixed_far1 = swap(mixed_far0, "core")
    cot11 = swap(cot10, "core")
    (normed_far,) = run(
        first_norm_kernel,
        [x_far, mixed_far0, mixed_far1, gains, shifts],
        [rows_of(half)],
        after=[low],
    )
    active_far, slope_far = run(
        other_kernel,
        [normed_far, up, hidden_bias],
        [((half, hidden), BF16), ((half, hidden), BF16)],
    )
    low0, low1 = run(
        lowered_kernel, [low, low_recv], [rows_of(rows), rows_of(rows)], after=[slope_far]
    )
    far_low0 = swap(low0, "zh")

    def finish(x_half, pieces, part, after=()):
        rows_part = slice(part * rest, (part + 1) * rest)
        cots = [
            cot00[rows_part],
            cot10[0, rows_part],
            cot01[rows_part],
            cot11[1, rows_part],
        ]
        return run(
            final_kernel,
            [x_half, *pieces, *cots, gains, shifts, b_down],
            [
                ((2, rest, width), BF16),
                ((2, rest, width), BF16),
                rows_of(half, F32),
                rows_of(half),
                rows_of(8, F32),
            ],
            after=after,
        )

    out_keep, out_send, second, dlow, sums_two = finish(x_own, [mixed0, mixed1, low0, low1], 0)
    hid, dup = run(
        middle_kernel,
        [dlow, up, down, up_partner, down_partner, slope],
        [rows_of(half), ((half, hidden), BF16)],
    )
    hid_recv = swap(hid, "zl")
    up_own, down_own, bias_own = run(
        ffn_own_kernel,
        [normed, (active, (0, None, None)), dlow, dup],
        [((width, hidden), F32), rows_of(hidden, F32), ((8, hidden), F32)],
        after=[hid],
    )
    out_core = swap(out_send, "core")
    out_y = swap(jnp.stack([out_keep[1], out_core[1]]), "y")
    hid_recv, far_low0, out_y = join(hid_recv, far_low0, out_y)
    far_low1 = swap(far_low0, "zl")
    first, dmix, sums_one = run(
        first_kernel,
        [x_own, mixed0, mixed1, second, hid, hid_recv, gains],
        [rows_of(half, F32), rows_of(half), rows_of(8, F32)],
        after=[bias_own],
    )
    dmix_core = swap(dmix, "core")
    datt, datt_send, dmix, pay = run(
        attended_kernel,
        [dmix, dmix_core, exit_own, exit_partner, sums_one, sums_two],
        [
            ((half, inner), BF16),
            ((half, inner), BF16),
            rows_of(half),
            rows_of(rest + 16),
        ],
    )
    datt_recv = swap(datt_send, "zh")
    far_keep, far_send, _, dlow_far, _ = finish(
        x_far, [mixed_far0, mixed_far1, far_low0, far_low1], 1, [datt]
    )
    up_keep, up_send, down_keep, down_send, bias_grad = run(
        ffn_grad_kernel,
        [
            up_own,
            down_own,
            bias_own,
            normed_far,
            active_far,
            dlow_far,
            slope_far,
            down,
        ],
        [
            ((width // 2, hidden), BF16),
            ((width // 2, hidden), BF16),
            rows_of(hidden // 2),
            rows_of(hidden // 2),
            ((8, hidden), F32),
        ],
        scratch=[pltpu.VMEM((width, hidden), BF16)],
        after=[datt],
    )
    up_recv = swap(up_send, "batch")
    down_recv = swap(down_send, "y")
    datt_recv, pay = join(datt_recv, pay)
    pay_recv = swap(pay, "zh")
    piece = rows_of(rows)
    dscore, dproj, dspat, dxk0, dxk1, dxs, dsk0, dsk1, dss = run(
        functools.partial(backward_kernel, heads=heads, block=128),
        [datt, datt_recv, first, (soft, "any"), proj, spat, weights, spatial_weights],
        [
            ((heads, length, length), BF16),
            ((3, length, inner), BF16),
            ((2, length, inner), BF16),
            piece,
            piece,
            ((2, rows, width), BF16),
            piece,
            piece,
            ((2, rows, width), BF16),
        ],
        scratch=[pltpu.VMEM((heads, length, length), F32), pltpu.SemaphoreType.DMA((heads,))],
        after=[bias_grad],
    )

    steps = batch_steps()[1:]

    def plus(pairs, after=(), over_batch=False):
        sums = run(
            plus_kernel,
            [array for pair_of in pairs for array in pair_of],
            [(left.shape, BF16) for left, _ in pairs],
            after=after,
        )
        if over_batch:
            for step in steps:
                sums = [added(value, swap(value, "batch", step)) for value in sums]
        return sums

    dxk1, dxs, dss, pay_recv = join(dxk1, dxs, dss, pay_recv)
    dxs, dss = swap(dxs, "core"), swap(dss, "core")
    near, far = run(
        units_kernel,
        [dxk0, dxk1, dxs, dsk0, dsk1, dss],
        [((3, rows, width), BF16), ((3, rows, width), BF16)],
    )
    far_zl = swap(far, "zl")
    up_half, down_half = plus([(up_keep, up_recv), (down_keep, down_recv)], after=[far])
    up_other = swap(up_half, "y")
    down_other = swap(down_half, "batch")
    pay_zl = swap(join(pay_recv, far)[0], "zl")
    few = inner // 2
    main = 3 * inner - few
    sp_keep, sp_send = run(
        spatial_grad_kernel, [sp, dspat], [rows_of(inner), rows_of(inner)], after=[up_half]
    )
    sp_recv = swap(sp_send, "core")
    one_keep, one_send, value_rest, lines = run(
        functools.partial(first_grad_kernel, heads=heads),
        [x, dscore, dproj, colidx, bias_grad],
        [rows_of(main // 2), rows_of(main // 2), rows_of(few), rows_of(16, F32)],
        scratch=[pltpu.VMEM((3 * inner, width), BF16)],
        after=[sp_keep],
    )
    keep, send = run(
        fold_kernel,
        [near, far_zl],
        [((3, rest, width), BF16), ((3, rest, width), BF16)],
        after=[lines],
    )
    send_zh = swap(send, "zh")
    up_half, down_half = plus(
        [(up_half, up_other), (down_half, down_other)], after=[send], over_batch=True
    )
    up_far = swap(up_half, "batch")
    down_far = swap(down_half, "y")
    mine, other = run(
        ends_first_kernel,
        [keep, send_zh],
        [((3, least, width), BF16), ((3, least, width), BF16)],
        after=[up_half],
    )
    got = swap(other, "y")
    pay_recv, pay_zl, far_send, send = join(pay_recv, pay_zl, far_send, send)
    pay_core, pay_zlcore = swap(pay_recv, "core"), swap(pay_zl, "core")
    far_core = swap(far_send, "core")
    base = few + 2 * inner + 32
    two_keep, two_send = run(
        second_grad_kernel,
        [
            dmix,
            pay,
            pay_recv,
            pay_zl,
            pay_core,
            pay_zlcore,
            att_own,
            att_send,
            value_rest,
            sp_keep,
            sp_recv,
            lines,
        ],
        [rows_of(base // 2), rows_of(base // 2)],
        scratch=[pltpu.VMEM((base, width), BF16)],
        after=[mine, up_far, down_far],
    )
    one_send, two_send, got, two_keep = join(one_send, two_send, got, two_keep)
    one_recv = swap(one_send, "batch")
    two_recv = swap(two_send, "y")
    pages = jnp.stack([mine, got])
    pages_zh = swap(pages, "zh")
    pages_zl = swap(pages, "zl")
    *halves, pages = join(up_half, up_far, down_half, down_far, pages)
    others = [swap(value, "core") for value in halves]
    grad_up, grad_down, spread_event = run(
        spread_kernel,
        halves[:2] + others[:2] + halves[2:] + others[2:],
        [
            ((2, 2, width // 2, hidden), F32),
            ((2, 2, hidden // 2, width), F32),
            ((8, NBUCK), F32),
        ],
        after=[pages],
    )
    one_half, two_half = plus(
        [(one_keep, one_recv), (two_keep, two_recv)], after=[spread_event]
    )
    one_other = swap(one_half, "y")
    two_other = swap(two_half, "batch")
    far_y = swap(jnp.stack([far_keep[1], far_core[1]]), "y")
    pages_zh, pages_zl = join(pages_zh, pages_zl)
    pages_zz = swap(pages_zh, "zl")
    one_half, two_half = plus(
        [(one_half, one_other), (two_half, two_other)],
        after=[pages_zz],
        over_batch=True,
    )
    one_far = swap(one_half, "batch")
    two_far = swap(two_half, "y")
    grad_tokens, grad_spatial, ends_event = run(
        ends_kernel,
        [mine, got, pages_zh, pages_zl, pages_zz],
        [((2, 2, 4, least, width), F32), ((2, 4, least, width), F32), ((8, NBUCK), F32)],
        after=[one_half],
    )
    output, out_event = run(
        out_kernel,
        [
            out_keep[0],
            out_core[0],
            out_y[0],
            out_y[1],
            far_keep[0],
            far_core[0],
            far_y[0],
            far_y[1],
        ],
        [((2, 2, 4, least, width), BF16), ((8, NBUCK), F32)],
        after=[one_half],
    )
    one_far, two_far, out_event, ends_event = join(one_far, two_far, out_event, ends_event)
    halves = [one_half, one_far, two_half, two_far]
    others = [swap(value, "core") for value in halves]
    part = width // (2 * lax.axis_size("zh"))
    grad_qkv, grad_spatial_w, grad_exit, tables, gains_grad, shifts_grad, grad_b_up, grad_b_down = run(
        functools.partial(last_kernel, heads=heads),
        halves[:2] + others[:2] + halves[2:] + others[2:],
        [
            ((2, 3 * inner, width), F32),
            ((2, inner, width), F32),
            ((2, inner, width), F32),
            ((3, heads, 2, NBUCK), F32),
            ((2, 2, part), F32),
            ((2, 2, part), F32),
            ((2, hidden), F32),
            ((2, part), F32),
        ],
        scratch=[pltpu.VMEM((base, width), F32)],
        after=[spread_event, out_event, ends_event],
    )
    return (
        output.reshape(tokens.shape),
        grad_tokens.reshape(tokens.shape),
        grad_spatial.reshape(spatial.shape),
        grad_qkv.reshape(2, 3, inner, width).swapaxes(2, 3),
        grad_spatial_w.reshape(2, inner, width).swapaxes(1, 2),
        tables.transpose(2, 0, 1, 3),
        grad_exit,
        gains_grad,
        shifts_grad,
        grad_up.reshape(2, width, hidden),
        grad_b_up,
        grad_down.reshape(2, hidden, width),
        grad_b_down,
    )


def solution(mesh):
    batch, seq, head = mesh.devices.shape
    fine = Mesh(
        mesh.devices.reshape(batch, seq // 2, 2, head // 2, 2),
        ("batch", "y", "core", "zh", "zl"),
    )
    seq = ("y", "core")
    head = ("zh", "zl")
    return jax.shard_map(
        shards,
        mesh=fine,
        in_specs=(
            P(None, "batch", seq, None),
            P("batch", seq, None),
            P("batch", seq),
            P(None, "batch", seq),
            P(None, None, None, head),
            P(None, None, head),
            P(None, None, head, None),
            P(None, head, None),
            P(),
            P(),
            P(None, None, head),
            P(None, head),
            P(None, head, None),
            P(),
            P(None, "batch", seq, None),
        ),
        out_specs=(
            P(None, "batch", seq, None),
            P(None, "batch", seq, None),
            P("batch", seq, None),
            P(None, None, None, head),
            P(None, None, head),
            P(None, None, head, None),
            P(None, head, None),
            P(None, None, head),
            P(None, None, head),
            P(None, None, head),
            P(None, head),
            P(None, head, None),
            P(None, head),
        ),
        check_vma=False,
    )
```

```python
import functools

import jax
import jax.numpy as jnp
from jax import lax
from jax.experimental import pallas as pl
from jax.experimental.pallas import tpu as pltpu
from jax.sharding import Mesh, PartitionSpec as P

DH = 64
NBUCK = 128
HALF = 64
EPSILON = 1e-05
F32 = jnp.float32
BF16 = jnp.bfloat16
VMEM_BYTES = 20 * 1024 * 1024
TIMES = (
    0.1, 2, 0.02, 30.0, 0.1, 0.1, 0.1, 0.1, 8, 0.1, 0.02,
    0.1, 0.1, 0.1, 0.1, 0.1, 8, 30.0, 30.0, 0.1, 0.1, 30,
    0.1, 0.1, 8, 0.1, 0.1, 0.1, 0.5, 0.1, 0.1, 0.1, 0.1,
)
PACK_VMEM = 60 * 1024 * 1024
NN = (((1,), (0,)), ((), ()))
NT = (((1,), (1,)), ((), ()))
TN = (((0,), (0,)), ((), ()))


def mm(left, right, dims=NN):
    return lax.dot_general(left, right, dims, preferred_element_type=F32)


def kernel_call(body, place, operands, outs, us, scratch=(), after=(), vmem=VMEM_BYTES):
    specs, arrays, hows = [], [], []
    for operand in operands:
        array, how = operand if isinstance(operand, tuple) else (operand, None)
        specs.append(pl.BlockSpec(memory_space=pltpu.HBM if how == "any" else pltpu.VMEM))
        arrays.append(array)
        hows.append(how)
    count = len(arrays)
    specs += [pl.BlockSpec(memory_space=pl.ANY)] * len(after)

    def view(s_ref, ref, how):
        if how == "stream":
            return ref.at[s_ref[0]]
        if how is None or how == "any":
            return ref
        return ref.at[tuple(slice(None) if at is None else at for at in how)]

    def kernel(s_ref, *refs):
        given = [view(s_ref, ref, how) for ref, how in zip(refs, hows)]
        body(s_ref, *given, *refs[count + len(after) :])

    return pl.pallas_call(
        kernel,
        out_shape=[jax.ShapeDtypeStruct(out[0], out[1]) for out in outs],
        in_specs=[pl.BlockSpec(memory_space=pltpu.SMEM)] + specs,
        out_specs=[
            pl.BlockSpec(memory_space=pltpu.HBM if len(out) > 2 else pltpu.VMEM) for out in outs
        ],
        scratch_shapes=list(scratch),
        compiler_params=pltpu.CompilerParams(vmem_limit_bytes=vmem),
        cost_estimate=pl.CostEstimate(
            flops=int(us * 1.1e9), bytes_accessed=int(us * 3.5e6), transcendentals=0
        ),
    )(place, *arrays, *after)


def centred(rows):
    centre = rows - jnp.mean(rows, axis=-1, keepdims=True)
    spread = lax.rsqrt(jnp.mean(centre * centre, axis=-1, keepdims=True) + EPSILON)
    return centre * spread, spread


def norm_back(unit, spread, tilted):
    return spread * (
        tilted
        - jnp.mean(tilted, axis=-1, keepdims=True)
        - unit * jnp.mean(tilted * unit, axis=-1, keepdims=True)
    )


def pick(table_row, index):
    width = index.shape[1]
    table = jnp.broadcast_to(table_row, (index.shape[0], NBUCK))
    parts = [
        jnp.take_along_axis(
            table,
            index[:, at : at + NBUCK],
            axis=1,
            mode="promise_in_bounds",
        )
        for at in range(0, width, NBUCK)
    ]
    return jnp.concatenate(parts, axis=1)


def stack_rows(pieces):
    return jnp.concatenate(pieces, axis=0)


def turned(rows, size):
    pieces = [rows[at : at + size] for at in range(0, rows.shape[0], size)]
    return stack_rows([pieces[i ^ 1] for i in range(len(pieces))])


def residual(x_ref, mixed_refs):
    rest = mixed_refs[0].shape[0] // 2
    pieces = []
    for y in range(2):
        for c in range(2):
            own = x_ref[y, c * rest : (c + 1) * rest, :].astype(F32)
            pieces.append(own + mixed_refs[c][y * rest : (y + 1) * rest, :].astype(F32))
    return stack_rows(pieces)


def dealt(rows_ref, side, keep_ref, send_ref):
    half = keep_ref.shape[0]
    keep_ref[...] = rows_ref[pl.ds(pl.multiple_of(side * half, 16), half), :]
    send_ref[...] = rows_ref[pl.ds(pl.multiple_of((1 - side) * half, 16), half), :]


def gathered(place_ref, refs, rows, to_ref):
    size = rows.stop - rows.start
    for turn, ref in enumerate(refs):
        q = (place_ref[1] ^ (turn // 2)) * 2 + (place_ref[2] ^ (turn % 2))
        to_ref[pl.ds(pl.multiple_of(q * size, 16), size), :] = ref[rows, :]


def copied(pairs, sems):
    started = [
        pltpu.make_async_copy(source, target, sems.at[n])
        for n, (source, target) in enumerate(pairs)
    ]
    for copy in started:
        copy.start()
    return started


def pack_kernel(
    p_ref,
    tok_ref,
    sp_ref,
    pos_ref,
    box_ref,
    exit_ref,
    up_ref,
    down_ref,
    bias_ref,
    far0_ref,
    far1_ref,
    far2_ref,
    near_ref,
    own_ref,
    ups_ref,
    downs_ref,
    posv_ref,
    boxv_ref,
    biasv_ref,
    sems,
):
    c, y, zl, zh = p_ref[0], p_ref[2], p_ref[3], p_ref[4]
    block = zh * 2 + zl
    least = tok_ref.shape[3]
    rows = 4 * least
    q = p_ref[1] * 2 + y
    many = down_ref.shape[1] // 4
    few = exit_ref.shape[1] // 4
    pairs = [
        (pos_ref, posv_ref),
        (box_ref, boxv_ref),
        (bias_ref, biasv_ref),
        (up_ref.at[c, pl.ds(pl.multiple_of(q * many, 16), many)], ups_ref.at[pl.ds(0, many)]),
        (
            exit_ref.at[c, pl.ds(pl.multiple_of(q * few, 16), few)],
            ups_ref.at[pl.ds(many + 16, few)],
        ),
        (down_ref.at[c, pl.ds(pl.multiple_of(q * many, 16), many)], downs_ref),
    ]
    for k in range(4):
        at = block ^ k
        to = pl.ds(k * least, least)
        pairs += [
            (tok_ref.at[1 - c, 1 - y, at], far0_ref.at[to]),
            (sp_ref.at[1 - y, at], far1_ref.at[to]),
            (tok_ref.at[c, 1 - y, at], far2_ref.at[to]),
            (tok_ref.at[1 - c, y, at], near_ref.at[to]),
            (sp_ref.at[y, at], near_ref.at[pl.ds(rows + k * least, least)]),
            (tok_ref.at[c, y, at], own_ref.at[to]),
        ]
    started = copied(pairs, sems)
    for copy in started[:3]:
        copy.wait()
    left = biasv_ref[pl.ds(c, 1), :]
    lines = []
    for _ in range(3):
        lines.append(left.astype(BF16).astype(F32))
        left = left - lines[-1]
    lines.append(jnp.zeros((13, left.shape[1]), F32))
    ups_ref[many : many + 16, :] = jnp.concatenate(lines, axis=0).astype(BF16)
    lane = lax.broadcasted_iota(jnp.int32, (8, NBUCK), 1)
    width = far0_ref.shape[1]
    for page, ref, at in ((1 - y, far0_ref, rows), (y, near_ref, 2 * rows)):
        place = posv_ref[pl.ds(page, 1), :]
        lines = [
            place & 255,
            place >> 8,
            boxv_ref[0, pl.ds(page, 1), :],
            boxv_ref[1, pl.ds(page, 1), :],
        ]
        value = jnp.concatenate(lines + [jnp.zeros((4, NBUCK), jnp.int32)], axis=0)
        crossed = jnp.where(
            (lane & 63) < 32, pltpu.roll(value, NBUCK - 32, 1), pltpu.roll(value, 32, 1)
        )
        value = jnp.where(zl == 0, value, crossed)
        value = jnp.where(zh == 0, value, pltpu.roll(value, 64, 1))
        value = jnp.concatenate([value.astype(F32), jnp.zeros((8, NBUCK), F32)], axis=0)
        ref[at : at + 16, 0:NBUCK] = value.astype(BF16)
        ref[at : at + 16, NBUCK:] = jnp.zeros((16, width - NBUCK), BF16)
    for copy in started[3:]:
        copy.wait()


def cotangent_kernel(p_ref, cot_ref, far_ref, near_ref, own_ref, sems):
    c, y, block = p_ref[0], p_ref[2], p_ref[4] * 2 + p_ref[3]
    least = cot_ref.shape[3]
    pairs = []
    for k in range(4):
        at = block ^ k
        to = pl.ds(k * least, least)
        pairs += [
            (cot_ref.at[c, 1 - y, at], far_ref.at[0, to]),
            (cot_ref.at[1 - c, 1 - y, at], far_ref.at[1, to]),
            (cot_ref.at[1 - c, y, at], near_ref.at[to]),
            (cot_ref.at[c, y, at], own_ref.at[to]),
        ]
    for copy in copied(pairs, sems):
        copy.wait()


def indices(ref, at):
    lines = ref[at : at + 16, 0:NBUCK].astype(F32).astype(jnp.int32)
    place = lines[0:1] + lines[1:2] * 256
    return jnp.concatenate([place, lines[2:4], jnp.zeros((5, NBUCK), jnp.int32)], axis=0)


def two_cores(index0, index1, half):
    lane = lax.broadcasted_iota(jnp.int32, (8, NBUCK), 1)
    if half == 0:
        return jnp.where(lane < 64, index0, pltpu.roll(index1, 64, 1))
    return jnp.where(lane < 64, pltpu.roll(index0, 64, 1), index1)


def arrange(x0_ref, x1_ref, s0_ref, s1_ref, i0_ref, i1_ref, at, x_ref, sp_ref):
    least = x_ref.shape[1]
    rest = least // 2
    found = []
    index0, index1 = indices(i0_ref, at), indices(i1_ref, at)
    for half in range(2):
        at = half * rest
        x_ref[half, 0:rest, :] = x0_ref[at : at + rest, :]
        x_ref[half, rest:, :] = x1_ref[at : at + rest, :]
        sp_ref[half, 0:rest, :] = s0_ref[at : at + rest, :]
        sp_ref[half, rest:, :] = s1_ref[at : at + rest, :]
        found.append(two_cores(index0, index1, half))
    return found


def project(x_ref, sp_ref, w_ref, ws_ref, proj_ref, spat_ref, at):
    width = x_ref.shape[-1]
    x = x_ref[...].reshape(-1, width)
    sp = sp_ref[...].reshape(-1, width)
    rows = slice(at, at + x.shape[0])
    for k in range(3):
        proj_ref[k, rows, :] = mm(x, w_ref[k], NT).astype(BF16)
    for k in range(2):
        spat_ref[k, rows, :] = mm(sp, ws_ref[k], NT).astype(BF16)


def near_kernel(
    p_ref,
    x00_ref,
    n01_ref,
    n00_ref,
    w_ref,
    ws_ref,
    up_hbm,
    down_hbm,
    exit_hbm,
    x_ref,
    sp_ref,
    index_ref,
    proj_ref,
    spat_ref,
    up_ref,
    down_ref,
    exit_ref,
    sems,
):
    fetched = [
        pltpu.make_async_copy(source.at[p_ref[0]], target, sems.at[n])
        for n, (source, target) in enumerate(
            ((exit_hbm, exit_ref), (up_hbm, up_ref), (down_hbm, down_ref))
        )
    ]
    for copy in fetched:
        copy.start()
    least = x_ref.shape[1]
    found = arrange(
        x00_ref,
        n01_ref,
        n00_ref.at[least:],
        n01_ref.at[least:],
        n00_ref,
        n01_ref,
        2 * least,
        x_ref,
        sp_ref,
    )
    index_ref[...] = jnp.concatenate(found, axis=1)
    project(x_ref, sp_ref, w_ref, ws_ref, proj_ref, spat_ref, 0)
    for copy in fetched:
        copy.wait()


def attention_kernel(
    p_ref,
    x10_ref,
    x11_ref,
    s10_ref,
    s11_ref,
    i10_ref,
    x0_ref,
    sp0_ref,
    index_ref,
    proj0_ref,
    spat0_ref,
    w_ref,
    ws_ref,
    table_ref,
    x_ref,
    sp_ref,
    colidx_ref,
    proj_hbm,
    spat_hbm,
    soft_hbm,
    own_ref,
    send_ref,
    att_ref,
    proj_ref,
    spat_ref,
    soft_ref,
    sems,
    *,
    heads,
):
    least = x_ref.shape[2]
    near = 2 * least
    x_ref[0] = x0_ref[...]
    sp_ref[0] = sp0_ref[...]
    proj_ref[:, 0:near, :] = proj0_ref[...]
    spat_ref[:, 0:near, :] = spat0_ref[...]
    found = arrange(
        x10_ref, x11_ref, s10_ref, s11_ref, i10_ref, x11_ref, least, x_ref.at[1], sp_ref.at[1]
    )
    places = jnp.concatenate([index_ref[...]] + found, axis=1)
    colidx_ref[...] = jnp.transpose(places.astype(F32)).astype(jnp.int32)
    project(x_ref.at[1], sp_ref.at[1], w_ref, ws_ref, proj_ref, spat_ref, near)
    length = 2 * near
    stored = [
        pltpu.make_async_copy(proj_ref, proj_hbm, sems.at[0]),
        pltpu.make_async_copy(spat_ref, spat_hbm, sems.at[1]),
    ]
    for copy in stored:
        copy.start()
    level = lax.broadcasted_iota(jnp.int32, (length, NBUCK), 1)
    chosen = [(colidx_ref[:, kind : kind + 1] == level).astype(BF16) for kind in (1, 2)]
    chosen = jnp.concatenate(chosen, axis=1)

    lane = lax.broadcasted_iota(jnp.int32, (length, NBUCK), 1)
    boxes = [
        jnp.clip(lane - colidx_ref[:, kind : kind + 1], -HALF, HALF - 1) + HALF
        for kind in (1, 2)
    ]
    index = jnp.clip(places[0:1, :] - colidx_ref[:, 0:1], -HALF, HALF - 1) + HALF
    for h in range(heads):
        cols = slice(h * DH, (h + 1) * DH)
        bias = jnp.concatenate(
            [pick(table_ref[k, h : h + 1, :], boxes[k - 1]) for k in (1, 2)], axis=1
        )
        coarse = bias.astype(BF16)
        fine = (bias - coarse.astype(F32)).astype(BF16)
        left = jnp.concatenate(
            [proj_ref[0, :, cols], spat_ref[0, :, cols]], axis=1
        ) * jnp.asarray(DH**-0.5, BF16)
        right = jnp.concatenate([proj_ref[1, :, cols], spat_ref[1, :, cols]], axis=1)
        scores = mm(
            jnp.concatenate([left, coarse, fine], axis=1),
            jnp.concatenate([right, chosen, chosen], axis=1),
            NT,
        ) + pick(table_ref[0, h : h + 1, :], index)
        top = jnp.max(scores, axis=-1, keepdims=True)
        raised = jnp.exp(scores - top)
        soft = raised * (1.0 / jnp.sum(raised, axis=-1, keepdims=True))
        soft_ref[h] = soft
        stored.append(pltpu.make_async_copy(soft_ref.at[h], soft_hbm.at[h], sems.at[2 + h]))
        stored[-1].start()
        att_ref[:, cols] = mm(soft.astype(BF16), proj_ref[2, :, cols]).astype(BF16)
    for copy in stored:
        copy.wait()
    part = length // 4
    own_ref[0:part, :] = att_ref[0:part, :]
    own_ref[part:, :] = att_ref[2 * part : 3 * part, :]
    send_ref[0:part, :] = att_ref[part : 2 * part, :]
    send_ref[part:, :] = att_ref[3 * part :, :]


def mixed_kernel(
    p_ref,
    own_ref,
    recv_ref,
    exit_ref,
    one0_ref,
    one1_ref,
    one2_ref,
    one3_ref,
    keep_ref,
    send_ref,
    partner_ref,
):
    rows = slice(one0_ref.shape[0] - exit_ref.shape[0] // 4, one0_ref.shape[0])
    gathered(p_ref, (one0_ref, one1_ref, one2_ref, one3_ref), rows, partner_ref)
    total = mm(own_ref[...], exit_ref[...]) + mm(recv_ref[...], partner_ref[...])
    rest = total.shape[0] // 4
    for y in range(2):
        at = 2 * y * rest
        keep_ref[y * rest : (y + 1) * rest, :] = total[at : at + rest]
        send_ref[y * rest : (y + 1) * rest, :] = total[at + rest : at + 2 * rest].astype(BF16)


def gelu_parts(upper):
    phi = 0.5 * (1.0 + lax.erf(upper * (0.5**0.5)))
    slope = phi + upper * (jnp.exp(-0.5 * upper * upper) * (0.5 / jnp.pi) ** 0.5)
    return (upper * phi).astype(BF16), slope


def forward_kernel(
    p_ref,
    x_ref,
    mixed0_ref,
    mixed1_ref,
    gain_ref,
    shift_ref,
    up_ref,
    hidden_ref,
    down_ref,
    one0_ref,
    one1_ref,
    one2_ref,
    one3_ref,
    two0_ref,
    two1_ref,
    two2_ref,
    two3_ref,
    low_ref,
    normed_ref,
    active_ref,
    slope_ref,
    upp_ref,
    downp_ref,
):
    many = two0_ref.shape[0]
    gathered(p_ref, (one0_ref, one1_ref, one2_ref, one3_ref), slice(0, many), upp_ref)
    gathered(p_ref, (two0_ref, two1_ref, two2_ref, two3_ref), slice(0, many), downp_ref)
    extra = one0_ref[many : many + 16, :].astype(F32)
    partner_bias = extra[0:1] + extra[1:2] + extra[2:3]
    unit, _ = centred(residual(x_ref, (mixed0_ref, mixed1_ref)))
    normed_low = (unit * gain_ref[0:1, :] + shift_ref[0:1, :]).astype(BF16)
    normed_ref[...] = normed_low
    active, slope = gelu_parts(mm(normed_low, up_ref[...]) + hidden_ref[pl.ds(p_ref[0], 1), :])
    active_ref[0] = active
    slope_ref[0] = slope.astype(BF16)
    total = mm(active, down_ref[...])
    active, slope = gelu_parts(mm(normed_low, upp_ref[...]) + partner_bias)
    active_ref[1] = active
    slope_ref[1] = slope.astype(BF16)
    low_ref[...] = (total + mm(active, downp_ref[...])).astype(BF16)


def other_kernel(
    p_ref,
    normed_ref,
    up_ref,
    hidden_ref,
    active_ref,
    slope_ref,
):
    active, slope = gelu_parts(
        mm(normed_ref[...], up_ref[...]) + hidden_ref[pl.ds(p_ref[0], 1), :]
    )
    active_ref[...] = active
    slope_ref[...] = slope.astype(BF16)


def first_norm_kernel(p_ref, x_ref, mixed0_ref, mixed1_ref, gain_ref, shift_ref, normed_ref):
    unit, _ = centred(residual(x_ref, (mixed0_ref, mixed1_ref)))
    normed_ref[...] = (unit * gain_ref[0:1, :] + shift_ref[0:1, :]).astype(BF16)


def lowered_kernel(p_ref, own_ref, far_ref, low0_ref, low1_ref):
    least = own_ref.shape[0] // 8
    total = own_ref[...].astype(F32) + turned(far_ref[...], least).astype(F32)
    total = total.astype(BF16)
    for i in range(4):
        low0_ref[i * least : (i + 1) * least, :] = total[2 * i * least : (2 * i + 1) * least]
        low1_ref[i * least : (i + 1) * least, :] = total[(2 * i + 1) * least : (2 * i + 2) * least]


def final_kernel(
    p_ref,
    x_ref,
    mixed0_ref,
    mixed1_ref,
    low0_ref,
    low1_ref,
    cot00_ref,
    cot10_ref,
    cot01_ref,
    cot11_ref,
    gain_ref,
    shift_ref,
    bdown_ref,
    outk_ref,
    outs_ref,
    second_ref,
    dlow_ref,
    sums_ref,
):
    unit, _ = centred(residual(x_ref, (mixed0_ref, mixed1_ref)))
    normed = unit * gain_ref[0:1, :] + shift_ref[0:1, :]
    least = low0_ref.shape[0] // 4
    pieces = []
    for i in range(4):
        pieces.append(low0_ref[i * least : (i + 1) * least, :])
        pieces.append(low1_ref[i * least : (i + 1) * least, :])
    lowered = stack_rows(pieces).astype(F32)
    unit2, spread2 = centred(normed + lowered + bdown_ref[pl.ds(p_ref[0], 1), :])
    out = (unit2 * gain_ref[1:2, :] + shift_ref[1:2, :]).astype(BF16)
    for y in range(2):
        at = 4 * y * least
        outk_ref[y] = out[at : at + 2 * least]
        outs_ref[y] = out[at + 2 * least : at + 4 * least]
    cot = stack_rows([cot00_ref[...], cot01_ref[...], cot10_ref[...], cot11_ref[...]]).astype(F32)
    second = norm_back(unit2, spread2, cot * gain_ref[1:2, :])
    second_ref[...] = second
    dlow_ref[...] = second.astype(BF16)
    sums_ref[...] = jnp.zeros_like(sums_ref)
    sums_ref[0:1, :] = jnp.sum(cot * unit2, axis=0, keepdims=True)
    sums_ref[1:2, :] = jnp.sum(cot, axis=0, keepdims=True)
    sums_ref[2:3, :] = jnp.sum(second, axis=0, keepdims=True)


def middle_kernel(
    p_ref,
    dlow_ref,
    up_ref,
    down_ref,
    upp_ref,
    downp_ref,
    slope_ref,
    hid_ref,
    dup_ref,
):
    dlow = dlow_ref[...]
    dup = (mm(dlow, down_ref[...], NT) * slope_ref[0].astype(F32)).astype(BF16)
    dup_ref[...] = dup
    total = mm(dup, up_ref[...], NT)
    dup = (mm(dlow, downp_ref[...], NT) * slope_ref[1].astype(F32)).astype(BF16)
    hid_ref[...] = (total + mm(dup, upp_ref[...], NT)).astype(BF16)


def ffn_own_kernel(p_ref, normed_ref, active_ref, dlow_ref, dup_ref, up_ref, down_ref, bias_ref):
    dup = dup_ref[...]
    up_ref[...] = mm(normed_ref[...], dup, TN)
    down_ref[...] = mm(active_ref[...], dlow_ref[...], TN)
    bias = jnp.sum(dup.astype(F32), axis=0, keepdims=True)
    bias_ref[...] = jnp.broadcast_to(bias, bias_ref.shape)


def ffn_grad_kernel(
    p_ref,
    upa_ref,
    downa_ref,
    biasa_ref,
    normedo_ref,
    activeo_ref,
    dlowo_ref,
    slopeo_ref,
    down_ref,
    upk_ref,
    ups_ref,
    downk_ref,
    downs_ref,
    bias_ref,
    all_ref,
):
    dlowo = dlowo_ref[...]
    dupo = (mm(dlowo, down_ref[...], NT) * slopeo_ref[...].astype(F32)).astype(BF16)
    all_ref[...] = (upa_ref[...] + mm(normedo_ref[...], dupo, TN)).astype(BF16)
    dealt(all_ref, p_ref[1], upk_ref, ups_ref)
    all_ref[...] = (downa_ref[...] + mm(activeo_ref[...], dlowo, TN)).astype(BF16)
    dealt(all_ref, p_ref[2], downk_ref, downs_ref)
    bias = jnp.sum(dupo.astype(F32), axis=0, keepdims=True)
    bias_ref[...] = biasa_ref[...] + jnp.broadcast_to(bias, bias_ref.shape)


def first_kernel(
    p_ref,
    x_ref,
    mixed0_ref,
    mixed1_ref,
    second_ref,
    hid_ref,
    hidr_ref,
    gain_ref,
    first_ref,
    dmix_ref,
    sums_ref,
):
    unit, spread = centred(residual(x_ref, (mixed0_ref, mixed1_ref)))
    hid = hid_ref[...].astype(F32) + turned(hidr_ref[...], hid_ref.shape[0] // 8).astype(F32)
    dnormed = second_ref[...] + hid
    first = norm_back(unit, spread, dnormed * gain_ref[0:1, :])
    first_ref[...] = first
    dmix_ref[...] = first.astype(BF16)
    sums_ref[...] = jnp.zeros_like(sums_ref)
    sums_ref[0:1, :] = jnp.sum(dnormed * unit, axis=0, keepdims=True)
    sums_ref[1:2, :] = jnp.sum(dnormed, axis=0, keepdims=True)


def attended_kernel(
    p_ref,
    dmix_ref,
    dmixr_ref,
    exit_ref,
    exitp_ref,
    sums1_ref,
    sums2_ref,
    own_ref,
    send_ref,
    total_ref,
    pay_ref,
):
    length = dmix_ref.shape[0]
    rest = length // 4
    total = dmix_ref[...].astype(F32) + turned(dmixr_ref[...], rest).astype(F32)
    total = total.astype(BF16)
    total_ref[...] = total
    own_ref[...] = mm(total, exit_ref[...], NT).astype(BF16)
    send_ref[...] = mm(total, exitp_ref[...], NT).astype(BF16)
    least = rest // 2
    pay_ref[0:least, :] = total[0:least]
    pay_ref[least:rest, :] = total[2 * rest : 2 * rest + least]
    pay_ref[rest:, :] = jnp.concatenate([sums1_ref[...], sums2_ref[...]], axis=0).astype(BF16)


def backward_kernel(
    p_ref,
    datt_ref,
    dattr_ref,
    first_ref,
    soft_hbm,
    proj_ref,
    spat_ref,
    w_ref,
    ws_ref,
    dscore_ref,
    dproj_ref,
    dspat_ref,
    dxk0_ref,
    dxk1_ref,
    dxs_ref,
    dsk0_ref,
    dsk1_ref,
    dss_ref,
    soft_ref,
    sems,
    *,
    heads,
    block,
):
    fetched = [
        pltpu.make_async_copy(soft_hbm.at[h], soft_ref.at[h], sems.at[h]) for h in range(heads)
    ]
    for copy in fetched:
        copy.start()
    length = 2 * datt_ref.shape[0]
    scale = DH**-0.5
    part = length // 4
    datt = stack_rows(
        [datt_ref[0:part, :], dattr_ref[0:part, :], datt_ref[part:, :], dattr_ref[part:, :]]
    )
    for h in range(heads):
        cols = slice(h * DH, (h + 1) * DH)
        value = proj_ref[2, :, cols]
        left = jnp.concatenate([proj_ref[0, :, cols], spat_ref[0, :, cols]], axis=1)
        right = jnp.concatenate([proj_ref[1, :, cols], spat_ref[1, :, cols]], axis=1)
        own = datt[:, cols]
        fetched[h].wait()
        for at in range(0, length, block):
            soft = soft_ref[h, at : at + block, :]
            dsoft = mm(own[at : at + block], value, NT)
            inner = jnp.sum(soft * dsoft, axis=-1, keepdims=True)
            dscore_ref[h, at : at + block, :] = (soft * (dsoft - inner)).astype(BF16)
        dscore = dscore_ref[h]
        dleft = (mm(dscore, right) * scale).astype(BF16)
        dright = (mm(dscore, left, TN) * scale).astype(BF16)
        dproj_ref[0, :, cols] = dleft[:, :DH]
        dspat_ref[0, :, cols] = dleft[:, DH:]
        dproj_ref[1, :, cols] = dright[:, :DH]
        dspat_ref[1, :, cols] = dright[:, DH:]
        dproj_ref[2, :, cols] = mm(soft_ref[h].astype(BF16), own, TN).astype(BF16)
    once = (p_ref[3] == 0).astype(F32)
    total = mm(dproj_ref[0], w_ref[0])
    for k in range(1, 3):
        total = total + mm(dproj_ref[k], w_ref[k])
    least = part // 4

    def deal(rows, refs):
        for y in range(2):
            for zh in range(2):
                for c in range(2):
                    for zl in range(2):
                        at = (((y * 2 + zh) * 2 + c) * 2 + zl) * least
                        to = (zh * 2 + y) * least
                        value = rows[at : at + least]
                        if zh == 0 and refs[0][0] is dxk0_ref:
                            of = ((y * 2 + c) * 2 + zl) * least
                            value = value + once * first_ref[of : of + least, :]
                        refs[c][zl][to : to + least, :] = value.astype(BF16)

    deal(total, ((dxk0_ref, dxk1_ref), (dxs_ref.at[0], dxs_ref.at[1])))
    total = mm(dspat_ref[0], ws_ref[0]) + mm(dspat_ref[1], ws_ref[1])
    deal(total, ((dsk0_ref, dsk1_ref), (dss_ref.at[0], dss_ref.at[1])))


def spatial_grad_kernel(p_ref, sp_ref, dspat_ref, keep_ref, send_ref):
    sp = sp_ref[...].reshape(-1, sp_ref.shape[-1])
    keep_ref[...] = mm(dspat_ref[p_ref[0]], sp, TN).astype(BF16)
    send_ref[...] = mm(dspat_ref[1 - p_ref[0]], sp, TN).astype(BF16)


def second_grad_kernel(
    p_ref,
    dmix_ref,
    pay_ref,
    payr_ref,
    payl_ref,
    payc_ref,
    paylc_ref,
    atto_ref,
    atts_ref,
    rest_ref,
    spk_ref,
    spr_ref,
    lines_ref,
    keep_ref,
    send_ref,
    second_ref,
):
    inner = spk_ref.shape[0]
    length = dmix_ref.shape[0]
    least = length // 8
    rest = 2 * least
    dmixo = stack_rows(
        [
            ref[y * least : (y + 1) * least, :]
            for y in range(2)
            for ref in (payr_ref, payl_ref, payc_ref, paylc_ref)
        ]
    )
    base = rest_ref.shape[0]
    second_ref[0:base, :] = rest_ref[...]
    second_ref[base : base + inner, :] = (
        mm(atto_ref[...], dmix_ref[...], TN) + mm(atts_ref[...], dmixo, TN)
    ).astype(BF16)
    base += inner
    second_ref[base : base + inner, :] = (
        spk_ref[...].astype(F32) + spr_ref[...].astype(F32)
    ).astype(BF16)
    base += inner
    small = pay_ref[rest:, :].astype(F32) + payr_ref[rest:, :].astype(F32)
    second_ref[base : base + 16, :] = small.astype(BF16)
    second_ref[base + 16 : base + 32, :] = lines_ref[...].astype(BF16)
    dealt(second_ref, p_ref[2], keep_ref, send_ref)


def first_grad_kernel(
    p_ref,
    x_ref,
    dscore_ref,
    dproj_ref,
    colidx_ref,
    bup_ref,
    keep_ref,
    send_ref,
    rest_ref,
    lines_ref,
    first_ref,
    *,
    heads,
):
    width = x_ref.shape[-1]
    x = x_ref[...].reshape(-1, width)
    length = x.shape[0]
    inner = dproj_ref.shape[-1]
    for k in range(3):
        first_ref[k * inner : (k + 1) * inner, :] = mm(dproj_ref[k], x, TN).astype(BF16)
    dealt(first_ref, p_ref[1], keep_ref, send_ref)
    rest_ref[...] = first_ref[2 * keep_ref.shape[0] :, :]
    lane = lax.broadcasted_iota(jnp.int32, (1, NBUCK), 1)
    found = []
    for kind in range(3):
        extent = length if kind == 0 else NBUCK
        own = colidx_ref[:, kind : kind + 1]
        level = lax.broadcasted_iota(jnp.int32, (length, extent), 1)
        chosen = (own == level).astype(BF16)
        place = own - HALF + lax.broadcasted_iota(jnp.int32, (length, NBUCK), 1)
        turn = place & (NBUCK - 1)
        piece = place >> 7
        for h in range(heads):
            spread = mm(dscore_ref[h], chosen)
            window = jnp.zeros((length, NBUCK), F32)
            for q in range(extent // NBUCK):
                part = jnp.take_along_axis(
                    spread[:, q * NBUCK : (q + 1) * NBUCK],
                    turn,
                    axis=1,
                    mode="promise_in_bounds",
                )
                window = window + jnp.where(piece == q, part, 0.0)
            row = jnp.sum(window, axis=0, keepdims=True)
            row = jnp.where((lane > 0) & (lane < NBUCK - 1), row, 0.0)
            least = jnp.sum(jnp.where(level <= own - HALF, spread, 0.0), axis=0, keepdims=True)
            most = jnp.sum(jnp.where(level >= own + HALF - 1, spread, 0.0), axis=0, keepdims=True)
            row = row + jnp.where(lane == 0, jnp.sum(least, axis=1, keepdims=True), 0.0)
            row = row + jnp.where(
                lane == NBUCK - 1, jnp.sum(most, axis=1, keepdims=True), 0.0
            )
            found.append(row)
    per = width // NBUCK
    found = found + [jnp.zeros((1, NBUCK), F32)] * (-len(found) % per)
    lines = [
        jnp.concatenate(found[at : at + per], axis=1) for at in range(0, len(found), per)
    ]
    lines.append(bup_ref[0:1, :])
    lines_ref[...] = jnp.concatenate(
        lines + [jnp.zeros((16 - len(lines), width), F32)], axis=0
    )


def ends_kernel(
    p_ref,
    w_ref,
    y_ref,
    zhw_ref,
    zlw_ref,
    zzw_ref,
    tok_ref,
    sp_ref,
    event_ref,
):
    c, y, block = p_ref[0], p_ref[2], p_ref[4] * 2 + p_ref[3]
    for turn, ref in enumerate((None, zlw_ref, zhw_ref, zzw_ref)):
        at = block ^ turn
        for far in range(2):
            for unit in range(3):
                if ref is None:
                    value = (y_ref if far else w_ref)[unit]
                else:
                    value = ref[far, unit]
                value = value.astype(F32)
                if unit < 2:
                    tok_ref[c ^ unit, y ^ far, at] = value
                else:
                    sp_ref[y ^ far, at] = value
    event_ref[...] = jnp.zeros_like(event_ref)


def out_kernel(p_ref, *refs):
    c, y, block = p_ref[0], p_ref[2], p_ref[4] * 2 + p_ref[3]
    out_ref, event_ref = refs[8:]
    least = out_ref.shape[3]
    for half in range(2):
        for far in range(2):
            for unit in range(2):
                ref = refs[half * 4 + far * 2 + unit]
                for turn in range(2):
                    at = block ^ (half * 2 + turn)
                    out_ref[c ^ unit, y ^ far, at] = ref[turn * least : (turn + 1) * least, :]
    event_ref[...] = jnp.zeros_like(event_ref)


def turn_kernel(p_ref, own_ref, far_ref, sum_ref, *, size):
    far = turned(far_ref[...], size).astype(F32)
    sum_ref[...] = (own_ref[...].astype(F32) + far).astype(BF16)


def plus_kernel(p_ref, *refs):
    count = len(refs) // 3
    for n in range(count):
        total = refs[2 * n][...].astype(F32) + refs[2 * n + 1][...].astype(F32)
        refs[2 * count + n][...] = total.astype(BF16)


def units_kernel(
    p_ref, own0_ref, own1_ref, other_ref, near_ref, far_ref, spat_ref, nears_ref, fars_ref
):
    nears_ref[0] = own0_ref[...]
    fars_ref[0] = own1_ref[...]
    nears_ref[1] = other_ref[0]
    fars_ref[1] = other_ref[1]
    nears_ref[2] = (near_ref[...].astype(F32) + spat_ref[0].astype(F32)).astype(BF16)
    fars_ref[2] = (far_ref[...].astype(F32) + spat_ref[1].astype(F32)).astype(BF16)


def fold_kernel(p_ref, own_ref, far_ref, keep_ref, send_ref):
    total = (own_ref[...].astype(F32) + far_ref[...].astype(F32)).astype(BF16)
    half = total.shape[-2] // 2
    keep_ref[...] = total[..., :half, :]
    send_ref[...] = total[..., half:, :]


def ends_first_kernel(p_ref, keep_ref, far_ref, mine_ref, other_ref):
    least = mine_ref.shape[1]
    total = (keep_ref[...].astype(F32) + far_ref[...].astype(F32)).astype(BF16)
    mine_ref[...] = total[:, :least]
    other_ref[...] = total[:, least:]


def spread_kernel(p_ref, *refs):
    c = p_ref[0]
    event_ref = refs[10]
    for n, out_ref in enumerate(refs[8:10]):
        side = p_ref[1 + n]
        for other in range(2):
            for far in range(2):
                out_ref[c ^ other, side ^ far] = refs[n * 4 + other * 2 + far][...].astype(F32)
    event_ref[...] = jnp.zeros_like(event_ref)


def last_kernel(
    p_ref,
    one0_ref,
    one1_ref,
    one2_ref,
    one3_ref,
    two0_ref,
    two1_ref,
    two2_ref,
    two3_ref,
    qkv_ref,
    spat_ref,
    exit_ref,
    tables_ref,
    gains_ref,
    shifts_ref,
    bup_ref,
    bdown_ref,
    second_ref,
    *,
    heads,
):
    c, head = p_ref[0], p_ref[4] * 2 + p_ref[3]
    inner = exit_ref.shape[1]
    width = exit_ref.shape[2]
    part = gains_ref.shape[2]
    per = width // NBUCK
    firsts = ((one0_ref, one1_ref), (one2_ref, one3_ref))
    seconds = ((two0_ref, two1_ref), (two2_ref, two3_ref))
    for other in range(2):
        s = c ^ other
        for far in range(2):
            size = one0_ref.shape[0]
            at = pl.multiple_of((p_ref[1] ^ far) * size, 16)
            qkv_ref[s, pl.ds(at, size), :] = firsts[other][far][...].astype(F32)
            size = two0_ref.shape[0]
            at = pl.multiple_of((p_ref[2] ^ far) * size, 16)
            second_ref[pl.ds(at, size), :] = seconds[other][far][...].astype(F32)
        base = 3 * inner - 2 * one0_ref.shape[0]
        qkv_ref[s, 2 * one0_ref.shape[0] :, :] = second_ref[0:base, :]
        exit_ref[s] = second_ref[base : base + inner, :]
        base += inner
        spat_ref[s] = second_ref[base : base + inner, :]
        base += inner
        sums = second_ref[base : base + 16, :]
        cut = sums[:, 0:part]
        for at in range(1, width // part):
            cut = jnp.where(head == at, sums[:, at * part : (at + 1) * part], cut)
        gains_ref[s] = jnp.concatenate([cut[0:1], cut[8:9]], axis=0)
        shifts_ref[s] = jnp.concatenate([cut[1:2], cut[9:10]], axis=0)
        bdown_ref[pl.ds(s, 1), :] = cut[10:11]
        lines = second_ref[base + 16 : base + 32, :]
        for n in range(3 * heads):
            at = (n % per) * NBUCK
            tables_ref[n // heads, n % heads, pl.ds(s, 1), :] = lines[
                n // per : n // per + 1, at : at + NBUCK
            ]
        bup_ref[pl.ds(s, 1), :] = lines[2:3]


def swap(value, axis, step=1):
    size = lax.axis_size(axis)
    return lax.ppermute(value, axis, [(i, i ^ step) for i in range(size)])


def swap_both(value):
    size = lax.axis_size("batch") * 2
    return lax.ppermute(value, ("batch", "y"), [(i, i ^ 3) for i in range(size)])


def added(left, right):
    return (left.astype(F32) + right.astype(F32)).astype(BF16)


def batch_steps():
    return [1 << bit for bit in range(lax.axis_size("batch").bit_length() - 1)]


def join(*values):
    return lax.optimization_barrier(values)


def shards(
    tokens,
    spatial,
    positions,
    boxes,
    query_key_value_weight,
    w_spatial,
    rel_tables,
    exit_matrix,
    ln_gains,
    ln_shifts,
    up_weight,
    hidden_bias,
    shrink_projection_array,
    b_down,
    cotangent,
):
    heads = rel_tables.shape[2]
    rows = tokens.shape[2]
    width = tokens.shape[3]
    inner = query_key_value_weight.shape[3]
    hidden = up_weight.shape[2]
    least = rows // 4
    rest = rows // 2
    length = 4 * rows
    half = length // 2
    page = lax.axis_index("y")
    core = lax.axis_index("core")
    zh = lax.axis_index("zh")
    zl = lax.axis_index("zl")
    pair = lax.axis_index("batch") & 1
    place = jnp.stack([core, pair, page, zl, zh]).astype(jnp.int32)

    times = iter(TIMES)

    def run(body, operands, outs, scratch=(), after=(), vmem=VMEM_BYTES):
        return kernel_call(body, place, operands, outs, next(times), scratch, after, vmem)

    def rows_of(count, dtype=BF16):
        return ((count, width), dtype)

    share = hidden // 4
    far0, far1, far2, near, x00, up_part, down_part = run(
        pack_kernel,
        [
            (tokens.reshape(2, 2, 4, least, width), "any"),
            (spatial.reshape(2, 4, least, width), "any"),
            (positions, "any"),
            (boxes, "any"),
            (exit_matrix, "any"),
            (up_weight, "any"),
            (shrink_projection_array, "any"),
            (hidden_bias, "any"),
        ],
        [
            rows_of(rows + 16),
            rows_of(rows),
            rows_of(rows),
            rows_of(2 * rows + 16),
            rows_of(rows),
            rows_of(share + 16 + inner // 4),
            rows_of(share),
        ],
        scratch=[
            pltpu.VMEM(positions.shape, jnp.int32),
            pltpu.VMEM(boxes.shape, jnp.int32),
            pltpu.VMEM(hidden_bias.shape, F32),
            pltpu.SemaphoreType.DMA((30,)),
        ],
        vmem=PACK_VMEM,
    )
    up_part = swap(up_part, "zh")
    i10, s10, x10 = swap(far0, "y"), swap(far1, "y"), swap(far2, "y")
    cot_far, cot_near, cot00 = run(
        cotangent_kernel,
        [(cotangent.reshape(2, 2, 4, least, width), "any")],
        [((2, rows, width), BF16), rows_of(rows), rows_of(rows)],
        scratch=[pltpu.SemaphoreType.DMA((16,))],
        vmem=PACK_VMEM,
        after=[x00],
    )
    n01 = swap(near, "core")
    weights = (jnp.swapaxes(query_key_value_weight, 2, 3), "stream")
    spatial_weights = jnp.swapaxes(w_spatial, 1, 2)
    x0, sp0, index0, proj0, spat0, up, down, exit_own = run(
        near_kernel,
        [
            x00,
            n01,
            near,
            weights,
            spatial_weights,
            (up_weight, "any"),
            (shrink_projection_array, "any"),
            (exit_matrix, "any"),
        ],
        [
            ((2, rows, width), BF16),
            ((2, rows, width), BF16),
            ((8, 2 * rows), jnp.int32),
            ((3, 2 * rows, inner), BF16),
            ((2, 2 * rows, inner), BF16),
            ((width, hidden), BF16),
            ((hidden, width), BF16),
            rows_of(inner),
        ],
        scratch=[pltpu.SemaphoreType.DMA((3,))],
        after=[cot00],
    )
    i10, s10, x10, x0, up_part, down_part = join(i10, s10, x10, x0, up_part, down_part)
    x11, s11 = swap(i10, "core"), swap(s10, "core")
    ups = [up_part, swap(up_part, "y"), swap(up_part, "batch"), swap_both(up_part)]
    down_part = swap(down_part, "zh")

    x, sp, colidx, proj, spat, soft, att_own, att_send = run(
        functools.partial(attention_kernel, heads=heads),
        [
            x10,
            x11,
            s10,
            s11,
            i10,
            x0,
            sp0,
            index0,
            proj0,
            spat0,
            weights,
            spatial_weights,
            (rel_tables, "stream"),
        ],
        [
            ((2, 2, rows, width), BF16),
            ((2, 2, rows, width), BF16),
            ((length, 8), jnp.int32),
            ((3, length, inner), BF16, "any"),
            ((2, length, inner), BF16, "any"),
            ((heads, length, length), F32, "any"),
            ((half, inner), BF16),
            ((half, inner), BF16),
        ],
        scratch=[
            pltpu.VMEM((length, inner), BF16),
            pltpu.VMEM((3, length, inner), BF16),
            pltpu.VMEM((2, length, inner), BF16),
            pltpu.VMEM((heads, length, length), F32),
            pltpu.SemaphoreType.DMA((2 + heads,)),
        ],
    )
    att_recv = swap(att_send, "zh")
    att_own, down_part, *ups = join(att_own, down_part, *ups)
    downs = [down_part, swap(down_part, "y"), swap(down_part, "batch"), swap_both(down_part)]

    keep, send, exit_partner = run(
        mixed_kernel,
        [att_own, att_recv, exit_own, *ups],
        [rows_of(rows, F32), rows_of(rows), rows_of(inner)],
    )
    (mixed0,) = run(
        plus_kernel, [keep, swap(send, "core")], [rows_of(rows)], after=downs[1:3]
    )
    mixed_zl = swap(mixed0, "zl")
    (mixed0,) = run(
        functools.partial(turn_kernel, size=least), [mixed0, mixed_zl], [rows_of(rows)]
    )
    mixed1 = swap(mixed0, "core")
    mixed_far0 = swap(mixed0, "zh")
    mixed1, *downs = join(mixed1, *downs)

    gains = (ln_gains, "stream")
    shifts = (ln_shifts, "stream")
    x_own = (x, (None, 0, None, None))
    x_far = (x, (None, 1, None, None))
    low, normed, active, slope, up_partner, down_partner = run(
        forward_kernel,
        [x_own, mixed0, mixed1, gains, shifts, up, hidden_bias, down, *ups, *downs],
        [
            rows_of(half),
            rows_of(half),
            ((2, half, hidden), BF16),
            ((2, half, hidden), BF16),
            ((width, hidden), BF16),
            ((hidden, width), BF16),
        ],
    )
    low_recv = swap(low, "zl")
    cot_far, cot_near, mixed0 = join(cot_far, cot_near, mixed0)
    cot10 = swap(cot_far, "y")
    cot01 = swap(cot_near, "core")
    mixed_far1 = swap(mixed_far0, "core")
    cot11 = swap(cot10, "core")
    (normed_far,) = run(
        first_norm_kernel,
        [x_far, mixed_far0, mixed_far1, gains, shifts],
        [rows_of(half)],
        after=[low],
    )
    active_far, slope_far = run(
        other_kernel,
        [normed_far, up, hidden_bias],
        [((half, hidden), BF16), ((half, hidden), BF16)],
    )
    low0, low1 = run(
        lowered_kernel, [low, low_recv], [rows_of(rows), rows_of(rows)], after=[slope_far]
    )
    far_low0 = swap(low0, "zh")

    def finish(x_half, pieces, part, after=()):
        rows_part = slice(part * rest, (part + 1) * rest)
        cots = [
            cot00[rows_part],
            cot10[0, rows_part],
            cot01[rows_part],
            cot11[1, rows_part],
        ]
        return run(
            final_kernel,
            [x_half, *pieces, *cots, gains, shifts, b_down],
            [
                ((2, rest, width), BF16),
                ((2, rest, width), BF16),
                rows_of(half, F32),
                rows_of(half),
                rows_of(8, F32),
            ],
            after=after,
        )

    out_keep, out_send, second, dlow, sums_two = finish(x_own, [mixed0, mixed1, low0, low1], 0)
    hid, dup = run(
        middle_kernel,
        [dlow, up, down, up_partner, down_partner, slope],
        [rows_of(half), ((half, hidden), BF16)],
    )
    hid_recv = swap(hid, "zl")
    up_own, down_own, bias_own = run(
        ffn_own_kernel,
        [normed, (active, (0, None, None)), dlow, dup],
        [((width, hidden), F32), rows_of(hidden, F32), ((8, hidden), F32)],
        after=[hid],
    )
    out_core = swap(out_send, "core")
    out_y = swap(jnp.stack([out_keep[1], out_core[1]]), "y")
    hid_recv, far_low0, out_y = join(hid_recv, far_low0, out_y)
    far_low1 = swap(far_low0, "zl")
    first, dmix, sums_one = run(
        first_kernel,
        [x_own, mixed0, mixed1, second, hid, hid_recv, gains],
        [rows_of(half, F32), rows_of(half), rows_of(8, F32)],
        after=[bias_own],
    )
    dmix_core = swap(dmix, "core")
    datt, datt_send, dmix, pay = run(
        attended_kernel,
        [dmix, dmix_core, exit_own, exit_partner, sums_one, sums_two],
        [
            ((half, inner), BF16),
            ((half, inner), BF16),
            rows_of(half),
            rows_of(rest + 16),
        ],
    )
    datt_recv = swap(datt_send, "zh")
    far_keep, far_send, _, dlow_far, _ = finish(
        x_far, [mixed_far0, mixed_far1, far_low0, far_low1], 1, [datt]
    )
    up_keep, up_send, down_keep, down_send, bias_grad = run(
        ffn_grad_kernel,
        [
            up_own,
            down_own,
            bias_own,
            normed_far,
            active_far,
            dlow_far,
            slope_far,
            down,
        ],
        [
            ((width // 2, hidden), BF16),
            ((width // 2, hidden), BF16),
            rows_of(hidden // 2),
            rows_of(hidden // 2),
            ((8, hidden), F32),
        ],
        scratch=[pltpu.VMEM((width, hidden), BF16)],
        after=[datt],
    )
    up_recv = swap(up_send, "batch")
    down_recv = swap(down_send, "y")
    datt_recv, pay = join(datt_recv, pay)
    pay_recv = swap(pay, "zh")
    piece = rows_of(rows)
    dscore, dproj, dspat, dxk0, dxk1, dxs, dsk0, dsk1, dss = run(
        functools.partial(backward_kernel, heads=heads, block=128),
        [datt, datt_recv, first, (soft, "any"), proj, spat, weights, spatial_weights],
        [
            ((heads, length, length), BF16),
            ((3, length, inner), BF16),
            ((2, length, inner), BF16),
            piece,
            piece,
            ((2, rows, width), BF16),
            piece,
            piece,
            ((2, rows, width), BF16),
        ],
        scratch=[pltpu.VMEM((heads, length, length), F32), pltpu.SemaphoreType.DMA((heads,))],
        after=[bias_grad],
    )

    steps = batch_steps()[1:]

    def plus(pairs, after=(), over_batch=False):
        sums = run(
            plus_kernel,
            [array for pair_of in pairs for array in pair_of],
            [(left.shape, BF16) for left, _ in pairs],
            after=after,
        )
        if over_batch:
            for step in steps:
                sums = [added(value, swap(value, "batch", step)) for value in sums]
        return sums

    dxk1, dxs, dss, pay_recv = join(dxk1, dxs, dss, pay_recv)
    dxs, dss = swap(dxs, "core"), swap(dss, "core")
    near, far = run(
        units_kernel,
        [dxk0, dxk1, dxs, dsk0, dsk1, dss],
        [((3, rows, width), BF16), ((3, rows, width), BF16)],
    )
    far_zl = swap(far, "zl")
    up_half, down_half = plus([(up_keep, up_recv), (down_keep, down_recv)], after=[far])
    up_other = swap(up_half, "y")
    down_other = swap(down_half, "batch")
    pay_zl = swap(join(pay_recv, far)[0], "zl")
    few = inner // 2
    main = 3 * inner - few
    sp_keep, sp_send = run(
        spatial_grad_kernel, [sp, dspat], [rows_of(inner), rows_of(inner)], after=[up_half]
    )
    sp_recv = swap(sp_send, "core")
    one_keep, one_send, value_rest, lines = run(
        functools.partial(first_grad_kernel, heads=heads),
        [x, dscore, dproj, colidx, bias_grad],
        [rows_of(main // 2), rows_of(main // 2), rows_of(few), rows_of(16, F32)],
        scratch=[pltpu.VMEM((3 * inner, width), BF16)],
        after=[sp_keep],
    )
    keep, send = run(
        fold_kernel,
        [near, far_zl],
        [((3, rest, width), BF16), ((3, rest, width), BF16)],
        after=[lines],
    )
    send_zh = swap(send, "zh")
    up_half, down_half = plus(
        [(up_half, up_other), (down_half, down_other)], after=[send], over_batch=True
    )
    up_far = swap(up_half, "batch")
    down_far = swap(down_half, "y")
    mine, other = run(
        ends_first_kernel,
        [keep, send_zh],
        [((3, least, width), BF16), ((3, least, width), BF16)],
        after=[up_half],
    )
    got = swap(other, "y")
    pay_recv, pay_zl, far_send, send = join(pay_recv, pay_zl, far_send, send)
    pay_core, pay_zlcore = swap(pay_recv, "core"), swap(pay_zl, "core")
    far_core = swap(far_send, "core")
    base = few + 2 * inner + 32
    two_keep, two_send = run(
        second_grad_kernel,
        [
            dmix,
            pay,
            pay_recv,
            pay_zl,
            pay_core,
            pay_zlcore,
            att_own,
            att_send,
            value_rest,
            sp_keep,
            sp_recv,
            lines,
        ],
        [rows_of(base // 2), rows_of(base // 2)],
        scratch=[pltpu.VMEM((base, width), BF16)],
        after=[mine, up_far, down_far],
    )
    one_send, two_send, got, two_keep = join(one_send, two_send, got, two_keep)
    one_recv = swap(one_send, "batch")
    two_recv = swap(two_send, "y")
    pages = jnp.stack([mine, got])
    pages_zh = swap(pages, "zh")
    pages_zl = swap(pages, "zl")
    *halves, pages = join(up_half, up_far, down_half, down_far, pages)
    others = [swap(value, "core") for value in halves]
    grad_up, grad_down, spread_event = run(
        spread_kernel,
        halves[:2] + others[:2] + halves[2:] + others[2:],
        [
            ((2, 2, width // 2, hidden), F32),
            ((2, 2, hidden // 2, width), F32),
            ((8, NBUCK), F32),
        ],
        after=[pages],
    )
    one_half, two_half = plus(
        [(one_keep, one_recv), (two_keep, two_recv)], after=[spread_event]
    )
    one_other = swap(one_half, "y")
    two_other = swap(two_half, "batch")
    far_y = swap(jnp.stack([far_keep[1], far_core[1]]), "y")
    pages_zh, pages_zl = join(pages_zh, pages_zl)
    pages_zz = swap(pages_zh, "zl")
    one_half, two_half = plus(
        [(one_half, one_other), (two_half, two_other)],
        after=[pages_zz],
        over_batch=True,
    )
    one_far = swap(one_half, "batch")
    two_far = swap(two_half, "y")
    grad_tokens, grad_spatial, ends_event = run(
        ends_kernel,
        [mine, got, pages_zh, pages_zl, pages_zz],
        [((2, 2, 4, least, width), F32), ((2, 4, least, width), F32), ((8, NBUCK), F32)],
        after=[one_half],
    )
    output, out_event = run(
        out_kernel,
        [
            out_keep[0],
            out_core[0],
            out_y[0],
            out_y[1],
            far_keep[0],
            far_core[0],
            far_y[0],
            far_y[1],
        ],
        [((2, 2, 4, least, width), BF16), ((8, NBUCK), F32)],
        after=[one_half],
    )
    one_far, two_far, out_event, ends_event = join(one_far, two_far, out_event, ends_event)
    halves = [one_half, one_far, two_half, two_far]
    others = [swap(value, "core") for value in halves]
    part = width // (2 * lax.axis_size("zh"))
    grad_qkv, grad_spatial_w, grad_exit, tables, gains_grad, shifts_grad, grad_b_up, grad_b_down = run(
        functools.partial(last_kernel, heads=heads),
        halves[:2] + others[:2] + halves[2:] + others[2:],
        [
            ((2, 3 * inner, width), F32),
            ((2, inner, width), F32),
            ((2, inner, width), F32),
            ((3, heads, 2, NBUCK), F32),
            ((2, 2, part), F32),
            ((2, 2, part), F32),
            ((2, hidden), F32),
            ((2, part), F32),
        ],
        scratch=[pltpu.VMEM((base, width), F32)],
        after=[spread_event, out_event, ends_event],
    )
    return (
        output.reshape(tokens.shape),
        grad_tokens.reshape(tokens.shape),
        grad_spatial.reshape(spatial.shape),
        grad_qkv.reshape(2, 3, inner, width).swapaxes(2, 3),
        grad_spatial_w.reshape(2, inner, width).swapaxes(1, 2),
        tables.transpose(2, 0, 1, 3),
        grad_exit,
        gains_grad,
        shifts_grad,
        grad_up.reshape(2, width, hidden),
        grad_b_up,
        grad_down.reshape(2, hidden, width),
        grad_b_down,
    )


def solution(mesh):
    batch, seq, head = mesh.devices.shape
    fine = Mesh(
        mesh.devices.reshape(batch, seq // 2, 2, head // 2, 2),
        ("batch", "y", "core", "zh", "zl"),
    )
    seq = ("y", "core")
    head = ("zh", "zl")
    return jax.shard_map(
        shards,
        mesh=fine,
        in_specs=(
            P(None, "batch", seq, None),
            P("batch", seq, None),
            P("batch", seq),
            P(None, "batch", seq),
            P(None, None, None, head),
            P(None, None, head),
            P(None, None, head, None),
            P(None, head, None),
            P(),
            P(),
            P(None, None, head),
            P(None, head),
            P(None, head, None),
            P(),
            P(None, "batch", seq, None),
        ),
        out_specs=(
            P(None, "batch", seq, None),
            P(None, "batch", seq, None),
            P("batch", seq, None),
            P(None, None, None, head),
            P(None, None, head),
            P(None, None, head, None),
            P(None, head, None),
            P(None, None, head),
            P(None, None, head),
            P(None, None, head),
            P(None, head),
            P(None, head, None),
            P(None, head),
        ),
        check_vma=False,
    )
```
